32 devices in a mesh: rep: 2 (over y), ep: 16 (over z, x, core).
Axes of the slice: x: 2, y: 2, z: 4, core: 2. Of those that a mesh axis runs over, the one named last changes fastest.
Arguments:
- out_grad: bfloat16 [8192, 3584], P(('rep', 'ep')), may hold values from -0.8984375 to 0.8984375
- expert_ids: int32 [8192, 8], P(('rep', 'ep')), may hold values from 0 to 127, as said below
- slots: int32 [8192, 8], P(('rep', 'ep')), may hold values from -1 to 11, as said below
- gate_weights: bfloat16 [8192, 8], P(('rep', 'ep')), may hold values from 0.049804688 to 0.59765625
- saved_gate_up: bfloat16 [2, 16, 192, 2048], P('rep', 'ep'), may hold values from -6 to 6
- master: float32 [16, 1024, 3584], P('ep', 'rep'), may hold values from -0.1875 to 0.1875
- moment1: bfloat16 [16, 1024, 3584], P('ep', 'rep'), may hold values from -0.59765625 to 0.59765625
- moment2: bfloat16 [16, 1024, 3584], P('ep', 'rep'), may hold values from 0.0009994507 to 0.0099487305
Outputs:
- grad_gate_up: bfloat16 [2, 16, 192, 2048], P('rep', 'ep')
- gate_grad: float32 [8192, 8], P(('rep', 'ep'))
- master_out: float32 [16, 1024, 3584], P('ep', 'rep')
- moment1_out: bfloat16 [16, 1024, 3584], P('ep', 'rep')
- moment2_out: bfloat16 [16, 1024, 3584], P('ep', 'rep')
The draws below stay inside these ranges and needn't reach their ends.
Inputs may be any that keep to these rules, and one draw needn't show every extreme that they name: `expert_ids`: each row names 8 different experts of 0 to 127. Within the rows of one device, the choices naming one expert, taken in order of token then choice, have slots 0, 1, 2 and so on; those from 12 on are -1. Every device has an expert of the window with more than 12 such choices.
All inputs are finite; a program needn't handle non-finite values.
Results may differ from the reference program's by a relative error of at most 0.025.
Values may be sent and summed in bfloat16 or wider, within the bound.
No kernel may reach another device: no remote copies, remote signals or barrier semaphores. Data moves between devices by JAX's collectives and lax.ppermute only.
A program may use at most 128 MiB of HBM per device.

```python
import math
import jax
import jax.numpy as jnp
from jax import lax

DW = 3584
FW = 1024
TOPK = 8
EXP_LOCAL = 8
TOK_DEV = 256
SEND = 12
SLOTS = 192
EXPERTS = 16
TOKENS = 8192
N_REP = 2
N_EP = 16


def route_table(key):
    total_rows = TOK_DEV * N_EP * N_REP
    experts_all = EXP_LOCAL * N_EP
    blocks = N_EP * N_REP
    key_noise, key_level, key_hot = jax.random.split(key, 3)
    noise = jax.random.randint(key_noise, (total_rows, experts_all), 0, 65536)
    level = jax.random.randint(key_level, (experts_all,), 0, 4)
    hot = jax.random.randint(key_hot, (blocks,), 0, N_EP) * EXP_LOCAL
    row_block = jnp.arange(total_rows) // TOK_DEV
    row_inner = jnp.arange(total_rows) % TOK_DEV
    columns = jnp.arange(experts_all)
    planted = (row_inner < SEND + 4)[:, None] & (columns[None, :] == hot[row_block][:, None])
    score = (noise + level[None, :] * 1024) * 256 + columns[None, :] + planted.astype(jnp.int32) * (1 << 27)
    chosen = lax.top_k(score, TOPK)[1]
    return chosen.astype(jnp.int32)


def draw_expert_ids(key, part):
    return route_table(key)


def draw_slots(key, part):
    chosen = route_table(key)
    experts_all = EXP_LOCAL * N_EP
    blocks = N_EP * N_REP
    flat = chosen.reshape(blocks, TOK_DEV * TOPK)

    def block_slots(block_ids):
        onehot = (block_ids[:, None] == jnp.arange(experts_all)[None, :]).astype(jnp.int32)
        rank = jnp.cumsum(onehot, axis=0) - 1
        mine = jnp.sum(rank * onehot, axis=1)
        return jnp.where(mine < SEND, mine, -1).astype(jnp.int32)
    result = lax.map(block_slots, flat)
    return result.reshape(TOK_DEV * N_EP * N_REP, TOPK)


def levels(rng, dims, cuts, low, high):
    level, own = 1.0, jax.random.fold_in(rng, 6)
    for dim, shards_of in cuts:
        steps = jnp.exp(jax.random.uniform(jax.random.fold_in(own, dim), (shards_of,), jnp.float32, low / len(cuts), high / len(cuts)))
        level = level * jnp.repeat(steps, dims[dim] // shards_of).reshape([-1 if axis == dim else 1 for axis in range(len(dims))])
    return level


def scatter_about(rng, dims, width, limit, cuts=(), held_as=jnp.bfloat16):
    loudness = levels(rng, dims, cuts, -0.22, 0.18) if cuts else 1.0
    array = jax.random.normal(rng, dims, jnp.float32) * width * loudness
    return jnp.minimum(jnp.maximum(array, -limit), limit).astype(held_as)


def setup_inputs(seed: int = 0) -> dict:
    keys = jax.random.split(jax.random.key(seed), 9)
    out_grad = scatter_about(keys[0], (TOKENS, DW), 0.15, 0.8984375, ((0, 32),))
    expert_ids = draw_expert_ids(jax.random.fold_in(keys[8], 71), 0)
    slots = draw_slots(jax.random.fold_in(keys[8], 71), 0)
    gate_weights = jnp.clip(0.049804688 + 0.54785156 * jax.random.uniform(keys[3], (TOKENS, TOPK), jnp.float32) ** levels(keys[3], (TOKENS, TOPK), ((0, 32),), -0.2, 0.2), 0.049804688, 0.59765625).astype(jnp.bfloat16)
    saved_gate_up = scatter_about(keys[4], (N_REP, EXPERTS, SLOTS, 2 * FW), 1.0, 6.0, ((0, 2), (1, 16)))
    master = scatter_about(keys[5], (EXPERTS, FW, DW), FW ** -0.5, 0.1875, ((0, 16), (1, 2)), jnp.float32)
    moment1 = scatter_about(keys[6], (EXPERTS, FW, DW), 0.1, 0.59765625, ((0, 16), (1, 2)))
    moment2 = jnp.clip(jnp.exp(math.log(0.0099487305) - 2.2979944 * jax.random.uniform(keys[7], (EXPERTS, FW, DW), jnp.float32) ** levels(keys[7], (EXPERTS, FW, DW), ((0, 16), (1, 2)), -0.2, 0.2)), 0.0009994507, 0.0099487305).astype(jnp.bfloat16)
    return {"out_grad": out_grad, "expert_ids": expert_ids, "slots": slots, "gate_weights": gate_weights, "saved_gate_up": saved_gate_up, "master": master, "moment1": moment1, "moment2": moment2}


beta_one = 0.9
beta_two = 0.95
learn_rate = 0.002
decay_rate = 0.1
adam_eps = 1e-08
adam_step = 50

def swiglu_backward(gate_up, weights, grad_proj):
    half_width = gate_up.shape[-1] // 2
    gate_part = gate_up[..., :half_width].astype(jnp.float32)
    up_part = gate_up[..., half_width:].astype(jnp.float32)
    sigmoid_gate = jax.nn.sigmoid(gate_part)
    silu_gate = gate_part * sigmoid_gate
    hidden = lax.optimization_barrier((silu_gate * up_part).astype(jnp.bfloat16))
    scale = weights.astype(jnp.float32)[..., None]
    scaled = (scale * hidden.astype(jnp.float32)).astype(jnp.bfloat16)
    grad_hidden = scale * grad_proj
    d_gate = grad_hidden * up_part * sigmoid_gate * (1.0 + gate_part * (1.0 - sigmoid_gate))
    d_up = grad_hidden * silu_gate
    return (hidden, scaled, jnp.concatenate([d_gate, d_up], axis=-1).astype(jnp.bfloat16))

def adamw(master, moment1, moment2, grad):
    m_new = beta_one * moment1.astype(jnp.float32) + (1.0 - beta_one) * grad
    v_new = beta_two * moment2.astype(jnp.float32) + (1.0 - beta_two) * grad * grad
    corr_one = 1.0 - beta_one ** adam_step
    corr_two = 1.0 - beta_two ** adam_step
    update = m_new / corr_one / (jnp.sqrt(v_new / corr_two) + adam_eps)
    master_new = master - learn_rate * (update + decay_rate * master)
    return (master_new, m_new.astype(jnp.bfloat16), v_new.astype(jnp.bfloat16))

def reference(out_grad, expert_ids, slots, gate_weights, saved_gate_up, master, moment1, moment2):
    rows_rep = N_EP * TOK_DEV
    dump = EXPERTS * SLOTS
    weight_bf = lax.optimization_barrier(master.astype(jnp.bfloat16))
    weight_f = weight_bf.astype(jnp.float32)
    grads = out_grad.reshape(N_REP, rows_rep, DW)
    id_all = expert_ids.reshape(N_REP, rows_rep, TOPK)
    slot_all = slots.reshape(N_REP, rows_rep, TOPK)
    weight_all = gate_weights.reshape(N_REP, rows_rep, TOPK)

    def one_replica(total, pieces):
        grad_rows, id_rows, slot_rows, weight_rows, gate_up = pieces
        live = (id_rows % EXP_LOCAL == 0) & (slot_rows >= 0)
        source = (jnp.arange(rows_rep, dtype=jnp.int32) // TOK_DEV)[:, None]
        position = jnp.where(live, id_rows // EXP_LOCAL * SLOTS + source * SEND + slot_rows, dump).astype(jnp.int32)
        token_of = jnp.broadcast_to(jnp.arange(rows_rep, dtype=jnp.int32)[:, None], position.shape)
        source_row = jnp.full((dump + 1,), rows_rep, jnp.int32).at[position.reshape(-1)].set(token_of.reshape(-1))[:dump]
        padded = jnp.concatenate([grad_rows, jnp.zeros((1, DW), grad_rows.dtype)], axis=0)
        dout = padded[source_row].reshape(EXPERTS, SLOTS, DW)
        slot_weight = jnp.zeros((dump + 1,), weight_rows.dtype).at[position.reshape(-1)].set(weight_rows.reshape(-1))
        slot_weight = slot_weight[:dump].reshape(EXPERTS, SLOTS)
        dout_f = dout.astype(jnp.float32)
        grad_proj = jnp.einsum('esd,efd->esf', dout_f, weight_f, precision=lax.Precision.HIGHEST)
        hidden, scaled, grad_gate_up = swiglu_backward(gate_up, slot_weight, grad_proj)
        partial_value = jnp.einsum('esf,esd->efd', scaled.astype(jnp.float32), dout_f, precision=lax.Precision.HIGHEST)
        partial_value = lax.optimization_barrier(partial_value.astype(jnp.bfloat16)).astype(jnp.float32)
        expert_out = jnp.einsum('esf,efd->esd', hidden.astype(jnp.float32), weight_f, precision=lax.Precision.HIGHEST)
        expert_out = expert_out.astype(jnp.bfloat16).reshape(dump, DW)
        out_pad = jnp.concatenate([expert_out, jnp.zeros((1, DW), jnp.bfloat16)], axis=0)
        grad_f = grad_rows.astype(jnp.float32)
        scores = [lax.optimization_barrier(jnp.sum(grad_f * out_pad[position[:, which]].astype(jnp.float32), axis=-1)) for which in range(TOPK)]
        gate_grad = jnp.where(live, jnp.stack(scores, axis=1), jnp.zeros((), jnp.float32))
        return (total + partial_value, (grad_gate_up, gate_grad))
    start = jnp.zeros((EXPERTS, FW, DW), jnp.float32)
    grad, outputs = lax.scan(one_replica, start, (grads, id_all, slot_all, weight_all, saved_gate_up))
    grad_gate_up, gate_grad = outputs
    master_out, moment1_out, moment2_out = adamw(master, moment1, moment2, grad)
    return (grad_gate_up, gate_grad.reshape(TOKENS, TOPK), master_out, moment1_out, moment2_out)
```

```python
import functools

import jax
import jax.numpy as jnp
from jax import lax
from jax.experimental import pallas as pl
from jax.experimental.pallas import tpu as pltpu
from jax.sharding import PartitionSpec as P

TOPK = 8
EXP_LOCAL = 8
SEND = 12
LANE = 128
UNIT = 512
ROWS = 16

beta_one = 0.9
beta_two = 0.95
learn_rate = 0.002
decay_rate = 0.1
adam_eps = 1e-08
adam_step = 50

f32 = jnp.float32
bf16 = jnp.bfloat16


def params(mib=48):
    return pltpu.CompilerParams(vmem_limit_bytes=mib * 1024 * 1024)


def cost(flops, nbytes, transcendentals=0):
    return pl.CostEstimate(
        flops=int(flops), bytes_accessed=int(nbytes), transcendentals=int(transcendentals)
    )


def div_send(index):
    return lax.shift_right_logical(index * 10923, 17)


def dispatch_kernel(ids_ref, slots_ref, gates_ref, grad_ref, *out_refs):
    blocks = len(out_refs)
    rows = blocks * ROWS
    me = lax.axis_index("ep")
    ids = ids_ref[...]
    slots = slots_ref[...]
    gates = gates_ref[...].astype(f32)
    tok, width = grad_ref.shape
    part = width // 4
    live = (ids % EXP_LOCAL == 0) & (slots >= 0)
    place = jnp.where(live, ((ids // EXP_LOCAL) ^ me) * ROWS + slots, -1)
    row = lax.broadcasted_iota(jnp.int32, (rows, tok), 0)

    def pick_rows(at):
        pick = jnp.zeros((rows, tok), f32)
        for k in range(TOPK):
            pick = jnp.where(row == at[k : k + 1], gates[k : k + 1], pick)
        return pick.astype(bf16)

    main = pick_rows(place)
    for j in range(3):
        inside = (slots >= 4 * j) & (slots < 4 * j + 4) & live
        tail = pick_rows(jnp.where(inside, place + SEND - 4 * j, -1))
        total = jnp.dot(
            main, grad_ref[:, j * part : (j + 1) * part], preferred_element_type=f32
        )
        total += jnp.dot(tail, grad_ref[:, 3 * part :], preferred_element_type=f32)
        total = total.astype(bf16)
        for k in range(blocks):
            out_refs[k][:, j * part : (j + 1) * part] = total[k * ROWS : (k + 1) * ROWS]


def dispatch(blocks, ids, slots, gates, out_grad):
    tok, width = out_grad.shape
    return pl.pallas_call(
        dispatch_kernel,
        out_shape=[jax.ShapeDtypeStruct((ROWS, width // 4 * 3), bf16)] * blocks,
        compiler_params=params(),
        cost_estimate=cost(2 * blocks * ROWS * tok * width, 4 * tok * width),
    )(ids, slots, gates, out_grad)


def hidden_kernel(gate_up_ref, hidden_ref, coef_gate_ref, coef_up_ref):
    shards, _, part = hidden_ref.shape
    width = shards * part
    for q in range(shards):
        gate = gate_up_ref[:, q * part : (q + 1) * part].astype(f32)
        up = gate_up_ref[:, width + q * part : width + (q + 1) * part].astype(f32)
        sig = jax.nn.sigmoid(gate)
        silu = gate * sig
        hidden_ref[q] = (silu * up).astype(bf16)
        coef_gate_ref[q] = up * sig * (1.0 + gate * (1.0 - sig))
        coef_up_ref[q] = silu


def hidden_parts(gate_up, shards):
    slots, width = gate_up.shape
    part = width // 2 // shards
    shape = (shards, slots, part)
    return pl.pallas_call(
        hidden_kernel,
        out_shape=[
            jax.ShapeDtypeStruct(shape, bf16),
            jax.ShapeDtypeStruct(shape, f32),
            jax.ShapeDtypeStruct(shape, f32),
        ],
        compiler_params=params(),
        cost_estimate=cost(8 * slots * width, 8 * slots * width, slots * width),
    )(gate_up)


def project_kernel(blocks, *refs):
    arrived, (weight_ref, hidden_ref) = refs[:blocks], refs[blocks : blocks + 2]
    rows_ref, proj_ref, send_ref, score_ref = refs[blocks + 2 :]
    me = lax.axis_index("ep")
    count = rows_ref.shape[0]
    part = arrived[0].shape[1] // 3
    stack = jnp.concatenate([ref[...] for ref in arrived], axis=0)
    slot = lax.broadcasted_iota(jnp.int32, (count, blocks * ROWS), 0)
    col = lax.broadcasted_iota(jnp.int32, (count, blocks * ROWS), 1)
    block = div_send(slot)
    inner = slot - SEND * block
    base = (block ^ me) * ROWS
    order = (col == base + inner).astype(f32).astype(bf16)
    rows_ref[:, : 3 * part] = jnp.dot(
        order, stack[:, : 3 * part], preferred_element_type=f32
    ).astype(bf16)
    tail = jnp.zeros((count, part), f32)
    for j in range(3):
        inside = (inner >= 4 * j) & (inner < 4 * j + 4)
        order = jnp.where(inside & (col == base + SEND + inner - 4 * j), 1.0, 0.0).astype(bf16)
        tail += jnp.dot(
            order, stack[:, j * part : (j + 1) * part], preferred_element_type=f32
        )
    rows_ref[:, 3 * part :] = tail.astype(bf16)
    proj = lax.dot_general(
        rows_ref[...], weight_ref[...], (((1,), (1,)), ((), ())), preferred_element_type=f32
    )
    proj_ref[...] = proj
    send_ref[...] = proj.astype(bf16)
    score = jnp.sum(proj * hidden_ref[...].astype(f32), axis=1, keepdims=True)
    slot_of = lax.broadcasted_iota(jnp.int32, (count, LANE), 0)
    lane_of = lax.broadcasted_iota(jnp.int32, (count, LANE), 1)
    spread = jnp.where(slot_of - SEND * div_send(slot_of) == lane_of, score, 0.0)
    block_of = lax.broadcasted_iota(jnp.int32, (blocks, count), 0)
    slot_at = lax.broadcasted_iota(jnp.int32, (blocks, count), 1)
    gather = (div_send(slot_at) == block_of).astype(f32)
    score_ref[...] = jnp.dot(
        gather, spread, precision=lax.Precision.HIGHEST, preferred_element_type=f32
    )


def project(arrived, weight, hidden):
    blocks = len(arrived)
    count = blocks * SEND
    part, width = weight.shape
    return pl.pallas_call(
        functools.partial(project_kernel, blocks),
        out_shape=[
            jax.ShapeDtypeStruct((count, width), bf16),
            jax.ShapeDtypeStruct((count, part), f32),
            jax.ShapeDtypeStruct((count, part), bf16),
            jax.ShapeDtypeStruct((blocks, LANE), f32),
        ],
        compiler_params=params(),
        cost_estimate=cost(4 * count * part * width, 2 * width * (part + 2 * count)),
    )(*arrived, weight, hidden)


def adamw_kernel(hidden_ref, *refs):
    rows_refs, (master_ref, one_ref, two_ref) = refs[:-6], refs[-6:-3]
    master_out, one_out, two_out = refs[-3:]
    count = rows_refs[0].shape[0]
    grad = jnp.dot(hidden_ref[:, :count], rows_refs[0][...], preferred_element_type=f32)
    for s in range(1, len(rows_refs)):
        grad += jnp.dot(
            hidden_ref[:, s * count : (s + 1) * count],
            rows_refs[s][...],
            preferred_element_type=f32,
        )
    m_new = beta_one * one_ref[0].astype(f32) + (1.0 - beta_one) * grad
    v_new = beta_two * two_ref[0].astype(f32) + (1.0 - beta_two) * grad * grad
    corr_one = 1.0 - beta_one**adam_step
    corr_two = 1.0 - beta_two**adam_step
    rate = learn_rate * corr_two**0.5 / corr_one
    root = v_new * lax.rsqrt(v_new) + adam_eps * corr_two**0.5
    keep = 1.0 - learn_rate * decay_rate
    master_out[0] = keep * master_ref[0] - rate * m_new / root
    one_out[0] = m_new.astype(bf16)
    two_out[0] = v_new.astype(bf16)


def adamw(hidden_t, rows, master, one, two):
    part, depth = hidden_t.shape
    count, width = rows[0].shape
    state = pl.BlockSpec((1, part, UNIT), lambda i: (0, 0, i))
    return pl.pallas_call(
        adamw_kernel,
        grid=(width // UNIT,),
        in_specs=[pl.BlockSpec((part, depth), lambda i: (0, 0))]
        + [pl.BlockSpec((count, UNIT), lambda i: (0, i))] * len(rows)
        + [state] * 3,
        out_specs=[state, state, state],
        out_shape=[
            jax.ShapeDtypeStruct(master.shape, f32),
            jax.ShapeDtypeStruct(one.shape, bf16),
            jax.ShapeDtypeStruct(two.shape, bf16),
        ],
        compiler_params=params(),
        cost_estimate=cost(2 * part * depth * width, 16 * part * width, part * width),
    )(hidden_t, *rows, master, one, two)


def gate_up_kernel(place_ref, coef_gate_ref, coef_up_ref, *refs):
    out_ref = refs[-1]
    shards, _, part = coef_gate_ref.shape
    for s in range(shards):
        at = place_ref[s]
        grad = refs[s][...].astype(f32)
        low = pl.multiple_of(at * part, part)
        out_ref[:, pl.ds(low, part)] = (grad * coef_gate_ref[at]).astype(bf16)
        high = pl.multiple_of(shards * part + at * part, part)
        out_ref[:, pl.ds(high, part)] = (grad * coef_up_ref[at]).astype(bf16)


def gate_up_grad(place, coef_gate, coef_up, grads):
    shards, slots, part = coef_gate.shape
    vmem = pl.BlockSpec(memory_space=pltpu.VMEM)
    return pl.pallas_call(
        gate_up_kernel,
        in_specs=[pl.BlockSpec(memory_space=pltpu.SMEM)] + [vmem] * (2 + shards),
        out_specs=vmem,
        out_shape=jax.ShapeDtypeStruct((slots, 2 * shards * part), bf16),
        compiler_params=params(),
        cost_estimate=cost(4 * shards * slots * part, 16 * shards * slots * part),
    )(place, coef_gate, coef_up, *grads)


def score_kernel(ids_ref, slots_ref, gates_ref, score_ref, out_ref):
    shards, blocks, _ = score_ref.shape
    score = score_ref[0]
    for s in range(1, shards):
        score += score_ref[s]
    ids = ids_ref[...]
    slots = slots_ref[...]
    tok = ids.shape[1]
    live = (ids % EXP_LOCAL == 0) & (slots >= 0)
    owner = ids // EXP_LOCAL
    lane = lax.broadcasted_iota(jnp.int32, (LANE, tok), 0)
    block = lax.broadcasted_iota(jnp.int32, (blocks, tok), 0)
    for k in range(TOPK):
        pick = (lane == slots[k : k + 1]).astype(f32)
        value = jnp.dot(score, pick, precision=lax.Precision.HIGHEST, preferred_element_type=f32)
        value = jnp.sum(jnp.where(block == owner[k : k + 1], value, 0.0), axis=0, keepdims=True)
        out_ref[k : k + 1] = jnp.where(
            live[k : k + 1], value / gates_ref[k : k + 1].astype(f32), 0.0
        )


def gate_scores(ids, slots, gates, score):
    return pl.pallas_call(
        score_kernel,
        out_shape=jax.ShapeDtypeStruct(ids.shape, f32),
        compiler_params=params(),
        cost_estimate=cost(1 << 24, 1 << 16),
    )(ids, slots, gates, score)


def exchange_order(blocks):
    half = blocks // 2
    order = [half]
    for k in range(1, half):
        order += [k, half + k]
    return order


def per_device(out_grad, expert_ids, slots, gate_weights, saved_gate_up, master, moment1, moment2):
    ep_size = lax.axis_size("ep")
    rep_size = lax.axis_size("rep")
    me = lax.axis_index("rep")
    ids_t, slots_t, gates_t = expert_ids.T, slots.T, gate_weights.T

    def shift(value, step):
        perm = [(i, (i + step) % rep_size) for i in range(rep_size)]
        return lax.ppermute(value, "rep", perm)

    sends = dispatch(ep_size, ids_t, slots_t, gates_t, out_grad)
    own = [sends[0]] + [None] * (ep_size - 1)
    for k in exchange_order(ep_size):
        own[k] = lax.ppermute(sends[k], "ep", [(i, i ^ k) for i in range(ep_size)])
    arrived = [own] + [[shift(block, s) for block in own] for s in range(1, rep_size)]

    hidden, coef_gate, coef_up = hidden_parts(saved_gate_up[0, 0], rep_size)
    parts = [
        lax.dynamic_index_in_dim(hidden, (me + s) % rep_size, 0, keepdims=False)
        for s in range(rep_size)
    ]
    parts = [parts[0]] + [shift(parts[s], s) for s in range(1, rep_size)]
    hidden_t = jnp.concatenate(parts, axis=0).T
    place = jnp.stack([(me + s) % rep_size for s in range(rep_size)]).astype(jnp.int32)
    weight = master[0].astype(bf16)

    outs = [project(arrived[s], weight, parts[s]) for s in range(rep_size)]
    rows, projs, halves, scores = zip(*outs)
    grads = [projs[0]] + [shift(halves[s], rep_size - s) for s in range(1, rep_size)]

    score = jnp.stack([scores[s] for s in range(rep_size)])
    order = jnp.stack([(me - i) % rep_size for i in range(rep_size)])
    score = jnp.take(score, order, axis=0).reshape(rep_size * ep_size, 1, LANE)
    score = lax.all_to_all(score, ("rep", "ep"), split_axis=0, concat_axis=0, tiled=True)

    done = adamw(hidden_t, rows, master, moment1, moment2)
    grad_gate_up = gate_up_grad(place, coef_gate, coef_up, grads)
    gate_grad = gate_scores(
        ids_t, slots_t, gates_t, score.reshape(rep_size, ep_size, LANE)
    ).T
    return (grad_gate_up.reshape(saved_gate_up.shape), gate_grad) + tuple(done)


def solution(mesh):
    in_specs = (
        P(("rep", "ep"), None),
        P(("rep", "ep"), None),
        P(("rep", "ep"), None),
        P(("rep", "ep"), None),
        P("rep", "ep", None, None),
        P("ep", "rep", None),
        P("ep", "rep", None),
        P("ep", "rep", None),
    )
    out_specs = (
        P("rep", "ep", None, None),
        P(("rep", "ep"), None),
        P("ep", "rep", None),
        P("ep", "rep", None),
        P("ep", "rep", None),
    )
    return jax.shard_map(
        per_device, mesh=mesh, in_specs=in_specs, out_specs=out_specs, check_vma=False
    )
```

```python
import functools

import jax
import jax.numpy as jnp
from jax import lax
from jax.experimental import pallas as pl
from jax.experimental.pallas import tpu as pltpu
from jax.sharding import PartitionSpec as P

TOPK = 8
EXP_LOCAL = 8
SEND = 12
LANE = 128
UNIT = 512
ROWS = 16

beta_one = 0.9
beta_two = 0.95
learn_rate = 0.002
decay_rate = 0.1
adam_eps = 1e-08
adam_step = 50

f32 = jnp.float32
bf16 = jnp.bfloat16
VMEM = pl.BlockSpec(memory_space=pltpu.VMEM)
HBM = pl.BlockSpec(memory_space=pltpu.HBM)


def in_hbm(*arrays):
    return [pltpu.with_memory_space_constraint(array, pltpu.HBM) for array in arrays]


def shape_of(dims, dtype):
    return jax.ShapeDtypeStruct(tuple(dims), dtype)


def params(nbytes):
    mib = min(56, max(12, 4 + 2 * int(nbytes) // 2**20))
    return pltpu.CompilerParams(vmem_limit_bytes=mib * 2**20)


def cost(flops, nbytes, transcendentals=0):
    return pl.CostEstimate(
        flops=int(flops), bytes_accessed=int(nbytes), transcendentals=int(transcendentals)
    )


def div_send(index):
    return lax.shift_right_logical(index * 10923, 17)


def split_width(width):
    units = width // UNIT
    return (units - max(1, round(units * 2 / 7))) * UNIT


def dispatch_kernel(first, ids_hbm, slots_hbm, gates_hbm, grad_hbm, *refs):
    outs, (ids_ref, slots_ref, gates_ref, grad_ref, sems) = refs[:2], refs[2:]
    copies = [
        pltpu.make_async_copy(source, target, sems.at[i])
        for i, (source, target) in enumerate(
            [
                (ids_hbm, ids_ref),
                (slots_hbm, slots_ref),
                (gates_hbm, gates_ref),
                (grad_hbm, grad_ref),
            ]
        )
    ]
    for copy in copies:
        copy.start()
    for copy in copies[:3]:
        copy.wait()
    rows = outs[0].shape[0]
    ids = ids_ref[...]
    slots = slots_ref[...]
    gates = gates_ref[...].astype(f32)
    tok, width = grad_ref.shape
    live = (ids % EXP_LOCAL == 0) & (slots >= 0)
    place = jnp.where(live, (ids // EXP_LOCAL) * ROWS + slots, -1)
    row = lax.broadcasted_iota(jnp.int32, (rows, tok), 0)

    def pick_rows(at):
        pick = jnp.zeros((rows, tok), f32)
        for k in range(TOPK):
            pick = jnp.where(row == at[k : k + 1], gates[k : k + 1], pick)
        return pick.astype(bf16)

    main = pick_rows(place)
    tails = []
    for j in range(3):
        inside = (slots >= 4 * j) & (slots < 4 * j + 4) & live
        tails.append(pick_rows(jnp.where(inside, place + SEND - 4 * j, -1)))
    copies[3].wait()
    for out_ref, low, high in ((outs[1], first, width), (outs[0], 0, first)):
        part = (high - low) // 4
        for j in range(3):
            total = jnp.dot(
                main,
                grad_ref[:, low + j * part : low + (j + 1) * part],
                preferred_element_type=f32,
            )
            total += jnp.dot(
                tails[j], grad_ref[:, low + 3 * part : high], preferred_element_type=f32
            )
            out_ref[:, j * part : (j + 1) * part] = total.astype(bf16)


def dispatch(blocks, first, ids, slots, gates, out_grad):
    tok, width = out_grad.shape
    rows = blocks * ROWS
    return pl.pallas_call(
        functools.partial(dispatch_kernel, first),
        in_specs=[HBM] * 4,
        out_specs=[VMEM] * 2,
        out_shape=[
            shape_of((rows, first // 4 * 3), bf16),
            shape_of((rows, (width - first) // 4 * 3), bf16),
        ],
        scratch_shapes=[
            pltpu.VMEM(ids.shape, jnp.int32),
            pltpu.VMEM(slots.shape, jnp.int32),
            pltpu.VMEM(gates.shape, bf16),
            pltpu.VMEM(out_grad.shape, bf16),
            pltpu.SemaphoreType.DMA((4,)),
        ],
        compiler_params=params(4 * rows * width + 2 * tok * width),
        cost_estimate=cost(2 * rows * tok * width, 4 * tok * width),
    )(*in_hbm(ids, slots, gates, out_grad))


def hidden_kernel(gate_up_ref, after_ref, hidden_ref, coef_gate_ref, coef_up_ref):
    del after_ref
    shards, _, part = hidden_ref.shape
    width = shards * part
    for q in range(shards):
        gate = gate_up_ref[:, q * part : (q + 1) * part].astype(f32)
        up = gate_up_ref[:, width + q * part : width + (q + 1) * part].astype(f32)
        sig = jax.nn.sigmoid(gate)
        silu = gate * sig
        hidden_ref[q] = (silu * up).astype(bf16)
        coef_gate_ref[q] = up * sig * (1.0 + gate * (1.0 - sig))
        coef_up_ref[q] = silu


def hidden_parts(gate_up, shards, after):
    slots, width = gate_up.shape
    shape = (shards, slots, width // 2 // shards)
    return pl.pallas_call(
        hidden_kernel,
        in_specs=[VMEM, pl.BlockSpec(memory_space=pl.ANY)],
        out_shape=[shape_of(shape, bf16), shape_of(shape, f32), shape_of(shape, f32)],
        compiler_params=params(8 * slots * width),
        cost_estimate=cost(8 * slots * width, 8 * slots * width, slots * width),
    )(gate_up, after)


def load_kernel(first, after_ref, master_hbm, one_hbm, two_hbm, *refs):
    del after_ref
    master_ref, one_ref, two_ref, weight_a, weight_b, sems = refs
    part = master_ref.shape[0]
    step = part // 4
    copies = []
    for i in range(4):
        own = pl.ds(i * step, step)
        copies.append(
            pltpu.make_async_copy(master_hbm.at[0, own], master_ref.at[own], sems.at[i])
        )
    copies.append(pltpu.make_async_copy(one_hbm.at[0], one_ref, sems.at[4]))
    copies.append(pltpu.make_async_copy(two_hbm.at[0], two_ref, sems.at[5]))
    for copy in copies:
        copy.start()
    for i in range(4):
        copies[i].wait()
        own = pl.ds(i * step, step)
        weight_a[own, :] = master_ref[own, :first].astype(bf16)
        weight_b[own, :] = master_ref[own, first:].astype(bf16)
    copies[4].wait()
    copies[5].wait()


def load_state(first, master, one, two, after):
    _, part, width = master.shape
    return pl.pallas_call(
        functools.partial(load_kernel, first),
        in_specs=[pl.BlockSpec(memory_space=pl.ANY)] + [HBM] * 3,
        out_specs=[VMEM] * 5,
        out_shape=[
            pltpu.VMEM((part, width), f32),
            pltpu.VMEM((part, width), bf16),
            pltpu.VMEM((part, width), bf16),
            pltpu.VMEM((part, first), bf16),
            pltpu.VMEM((part, width - first), bf16),
        ],
        scratch_shapes=[pltpu.SemaphoreType.DMA((6,))],
        compiler_params=params(0),
        cost_estimate=cost(part * width, 14 * part * width),
    )(after, *in_hbm(master, one, two))


def reorder(arrived, rows_ref):
    count, width = rows_ref.shape
    part = width // 4
    total = arrived.shape[0]
    slot = lax.broadcasted_iota(jnp.int32, (count, total), 0)
    col = lax.broadcasted_iota(jnp.int32, (count, total), 1)
    block = div_send(slot)
    inner = slot - SEND * block
    base = block * ROWS
    order = jnp.where(col == base + inner, 1.0, 0.0).astype(bf16)
    rows_ref[:, : 3 * part] = jnp.dot(order, arrived, preferred_element_type=f32).astype(bf16)
    tail = jnp.zeros((count, part), f32)
    for j in range(3):
        inside = (inner >= 4 * j) & (inner < 4 * j + 4)
        order = jnp.where(inside & (col == base + SEND + inner - 4 * j), 1.0, 0.0).astype(bf16)
        tail += jnp.dot(
            order, arrived[:, j * part : (j + 1) * part], preferred_element_type=f32
        )
    rows_ref[:, 3 * part :] = tail.astype(bf16)


def times_weight(rows_ref, weight_ref):
    return lax.dot_general(
        rows_ref[...], weight_ref[...], (((1,), (1,)), ((), ())), preferred_element_type=f32
    )


def begin_kernel(arrived_ref, weight_ref, *refs):
    hidden_refs, (rows_ref, proj_ref, hidden_t_ref) = refs[:-3], refs[-3:]
    reorder(arrived_ref[...], rows_ref)
    proj_ref[...] = times_weight(rows_ref, weight_ref)
    count = rows_ref.shape[0]
    for s, hidden_ref in enumerate(hidden_refs):
        hidden_t_ref[:, s * count : (s + 1) * count] = (
            hidden_ref[...].astype(f32).T.astype(bf16)
        )


def begin(blocks, arrived, weight, hidden):
    count = blocks * SEND
    part, width = weight.shape
    return pl.pallas_call(
        begin_kernel,
        out_shape=[
            shape_of((count, width), bf16),
            shape_of((count, part), f32),
            shape_of((part, len(hidden) * count), bf16),
        ],
        compiler_params=params(
            2 * (arrived.size + weight.size + count * width) + 6 * count * part * len(hidden)
        ),
        cost_estimate=cost(4 * count * part * width, 2 * width * (part + 2 * count)),
    )(arrived, weight, *hidden)


def finish_kernel(group, blocks, shards, weight_a, weight_b, *refs):
    refs = list(refs)
    own = group[0] == 0
    proj_in = refs.pop(0) if own else None
    peers = [s for s in group if s > 0]
    arrived_a = {s: refs.pop(0) for s in peers}
    arrived_b = {s: refs.pop(0) for s in group}
    hidden = {s: refs.pop(0) for s in group}
    score_ref = refs.pop(0)
    rows_a = {s: refs.pop(0) for s in peers}
    rows_b = {s: refs.pop(0) for s in group}
    proj_out = {s: refs.pop(0) for s in group}
    me = lax.axis_index("rep")
    if len(group) < shards:
        score_ref[...] = jnp.zeros(score_ref.shape, f32)
    count = blocks * SEND
    slot_of = lax.broadcasted_iota(jnp.int32, (count, LANE), 0)
    lane_of = lax.broadcasted_iota(jnp.int32, (count, LANE), 1)
    block_of = lax.broadcasted_iota(jnp.int32, (blocks, count), 0)
    slot_at = lax.broadcasted_iota(jnp.int32, (blocks, count), 1)
    gather = (div_send(slot_at) == block_of).astype(f32)
    for s in reversed(group):
        arrived = arrived_b[s][...]
        reorder(arrived.reshape(blocks * ROWS, arrived.shape[-1]), rows_b[s])
        proj = times_weight(rows_b[s], weight_b)
        if s == 0:
            proj += proj_in[...]
        else:
            reorder(arrived_a[s][...], rows_a[s])
            proj += times_weight(rows_a[s], weight_a)
        proj_out[s][...] = proj.astype(proj_out[s].dtype)
        score = jnp.sum(proj * hidden[s][...].astype(f32), axis=1, keepdims=True)
        spread = jnp.where(slot_of - SEND * div_send(slot_of) == lane_of, score, 0.0)
        score = jnp.dot(
            gather, spread, precision=lax.Precision.HIGHEST, preferred_element_type=f32
        )
        at = lax.rem(me + shards - s, shards)
        score_ref[pl.ds(at * blocks, blocks)] = score.reshape(blocks, 1, LANE)


def finish(group, weight_a, weight_b, proj, arrived_a, arrived_b, hidden):
    blocks, shards, _, packed = arrived_b.shape
    count = blocks * SEND
    part, first = weight_a.shape
    rest = weight_b.shape[1]
    peers = [s for s in group if s > 0]
    args = [weight_a, weight_b] + ([proj] if group[0] == 0 else [])
    args += [arrived_a[s] for s in peers]
    specs = [pl.BlockSpec(arg.shape, lambda i: (0, 0)) for arg in args]
    for s in group:
        args.append(arrived_b)
        specs.append(
            pl.BlockSpec((blocks, 1, ROWS, packed), lambda i, s=s: (0, s, 0, 0))
        )
    for s in group:
        args.append(hidden[s])
        specs.append(pl.BlockSpec(hidden[s].shape, lambda i: (0, 0)))
    out = [shape_of((shards * blocks, 1, LANE), f32)]
    out += [shape_of((count, first), bf16) for s in peers]
    out += [shape_of((count, rest), bf16) for s in group]
    out += [shape_of((count, part), bf16 if s else f32) for s in group]
    nbytes = sum(a.size * a.dtype.itemsize for a in args if a is not arrived_b)
    nbytes += sum(a.size * a.dtype.itemsize for a in out)
    nbytes += len(group) * blocks * ROWS * packed * 2
    outs = list(
        pl.pallas_call(
            functools.partial(finish_kernel, tuple(group), blocks, shards),
            grid=(1,),
            in_specs=specs,
            out_specs=[
                pl.BlockSpec(o.shape, lambda i, n=len(o.shape): (0,) * n) for o in out
            ],
            out_shape=out,
            compiler_params=params(nbytes),
            cost_estimate=cost(
                4 * len(group) * count * part * (first + rest), nbytes
            ),
        )(*args)
    )
    score = outs.pop(0)
    rows_a = {s: outs.pop(0) for s in peers}
    rows_b = {s: outs.pop(0) for s in group}
    projs = {s: outs.pop(0) for s in group}
    return score, rows_a, rows_b, projs


def adamw_kernel(shards, hidden_ref, *refs):
    rows_a, rows_b = refs[:shards], refs[shards : 2 * shards]
    master_ref, one_ref, two_ref = refs[2 * shards : 2 * shards + 3]
    outs, news, sems = refs[-7:-4], refs[-4:-1], refs[-1]
    count, first = rows_a[0].shape
    width = master_ref.shape[1]
    corr_one = 1.0 - beta_one**adam_step
    corr_two = 1.0 - beta_two**adam_step
    rate = learn_rate * corr_two**0.5 / corr_one
    keep = 1.0 - learn_rate * decay_rate

    def write(col, index):
        return [
            pltpu.make_async_copy(
                new.at[:, pl.ds(col, UNIT)], out.at[0, :, pl.ds(col, UNIT)], sems.at[j, index]
            )
            for j, (new, out) in enumerate(zip(news, outs))
        ]

    def update(rows, base, i):
        at = pl.multiple_of(i * UNIT, UNIT)
        grad = jnp.dot(
            hidden_ref[:, :count], rows[0][:, pl.ds(at, UNIT)], preferred_element_type=f32
        )
        for s in range(1, shards):
            grad += jnp.dot(
                hidden_ref[:, s * count : (s + 1) * count],
                rows[s][:, pl.ds(at, UNIT)],
                preferred_element_type=f32,
            )
        cols = pl.ds(pl.multiple_of(base + at, UNIT), UNIT)
        m_new = beta_one * one_ref[:, cols].astype(f32) + (1.0 - beta_one) * grad
        v_new = beta_two * two_ref[:, cols].astype(f32) + (1.0 - beta_two) * (grad * grad)
        root = v_new * lax.rsqrt(v_new) + adam_eps * corr_two**0.5
        news[0][:, cols] = keep * master_ref[:, cols] - rate * m_new / root
        news[1][:, cols] = m_new.astype(bf16)
        news[2][:, cols] = v_new.astype(bf16)
        for copy in write(pl.multiple_of(base + at, UNIT), base // UNIT + i):
            copy.start()

    @pl.loop(0, first // UNIT)
    def _(i):
        update(rows_a, 0, i)

    @pl.loop(0, (width - first) // UNIT)
    def _(i):
        update(rows_b, first, i)

    for index in range(width // UNIT):
        for copy in write(index * UNIT, index):
            copy.wait()


def adamw(hidden_t, rows_a, rows_b, master, one, two):
    part, depth = hidden_t.shape
    width = master.shape[1]
    shards = len(rows_a)
    shape = (1, part, width)
    return pl.pallas_call(
        functools.partial(adamw_kernel, shards),
        in_specs=[VMEM] * (4 + 2 * shards),
        out_specs=[HBM] * 3,
        out_shape=[shape_of(shape, f32), shape_of(shape, bf16), shape_of(shape, bf16)],
        scratch_shapes=[
            pltpu.VMEM((part, width), f32),
            pltpu.VMEM((part, width), bf16),
            pltpu.VMEM((part, width), bf16),
            pltpu.SemaphoreType.DMA((3, width // UNIT)),
        ],
        compiler_params=params(6 * part * width + 2 * depth * width),
        cost_estimate=cost(2 * part * depth * width, 16 * part * width, part * width),
    )(hidden_t, *rows_a, *rows_b, master, one, two)


def gate_up_kernel(place_ref, coef_gate_ref, coef_up_ref, *refs):
    out_ref = refs[-1]
    shards, _, part = coef_gate_ref.shape
    for s in range(shards):
        at = place_ref[s]
        grad = refs[s][...].astype(f32)
        low = pl.multiple_of(at * part, part)
        out_ref[:, pl.ds(low, part)] = (grad * coef_gate_ref[at]).astype(bf16)
        high = pl.multiple_of(shards * part + at * part, part)
        out_ref[:, pl.ds(high, part)] = (grad * coef_up_ref[at]).astype(bf16)


def gate_up_grad(place, coef_gate, coef_up, grads):
    shards, slots, part = coef_gate.shape
    return pl.pallas_call(
        gate_up_kernel,
        in_specs=[pl.BlockSpec(memory_space=pltpu.SMEM)] + [VMEM] * (2 + shards),
        out_specs=VMEM,
        out_shape=shape_of((slots, 2 * shards * part), bf16),
        compiler_params=params(16 * shards * slots * part),
        cost_estimate=cost(4 * shards * slots * part, 16 * shards * slots * part),
    )(place, coef_gate, coef_up, *grads)


def score_kernel(ids_ref, slots_ref, gates_ref, score_ref, out_ref):
    shards, blocks = score_ref.shape[:2]
    score = score_ref[0].reshape(blocks, LANE)
    for s in range(1, shards):
        score += score_ref[s].reshape(blocks, LANE)
    ids = ids_ref[...]
    slots = slots_ref[...]
    tok = ids.shape[1]
    live = (ids % EXP_LOCAL == 0) & (slots >= 0)
    owner = ids // EXP_LOCAL
    lane = lax.broadcasted_iota(jnp.int32, (LANE, tok), 0)
    block = lax.broadcasted_iota(jnp.int32, (blocks, tok), 0)
    for k in range(TOPK):
        pick = (lane == slots[k : k + 1]).astype(f32)
        value = jnp.dot(score, pick, precision=lax.Precision.HIGHEST, preferred_element_type=f32)
        value = jnp.sum(jnp.where(block == owner[k : k + 1], value, 0.0), axis=0, keepdims=True)
        out_ref[k : k + 1] = jnp.where(
            live[k : k + 1], value / gates_ref[k : k + 1].astype(f32), 0.0
        )


def gate_scores(ids, slots, gates, score):
    return pl.pallas_call(
        score_kernel,
        out_shape=shape_of(ids.shape, f32),
        compiler_params=params(0),
        cost_estimate=cost(1 << 24, 1 << 16),
    )(ids, slots, gates, score)


def per_device(out_grad, expert_ids, slots, gate_weights, saved_gate_up, master, moment1, moment2):
    ep_size = lax.axis_size("ep")
    rep_size = lax.axis_size("rep")
    me = lax.axis_index("rep")
    ids_t, slots_t, gates_t = expert_ids.T, slots.T, gate_weights.T
    first = split_width(out_grad.shape[1])
    steps = range(1, rep_size)

    def shift(value, step):
        perm = [(i, (i + step) % rep_size) for i in range(rep_size)]
        return lax.ppermute(value, "rep", perm)

    def exchange(value):
        return lax.all_to_all(value, "ep", split_axis=0, concat_axis=0, tiled=True)

    send_a, send_b = dispatch(ep_size, first, ids_t, slots_t, gates_t, out_grad)
    mixed = [send_b] + [shift(send_b, s) for s in steps]
    arrived_a = exchange(send_a.reshape(ep_size, ROWS, -1)).reshape(send_a.shape)
    arrived_a = [arrived_a] + [shift(arrived_a, s) for s in steps]
    mixed = jnp.stack([part.reshape(ep_size, ROWS, -1) for part in mixed], axis=1)
    arrived_b = exchange(mixed.reshape(ep_size, rep_size * ROWS, -1)).reshape(mixed.shape)

    hidden, coef_gate, coef_up = hidden_parts(saved_gate_up[0, 0], rep_size, send_b)
    parts = [
        lax.dynamic_index_in_dim(hidden, (me + s) % rep_size, 0, keepdims=False)
        for s in range(rep_size)
    ]
    parts = [parts[0]] + [shift(parts[s], s) for s in steps]
    place = jnp.stack([(me + s) % rep_size for s in range(rep_size)]).astype(jnp.int32)
    master_v, one_v, two_v, weight_a, weight_b = load_state(
        first, master, moment1, moment2, send_b
    )

    rows_own, proj, hidden_t = begin(ep_size, arrived_a[0], weight_a, parts)
    score, rows_a, rows_b, projs = None, {0: rows_own}, {}, {}
    for low in range(0, rep_size, 2):
        group = list(range(low, min(low + 2, rep_size)))
        partial, more_a, more_b, more = finish(
            group, weight_a, weight_b, proj, arrived_a, arrived_b, parts
        )
        score = partial if score is None else score + partial
        rows_a.update(more_a)
        rows_b.update(more_b)
        projs.update(more)
    grads = [projs[0]] + [shift(projs[s], rep_size - s) for s in steps]
    score = lax.all_to_all(score, ("rep", "ep"), split_axis=0, concat_axis=0, tiled=True)

    every = range(rep_size)
    done = adamw(
        hidden_t, [rows_a[s] for s in every], [rows_b[s] for s in every], master_v, one_v, two_v
    )
    grad_gate_up = gate_up_grad(place, coef_gate, coef_up, grads)
    gate_grad = gate_scores(
        ids_t, slots_t, gates_t, score.reshape(rep_size, ep_size, 1, LANE)
    ).T
    return (grad_gate_up.reshape(saved_gate_up.shape), gate_grad) + tuple(done)


def solution(mesh):
    in_specs = (
        P(("rep", "ep"), None),
        P(("rep", "ep"), None),
        P(("rep", "ep"), None),
        P(("rep", "ep"), None),
        P("rep", "ep", None, None),
        P("ep", "rep", None),
        P("ep", "rep", None),
        P("ep", "rep", None),
    )
    out_specs = (
        P("rep", "ep", None, None),
        P(("rep", "ep"), None),
        P("ep", "rep", None),
        P("ep", "rep", None),
        P("ep", "rep", None),
    )
    return jax.shard_map(
        per_device, mesh=mesh, in_specs=in_specs, out_specs=out_specs, check_vma=False
    )
```

```python
import functools

import jax
import jax.numpy as jnp
from jax import lax
from jax.experimental import pallas as pl
from jax.experimental.pallas import tpu as pltpu
from jax.sharding import PartitionSpec as P

TOPK = 8
EXP_LOCAL = 8
SEND = 12
LANE = 128
UNIT = 512
ROWS = 16

beta_one = 0.9
beta_two = 0.95
learn_rate = 0.002
decay_rate = 0.1
adam_eps = 1e-08
adam_step = 50

f32 = jnp.float32
bf16 = jnp.bfloat16
HBM = pl.BlockSpec(memory_space=pltpu.HBM)
ANY = pl.BlockSpec(memory_space=pl.ANY)


def in_hbm(*arrays):
    return [pltpu.with_memory_space_constraint(array, pltpu.HBM) for array in arrays]


def out_hbm(dims, dtype):
    return pltpu.HBM(tuple(dims), dtype)


def block(dims, at=None):
    at = at or (0,) * len(dims)
    return pl.BlockSpec(tuple(dims), lambda i: at)


def params(nbytes):
    mib = min(60, max(16, 8 + 3 * int(nbytes) // 2**20))
    return pltpu.CompilerParams(vmem_limit_bytes=mib * 2**20)


def cost(flops, nbytes, transcendentals=0):
    return pl.CostEstimate(
        flops=int(flops), bytes_accessed=int(nbytes), transcendentals=int(transcendentals)
    )


def div_send(index):
    return lax.shift_right_logical(index * 10923, 17)


def pack(cols):
    return cols // 4 * 3


def chunk_edges(width):
    units = width // UNIT
    last = units - max(1, round(units * 2 / 7))
    return (0, last * 2 // 5 * UNIT, last * UNIT, width)


def tail_order(count, total, j, slots_first):
    a = lax.broadcasted_iota(jnp.int32, (count, total), 0)
    b = lax.broadcasted_iota(jnp.int32, (count, total), 1)
    if slots_first:
        block_of = div_send(a)
        inner = a - SEND * block_of
        hit = b == block_of * ROWS + SEND + inner - 4 * j
    else:
        inner = (a & (ROWS - 1)) - SEND + 4 * j
        hit = (b == a - SEND + 4 * j) & ((a & (ROWS - 1)) >= SEND)
    return jnp.where(hit & (inner >= 4 * j) & (inner < 4 * j + 4), 1.0, 0.0).astype(bf16)


def dispatch_kernel(edges, ids_hbm, slots_hbm, gates_hbm, grad_hbm, *refs):
    outs, (ids_ref, slots_ref, gates_ref, grad_ref, sems) = refs[:2], refs[2:]
    pairs = [
        (ids_hbm, ids_ref),
        (slots_hbm, slots_ref),
        (gates_hbm, gates_ref),
        (grad_hbm, grad_ref),
    ]
    copies = [
        pltpu.make_async_copy(source, target, sems.at[i])
        for i, (source, target) in enumerate(pairs)
    ]
    for copy in copies:
        copy.start()
    for copy in copies[:3]:
        copy.wait()
    rows = outs[0].shape[0]
    ids = ids_ref[...]
    slots = slots_ref[...]
    gates = gates_ref[...].astype(f32)
    tok = ids.shape[1]
    live = ((ids & (EXP_LOCAL - 1)) == 0) & (slots >= 0)
    place = jnp.where(live, ids // EXP_LOCAL * ROWS + slots, -1)
    row = lax.broadcasted_iota(jnp.int32, (rows, tok), 0)
    main = jnp.zeros((rows, tok), f32)
    for k in range(TOPK):
        main = jnp.where(row == place[k : k + 1], gates[k : k + 1], main)
    main = main.astype(bf16)
    tails = [
        jnp.dot(
            tail_order(rows, rows, j, False), main, preferred_element_type=f32
        ).astype(bf16)
        for j in range(3)
    ]
    copies[3].wait()
    chunks = list(zip(edges[:-1], edges[1:]))
    base = 0
    for index, (low, high) in enumerate(chunks):
        out_ref = outs[int(index == len(chunks) - 1)]
        base = 0 if index == len(chunks) - 1 else base
        part = (high - low) // 4
        for j in range(3):
            total = jnp.dot(
                main,
                grad_ref[:, low + j * part : low + (j + 1) * part],
                preferred_element_type=f32,
            )
            total += jnp.dot(
                tails[j], grad_ref[:, low + 3 * part : high], preferred_element_type=f32
            )
            out_ref[:, base : base + part] = total.astype(bf16)
            base += part


def dispatch(blocks, edges, ids, slots, gates, out_grad):
    tok, width = out_grad.shape
    rows = blocks * ROWS
    shapes = [(rows, pack(edges[-2])), (rows, pack(width - edges[-2]))]
    return pl.pallas_call(
        functools.partial(dispatch_kernel, edges),
        grid=(1,),
        in_specs=[HBM] * 4,
        out_specs=[block(shape) for shape in shapes],
        out_shape=[out_hbm(shape, bf16) for shape in shapes],
        scratch_shapes=[
            pltpu.VMEM(ids.shape, jnp.int32),
            pltpu.VMEM(slots.shape, jnp.int32),
            pltpu.VMEM(gates.shape, bf16),
            pltpu.VMEM(out_grad.shape, bf16),
            pltpu.SemaphoreType.DMA((4,)),
        ],
        compiler_params=params(2 * rows * width + 2 * tok * width),
        cost_estimate=cost(2 * rows * tok * width, 4 * tok * width),
    )(*in_hbm(ids, slots, gates, out_grad))


def swiglu_part(gate_up_ref, shards, step, part):
    at = lax.rem(lax.axis_index("rep") + step, shards)
    low = pl.multiple_of(at * part, part)
    high = pl.multiple_of((shards + at) * part, part)
    gate = gate_up_ref[:, pl.ds(low, part)].astype(f32)
    up = gate_up_ref[:, pl.ds(high, part)].astype(f32)
    return low, high, gate, up, jax.nn.sigmoid(gate)


def hidden_kernel(gate_up_ref, after_ref, *out_refs):
    del after_ref
    for s, out_ref in enumerate(out_refs):
        _, _, gate, up, sig = swiglu_part(gate_up_ref, len(out_refs), s, out_ref.shape[1])
        out_ref[...] = (gate * sig * up).astype(bf16)


def hidden_parts(gate_up, shards, after):
    slots, width = gate_up.shape
    shape = (slots, width // 2 // shards)
    return pl.pallas_call(
        hidden_kernel,
        grid=(1,),
        in_specs=[block(gate_up.shape), HBM],
        out_specs=[block(shape)] * shards,
        out_shape=[out_hbm(shape, bf16)] * shards,
        compiler_params=params(3 * slots * width),
        cost_estimate=cost(8 * slots * width, 3 * slots * width, slots * width),
    )(*in_hbm(gate_up, after))


def cast_kernel(master_ref, after_ref, weight_ref):
    del after_ref
    weight_ref[...] = master_ref[0].astype(bf16)


def cast_weight(master, after):
    _, part, width = master.shape
    rows = part // 4
    return pl.pallas_call(
        cast_kernel,
        grid=(4,),
        in_specs=[pl.BlockSpec((1, rows, width), lambda i: (0, i, 0)), HBM],
        out_specs=pl.BlockSpec((rows, width), lambda i: (i, 0)),
        out_shape=out_hbm((part, width), bf16),
        compiler_params=params(6 * rows * width),
        cost_estimate=cost(part * width, 6 * part * width),
    )(*in_hbm(master, after))


def mix_kernel(count, *refs):
    out_ref = refs[-1]
    for s in range(count):
        value = refs[s][...]
        out_ref[:, s * ROWS : (s + 1) * ROWS, :] = value


def mix(parts, blocks, weight, after):
    packed = parts[0].shape[1]
    parts = [part.reshape(blocks, ROWS, packed) for part in parts]
    shape = (blocks, len(parts) * ROWS, packed)
    return pl.pallas_call(
        functools.partial(mix_kernel, len(parts)),
        grid=(1,),
        in_specs=[block(part.shape) for part in parts] + [HBM] + [ANY] * len(after),
        out_specs=block(shape),
        out_shape=out_hbm(shape, bf16),
        compiler_params=params(4 * parts[0].size * len(parts)),
        cost_estimate=cost(0, 4 * parts[0].size * len(parts)),
    )(*in_hbm(parts[0]), *parts[1:], *in_hbm(weight), *after)


def reorder(arrived, rows_ref):
    count, width = rows_ref.shape
    part = width // 4
    total = arrived.shape[0]
    slot = lax.broadcasted_iota(jnp.int32, (count, total), 0)
    col = lax.broadcasted_iota(jnp.int32, (count, total), 1)
    order = jnp.where(col == slot + (ROWS - SEND) * div_send(slot), 1.0, 0.0).astype(bf16)
    rows_ref[:, : 3 * part] = jnp.dot(order, arrived, preferred_element_type=f32).astype(bf16)
    tail = jnp.zeros((count, part), f32)
    for j in range(3):
        tail += jnp.dot(
            tail_order(count, total, j, True),
            arrived[:, j * part : (j + 1) * part],
            preferred_element_type=f32,
        )
    rows_ref[:, 3 * part :] = tail.astype(bf16)


def times_weight(rows_ref, weight_ref):
    return lax.dot_general(
        rows_ref[...], weight_ref[...], (((1,), (1,)), ((), ())), preferred_element_type=f32
    )


def score_block(blocks, proj, hidden):
    count = blocks * SEND
    score = jnp.sum(proj * hidden.astype(f32), axis=1, keepdims=True)
    slot_of = lax.broadcasted_iota(jnp.int32, (count, LANE), 0)
    lane_of = lax.broadcasted_iota(jnp.int32, (count, LANE), 1)
    spread = jnp.where(slot_of - SEND * div_send(slot_of) == lane_of, score, 0.0)
    block_of = lax.broadcasted_iota(jnp.int32, (blocks, count), 0)
    slot_at = lax.broadcasted_iota(jnp.int32, (blocks, count), 1)
    gather = (div_send(slot_at) == block_of).astype(f32)
    score = jnp.dot(
        gather, spread, precision=lax.Precision.HIGHEST, preferred_element_type=f32
    )
    return score.reshape(blocks, 1, LANE)


def absorb_kernel(chunks, more, *refs):
    refs = list(refs)
    arrived = [refs.pop(0) for _ in range(chunks)]
    weights = [refs.pop(0) for _ in range(chunks)]
    before_ref = refs.pop(0) if more else None
    rows_refs, proj_ref = refs[:-1], refs[-1]
    proj = before_ref[...] if more else 0.0
    for arrived_ref, weight_ref, rows_ref in zip(arrived, weights, rows_refs):
        reorder(arrived_ref[...], rows_ref)
        proj += times_weight(rows_ref, weight_ref)
    proj_ref[...] = proj


def absorb(blocks, edges, chunks, arrived, weight, before):
    count = blocks * SEND
    part = weight.shape[0]
    base, specs, weight_specs, out = 0, [], [], []
    for c in chunks:
        width = edges[c + 1] - edges[c]
        specs.append(pl.BlockSpec((pl.Element(arrived.shape[0]), pl.Element(pack(width))),
                                  lambda i, base=base: (0, base)))
        weight_specs.append(pl.BlockSpec((pl.Element(part), pl.Element(width)),
                                         lambda i, low=edges[c]: (0, low)))
        out.append(((count, width), bf16))
        base += pack(width)
    out.append(((count, part), f32))
    args = [arrived] * len(chunks) + in_hbm(*[weight] * len(chunks))
    specs += weight_specs
    if before is not None:
        args += in_hbm(before)
        specs.append(block(before.shape))
    cols = sum(edges[c + 1] - edges[c] for c in chunks)
    nbytes = 4 * count * cols + 2 * part * cols + 8 * count * part
    return pl.pallas_call(
        functools.partial(absorb_kernel, len(chunks), before is not None),
        grid=(1,),
        in_specs=specs,
        out_specs=[block(shape) for shape, _ in out],
        out_shape=[out_hbm(shape, dtype) for shape, dtype in out],
        compiler_params=params(nbytes),
        cost_estimate=cost(4 * count * part * cols, nbytes),
    )(*args)


def finish_kernel(group, blocks, shards, weight_ref, *refs):
    refs, size = list(refs), len(group)
    arrived, before, hidden = refs[:size], refs[size : 2 * size], refs[2 * size : 3 * size]
    outs = refs[3 * size + 1 :]
    score_ref, rows_refs, proj_refs = outs[0], outs[1 : size + 1], outs[size + 1 :]
    me = lax.axis_index("rep")
    if size < shards:
        score_ref[...] = jnp.zeros(score_ref.shape, f32)
    for i, s in enumerate(group):
        value = arrived[i][...]
        reorder(value.reshape(blocks * ROWS, value.shape[-1]), rows_refs[i])
        proj = before[i][...] + times_weight(rows_refs[i], weight_ref)
        proj_refs[i][...] = proj.astype(bf16)
        at = lax.rem(me + shards - s, shards)
        score_ref[pl.ds(at * blocks, blocks)] = score_block(blocks, proj, hidden[i][...])


def finish(group, edges, weight, before, arrived, hidden, after):
    blocks, shards, _, packed = arrived.shape
    count = blocks * SEND
    part = weight.shape[0]
    low, high = edges[-2:]
    args = in_hbm(weight) + [arrived] * len(group)
    specs = [
        pl.BlockSpec((pl.Element(part), pl.Element(high - low)), lambda i: (0, low))
    ]
    specs += [block((blocks, 1, ROWS, packed), (0, s, 0, 0)) for s in group]
    for s in group:
        args += in_hbm(before[s])
        specs.append(block((count, part)))
    for s in group:
        args.append(hidden[s])
        specs.append(block((count, part)))
    args += in_hbm(after)
    specs.append(HBM)
    out = [((shards * blocks, 1, LANE), f32)]
    out += [((count, high - low), bf16)] * len(group)
    out += [((count, part), bf16)] * len(group)
    nbytes = 2 * part * (high - low) + 4 * len(group) * count * (high - low + 3 * part)
    outs = pl.pallas_call(
        functools.partial(finish_kernel, tuple(group), blocks, shards),
        grid=(1,),
        in_specs=specs,
        out_specs=[block(shape) for shape, _ in out],
        out_shape=[jax.ShapeDtypeStruct(*out[0])]
        + [out_hbm(shape, dtype) for shape, dtype in out[1:]],
        compiler_params=params(nbytes),
        cost_estimate=cost(4 * len(group) * count * part * (high - low), nbytes),
    )(*args)
    size = len(group)
    return outs[0], outs[1 : size + 1], outs[size + 1 :]


def adamw_kernel(shards, *refs):
    hidden_refs, rows_refs = refs[:shards], refs[shards : 2 * shards]
    master_ref, one_ref, two_ref = refs[2 * shards : 2 * shards + 3]
    master_out, one_out, two_out = refs[-3:]
    corr_one = 1.0 - beta_one**adam_step
    corr_two = 1.0 - beta_two**adam_step
    rate = learn_rate * corr_two**0.5 / corr_one
    keep = 1.0 - learn_rate * decay_rate
    grad = 0.0
    for hidden_ref, rows_ref in zip(hidden_refs, rows_refs):
        grad += lax.dot_general(
            hidden_ref[...], rows_ref[...], (((0,), (0,)), ((), ())),
            preferred_element_type=f32,
        )
    m_new = beta_one * one_ref[0].astype(f32) + (1.0 - beta_one) * grad
    v_new = beta_two * two_ref[0].astype(f32) + (1.0 - beta_two) * (grad * grad)
    root = v_new * lax.rsqrt(v_new) + adam_eps * corr_two**0.5
    master_out[0] = keep * master_ref[0] - rate * m_new / root
    one_out[0] = m_new.astype(bf16)
    two_out[0] = v_new.astype(bf16)


def adamw(low, high, hidden, rows, state, done):
    part = hidden[0].shape[1]
    count = rows[0].shape[0]
    shards = len(rows)
    base = low // UNIT
    spec = pl.BlockSpec((1, part, UNIT), lambda i: (0, 0, base + i))
    args = list(hidden) + in_hbm(*rows, *state, *done)
    depth = count * shards
    cols = high - low
    return pl.pallas_call(
        functools.partial(adamw_kernel, shards),
        grid=(cols // UNIT,),
        in_specs=[block((count, part))] * shards
        + [pl.BlockSpec((count, UNIT), lambda i: (0, i))] * shards
        + [spec] * 3
        + [HBM] * len(done),
        out_specs=[spec] * 3,
        out_shape=[out_hbm(array.shape, array.dtype) for array in state],
        input_output_aliases={2 * shards + 3 + i: i for i in range(len(done))},
        compiler_params=params(16 * part * UNIT + 2 * depth * (part + UNIT)),
        cost_estimate=cost(2 * part * depth * cols, 16 * part * cols, part * cols),
    )(*args)


def gate_up_kernel(gate_up_ref, *refs):
    grad_refs, out_ref = refs[:-1], refs[-1]
    shards, part = len(grad_refs), grad_refs[0].shape[1]
    for s, grad_ref in enumerate(grad_refs):
        low, high, gate, up, sig = swiglu_part(gate_up_ref, shards, s, part)
        grad = grad_ref[...].astype(f32)
        out_ref[:, pl.ds(low, part)] = (
            grad * up * sig * (1.0 + gate * (1.0 - sig))
        ).astype(bf16)
        out_ref[:, pl.ds(high, part)] = (grad * (gate * sig)).astype(bf16)


def gate_up_grad(gate_up, grads):
    size = gate_up.size
    return pl.pallas_call(
        gate_up_kernel,
        grid=(1,),
        in_specs=[block(gate_up.shape)] + [block(grad.shape) for grad in grads],
        out_specs=block(gate_up.shape),
        out_shape=out_hbm(gate_up.shape, bf16),
        compiler_params=params(8 * size),
        cost_estimate=cost(12 * size, 5 * size, size),
    )(*in_hbm(gate_up, grads[0]), *grads[1:])


def score_kernel(ids_ref, slots_ref, gates_ref, score_ref, out_ref):
    shards, blocks = score_ref.shape[:2]
    score = score_ref[0].reshape(blocks, LANE)
    for s in range(1, shards):
        score += score_ref[s].reshape(blocks, LANE)
    ids = ids_ref[...]
    slots = slots_ref[...]
    tok = ids.shape[1]
    live = ((ids & (EXP_LOCAL - 1)) == 0) & (slots >= 0)
    owner = ids // EXP_LOCAL
    lane = lax.broadcasted_iota(jnp.int32, (LANE, tok), 0)
    block_of = lax.broadcasted_iota(jnp.int32, (blocks, tok), 0)
    for k in range(TOPK):
        pick = (lane == slots[k : k + 1]).astype(f32)
        value = jnp.dot(score, pick, precision=lax.Precision.HIGHEST, preferred_element_type=f32)
        value = jnp.where(block_of == owner[k : k + 1], value, 0.0)
        value = jnp.sum(value, axis=0, keepdims=True)
        out_ref[k : k + 1] = jnp.where(
            live[k : k + 1], value / gates_ref[k : k + 1].astype(f32), 0.0
        )


def gate_scores(ids, slots, gates, score):
    return pl.pallas_call(
        score_kernel,
        grid=(1,),
        in_specs=[block(array.shape) for array in (ids, slots, gates, score)],
        out_specs=block(ids.shape),
        out_shape=out_hbm(ids.shape, f32),
        compiler_params=params(0),
        cost_estimate=cost(1 << 24, 1 << 16),
    )(*in_hbm(ids, slots, gates), score)


def per_device(out_grad, expert_ids, slots, gate_weights, saved_gate_up, master, moment1, moment2):
    ep_size = lax.axis_size("ep")
    rep_size = lax.axis_size("rep")
    ids_t, slots_t, gates_t = expert_ids.T, slots.T, gate_weights.T
    gate_up = saved_gate_up[0, 0]
    state = (master, moment1, moment2)
    edges = chunk_edges(out_grad.shape[1])
    steps = range(1, rep_size)
    every = range(rep_size)

    def shift(value, step):
        perm = [(i, (i + step) % rep_size) for i in every]
        return lax.ppermute(value, "rep", perm)

    def exchange(value):
        return lax.all_to_all(value, "ep", split_axis=0, concat_axis=0, tiled=True)

    send_a, send_b = dispatch(ep_size, edges, ids_t, slots_t, gates_t, out_grad)
    mixed = [send_b] + [shift(send_b, s) for s in steps]
    parts = hidden_parts(gate_up, rep_size, send_b)
    hidden = [parts[0]] + [shift(parts[s], s) for s in steps]
    weight = cast_weight(master, send_b)
    arrived = exchange(send_a.reshape(ep_size, ROWS, -1)).reshape(send_a.shape)
    mixed = mix(mixed, ep_size, weight, hidden[1:])
    arrived_b = exchange(mixed).reshape(ep_size, rep_size, ROWS, -1)

    half = pack(edges[1])
    peers = [[shift(arrived[:, :half], s), shift(arrived[:, half:], s)] for s in steps]

    rows_0, rows_1, proj = absorb(ep_size, edges, (0, 1), arrived, weight, None)
    rows, before = [[rows_0], [rows_1], []], [proj]
    for s in steps:
        more, proj = absorb(ep_size, edges, (0,), peers[s - 1][0], weight, None)
        rows[0].append(more)
        before.append(proj)
    done = adamw(edges[0], edges[1], hidden, rows[0], state, ())
    for s in steps:
        more, before[s] = absorb(ep_size, edges, (1,), peers[s - 1][1], weight, before[s])
        rows[1].append(more)

    score, projs = None, []
    for low in range(0, rep_size, 2):
        group = list(range(low, min(low + 2, rep_size)))
        partial, more, final = finish(
            group, edges, weight, before, arrived_b, hidden, done[2]
        )
        score = partial if score is None else score + partial
        rows[2] += more
        projs += final
    grads = [projs[0]] + [shift(projs[s], rep_size - s) for s in steps]
    score = lax.all_to_all(score, ("rep", "ep"), split_axis=0, concat_axis=0, tiled=True)

    for c in (1, 2):
        done = adamw(edges[c], edges[c + 1], hidden, rows[c], state, done)
    grad_gate_up = gate_up_grad(gate_up, grads)
    gate_grad = gate_scores(
        ids_t, slots_t, gates_t, score.reshape(rep_size, ep_size, 1, LANE)
    ).T
    return (grad_gate_up.reshape(saved_gate_up.shape), gate_grad) + tuple(done)


def solution(mesh):
    in_specs = (
        P(("rep", "ep"), None),
        P(("rep", "ep"), None),
        P(("rep", "ep"), None),
        P(("rep", "ep"), None),
        P("rep", "ep", None, None),
        P("ep", "rep", None),
        P("ep", "rep", None),
        P("ep", "rep", None),
    )
    out_specs = (
        P("rep", "ep", None, None),
        P(("rep", "ep"), None),
        P("ep", "rep", None),
        P("ep", "rep", None),
        P("ep", "rep", None),
    )
    return jax.shard_map(
        per_device, mesh=mesh, in_specs=in_specs, out_specs=out_specs, check_vma=False
    )
```

```python
import functools

import jax
import jax.numpy as jnp
from jax import lax
from jax.experimental import pallas as pl
from jax.experimental.pallas import tpu as pltpu
from jax.sharding import PartitionSpec as P

TOPK = 8
EXP_LOCAL = 8
SEND = 12
LANE = 128
UNIT = 512
MIX_COST = 50
SETTLE_COST = 44
ROWS = 16

beta_one = 0.9
beta_two = 0.95
learn_rate = 0.002
decay_rate = 0.1
adam_eps = 1e-08
adam_step = 50

f32 = jnp.float32
bf16 = jnp.bfloat16
HBM = pl.BlockSpec(memory_space=pltpu.HBM)
ANY = pl.BlockSpec(memory_space=pl.ANY)


def in_hbm(*arrays):
    return [pltpu.with_memory_space_constraint(array, pltpu.HBM) for array in arrays]


def out_hbm(dims, dtype):
    return pltpu.HBM(tuple(dims), dtype)


def block(dims, at=None):
    at = at or (0,) * len(dims)
    return pl.BlockSpec(tuple(dims), lambda i: at, pipeline_mode=pl.Buffered(1))


def params(nbytes):
    mib = min(60, max(16, 10 + 5 * int(nbytes) // 2**22))
    return pltpu.CompilerParams(vmem_limit_bytes=mib * 2**20)


def cost(flops, nbytes, transcendentals=0):
    return pl.CostEstimate(
        flops=int(flops), bytes_accessed=int(nbytes), transcendentals=int(transcendentals)
    )


def div_send(index):
    return lax.shift_right_logical(index * 10923, 17)


def pack(cols):
    return cols // 4 * 3


def chunk_edges(width):
    units = width // UNIT
    return (0, (units - max(1, units * 3 // 7)) * UNIT, width)


def tail_order(count, total, j, slots_first):
    a = lax.broadcasted_iota(jnp.int32, (count, total), 0)
    b = lax.broadcasted_iota(jnp.int32, (count, total), 1)
    if slots_first:
        block_of = div_send(a)
        inner = a - SEND * block_of
        hit = b == block_of * ROWS + SEND + inner - 4 * j
    else:
        inner = (a & (ROWS - 1)) - SEND + 4 * j
        hit = (b == a - SEND + 4 * j) & ((a & (ROWS - 1)) >= SEND)
    return jnp.where(hit & (inner >= 4 * j) & (inner < 4 * j + 4), 1.0, 0.0).astype(bf16)


def dispatch_kernel(edges, ids_hbm, slots_hbm, gates_hbm, grad_hbm, *refs):
    outs, (ids_ref, slots_ref, gates_ref, grad_ref) = refs[:2], refs[2:6]
    sends, sems, out_sems = refs[6:8], refs[8], refs[9]
    pairs = [
        (ids_hbm, ids_ref),
        (slots_hbm, slots_ref),
        (gates_hbm, gates_ref),
        (grad_hbm, grad_ref),
    ]
    copies = [
        pltpu.make_async_copy(source, target, sems.at[i])
        for i, (source, target) in enumerate(pairs)
    ]
    for copy in copies:
        copy.start()
    rows = outs[0].shape[0]
    tok = ids_ref.shape[1]
    orders = [tail_order(rows, rows, j, False) for j in range(3)]
    for copy in copies[:3]:
        copy.wait()
    ids = ids_ref[...]
    slots = slots_ref[...]
    gates = gates_ref[...].astype(f32)
    live = ((ids & (EXP_LOCAL - 1)) == 0) & (slots >= 0)
    place = jnp.where(live, ids // EXP_LOCAL * ROWS + slots, -1)
    row = lax.broadcasted_iota(jnp.int32, (rows, tok), 0)
    main = jnp.zeros((rows, tok), f32)
    for k in range(TOPK):
        main = jnp.where(row == place[k : k + 1], gates[k : k + 1], main)
    main = main.astype(bf16)
    tails = [
        jnp.dot(order, main, preferred_element_type=f32).astype(bf16) for order in orders
    ]
    copies[3].wait()
    out_copies = []
    for c in (1, 0):
        low, high = edges[c], edges[c + 1]
        part = (high - low) // 4
        for j in range(3):
            total = jnp.dot(
                main,
                grad_ref[:, low + j * part : low + (j + 1) * part],
                preferred_element_type=f32,
            )
            total += jnp.dot(
                tails[j], grad_ref[:, low + 3 * part : high], preferred_element_type=f32
            )
            own = (slice(None), pl.ds(j * part, part))
            sends[c][own] = total.astype(bf16)
            copy = pltpu.make_async_copy(
                sends[c].at[own], outs[c].at[own], out_sems.at[c, j]
            )
            copy.start()
            out_copies.append(copy)
    for copy in out_copies:
        copy.wait()


def dispatch(blocks, edges, ids, slots, gates, out_grad):
    tok, width = out_grad.shape
    rows = blocks * ROWS
    shapes = [(rows, pack(high - low)) for low, high in zip(edges[:-1], edges[1:])]
    return pl.pallas_call(
        functools.partial(dispatch_kernel, edges),
        in_specs=[HBM] * 4,
        out_specs=[HBM] * 2,
        out_shape=[out_hbm(shape, bf16) for shape in shapes],
        scratch_shapes=[
            pltpu.VMEM(ids.shape, jnp.int32),
            pltpu.VMEM(slots.shape, jnp.int32),
            pltpu.VMEM(gates.shape, bf16),
            pltpu.VMEM(out_grad.shape, bf16),
        ]
        + [pltpu.VMEM(shape, bf16) for shape in shapes]
        + [pltpu.SemaphoreType.DMA((4,)), pltpu.SemaphoreType.DMA((2, 3))],
        compiler_params=params(2 * rows * width + 2 * tok * width),
        cost_estimate=cost(2 * rows * tok * width, 4 * tok * width),
    )(*in_hbm(ids, slots, gates, out_grad))


def swiglu_part(gate_up_ref, shards, step, part):
    at = lax.rem(lax.axis_index("rep") + step, shards)
    low = pl.multiple_of(at * part, part)
    high = pl.multiple_of((shards + at) * part, part)
    gate = gate_up_ref[:, pl.ds(low, part)].astype(f32)
    up = gate_up_ref[:, pl.ds(high, part)].astype(f32)
    return low, high, gate, up, jax.nn.sigmoid(gate)


def hidden_kernel(gate_up_ref, after_ref, *out_refs):
    del after_ref
    for s, out_ref in enumerate(out_refs):
        _, _, gate, up, sig = swiglu_part(gate_up_ref, len(out_refs), s, out_ref.shape[1])
        out_ref[...] = (gate * sig * up).astype(bf16)


def hidden_parts(gate_up, shards, after):
    slots, width = gate_up.shape
    shape = (slots, width // 2 // shards)
    return pl.pallas_call(
        hidden_kernel,
        grid=(1,),
        in_specs=[block(gate_up.shape), HBM],
        out_specs=[block(shape)] * shards,
        out_shape=[out_hbm(shape, bf16)] * shards,
        compiler_params=params(3 * slots * width),
        cost_estimate=cost(8 * slots * width, 3 * slots * width, slots * width),
    )(*in_hbm(gate_up, after))


def cast_kernel(master_ref, after_ref, weight_ref):
    del after_ref
    weight_ref[...] = master_ref[0].astype(bf16)


def cast_weight(master, after):
    _, part, width = master.shape
    rows = part // 4
    return pl.pallas_call(
        cast_kernel,
        grid=(4,),
        in_specs=[pl.BlockSpec((1, rows, width), lambda i: (0, i, 0)), HBM],
        out_specs=pl.BlockSpec((rows, width), lambda i: (i, 0)),
        out_shape=out_hbm((part, width), bf16),
        compiler_params=params(6 * rows * width),
        cost_estimate=cost(part * width, 6 * part * width),
    )(*in_hbm(master, after))


def mixed_place(index, shards):
    group = div_send(index)
    bits = shards.bit_length() - 1
    step = group & (shards - 1)
    return lax.shift_right_logical(group, bits), step, index - SEND * group


def mix_kernel(shards, *refs):
    parts, out_ref = refs[:shards], refs[-1]
    part = parts[0].shape[1] // 3
    blocks = parts[0].shape[0] // ROWS
    some = max(1, min(blocks, 32 // shards))
    rows, packed = some * shards * SEND, some * shards * ROWS
    row = lax.broadcasted_iota(jnp.int32, (rows, packed), 0)
    col = lax.broadcasted_iota(jnp.int32, (rows, packed), 1)
    at, step, slot = mixed_place(row, shards)
    base = (step * some + at) * ROWS
    orders = [jnp.where(col == base + slot, 1.0, 0.0).astype(bf16)]
    for j in range(3):
        hit = (col == base + SEND + slot - 4 * j) & (slot >= 4 * j) & (slot < 4 * j + 4)
        orders.append(jnp.where(hit, 1.0, 0.0).astype(bf16))
    for first in range(0, blocks, some):
        stack = jnp.concatenate(
            [ref[first * ROWS : (first + some) * ROWS, :] for ref in parts], axis=0
        )
        own = slice(first * shards * SEND, (first + some) * shards * SEND)
        out_ref[own, : 3 * part] = jnp.dot(
            orders[0], stack, preferred_element_type=f32
        ).astype(bf16)
        tail = jnp.zeros((rows, part), f32)
        for j in range(3):
            tail += jnp.dot(
                orders[1 + j],
                stack[:, j * part : (j + 1) * part],
                preferred_element_type=f32,
            )
        out_ref[own, 3 * part :] = tail.astype(bf16)


def mix(parts, weight, after):
    shards = len(parts)
    rows, packed = parts[0].shape
    shape = (rows // ROWS * SEND * shards, packed // 3 * 4)
    return pl.pallas_call(
        functools.partial(mix_kernel, shards),
        grid=(1,),
        in_specs=[block(part.shape) for part in parts] + [HBM] + [ANY] * len(after),
        out_specs=block(shape),
        out_shape=out_hbm(shape, bf16),
        compiler_params=params(12 * rows * packed * shards),
        cost_estimate=cost(0, MIX_COST * rows * packed * shards),
    )(*in_hbm(parts[0]), *parts[1:], *in_hbm(weight), *after)


def reorder(arrived, rows_ref):
    count, width = rows_ref.shape
    part = width // 4
    total = arrived.shape[0]
    slot = lax.broadcasted_iota(jnp.int32, (count, total), 0)
    col = lax.broadcasted_iota(jnp.int32, (count, total), 1)
    order = jnp.where(col == slot + (ROWS - SEND) * div_send(slot), 1.0, 0.0).astype(bf16)
    rows_ref[:, : 3 * part] = jnp.dot(order, arrived, preferred_element_type=f32).astype(bf16)
    tail = jnp.zeros((count, part), f32)
    for j in range(3):
        tail += jnp.dot(
            tail_order(count, total, j, True),
            arrived[:, j * part : (j + 1) * part],
            preferred_element_type=f32,
        )
    rows_ref[:, 3 * part :] = tail.astype(bf16)


def times_weight(rows_ref, weight_ref):
    return lax.dot_general(
        rows_ref[...], weight_ref[...], (((1,), (1,)), ((), ())), preferred_element_type=f32
    )


def score_block(blocks, proj, hidden, picked):
    count = proj.shape[0]
    score = jnp.sum(proj * hidden.astype(f32), axis=1, keepdims=True)
    row = lax.broadcasted_iota(jnp.int32, (count, LANE), 0)
    lane = lax.broadcasted_iota(jnp.int32, (count, LANE), 1)
    spread = jnp.where(row - SEND * div_send(row) == lane, score, 0.0)
    at = lax.broadcasted_iota(jnp.int32, (blocks, count), 1)
    out = []
    for pick in picked:
        gather = (div_send(at) == pick).astype(f32)
        value = jnp.dot(
            gather, spread, precision=lax.Precision.HIGHEST, preferred_element_type=f32
        )
        out.append(value.reshape(blocks, 1, LANE))
    return out


def block_index(blocks, count):
    return lax.broadcasted_iota(jnp.int32, (blocks, count), 0)


def begin_kernel(blocks, arrived_ref, weight_ref, *refs):
    hidden, (rows_ref, proj_ref, score_ref, mixed_ref) = refs[:-4], refs[-4:]
    reorder(arrived_ref[...], rows_ref)
    proj = times_weight(rows_ref, weight_ref)
    proj_ref[...] = proj
    count = proj.shape[0]
    score_ref[...] = score_block(
        blocks, proj, hidden[0][...], [block_index(blocks, count)]
    )[0]
    shards = len(hidden)
    row = lax.broadcasted_iota(jnp.int32, (shards * count, count), 0)
    col = lax.broadcasted_iota(jnp.int32, (shards * count, count), 1)
    at, step, slot = mixed_place(row, shards)
    mixed = 0.0
    for s in range(shards):
        order = jnp.where((step == s) & (col == at * SEND + slot), 1.0, 0.0).astype(bf16)
        mixed += jnp.dot(order, hidden[s][...], preferred_element_type=f32)
    mixed_ref[...] = mixed.astype(bf16)


def begin(blocks, cols, arrived, weight, hidden):
    count = blocks * SEND
    part = weight.shape[0]
    shards = len(hidden)
    out = [
        ((count, cols), bf16),
        ((count, part), f32),
        ((blocks, 1, LANE), f32),
        ((shards * count, part), bf16),
    ]
    nbytes = 4 * count * cols + 2 * part * cols + 4 * count * part * (1 + 3 * shards)
    return pl.pallas_call(
        functools.partial(begin_kernel, blocks),
        grid=(1,),
        in_specs=[block(arrived.shape), block((part, cols))]
        + [block((count, part))] * shards,
        out_specs=[block(shape) for shape, _ in out],
        out_shape=[out_hbm(shape, dtype) for shape, dtype in out],
        compiler_params=params(nbytes),
        cost_estimate=cost(4 * count * part * cols, nbytes),
    )(arrived, *in_hbm(weight, hidden[0]), *hidden[1:])


def finish_kernel(shards, blocks, low, arrived_ref, hidden_ref, weight_ref, *refs):
    before, score_in = refs[:shards], refs[shards : 2 * shards]
    projs, score_ref = refs[2 * shards : 3 * shards], refs[-1]
    proj = times_weight(arrived_ref, weight_ref)
    rounded = proj.astype(bf16)
    total = proj.shape[0]
    count = total // shards
    picked = [block_index(blocks, total) * shards + s for s in range(shards)]
    scores = score_block(blocks, proj, hidden_ref[...], picked)
    me = lax.axis_index("rep")
    slot = lax.broadcasted_iota(jnp.int32, (count, total), 0)
    row = lax.broadcasted_iota(jnp.int32, (count, total), 1)
    for s in range(shards):
        order = row == slot + SEND * (div_send(slot) * (shards - 1) + s)
        order = jnp.where(order, 1.0, 0.0).astype(bf16)
        own = before[s][...] + jnp.dot(order, rounded, preferred_element_type=f32)
        projs[s][...] = own.astype(bf16)
        at = lax.rem(me + shards - s, shards)
        score_ref[pl.ds(at * blocks, blocks)] = score_in[s][...] + scores[s]


def finish(edges, blocks, arrived, hidden, weight, before, scores):
    low, high = edges[-2:]
    shards = len(before)
    total, part = hidden.shape
    count = total // shards
    out = [((count, part), bf16)] * shards + [((shards * blocks, 1, LANE), f32)]
    nbytes = 2 * (total + part) * (high - low) + 14 * total * part
    outs = pl.pallas_call(
        functools.partial(finish_kernel, shards, blocks, low),
        grid=(1,),
        in_specs=[
            block(arrived.shape),
            block(hidden.shape),
            pl.BlockSpec(
                (pl.Element(part), pl.Element(high - low)),
                lambda i: (0, low),
                pipeline_mode=pl.Buffered(1),
            ),
        ]
        + [block((count, part))] * shards
        + [block((blocks, 1, LANE))] * shards,
        out_specs=[block(shape) for shape, _ in out],
        out_shape=[out_hbm(shape, dtype) for shape, dtype in out[:-1]]
        + [jax.ShapeDtypeStruct(*out[-1])],
        compiler_params=params(nbytes),
        cost_estimate=cost(2 * total * part * (high - low), nbytes),
    )(*in_hbm(arrived, hidden, weight, *before, *scores))
    return list(outs[:-1]), outs[-1]


def settle_kernel(low, fresh, blocks, *refs):
    refs = list(refs)

    def take(number):
        out = refs[:number]
        del refs[:number]
        return out

    arrived = take(len(fresh))
    hidden = take(1 + len(fresh))
    given_hbm, *state_hbm = take(4)
    weight_hbm = take(1)[0] if fresh else None
    take(3 if low else 0)
    projs, scores, outs = take(len(fresh)), take(len(fresh)), take(3)
    rows_ref, hidden_t, weight_ref = take(3)
    state, news = take(3), take(3)
    sem, in_sems, out_sems = refs
    cols = rows_ref.shape[1]
    given = given_hbm.shape[0]
    loads = [
        pltpu.make_async_copy(given_hbm, rows_ref.at[pl.ds(0, given)], sem.at[0])
    ]
    if fresh:
        loads.append(
            pltpu.make_async_copy(weight_hbm.at[:, pl.ds(low, cols)], weight_ref, sem.at[1])
        )
    for copy in loads:
        copy.start()

    def load(i):
        return [
            pltpu.make_async_copy(
                source.at[0, :, pl.ds(low + i * UNIT, UNIT)],
                target.at[:, pl.ds(i * UNIT, UNIT)],
                in_sems.at[j, i],
            )
            for j, (source, target) in enumerate(zip(state_hbm, state))
        ]

    def store(i):
        return [
            pltpu.make_async_copy(
                source.at[:, pl.ds(i * UNIT, UNIT)],
                target.at[0, :, pl.ds(low + i * UNIT, UNIT)],
                out_sems.at[j, i],
            )
            for j, (source, target) in enumerate(zip(news, outs))
        ]

    units = cols // UNIT
    for i in range(units):
        for copy in load(i):
            copy.start()
    base = 0
    for ref in hidden:
        count = ref.shape[0]
        hidden_t[:, base : base + count] = ref[...].astype(f32).T.astype(bf16)
        base += count
    for copy in loads:
        copy.wait()
    base = given
    for i, arrived_ref in enumerate(arrived):
        count = blocks * SEND
        own = rows_ref.at[base : base + count]
        base += count
        reorder(arrived_ref[...], own)
        proj = times_weight(own, weight_ref)
        projs[i][...] = proj
        scores[i][...] = score_block(
            blocks, proj, hidden[1 + i][...], [block_index(blocks, count)]
        )[0]

    corr_one = 1.0 - beta_one**adam_step
    corr_two = 1.0 - beta_two**adam_step
    rate = learn_rate * corr_two**0.5 / corr_one
    keep = 1.0 - learn_rate * decay_rate
    for i in range(units):
        for copy in load(i):
            copy.wait()
        own = slice(i * UNIT, (i + 1) * UNIT)
        grad = jnp.dot(hidden_t[...], rows_ref[:, own], preferred_element_type=f32)
        m_new = beta_one * state[1][:, own].astype(f32) + (1.0 - beta_one) * grad
        v_new = beta_two * state[2][:, own].astype(f32) + (1.0 - beta_two) * (grad * grad)
        root = v_new * lax.rsqrt(v_new) + adam_eps * corr_two**0.5
        news[0][:, own] = keep * state[0][:, own] - rate * m_new / root
        news[1][:, own] = m_new.astype(bf16)
        news[2][:, own] = v_new.astype(bf16)
        for copy in store(i):
            copy.start()
    for i in range(units):
        for copy in store(i):
            copy.wait()


def settle(low, blocks, arrived, given, hidden, weight, state, done):
    cols = given.shape[1]
    part = weight.shape[0]
    count = blocks * SEND
    fresh = tuple(range(1, 1 + len(arrived)))
    total = given.shape[0] + count * len(fresh)
    args = list(arrived) + in_hbm(hidden[0]) + list(hidden[1:])
    specs = [block(array.shape) for array in args]
    args += in_hbm(given, *state, *([weight] if fresh else []), *done)
    specs += [HBM] * (4 + bool(fresh) + len(done))
    out = [((count, part), f32)] * len(fresh) + [((blocks, 1, LANE), f32)] * len(fresh)
    kinds = [f32, bf16, bf16]
    scratch = [
        pltpu.VMEM((total, cols), bf16),
        pltpu.VMEM((part, total), bf16),
        pltpu.VMEM((part, cols) if fresh else (ROWS, LANE), bf16),
    ]
    scratch += [pltpu.VMEM((part, cols), kind) for kind in kinds * 2]
    scratch += [pltpu.SemaphoreType.DMA((2,))]
    scratch += [pltpu.SemaphoreType.DMA((3, cols // UNIT))] * 2
    nbytes = 18 * part * cols + 4 * total * cols + 8 * total * part
    outs = pl.pallas_call(
        functools.partial(settle_kernel, low, fresh, blocks),
        grid=(1,),
        in_specs=specs,
        out_specs=[block(shape) for shape, _ in out] + [HBM] * 3,
        out_shape=[out_hbm(shape, dtype) for shape, dtype in out]
        + [out_hbm(array.shape, array.dtype) for array in state],
        scratch_shapes=scratch,
        input_output_aliases={
            len(args) - len(done) + i: len(out) + i for i in range(len(done))
        },
        compiler_params=params(nbytes),
        cost_estimate=cost(4 * total * part * cols, SETTLE_COST * part * cols, part * cols),
    )(*args)
    outs = list(outs)
    return outs[: len(fresh)], outs[len(fresh) : 2 * len(fresh)], outs[-3:]


def close_kernel(shards, gate_up_ref, ids_ref, slots_ref, gates_ref, score_ref, *refs):
    grad_refs, (out_ref, gate_ref) = refs[:-2], refs[-2:]
    part = grad_refs[0].shape[1]
    for s, grad_ref in enumerate(grad_refs):
        low, high, gate, up, sig = swiglu_part(gate_up_ref, shards, s, part)
        grad = grad_ref[...].astype(f32)
        out_ref[:, pl.ds(low, part)] = (
            grad * up * sig * (1.0 + gate * (1.0 - sig))
        ).astype(bf16)
        out_ref[:, pl.ds(high, part)] = (grad * (gate * sig)).astype(bf16)

    blocks = score_ref.shape[1]
    score = score_ref[0].reshape(blocks, LANE)
    for s in range(1, shards):
        score += score_ref[s].reshape(blocks, LANE)
    ids = ids_ref[...]
    slots = slots_ref[...]
    tok = ids.shape[1]
    live = ((ids & (EXP_LOCAL - 1)) == 0) & (slots >= 0)
    owner = ids // EXP_LOCAL
    lane = lax.broadcasted_iota(jnp.int32, (LANE, tok), 0)
    block_of = lax.broadcasted_iota(jnp.int32, (blocks, tok), 0)
    for k in range(TOPK):
        pick = (lane == slots[k : k + 1]).astype(f32)
        value = jnp.dot(score, pick, precision=lax.Precision.HIGHEST, preferred_element_type=f32)
        value = jnp.where(block_of == owner[k : k + 1], value, 0.0)
        value = jnp.sum(value, axis=0, keepdims=True)
        gate_ref[k : k + 1] = jnp.where(
            live[k : k + 1], value / gates_ref[k : k + 1].astype(f32), 0.0
        )


def close(gate_up, ids, slots, gates, score, grads):
    size = gate_up.size
    args = in_hbm(gate_up, ids, slots, gates) + [score] + in_hbm(grads[0]) + grads[1:]
    shapes = [(gate_up.shape, bf16), (ids.shape, f32)]
    return pl.pallas_call(
        functools.partial(close_kernel, len(grads)),
        grid=(1,),
        in_specs=[block(array.shape) for array in args],
        out_specs=[block(shape) for shape, _ in shapes],
        out_shape=[out_hbm(shape, dtype) for shape, dtype in shapes],
        compiler_params=params(8 * size),
        cost_estimate=cost(12 * size, 5 * size, size),
    )(*args)


def per_device(out_grad, expert_ids, slots, gate_weights, saved_gate_up, master, moment1, moment2):
    ep_size = lax.axis_size("ep")
    rep_size = lax.axis_size("rep")
    ids_t, slots_t, gates_t = expert_ids.T, slots.T, gate_weights.T
    gate_up = saved_gate_up[0, 0]
    state = (master, moment1, moment2)
    edges = chunk_edges(out_grad.shape[1])
    steps = range(1, rep_size)

    def shift(value, step):
        perm = [(i, (i + step) % rep_size) for i in range(rep_size)]
        return lax.ppermute(value, "rep", perm)

    def exchange(value):
        return lax.all_to_all(value, "ep", split_axis=0, concat_axis=0, tiled=True)

    send_a, send_b = dispatch(ep_size, edges, ids_t, slots_t, gates_t, out_grad)
    mixed = [send_b] + [shift(send_b, s) for s in steps]
    parts = hidden_parts(gate_up, rep_size, send_b)
    hidden = [parts[0]] + [shift(parts[s], s) for s in steps]
    weight = cast_weight(master, send_b)
    arrived = exchange(send_a.reshape(ep_size, ROWS, -1)).reshape(send_a.shape)
    mixed = mix(mixed, weight, hidden[1:])
    arrived_b = exchange(mixed.reshape(ep_size, rep_size * SEND, -1)).reshape(mixed.shape)

    peers = [shift(arrived, s) for s in steps]
    rows, proj, score_own, hidden_mixed = begin(ep_size, edges[1], arrived, weight, hidden)
    before, scores, done = settle(0, ep_size, peers, rows, hidden, weight, state, ())
    projs, score = finish(
        edges,
        ep_size,
        arrived_b,
        hidden_mixed,
        weight,
        [proj] + before,
        [score_own] + scores,
    )
    grads = [projs[0]] + [shift(projs[s], rep_size - s) for s in steps]
    score = lax.all_to_all(score, ("rep", "ep"), split_axis=0, concat_axis=0, tiled=True)

    _, _, done = settle(
        edges[1], ep_size, [], arrived_b, [hidden_mixed], weight, state, done
    )
    grad_gate_up, gate_grad = close(
        gate_up, ids_t, slots_t, gates_t, score.reshape(rep_size, ep_size, 1, LANE), grads
    )
    return (grad_gate_up.reshape(saved_gate_up.shape), gate_grad.T) + tuple(done)


def solution(mesh):
    in_specs = (
        P(("rep", "ep"), None),
        P(("rep", "ep"), None),
        P(("rep", "ep"), None),
        P(("rep", "ep"), None),
        P("rep", "ep", None, None),
        P("ep", "rep", None),
        P("ep", "rep", None),
        P("ep", "rep", None),
    )
    out_specs = (
        P("rep", "ep", None, None),
        P(("rep", "ep"), None),
        P("ep", "rep", None),
        P("ep", "rep", None),
        P("ep", "rep", None),
    )
    return jax.shard_map(
        per_device, mesh=mesh, in_specs=in_specs, out_specs=out_specs, check_vma=False
    )
```

```python
import functools

import jax
import jax.numpy as jnp
from jax import lax
from jax.experimental import pallas as pl
from jax.experimental.pallas import tpu as pltpu
from jax.sharding import PartitionSpec as P

TOPK = 8
EXP_LOCAL = 8
SEND = 12
LANE = 128
UNIT = 512
DEPTH = 4
ROWS = 16

beta_one = 0.9
beta_two = 0.95
learn_rate = 0.002
decay_rate = 0.1
adam_eps = 1e-08
adam_step = 50

f32 = jnp.float32
bf16 = jnp.bfloat16
HBM = pl.BlockSpec(memory_space=pltpu.HBM)


def in_hbm(*arrays):
    return [pltpu.with_memory_space_constraint(array, pltpu.HBM) for array in arrays]


def out_hbm(dims, dtype):
    return pltpu.HBM(tuple(dims), dtype)


def block(dims, at=None):
    at = at or (0,) * len(dims)
    return pl.BlockSpec(tuple(dims), lambda i: at, pipeline_mode=pl.Buffered(1))


def params(nbytes):
    mib = min(60, max(16, 10 + 5 * int(nbytes) // 2**22))
    return pltpu.CompilerParams(vmem_limit_bytes=mib * 2**20)


def cost(flops, nbytes, transcendentals=0):
    return pl.CostEstimate(
        flops=int(flops), bytes_accessed=int(nbytes), transcendentals=int(transcendentals)
    )


def div_send(index):
    return lax.shift_right_logical(index * 10923, 17)


def pack(cols):
    return cols // 4 * 3


def chunk_edges(width):
    units = width // UNIT
    return (0, (units - max(1, units * 3 // 7)) * UNIT, width)


def tail_order(count, total, j, slots_first):
    a = lax.broadcasted_iota(jnp.int32, (count, total), 0)
    b = lax.broadcasted_iota(jnp.int32, (count, total), 1)
    if slots_first:
        block_of = div_send(a)
        inner = a - SEND * block_of
        hit = b == block_of * ROWS + SEND + inner - 4 * j
    else:
        inner = (a & (ROWS - 1)) - SEND + 4 * j
        hit = (b == a - SEND + 4 * j) & ((a & (ROWS - 1)) >= SEND)
    return jnp.where(hit & (inner >= 4 * j) & (inner < 4 * j + 4), 1.0, 0.0).astype(bf16)


def dispatch_kernel(edges, ids_hbm, slots_hbm, gates_hbm, grad_hbm, *refs):
    outs, (ids_ref, slots_ref, gates_ref, grad_ref) = refs[:2], refs[2:6]
    sends, sems, out_sems = refs[6:8], refs[8], refs[9]
    pairs = [
        (ids_hbm, ids_ref),
        (slots_hbm, slots_ref),
        (gates_hbm, gates_ref),
        (grad_hbm, grad_ref),
    ]
    copies = [
        pltpu.make_async_copy(source, target, sems.at[i])
        for i, (source, target) in enumerate(pairs)
    ]
    for copy in copies:
        copy.start()
    rows = outs[0].shape[0]
    tok = ids_ref.shape[1]
    orders = [tail_order(rows, rows, j, False) for j in range(3)]
    for copy in copies[:3]:
        copy.wait()
    ids = ids_ref[...]
    slots = slots_ref[...]
    gates = gates_ref[...].astype(f32)
    live = ((ids & (EXP_LOCAL - 1)) == 0) & (slots >= 0)
    place = jnp.where(live, ids // EXP_LOCAL * ROWS + slots, -1)
    row = lax.broadcasted_iota(jnp.int32, (rows, tok), 0)
    main = jnp.zeros((rows, tok), f32)
    for k in range(TOPK):
        main = jnp.where(row == place[k : k + 1], gates[k : k + 1], main)
    main = main.astype(bf16)
    tails = [
        jnp.dot(order, main, preferred_element_type=f32).astype(bf16) for order in orders
    ]
    copies[3].wait()
    out_copies = []
    for c in (1, 0):
        low, high = edges[c], edges[c + 1]
        part = (high - low) // 4
        for j in range(3):
            total = jnp.dot(
                main,
                grad_ref[:, low + j * part : low + (j + 1) * part],
                preferred_element_type=f32,
            )
            total += jnp.dot(
                tails[j], grad_ref[:, low + 3 * part : high], preferred_element_type=f32
            )
            own = (slice(None), pl.ds(j * part, part))
            sends[c][own] = total.astype(bf16)
            copy = pltpu.make_async_copy(
                sends[c].at[own], outs[c].at[own], out_sems.at[c, j]
            )
            copy.start()
            out_copies.append(copy)
    for copy in out_copies:
        copy.wait()


def dispatch(blocks, edges, ids, slots, gates, out_grad):
    tok, width = out_grad.shape
    rows = blocks * ROWS
    shapes = [(rows, pack(high - low)) for low, high in zip(edges[:-1], edges[1:])]
    return pl.pallas_call(
        functools.partial(dispatch_kernel, edges),
        in_specs=[HBM] * 4,
        out_specs=[HBM] * 2,
        out_shape=[out_hbm(shape, bf16) for shape in shapes],
        scratch_shapes=[
            pltpu.VMEM(ids.shape, jnp.int32),
            pltpu.VMEM(slots.shape, jnp.int32),
            pltpu.VMEM(gates.shape, bf16),
            pltpu.VMEM(out_grad.shape, bf16),
        ]
        + [pltpu.VMEM(shape, bf16) for shape in shapes]
        + [pltpu.SemaphoreType.DMA((4,)), pltpu.SemaphoreType.DMA((2, 3))],
        compiler_params=params(2 * rows * width + 2 * tok * width),
        cost_estimate=cost(2 * rows * tok * width, 4 * tok * width),
    )(*in_hbm(ids, slots, gates, out_grad))


def swiglu_part(gate_up_ref, shards, step, part):
    at = lax.rem(lax.axis_index("rep") + step, shards)
    low = pl.multiple_of(at * part, part)
    high = pl.multiple_of((shards + at) * part, part)
    gate = gate_up_ref[:, pl.ds(low, part)].astype(f32)
    up = gate_up_ref[:, pl.ds(high, part)].astype(f32)
    return low, high, gate, up, jax.nn.sigmoid(gate)


def hidden_kernel(gate_up_ref, after_ref, *out_refs):
    del after_ref
    for s, out_ref in enumerate(out_refs):
        _, _, gate, up, sig = swiglu_part(gate_up_ref, len(out_refs), s, out_ref.shape[1])
        out_ref[...] = (gate * sig * up).astype(bf16)


def hidden_parts(gate_up, shards, after):
    slots, width = gate_up.shape
    shape = (slots, width // 2 // shards)
    return pl.pallas_call(
        hidden_kernel,
        grid=(1,),
        in_specs=[block(gate_up.shape), HBM],
        out_specs=[block(shape)] * shards,
        out_shape=[out_hbm(shape, bf16)] * shards,
        compiler_params=params(3 * slots * width),
        cost_estimate=cost(8 * slots * width, 3 * slots * width, slots * width),
    )(*in_hbm(gate_up, after))


def cast_kernel(master_ref, after_ref, weight_ref):
    del after_ref
    weight_ref[...] = master_ref[0].astype(bf16)


def cast_weight(master, after):
    _, part, width = master.shape
    rows = part // 4
    return pl.pallas_call(
        cast_kernel,
        grid=(4,),
        in_specs=[pl.BlockSpec((1, rows, width), lambda i: (0, i, 0)), HBM],
        out_specs=pl.BlockSpec((rows, width), lambda i: (i, 0)),
        out_shape=out_hbm((part, width), bf16),
        compiler_params=params(6 * rows * width),
        cost_estimate=cost(part * width, 6 * part * width),
    )(*in_hbm(master, after))


def mixed_place(index, shards):
    group = div_send(index)
    bits = shards.bit_length() - 1
    step = group & (shards - 1)
    return lax.shift_right_logical(group, bits), step, index - SEND * group


def mix_kernel(shards, *refs):
    parts, out_ref = refs[:shards], refs[-1]
    part = parts[0].shape[1] // 3
    blocks = parts[0].shape[0] // ROWS
    some = max(1, min(blocks, 32 // shards))
    rows, packed = some * shards * SEND, some * shards * ROWS
    row = lax.broadcasted_iota(jnp.int32, (rows, packed), 0)
    col = lax.broadcasted_iota(jnp.int32, (rows, packed), 1)
    at, step, slot = mixed_place(row, shards)
    base = (step * some + at) * ROWS
    orders = [jnp.where(col == base + slot, 1.0, 0.0).astype(bf16)]
    for j in range(3):
        hit = (col == base + SEND + slot - 4 * j) & (slot >= 4 * j) & (slot < 4 * j + 4)
        orders.append(jnp.where(hit, 1.0, 0.0).astype(bf16))
    for first in range(0, blocks, some):
        stack = jnp.concatenate(
            [ref[first * ROWS : (first + some) * ROWS, :] for ref in parts], axis=0
        )
        own = slice(first * shards * SEND, (first + some) * shards * SEND)
        out_ref[own, : 3 * part] = jnp.dot(
            orders[0], stack, preferred_element_type=f32
        ).astype(bf16)
        tail = jnp.zeros((rows, part), f32)
        for j in range(3):
            tail += jnp.dot(
                orders[1 + j],
                stack[:, j * part : (j + 1) * part],
                preferred_element_type=f32,
            )
        out_ref[own, 3 * part :] = tail.astype(bf16)


def mix(parts, weight):
    shards = len(parts)
    rows, packed = parts[0].shape
    shape = (rows // ROWS * SEND * shards, packed // 3 * 4)
    return pl.pallas_call(
        functools.partial(mix_kernel, shards),
        grid=(1,),
        in_specs=[block(part.shape) for part in parts] + [HBM],
        out_specs=block(shape),
        out_shape=out_hbm(shape, bf16),
        compiler_params=params(12 * rows * packed * shards),
        cost_estimate=cost(0, 5 * rows * packed * shards),
    )(*in_hbm(parts[0]), *parts[1:], *in_hbm(weight))


def reorder(arrived, rows_ref):
    count, width = rows_ref.shape
    part = width // 4
    total = arrived.shape[0]
    slot = lax.broadcasted_iota(jnp.int32, (count, total), 0)
    col = lax.broadcasted_iota(jnp.int32, (count, total), 1)
    order = jnp.where(col == slot + (ROWS - SEND) * div_send(slot), 1.0, 0.0).astype(bf16)
    rows_ref[:, : 3 * part] = jnp.dot(order, arrived, preferred_element_type=f32).astype(bf16)
    tail = jnp.zeros((count, part), f32)
    for j in range(3):
        tail += jnp.dot(
            tail_order(count, total, j, True),
            arrived[:, j * part : (j + 1) * part],
            preferred_element_type=f32,
        )
    rows_ref[:, 3 * part :] = tail.astype(bf16)


def times_weight(rows_ref, weight_ref):
    return lax.dot_general(
        rows_ref[...], weight_ref[...], (((1,), (1,)), ((), ())), preferred_element_type=f32
    )


def score_block(blocks, proj, hidden, picked):
    count = proj.shape[0]
    score = jnp.sum(proj * hidden.astype(f32), axis=1, keepdims=True)
    row = lax.broadcasted_iota(jnp.int32, (count, LANE), 0)
    lane = lax.broadcasted_iota(jnp.int32, (count, LANE), 1)
    spread = jnp.where(row - SEND * div_send(row) == lane, score, 0.0)
    high = spread.astype(bf16)
    rest = (spread - high.astype(f32)).astype(bf16)
    at = lax.broadcasted_iota(jnp.int32, (blocks, count), 1)
    gather = [jnp.where(div_send(at) == pick, 1.0, 0.0) for pick in picked]
    gather = jnp.concatenate(gather, axis=0).astype(bf16)
    value = jnp.dot(gather, high, preferred_element_type=f32)
    value += jnp.dot(gather, rest, preferred_element_type=f32)
    return [
        value[i * blocks : (i + 1) * blocks].reshape(blocks, 1, LANE)
        for i in range(len(picked))
    ]


def block_index(blocks, count):
    return lax.broadcasted_iota(jnp.int32, (blocks, count), 0)


def begin_kernel(blocks, arrived_ref, weight_ref, *refs):
    hidden, (rows_ref, proj_ref, score_ref, mixed_ref) = refs[:-4], refs[-4:]
    reorder(arrived_ref[...], rows_ref)
    proj = times_weight(rows_ref, weight_ref)
    proj_ref[...] = proj
    count = proj.shape[0]
    score_ref[...] = score_block(
        blocks, proj, hidden[0][...], [block_index(blocks, count)]
    )[0]
    shards = len(hidden)
    row = lax.broadcasted_iota(jnp.int32, (shards * count, count), 0)
    col = lax.broadcasted_iota(jnp.int32, (shards * count, count), 1)
    at, step, slot = mixed_place(row, shards)
    mixed = 0.0
    for s in range(shards):
        order = jnp.where((step == s) & (col == at * SEND + slot), 1.0, 0.0).astype(bf16)
        mixed += jnp.dot(order, hidden[s][...], preferred_element_type=f32)
    mixed_ref[...] = mixed.astype(bf16)


def begin(blocks, cols, arrived, weight, hidden):
    count = blocks * SEND
    part = weight.shape[0]
    shards = len(hidden)
    out = [
        ((count, cols), bf16),
        ((count, part), f32),
        ((blocks, 1, LANE), f32),
        ((shards * count, part), bf16),
    ]
    nbytes = 4 * count * cols + 2 * part * cols + 4 * count * part * (1 + 3 * shards)
    return pl.pallas_call(
        functools.partial(begin_kernel, blocks),
        grid=(1,),
        in_specs=[block(arrived.shape), block((part, cols))]
        + [block((count, part))] * shards,
        out_specs=[block(shape) for shape, _ in out],
        out_shape=[out_hbm(shape, dtype) for shape, dtype in out],
        compiler_params=params(nbytes),
        cost_estimate=cost(4 * count * part * cols, nbytes),
    )(arrived, *in_hbm(weight, hidden[0]), *hidden[1:])


def finish_kernel(shards, blocks, low, arrived_ref, hidden_ref, weight_ref, *refs):
    before, score_in = refs[:shards], refs[shards : 2 * shards]
    projs, score_ref = refs[2 * shards : 3 * shards], refs[-1]
    proj = times_weight(arrived_ref, weight_ref)
    rounded = proj.astype(bf16)
    total = proj.shape[0]
    count = total // shards
    picked = [block_index(blocks, total) * shards + s for s in range(shards)]
    scores = score_block(blocks, proj, hidden_ref[...], picked)
    me = lax.axis_index("rep")
    slot = lax.broadcasted_iota(jnp.int32, (count, total), 0)
    row = lax.broadcasted_iota(jnp.int32, (count, total), 1)
    for s in range(shards):
        order = row == slot + SEND * (div_send(slot) * (shards - 1) + s)
        order = jnp.where(order, 1.0, 0.0).astype(bf16)
        own = before[s][...] + jnp.dot(order, rounded, preferred_element_type=f32)
        projs[s][...] = own.astype(bf16)
        at = lax.rem(me + shards - s, shards)
        score_ref[pl.ds(at * blocks, blocks)] = score_in[s][...] + scores[s]


def finish(edges, blocks, arrived, hidden, weight, before, scores):
    low, high = edges[-2:]
    shards = len(before)
    total, part = hidden.shape
    count = total // shards
    out = [((count, part), bf16)] * shards + [((shards * blocks, 1, LANE), f32)]
    nbytes = 2 * (total + part) * (high - low) + 14 * total * part
    outs = pl.pallas_call(
        functools.partial(finish_kernel, shards, blocks, low),
        grid=(1,),
        in_specs=[
            block(arrived.shape),
            block(hidden.shape),
            pl.BlockSpec(
                (pl.Element(part), pl.Element(high - low)),
                lambda i: (0, low),
                pipeline_mode=pl.Buffered(1),
            ),
        ]
        + [block((count, part))] * shards
        + [block((blocks, 1, LANE))] * shards,
        out_specs=[block(shape) for shape, _ in out],
        out_shape=[out_hbm(shape, dtype) for shape, dtype in out[:-1]]
        + [jax.ShapeDtypeStruct(*out[-1])],
        compiler_params=params(nbytes),
        cost_estimate=cost(2 * total * part * (high - low), nbytes),
    )(arrived, *in_hbm(hidden, weight, *before, *scores))
    return list(outs[:-1]), outs[-1]


def settle_kernel(low, fresh, blocks, *refs):
    refs = list(refs)

    def take(number):
        out = refs[:number]
        del refs[:number]
        return out

    arrived = take(len(fresh))
    hidden = take(1 + len(fresh))
    given_ref, *state_hbm = take(4)
    weight_hbm = take(1)[0] if fresh else None
    take(3 if low else 0)
    projs, scores, outs = take(len(fresh)), take(len(fresh)), take(3)
    hidden_t, grad_ref = take(2)
    state = take(3)
    in_sems, out_sems = take(2)
    part, cols = grad_ref.shape
    given = given_ref.shape[0]
    step = part // out_sems.shape[1]
    steps = part // step

    def load(i):
        rows = pl.ds(pl.multiple_of(i * step, step), step)
        return [
            pltpu.make_async_copy(
                source.at[0, rows, pl.ds(low, cols)], target.at[rows], in_sems.at[j, i]
            )
            for j, (source, target) in enumerate(zip(state_hbm, state))
        ]

    def store(i):
        rows = pl.ds(pl.multiple_of(i * step, step), step)
        return [
            pltpu.make_async_copy(
                source.at[rows], target.at[0, rows, pl.ds(low, cols)], out_sems.at[j, i]
            )
            for j, (source, target) in enumerate(zip(state, outs))
        ]

    def start_loads(first, end):
        for i in range(first, end):
            for copy in load(i):
                copy.start()

    if fresh:
        rows_ref, weight_ref, sems = take(3)
        loads = [
            pltpu.make_async_copy(weight_hbm.at[:, pl.ds(low, cols)], weight_ref, sems.at[0]),
            pltpu.make_async_copy(given_ref, rows_ref.at[pl.ds(0, given)], sems.at[1]),
        ]
        for copy in loads:
            copy.start()
    else:
        rows_ref = given_ref
        start_loads(0, min(DEPTH, steps))
    base = 0
    for ref in hidden:
        count = ref.shape[0]
        hidden_t[:, base : base + count] = ref[...].astype(f32).T.astype(bf16)
        base += count
    if fresh:
        count = blocks * SEND
        for i, arrived_ref in enumerate(arrived):
            reorder(
                arrived_ref[...],
                rows_ref.at[given + i * count : given + (i + 1) * count],
            )
        loads[0].wait()
        start_loads(0, min(DEPTH, steps))
        for i in range(len(fresh)):
            own = rows_ref.at[given + i * count : given + (i + 1) * count]
            proj = times_weight(own, weight_ref)
            projs[i][...] = proj
            scores[i][...] = score_block(
                blocks, proj, hidden[1 + i][...], [block_index(blocks, count)]
            )[0]
        loads[1].wait()
    for i in range(cols // UNIT):
        own = slice(i * UNIT, (i + 1) * UNIT)
        grad_ref[:, own] = jnp.dot(
            hidden_t[...], rows_ref[:, own], preferred_element_type=f32
        )

    corr_one = 1.0 - beta_one**adam_step
    corr_two = 1.0 - beta_two**adam_step
    rate = learn_rate * corr_two**0.5 / corr_one
    keep = 1.0 - learn_rate * decay_rate
    eps = adam_eps * corr_two**0.5

    @pl.loop(0, steps)
    def _(i):
        for copy in load(i):
            copy.wait()

        @pl.when(i + DEPTH < steps)
        def _():
            for copy in load(i + DEPTH):
                copy.start()

        own = pl.ds(pl.multiple_of(i * step, step), step)
        grad = grad_ref[own, :]
        m_new = beta_one * state[1][own, :].astype(f32) + (1.0 - beta_one) * grad
        v_new = beta_two * state[2][own, :].astype(f32) + (1.0 - beta_two) * (grad * grad)
        root = lax.rsqrt(v_new)
        below = 1.0 + eps * root
        inverse = pl.reciprocal(below, approx=True)
        inverse = inverse * (2.0 - below * inverse)
        state[0][own, :] = keep * state[0][own, :] - (rate * m_new) * (root * inverse)
        state[1][own, :] = m_new.astype(bf16)
        state[2][own, :] = v_new.astype(bf16)
        for copy in store(i):
            copy.start()

    @pl.loop(0, steps)
    def _(i):
        for copy in store(i):
            copy.wait()


def settle(low, blocks, arrived, given, hidden, weight, state, done):
    cols = given.shape[1]
    part = weight.shape[0]
    count = blocks * SEND
    fresh = tuple(range(1, 1 + len(arrived)))
    total = given.shape[0] + count * len(fresh)
    steps = max(1, part // 64)
    args = list(arrived) + in_hbm(hidden[0]) + list(hidden[1:])
    specs = [block(array.shape) for array in args]
    if fresh:
        args += in_hbm(given)
        specs.append(HBM)
    else:
        args.append(given)
        specs.append(block(given.shape))
    args += in_hbm(*state, *([weight] if fresh else []), *done)
    specs += [HBM] * (3 + bool(fresh) + len(done))
    out = [((count, part), f32)] * len(fresh) + [((blocks, 1, LANE), f32)] * len(fresh)
    scratch = [pltpu.VMEM((part, total), bf16), pltpu.VMEM((part, cols), f32)]
    scratch += [pltpu.VMEM((part, cols), kind) for kind in (f32, bf16, bf16)]
    scratch += [pltpu.SemaphoreType.DMA((3, steps))] * 2
    if fresh:
        scratch += [
            pltpu.VMEM((total, cols), bf16),
            pltpu.VMEM((part, cols), bf16),
            pltpu.SemaphoreType.DMA((2,)),
        ]
    nbytes = 14 * part * cols + 4 * total * cols + 8 * total * part
    outs = pl.pallas_call(
        functools.partial(settle_kernel, low, fresh, blocks),
        grid=(1,),
        in_specs=specs,
        out_specs=[block(shape) for shape, _ in out] + [HBM] * 3,
        out_shape=[out_hbm(shape, dtype) for shape, dtype in out]
        + [out_hbm(array.shape, array.dtype) for array in state],
        scratch_shapes=scratch,
        input_output_aliases={
            len(args) - len(done) + i: len(out) + i for i in range(len(done))
        },
        compiler_params=params(nbytes),
        cost_estimate=cost(4 * total * part * cols, 22 * part * cols, part * cols),
    )(*args)
    outs = list(outs)
    return outs[: len(fresh)], outs[len(fresh) : 2 * len(fresh)], outs[-3:]


def close_kernel(shards, gate_up_ref, ids_ref, slots_ref, gates_ref, score_ref, *refs):
    grad_refs, (out_ref, gate_ref) = refs[:-2], refs[-2:]
    part = grad_refs[0].shape[1]
    for s, grad_ref in enumerate(grad_refs):
        low, high, gate, up, sig = swiglu_part(gate_up_ref, shards, s, part)
        grad = grad_ref[...].astype(f32)
        out_ref[:, pl.ds(low, part)] = (
            grad * up * sig * (1.0 + gate * (1.0 - sig))
        ).astype(bf16)
        out_ref[:, pl.ds(high, part)] = (grad * (gate * sig)).astype(bf16)

    ids = ids_ref[...]
    slots = slots_ref[...]
    live = ((ids & (EXP_LOCAL - 1)) == 0) & (slots >= 0)
    place = jnp.where(live, ids // EXP_LOCAL * SEND + slots, -1)
    blocks = score_ref.shape[0] // shards
    value = jnp.zeros(ids.shape, f32)
    for b in range(blocks):
        for slot in range(SEND):
            score = score_ref[b, 0, slot]
            for s in range(1, shards):
                score += score_ref[s * blocks + b, 0, slot]
            value = jnp.where(place == b * SEND + slot, score, value)
    gate_ref[...] = jnp.where(live, value / gates_ref[...].astype(f32), 0.0)


def close(gate_up, ids, slots, gates, score, grads):
    size = gate_up.size
    args = in_hbm(gate_up, ids, slots, gates) + [score] + in_hbm(grads[0]) + grads[1:]
    shapes = [(gate_up.shape, bf16), (ids.shape, f32)]
    return pl.pallas_call(
        functools.partial(close_kernel, len(grads)),
        grid=(1,),
        in_specs=[block(array.shape) for array in args[:4]]
        + [pl.BlockSpec(memory_space=pltpu.SMEM)]
        + [block(grad.shape) for grad in grads],
        out_specs=[block(shape) for shape, _ in shapes],
        out_shape=[out_hbm(shape, dtype) for shape, dtype in shapes],
        compiler_params=params(8 * size),
        cost_estimate=cost(12 * size, 5 * size, size),
    )(*args)


def per_device(out_grad, expert_ids, slots, gate_weights, saved_gate_up, master, moment1, moment2):
    ep_size = lax.axis_size("ep")
    rep_size = lax.axis_size("rep")
    ids_t, slots_t, gates_t = expert_ids.T, slots.T, gate_weights.T
    gate_up = saved_gate_up[0, 0]
    state = (master, moment1, moment2)
    edges = chunk_edges(out_grad.shape[1])
    steps = range(1, rep_size)

    def shift(value, step):
        perm = [(i, (i + step) % rep_size) for i in range(rep_size)]
        return lax.ppermute(value, "rep", perm)

    def exchange(value):
        return lax.all_to_all(value, "ep", split_axis=0, concat_axis=0, tiled=True)

    send_a, send_b = dispatch(ep_size, edges, ids_t, slots_t, gates_t, out_grad)
    mixed = [send_b] + [shift(send_b, s) for s in steps]
    parts = hidden_parts(gate_up, rep_size, send_b)
    hidden = [parts[0]] + [shift(parts[s], s) for s in steps]
    weight = cast_weight(master, send_b)
    arrived = exchange(send_a.reshape(ep_size, ROWS, -1)).reshape(send_a.shape)
    mixed = mix(mixed, weight)
    arrived_b = exchange(mixed.reshape(ep_size, rep_size * SEND, -1)).reshape(mixed.shape)

    arrived, *hidden[1:] = lax.optimization_barrier([arrived] + hidden[1:])
    peers = [shift(arrived, s) for s in steps]
    rows, proj, score_own, hidden_mixed = begin(ep_size, edges[1], arrived, weight, hidden)
    before, scores, done = settle(0, ep_size, peers, rows, hidden, weight, state, ())
    projs, score = finish(
        edges,
        ep_size,
        arrived_b,
        hidden_mixed,
        weight,
        [proj] + before,
        [score_own] + scores,
    )
    grads = [projs[0]] + [shift(projs[s], rep_size - s) for s in steps]
    score = lax.all_to_all(score, ("rep", "ep"), split_axis=0, concat_axis=0, tiled=True)

    _, _, done = settle(
        edges[1], ep_size, [], arrived_b, [hidden_mixed], weight, state, done
    )
    grad_gate_up, gate_grad = close(
        gate_up, ids_t, slots_t, gates_t, score, grads
    )
    return (grad_gate_up.reshape(saved_gate_up.shape), gate_grad.T) + tuple(done)


def solution(mesh):
    in_specs = (
        P(("rep", "ep"), None),
        P(("rep", "ep"), None),
        P(("rep", "ep"), None),
        P(("rep", "ep"), None),
        P("rep", "ep", None, None),
        P("ep", "rep", None),
        P("ep", "rep", None),
        P("ep", "rep", None),
    )
    out_specs = (
        P("rep", "ep", None, None),
        P(("rep", "ep"), None),
        P("ep", "rep", None),
        P("ep", "rep", None),
        P("ep", "rep", None),
    )
    return jax.shard_map(
        per_device, mesh=mesh, in_specs=in_specs, out_specs=out_specs, check_vma=False
    )
```

```python
import functools

import jax
import jax.numpy as jnp
from jax import lax
from jax.experimental import pallas as pl
from jax.experimental.pallas import tpu as pltpu
from jax.sharding import PartitionSpec as P

TOPK = 8
EXP_LOCAL = 8
SEND = 12
LANE = 128
UNIT = 512
SETTLE_COST = 140
ROWS = 16

beta_one = 0.9
beta_two = 0.95
learn_rate = 0.002
decay_rate = 0.1
adam_eps = 1e-08
adam_step = 50

f32 = jnp.float32
bf16 = jnp.bfloat16
HBM = pl.BlockSpec(memory_space=pltpu.HBM)
ANY = pl.BlockSpec(memory_space=pl.ANY)
VMEM = pl.BlockSpec(memory_space=pltpu.VMEM)


def in_hbm(*arrays):
    return [pltpu.with_memory_space_constraint(array, pltpu.HBM) for array in arrays]


def plain(dims, dtype):
    return jax.ShapeDtypeStruct(tuple(dims), dtype)


def out_hbm(dims, dtype):
    return pltpu.HBM(tuple(dims), dtype)


def block(dims, at=None):
    at = at or (0,) * len(dims)
    return pl.BlockSpec(tuple(dims), lambda i: at, pipeline_mode=pl.Buffered(1))


def params(nbytes):
    mib = min(60, max(16, 10 + 5 * int(nbytes) // 2**22))
    return pltpu.CompilerParams(vmem_limit_bytes=mib * 2**20)


def cost(flops, nbytes, transcendentals=0):
    return pl.CostEstimate(
        flops=int(flops), bytes_accessed=int(nbytes), transcendentals=int(transcendentals)
    )


def div_send(index):
    return lax.shift_right_logical(index * 10923, 17)


def pack(cols):
    return cols // 4 * 3


def chunk_edges(width):
    units = width // UNIT
    return (0, (units - max(1, units * 3 // 7)) * UNIT, width)


def tail_order(count, total, j, slots_first):
    a = lax.broadcasted_iota(jnp.int32, (count, total), 0)
    b = lax.broadcasted_iota(jnp.int32, (count, total), 1)
    if slots_first:
        block_of = div_send(a)
        inner = a - SEND * block_of
        hit = b == block_of * ROWS + SEND + inner - 4 * j
    else:
        inner = (a & (ROWS - 1)) - SEND + 4 * j
        hit = (b == a - SEND + 4 * j) & ((a & (ROWS - 1)) >= SEND)
    return jnp.where(hit & (inner >= 4 * j) & (inner < 4 * j + 4), 1.0, 0.0).astype(bf16)


def dispatch_kernel(edges, ids_hbm, slots_hbm, gates_hbm, grad_hbm, *refs):
    outs, (ids_ref, slots_ref, gates_ref, grad_ref) = refs[:2], refs[2:6]
    sends, sems, out_sems = refs[6:8], refs[8], refs[9]
    pairs = [
        (ids_hbm, ids_ref),
        (slots_hbm, slots_ref),
        (gates_hbm, gates_ref),
        (grad_hbm, grad_ref),
    ]
    copies = [
        pltpu.make_async_copy(source, target, sems.at[i])
        for i, (source, target) in enumerate(pairs)
    ]
    for copy in copies:
        copy.start()
    rows = outs[0].shape[0]
    tok = ids_ref.shape[1]
    orders = [tail_order(rows, rows, j, False) for j in range(3)]
    for copy in copies[:3]:
        copy.wait()
    ids = ids_ref[...]
    slots = slots_ref[...]
    gates = gates_ref[...].astype(f32)
    live = ((ids & (EXP_LOCAL - 1)) == 0) & (slots >= 0)
    place = jnp.where(live, ids // EXP_LOCAL * ROWS + slots, -1)
    row = lax.broadcasted_iota(jnp.int32, (rows, tok), 0)
    main = jnp.zeros((rows, tok), f32)
    for k in range(TOPK):
        main = jnp.where(row == place[k : k + 1], gates[k : k + 1], main)
    main = main.astype(bf16)
    tails = [
        jnp.dot(order, main, preferred_element_type=f32).astype(bf16) for order in orders
    ]
    copies[3].wait()
    out_copies = []
    for c in (1, 0):
        low, high = edges[c], edges[c + 1]
        part = (high - low) // 4
        for j in range(3):
            total = jnp.dot(
                main,
                grad_ref[:, low + j * part : low + (j + 1) * part],
                preferred_element_type=f32,
            )
            total += jnp.dot(
                tails[j], grad_ref[:, low + 3 * part : high], preferred_element_type=f32
            )
            own = (slice(None), pl.ds(j * part, part))
            sends[c][own] = total.astype(bf16)
            copy = pltpu.make_async_copy(
                sends[c].at[own], outs[c].at[own], out_sems.at[c, j]
            )
            copy.start()
            out_copies.append(copy)
    for copy in out_copies:
        copy.wait()


def dispatch(blocks, edges, ids, slots, gates, out_grad):
    tok, width = out_grad.shape
    rows = blocks * ROWS
    shapes = [(rows, pack(high - low)) for low, high in zip(edges[:-1], edges[1:])]
    return pl.pallas_call(
        functools.partial(dispatch_kernel, edges),
        in_specs=[HBM] * 4,
        out_specs=[HBM] * 2,
        out_shape=[out_hbm(shape, bf16) for shape in shapes],
        scratch_shapes=[
            pltpu.VMEM(ids.shape, jnp.int32),
            pltpu.VMEM(slots.shape, jnp.int32),
            pltpu.VMEM(gates.shape, bf16),
            pltpu.VMEM(out_grad.shape, bf16),
        ]
        + [pltpu.VMEM(shape, bf16) for shape in shapes]
        + [pltpu.SemaphoreType.DMA((4,)), pltpu.SemaphoreType.DMA((2, 3))],
        compiler_params=params(2 * rows * width + 2 * tok * width),
        cost_estimate=cost(2 * rows * tok * width, 4 * tok * width),
    )(*in_hbm(ids, slots, gates, out_grad))


def swiglu_part(gate_up_ref, shards, step, part):
    at = lax.rem(lax.axis_index("rep") + step, shards)
    low = pl.multiple_of(at * part, part)
    high = pl.multiple_of((shards + at) * part, part)
    gate = gate_up_ref[:, pl.ds(low, part)].astype(f32)
    up = gate_up_ref[:, pl.ds(high, part)].astype(f32)
    return low, high, gate, up, jax.nn.sigmoid(gate)


def hidden_kernel(gate_up_ref, after_ref, *out_refs):
    del after_ref
    for s, out_ref in enumerate(out_refs):
        _, _, gate, up, sig = swiglu_part(gate_up_ref, len(out_refs), s, out_ref.shape[1])
        out_ref[...] = (gate * sig * up).astype(bf16)


def hidden_parts(gate_up, shards, after):
    slots, width = gate_up.shape
    shape = (slots, width // 2 // shards)
    return pl.pallas_call(
        hidden_kernel,
        grid=(1,),
        in_specs=[block(gate_up.shape), HBM],
        out_specs=[block(shape)] * shards,
        out_shape=[plain(shape, bf16)] * shards,
        compiler_params=params(3 * slots * width),
        cost_estimate=cost(8 * slots * width, 3 * slots * width, slots * width),
    )(*in_hbm(gate_up, after))


def load_kernel(middle, after_ref, master_hbm, one_hbm, two_hbm, *refs):
    del after_ref
    master_ref, one_ref, two_ref, weight_a, weight_b, sems = refs
    part = master_ref.shape[0]
    step = part // 4
    copies = []
    for i in range(4):
        own = pl.ds(i * step, step)
        copies.append(
            pltpu.make_async_copy(master_hbm.at[0, own], master_ref.at[own], sems.at[i])
        )
    copies.append(pltpu.make_async_copy(one_hbm.at[0], one_ref, sems.at[4]))
    copies.append(pltpu.make_async_copy(two_hbm.at[0], two_ref, sems.at[5]))
    for copy in copies:
        copy.start()
    for i in range(4):
        copies[i].wait()
        own = slice(i * step, (i + 1) * step)
        weight_a[own, :] = master_ref[own, :middle].astype(bf16)
        weight_b[own, :] = master_ref[own, middle:].astype(bf16)
    copies[4].wait()
    copies[5].wait()


def load_state(middle, master, one, two, after):
    _, part, width = master.shape
    return pl.pallas_call(
        functools.partial(load_kernel, middle),
        in_specs=[HBM] * 4,
        out_specs=[VMEM] * 5,
        out_shape=[
            pltpu.VMEM((part, width), f32),
            pltpu.VMEM((part, width), bf16),
            pltpu.VMEM((part, width), bf16),
            pltpu.VMEM((part, middle), bf16),
            pltpu.VMEM((part, width - middle), bf16),
        ],
        scratch_shapes=[pltpu.SemaphoreType.DMA((6,))],
        compiler_params=params(0),
        cost_estimate=cost(part * width, 14 * part * width),
    )(*in_hbm(after, master, one, two))


def mixed_place(index, shards):
    group = div_send(index)
    bits = shards.bit_length() - 1
    step = group & (shards - 1)
    return lax.shift_right_logical(group, bits), step, index - SEND * group


def mix_kernel(shards, *refs):
    parts, out_ref = refs[:shards], refs[-1]
    part = parts[0].shape[1] // 3
    blocks = parts[0].shape[0] // ROWS
    some = max(1, min(blocks, 32 // shards))
    rows, packed = some * shards * SEND, some * shards * ROWS
    row = lax.broadcasted_iota(jnp.int32, (rows, packed), 0)
    col = lax.broadcasted_iota(jnp.int32, (rows, packed), 1)
    at, step, slot = mixed_place(row, shards)
    base = (step * some + at) * ROWS
    orders = [jnp.where(col == base + slot, 1.0, 0.0).astype(bf16)]
    for j in range(3):
        hit = (col == base + SEND + slot - 4 * j) & (slot >= 4 * j) & (slot < 4 * j + 4)
        orders.append(jnp.where(hit, 1.0, 0.0).astype(bf16))
    for first in range(0, blocks, some):
        stack = jnp.concatenate(
            [ref[first * ROWS : (first + some) * ROWS, :] for ref in parts], axis=0
        )
        own = slice(first * shards * SEND, (first + some) * shards * SEND)
        out_ref[own, : 3 * part] = jnp.dot(
            orders[0], stack, preferred_element_type=f32
        ).astype(bf16)
        tail = jnp.zeros((rows, part), f32)
        for j in range(3):
            tail += jnp.dot(
                orders[1 + j],
                stack[:, j * part : (j + 1) * part],
                preferred_element_type=f32,
            )
        out_ref[own, 3 * part :] = tail.astype(bf16)


def mix(parts, after):
    shards = len(parts)
    rows, packed = parts[0].shape
    shape = (rows // ROWS * SEND * shards, packed // 3 * 4)
    return pl.pallas_call(
        functools.partial(mix_kernel, shards),
        grid=(1,),
        in_specs=[block(part.shape) for part in parts] + [ANY] * len(after),
        out_specs=block(shape),
        out_shape=out_hbm(shape, bf16),
        compiler_params=params(12 * rows * packed * shards),
        cost_estimate=cost(0, 5 * rows * packed * shards),
    )(*in_hbm(parts[0]), *parts[1:], *after)


def reorder(arrived, rows_ref):
    count, width = rows_ref.shape
    part = width // 4
    total = arrived.shape[0]
    slot = lax.broadcasted_iota(jnp.int32, (count, total), 0)
    col = lax.broadcasted_iota(jnp.int32, (count, total), 1)
    order = jnp.where(col == slot + (ROWS - SEND) * div_send(slot), 1.0, 0.0).astype(bf16)
    rows_ref[:, : 3 * part] = jnp.dot(order, arrived, preferred_element_type=f32).astype(bf16)
    tail = jnp.zeros((count, part), f32)
    for j in range(3):
        tail += jnp.dot(
            tail_order(count, total, j, True),
            arrived[:, j * part : (j + 1) * part],
            preferred_element_type=f32,
        )
    rows_ref[:, 3 * part :] = tail.astype(bf16)


def times_weight(rows_ref, weight_ref):
    return lax.dot_general(
        rows_ref[...], weight_ref[...], (((1,), (1,)), ((), ())), preferred_element_type=f32
    )


def score_block(blocks, proj, hidden, picked):
    count = proj.shape[0]
    score = jnp.sum(proj * hidden.astype(f32), axis=1, keepdims=True)
    row = lax.broadcasted_iota(jnp.int32, (count, LANE), 0)
    lane = lax.broadcasted_iota(jnp.int32, (count, LANE), 1)
    spread = jnp.where(row - SEND * div_send(row) == lane, score, 0.0)
    high = spread.astype(bf16)
    rest = (spread - high.astype(f32)).astype(bf16)
    at = lax.broadcasted_iota(jnp.int32, (blocks, count), 1)
    gather = [jnp.where(div_send(at) == pick, 1.0, 0.0) for pick in picked]
    gather = jnp.concatenate(gather, axis=0).astype(bf16)
    value = jnp.dot(gather, high, preferred_element_type=f32)
    value += jnp.dot(gather, rest, preferred_element_type=f32)
    return [
        value[i * blocks : (i + 1) * blocks].reshape(blocks, 1, LANE)
        for i in range(len(picked))
    ]


def block_index(blocks, count):
    return lax.broadcasted_iota(jnp.int32, (blocks, count), 0)


def begin_kernel(blocks, arrived_ref, weight_ref, hidden_ref, rows_ref, proj_ref, score_ref):
    reorder(arrived_ref[...], rows_ref)
    proj = times_weight(rows_ref, weight_ref)
    proj_ref[...] = proj
    score_ref[...] = score_block(
        blocks, proj, hidden_ref[...], [block_index(blocks, proj.shape[0])]
    )[0]


def begin(blocks, arrived, weight, hidden):
    count = blocks * SEND
    part, cols = weight.shape
    return pl.pallas_call(
        functools.partial(begin_kernel, blocks),
        in_specs=[VMEM] * 3,
        out_specs=[VMEM] * 3,
        out_shape=[
            plain((count, cols), bf16),
            plain((count, part), f32),
            plain((blocks, 1, LANE), f32),
        ],
        compiler_params=params(8 * count * cols + 8 * count * part),
        cost_estimate=cost(4 * count * part * cols, 2 * part * cols),
    )(arrived, weight, hidden)


def finish_kernel(shards, blocks, arrived_ref, hidden_ref, weight_ref, *refs):
    before, score_in = refs[:shards], refs[shards : 2 * shards]
    projs, score_ref = refs[2 * shards : 3 * shards], refs[-1]
    proj = times_weight(arrived_ref, weight_ref)
    rounded = proj.astype(bf16)
    total = proj.shape[0]
    count = total // shards
    picked = [block_index(blocks, total) * shards + s for s in range(shards)]
    scores = score_block(blocks, proj, hidden_ref[...], picked)
    me = lax.axis_index("rep")
    slot = lax.broadcasted_iota(jnp.int32, (count, total), 0)
    row = lax.broadcasted_iota(jnp.int32, (count, total), 1)
    for s in range(shards):
        order = row == slot + SEND * (div_send(slot) * (shards - 1) + s)
        order = jnp.where(order, 1.0, 0.0).astype(bf16)
        own = before[s][...] + jnp.dot(order, rounded, preferred_element_type=f32)
        projs[s][...] = own.astype(bf16)
        at = lax.rem(me + shards - s, shards)
        score_ref[pl.ds(at * blocks, blocks)] = score_in[s][...] + scores[s]


def finish(blocks, arrived, hidden, weight, before, scores):
    shards = len(before)
    total, part = hidden.shape
    count = total // shards
    cols = weight.shape[1]
    outs = pl.pallas_call(
        functools.partial(finish_kernel, shards, blocks),
        in_specs=[VMEM] * (3 + 2 * shards),
        out_specs=[VMEM] * (shards + 1),
        out_shape=[plain((count, part), bf16)] * shards
        + [plain((shards * blocks, 1, LANE), f32)],
        compiler_params=params(20 * total * part),
        cost_estimate=cost(2 * total * part * cols, 2 * part * cols),
    )(arrived, hidden, weight, *before, *scores)
    return list(outs[:-1]), outs[-1]


def settle_kernel(low, fresh, blocks, *refs):
    refs = list(refs)

    def take(number):
        out = refs[:number]
        del refs[:number]
        return out

    arrived = take(len(fresh))
    hidden = take(1 + len(fresh))
    given_ref, weight_ref, *state = take(5)
    take(3 if low else 0)
    projs, scores, mixed = take(len(fresh)), take(len(fresh)), take(min(1, len(fresh)))
    outs, news = take(3), take(3)
    rows_refs = take(len(fresh))
    hidden_t, grad_ref, sems = refs
    part, cols = grad_ref.shape
    count = blocks * SEND
    shards = 1 + len(fresh)
    for i, s in enumerate(fresh):
        reorder(arrived[i][...], rows_refs[i])
        proj = times_weight(rows_refs[i], weight_ref)
        projs[i][...] = proj
        scores[i][...] = score_block(
            blocks, proj, hidden[s][...], [block_index(blocks, count)]
        )[0]
    base = 0
    for ref in hidden:
        high = base + ref.shape[0]
        hidden_t[:, base:high] = ref[...].astype(f32).T.astype(bf16)
        base = high
    for i in range(cols // UNIT):
        own = slice(i * UNIT, (i + 1) * UNIT)
        base = 0
        grad = 0.0
        for rows_ref in [given_ref] + rows_refs:
            high = base + rows_ref.shape[0]
            grad += jnp.dot(
                hidden_t[:, base:high], rows_ref[:, own], preferred_element_type=f32
            )
            base = high
        grad_ref[:, own] = grad

    step = part // sems.shape[1]
    corr_one = 1.0 - beta_one**adam_step
    corr_two = 1.0 - beta_two**adam_step
    rate = learn_rate * corr_two**0.5 / corr_one
    keep = 1.0 - learn_rate * decay_rate
    eps = adam_eps * corr_two**0.5

    def store(i):
        rows = pl.ds(pl.multiple_of(i * step, step), step)
        return [
            pltpu.make_async_copy(
                source.at[rows], target.at[0, rows, pl.ds(low, cols)], sems.at[j, i]
            )
            for j, (source, target) in enumerate(zip(news, outs))
        ]

    @pl.loop(0, part // step)
    def _(i):
        own = pl.ds(pl.multiple_of(i * step, step), step)
        at = (own, pl.ds(low, cols))
        grad = grad_ref[own, :]
        m_new = beta_one * state[1][at].astype(f32) + (1.0 - beta_one) * grad
        v_new = beta_two * state[2][at].astype(f32) + (1.0 - beta_two) * (grad * grad)
        root = lax.rsqrt(v_new)
        below = 1.0 + eps * root
        inverse = pl.reciprocal(below, approx=True)
        inverse = inverse * (2.0 - below * inverse)
        news[0][own, :] = keep * state[0][at] - (rate * m_new) * (root * inverse)
        news[1][own, :] = m_new.astype(bf16)
        news[2][own, :] = v_new.astype(bf16)
        for copy in store(i):
            copy.start()

    if mixed:
        row = lax.broadcasted_iota(jnp.int32, (shards * count, count), 0)
        col = lax.broadcasted_iota(jnp.int32, (shards * count, count), 1)
        at, step_of, slot = mixed_place(row, shards)
        total = 0.0
        for s in range(shards):
            order = (step_of == s) & (col == at * SEND + slot)
            order = jnp.where(order, 1.0, 0.0).astype(bf16)
            total += jnp.dot(order, hidden[s][...], preferred_element_type=f32)
        mixed[0][...] = total.astype(bf16)

    @pl.loop(0, part // step)
    def _(i):
        for copy in store(i):
            copy.wait()


def settle(low, blocks, arrived, given, hidden, weight, state, shapes, done):
    cols = given.shape[1]
    part = weight.shape[0]
    count = blocks * SEND
    fresh = tuple(range(1, 1 + len(arrived)))
    total = given.shape[0] + count * len(fresh)
    step = min(part, 64)
    args = [*arrived, *hidden, given, weight, *state] + in_hbm(*done)
    out = [plain((count, part), f32)] * len(fresh)
    out += [plain((blocks, 1, LANE), f32)] * len(fresh)
    out += [plain((total, part), bf16)] * min(1, len(fresh))
    scratch = [pltpu.VMEM((part, cols), kind) for kind in (f32, bf16, bf16)]
    scratch += [pltpu.VMEM((count, cols), bf16)] * len(fresh)
    scratch += [
        pltpu.VMEM((part, total), bf16),
        pltpu.VMEM((part, cols), f32),
        pltpu.SemaphoreType.DMA((3, part // step)),
    ]
    nbytes = 14 * part * cols + 4 * total * cols + 8 * total * part
    outs = pl.pallas_call(
        functools.partial(settle_kernel, low, fresh, blocks),
        in_specs=[VMEM] * (len(args) - len(done)) + [HBM] * len(done),
        out_specs=[VMEM] * len(out) + [HBM] * 3,
        out_shape=out + [out_hbm(array.shape, array.dtype) for array in shapes],
        scratch_shapes=scratch,
        input_output_aliases={
            len(args) - len(done) + i: len(out) + i for i in range(len(done))
        },
        compiler_params=params(nbytes),
        cost_estimate=cost(
            4 * total * part * cols,
            (SETTLE_COST if fresh else 16) * part * cols,
            part * cols,
        ),
    )(*args)
    outs = list(outs)
    size = len(fresh)
    return outs[:size], outs[size : 2 * size], outs[2 * size : -3], outs[-3:]


def close_kernel(shards, gate_up_ref, ids_ref, slots_ref, gates_ref, score_ref, *refs):
    grad_refs, (out_ref, gate_ref) = refs[:-2], refs[-2:]
    part = grad_refs[0].shape[1]
    for s, grad_ref in enumerate(grad_refs):
        low, high, gate, up, sig = swiglu_part(gate_up_ref, shards, s, part)
        grad = grad_ref[...].astype(f32)
        out_ref[:, pl.ds(low, part)] = (
            grad * up * sig * (1.0 + gate * (1.0 - sig))
        ).astype(bf16)
        out_ref[:, pl.ds(high, part)] = (grad * (gate * sig)).astype(bf16)

    ids = ids_ref[...]
    slots = slots_ref[...]
    live = ((ids & (EXP_LOCAL - 1)) == 0) & (slots >= 0)
    place = jnp.where(live, ids // EXP_LOCAL * SEND + slots, -1)
    blocks = score_ref.shape[0] // shards
    value = jnp.zeros(ids.shape, f32)
    for b in range(blocks):
        for slot in range(SEND):
            score = score_ref[b, 0, slot]
            for s in range(1, shards):
                score += score_ref[s * blocks + b, 0, slot]
            value = jnp.where(place == b * SEND + slot, score, value)
    gate_ref[...] = jnp.where(live, value / gates_ref[...].astype(f32), 0.0)


def close(gate_up, ids, slots, gates, score, grads):
    size = gate_up.size
    args = in_hbm(gate_up, ids, slots, gates) + [score] + list(grads)
    shapes = [(gate_up.shape, bf16), (ids.shape, f32)]
    return pl.pallas_call(
        functools.partial(close_kernel, len(grads)),
        grid=(1,),
        in_specs=[block(array.shape) for array in args[:4]]
        + [pl.BlockSpec(memory_space=pltpu.SMEM)]
        + [block(grad.shape) for grad in grads],
        out_specs=[block(shape) for shape, _ in shapes],
        out_shape=[out_hbm(shape, dtype) for shape, dtype in shapes],
        compiler_params=params(8 * size),
        cost_estimate=cost(12 * size, 5 * size, size),
    )(*args)


def per_device(out_grad, expert_ids, slots, gate_weights, saved_gate_up, master, moment1, moment2):
    ep_size = lax.axis_size("ep")
    rep_size = lax.axis_size("rep")
    ids_t, slots_t, gates_t = expert_ids.T, slots.T, gate_weights.T
    gate_up = saved_gate_up[0, 0]
    state = (master, moment1, moment2)
    edges = chunk_edges(out_grad.shape[1])
    steps = range(1, rep_size)

    def shift(value, step):
        perm = [(i, (i + step) % rep_size) for i in range(rep_size)]
        return lax.ppermute(value, "rep", perm)

    def exchange(value):
        return lax.all_to_all(value, "ep", split_axis=0, concat_axis=0, tiled=True)

    send_a, send_b = dispatch(ep_size, edges, ids_t, slots_t, gates_t, out_grad)
    mixed = [send_b] + [shift(send_b, s) for s in steps]
    parts = list(hidden_parts(gate_up, rep_size, send_b))
    hidden = [parts[0]] + [shift(parts[s], s) for s in steps]
    *held, weight_a, weight_b = load_state(edges[1], *state, send_b)
    arrived = exchange(send_a.reshape(ep_size, ROWS, -1)).reshape(send_a.shape)
    mixed = mix(mixed, [weight_a] + parts[1:])
    arrived_b = exchange(mixed.reshape(ep_size, rep_size * SEND, -1)).reshape(mixed.shape)

    peers = [shift(arrived, s) for s in steps]
    rows, proj, score_own = begin(ep_size, arrived, weight_a, hidden[0])
    before, scores, (hidden_mixed,), done = settle(
        0, ep_size, peers, rows, hidden, weight_a, held, state, ()
    )
    projs, score = finish(
        ep_size, arrived_b, hidden_mixed, weight_b, [proj] + before, [score_own] + scores
    )
    grads = [projs[0]] + [shift(projs[s], rep_size - s) for s in steps]
    score = lax.all_to_all(score, ("rep", "ep"), split_axis=0, concat_axis=0, tiled=True)

    *_, done = settle(
        edges[1], ep_size, [], arrived_b, [hidden_mixed], weight_b, held, state, done
    )
    grad_gate_up, gate_grad = close(
        gate_up, ids_t, slots_t, gates_t, score, grads
    )
    return (grad_gate_up.reshape(saved_gate_up.shape), gate_grad.T) + tuple(done)


def solution(mesh):
    in_specs = (
        P(("rep", "ep"), None),
        P(("rep", "ep"), None),
        P(("rep", "ep"), None),
        P(("rep", "ep"), None),
        P("rep", "ep", None, None),
        P("ep", "rep", None),
        P("ep", "rep", None),
        P("ep", "rep", None),
    )
    out_specs = (
        P("rep", "ep", None, None),
        P(("rep", "ep"), None),
        P("ep", "rep", None),
        P("ep", "rep", None),
        P("ep", "rep", None),
    )
    return jax.shard_map(
        per_device, mesh=mesh, in_specs=in_specs, out_specs=out_specs, check_vma=False
    )
```

```python
import functools

import jax
import jax.numpy as jnp
from jax import lax
from jax.experimental import pallas as pl
from jax.experimental.pallas import tpu as pltpu
from jax.sharding import PartitionSpec as P

TOPK = 8
EXP_LOCAL = 8
SEND = 12
LANE = 128
UNIT = 512
ROWS = 16

beta_one = 0.9
beta_two = 0.95
learn_rate = 0.002
decay_rate = 0.1
adam_eps = 1e-08
adam_step = 50

f32 = jnp.float32
bf16 = jnp.bfloat16
HBM = pl.BlockSpec(memory_space=pltpu.HBM)
ANY = pl.BlockSpec(memory_space=pl.ANY)
VMEM = pl.BlockSpec(memory_space=pltpu.VMEM)


def in_hbm(*arrays):
    return [pltpu.with_memory_space_constraint(array, pltpu.HBM) for array in arrays]


def plain(dims, dtype):
    return jax.ShapeDtypeStruct(tuple(dims), dtype)


def out_hbm(dims, dtype):
    return pltpu.HBM(tuple(dims), dtype)


def block(dims, at=None):
    at = at or (0,) * len(dims)
    return pl.BlockSpec(tuple(dims), lambda i: at, pipeline_mode=pl.Buffered(1))


def params(nbytes):
    mib = min(60, max(16, 10 + 5 * int(nbytes) // 2**22))
    return pltpu.CompilerParams(vmem_limit_bytes=mib * 2**20)


def cost(flops, nbytes, transcendentals=0):
    return pl.CostEstimate(
        flops=int(flops), bytes_accessed=int(nbytes), transcendentals=int(transcendentals)
    )


def div_send(index):
    return lax.shift_right_logical(index * 10923, 17)


def pack(cols):
    return cols // 4 * 3


def chunk_edges(width):
    units = width // UNIT
    return (0, (units - max(1, units * 3 // 7)) * UNIT, width)


def tail_order(count, total, j, slots_first):
    a = lax.broadcasted_iota(jnp.int32, (count, total), 0)
    b = lax.broadcasted_iota(jnp.int32, (count, total), 1)
    if slots_first:
        block_of = div_send(a)
        inner = a - SEND * block_of
        hit = b == block_of * ROWS + SEND + inner - 4 * j
    else:
        inner = (a & (ROWS - 1)) - SEND + 4 * j
        hit = (b == a - SEND + 4 * j) & ((a & (ROWS - 1)) >= SEND)
    return jnp.where(hit & (inner >= 4 * j) & (inner < 4 * j + 4), 1.0, 0.0).astype(bf16)


def dispatch_kernel(edges, ids_hbm, slots_hbm, gates_hbm, grad_hbm, *refs):
    outs, (ids_ref, slots_ref, gates_ref, grad_ref) = refs[:2], refs[2:6]
    sends, sems, out_sems = refs[6:8], refs[8], refs[9]
    pairs = [
        (ids_hbm, ids_ref),
        (slots_hbm, slots_ref),
        (gates_hbm, gates_ref),
        (grad_hbm, grad_ref),
    ]
    copies = [
        pltpu.make_async_copy(source, target, sems.at[i])
        for i, (source, target) in enumerate(pairs)
    ]
    for copy in copies:
        copy.start()
    rows = outs[0].shape[0]
    tok = ids_ref.shape[1]
    orders = [tail_order(rows, rows, j, False) for j in range(3)]
    for copy in copies[:3]:
        copy.wait()
    ids = ids_ref[...]
    slots = slots_ref[...]
    gates = gates_ref[...].astype(f32)
    live = ((ids & (EXP_LOCAL - 1)) == 0) & (slots >= 0)
    place = jnp.where(live, ids // EXP_LOCAL * ROWS + slots, -1)
    row = lax.broadcasted_iota(jnp.int32, (rows, tok), 0)
    main = jnp.zeros((rows, tok), f32)
    for k in range(TOPK):
        main = jnp.where(row == place[k : k + 1], gates[k : k + 1], main)
    main = main.astype(bf16)
    tails = [
        jnp.dot(order, main, preferred_element_type=f32).astype(bf16) for order in orders
    ]
    copies[3].wait()
    out_copies = []
    for c in (1, 0):
        low, high = edges[c], edges[c + 1]
        part = (high - low) // 4
        for j in range(3):
            total = jnp.dot(
                main,
                grad_ref[:, low + j * part : low + (j + 1) * part],
                preferred_element_type=f32,
            )
            total += jnp.dot(
                tails[j], grad_ref[:, low + 3 * part : high], preferred_element_type=f32
            )
            own = (slice(None), pl.ds(j * part, part))
            sends[c][own] = total.astype(bf16)
            copy = pltpu.make_async_copy(
                sends[c].at[own], outs[c].at[own], out_sems.at[c, j]
            )
            copy.start()
            out_copies.append(copy)
    for copy in out_copies:
        copy.wait()


def dispatch(blocks, edges, ids, slots, gates, out_grad):
    tok, width = out_grad.shape
    rows = blocks * ROWS
    shapes = [(rows, pack(high - low)) for low, high in zip(edges[:-1], edges[1:])]
    return pl.pallas_call(
        functools.partial(dispatch_kernel, edges),
        in_specs=[HBM] * 4,
        out_specs=[HBM] * 2,
        out_shape=[out_hbm(shape, bf16) for shape in shapes],
        scratch_shapes=[
            pltpu.VMEM(ids.shape, jnp.int32),
            pltpu.VMEM(slots.shape, jnp.int32),
            pltpu.VMEM(gates.shape, bf16),
            pltpu.VMEM(out_grad.shape, bf16),
        ]
        + [pltpu.VMEM(shape, bf16) for shape in shapes]
        + [pltpu.SemaphoreType.DMA((4,)), pltpu.SemaphoreType.DMA((2, 3))],
        compiler_params=params(2 * rows * width + 2 * tok * width),
        cost_estimate=cost(2 * rows * tok * width, 4 * tok * width),
    )(*in_hbm(ids, slots, gates, out_grad))


def swiglu_part(gate_up_ref, shards, step, part):
    at = lax.rem(lax.axis_index("rep") + step, shards)
    low = pl.multiple_of(at * part, part)
    high = pl.multiple_of((shards + at) * part, part)
    gate = gate_up_ref[:, pl.ds(low, part)].astype(f32)
    up = gate_up_ref[:, pl.ds(high, part)].astype(f32)
    return low, high, gate, up, jax.nn.sigmoid(gate)


def hidden_kernel(gate_up_ref, after_ref, *out_refs):
    del after_ref
    for s, out_ref in enumerate(out_refs):
        _, _, gate, up, sig = swiglu_part(gate_up_ref, len(out_refs), s, out_ref.shape[1])
        out_ref[...] = (gate * sig * up).astype(bf16)


def hidden_parts(gate_up, shards, after):
    slots, width = gate_up.shape
    shape = (slots, width // 2 // shards)
    return pl.pallas_call(
        hidden_kernel,
        grid=(1,),
        in_specs=[block(gate_up.shape), HBM],
        out_specs=[block(shape)] * shards,
        out_shape=[plain(shape, bf16)] * shards,
        compiler_params=params(3 * slots * width),
        cost_estimate=cost(8 * slots * width, 3 * slots * width, slots * width),
    )(*in_hbm(gate_up, after))


def load_kernel(middle, after_ref, master_hbm, one_hbm, two_hbm, *refs):
    del after_ref
    master_ref, one_ref, two_ref, weight_a, weight_b, rest_ref, sems = refs
    part = master_ref.shape[0]
    rest = rest_ref.shape[1]
    step = part // 4
    copies = []
    for i in range(4):
        own = pl.ds(i * step, step)
        copies.append(
            pltpu.make_async_copy(
                master_hbm.at[0, own, pl.ds(0, middle)], master_ref.at[own], sems.at[i]
            )
        )
    for i in range(4):
        own = pl.ds(i * step, step)
        copies.append(
            pltpu.make_async_copy(
                master_hbm.at[0, own, pl.ds(middle, rest)], rest_ref.at[own], sems.at[4 + i]
            )
        )
    for i, (source, target) in enumerate([(one_hbm, one_ref), (two_hbm, two_ref)]):
        copies.append(
            pltpu.make_async_copy(source.at[0, :, pl.ds(0, middle)], target, sems.at[8 + i])
        )
    for copy in copies:
        copy.start()
    for i in range(4):
        copies[i].wait()
        own = slice(i * step, (i + 1) * step)
        weight_a[own, :] = master_ref[own, :].astype(bf16)
    for i in range(4):
        copies[4 + i].wait()
        own = slice(i * step, (i + 1) * step)
        weight_b[own, :] = rest_ref[own, :].astype(bf16)
    copies[8].wait()
    copies[9].wait()


def load_state(middle, master, one, two, after):
    _, part, width = master.shape
    return pl.pallas_call(
        functools.partial(load_kernel, middle),
        in_specs=[ANY] + [HBM] * 3,
        out_specs=[VMEM] * 5,
        out_shape=[
            pltpu.VMEM((part, middle), f32),
            pltpu.VMEM((part, middle), bf16),
            pltpu.VMEM((part, middle), bf16),
            pltpu.VMEM((part, middle), bf16),
            pltpu.VMEM((part, width - middle), bf16),
        ],
        scratch_shapes=[
            pltpu.VMEM((part, width - middle), f32),
            pltpu.SemaphoreType.DMA((10,)),
        ],
        compiler_params=params(4 * part * (width - middle)),
        cost_estimate=cost(part * width, 14 * part * width),
    )(after, *in_hbm(master, one, two))


def mixed_place(index, shards):
    group = div_send(index)
    bits = shards.bit_length() - 1
    step = group & (shards - 1)
    return lax.shift_right_logical(group, bits), step, index - SEND * group


def mix_kernel(shards, *refs):
    parts, out_ref = refs[:shards], refs[-1]
    part = parts[0].shape[1] // 3
    blocks = parts[0].shape[0] // ROWS
    some = max(1, min(blocks, 32 // shards))
    rows, packed = some * shards * SEND, some * shards * ROWS
    row = lax.broadcasted_iota(jnp.int32, (rows, packed), 0)
    col = lax.broadcasted_iota(jnp.int32, (rows, packed), 1)
    at, step, slot = mixed_place(row, shards)
    base = (step * some + at) * ROWS
    orders = [jnp.where(col == base + slot, 1.0, 0.0).astype(bf16)]
    for j in range(3):
        hit = (col == base + SEND + slot - 4 * j) & (slot >= 4 * j) & (slot < 4 * j + 4)
        orders.append(jnp.where(hit, 1.0, 0.0).astype(bf16))
    for first in range(0, blocks, some):
        stack = jnp.concatenate(
            [ref[first * ROWS : (first + some) * ROWS, :] for ref in parts], axis=0
        )
        own = slice(first * shards * SEND, (first + some) * shards * SEND)
        out_ref[own, : 3 * part] = jnp.dot(
            orders[0], stack, preferred_element_type=f32
        ).astype(bf16)
        tail = jnp.zeros((rows, part), f32)
        for j in range(3):
            tail += jnp.dot(
                orders[1 + j],
                stack[:, j * part : (j + 1) * part],
                preferred_element_type=f32,
            )
        out_ref[own, 3 * part :] = tail.astype(bf16)


def mix(parts, after):
    shards = len(parts)
    rows, packed = parts[0].shape
    shape = (rows // ROWS * SEND * shards, packed // 3 * 4)
    return pl.pallas_call(
        functools.partial(mix_kernel, shards),
        grid=(1,),
        in_specs=[block(part.shape) for part in parts] + [ANY] * len(after),
        out_specs=block(shape),
        out_shape=out_hbm(shape, bf16),
        compiler_params=params(12 * rows * packed * shards),
        cost_estimate=cost(0, 5 * rows * packed * shards),
    )(*in_hbm(parts[0]), *parts[1:], *after)


def reorder(arrived, rows_ref):
    count, width = rows_ref.shape
    part = width // 4
    total = arrived.shape[0]
    slot = lax.broadcasted_iota(jnp.int32, (count, total), 0)
    col = lax.broadcasted_iota(jnp.int32, (count, total), 1)
    order = jnp.where(col == slot + (ROWS - SEND) * div_send(slot), 1.0, 0.0).astype(bf16)
    rows_ref[:, : 3 * part] = jnp.dot(order, arrived, preferred_element_type=f32).astype(bf16)
    tail = jnp.zeros((count, part), f32)
    for j in range(3):
        tail += jnp.dot(
            tail_order(count, total, j, True),
            arrived[:, j * part : (j + 1) * part],
            preferred_element_type=f32,
        )
    rows_ref[:, 3 * part :] = tail.astype(bf16)


def times_weight(rows_ref, weight_ref):
    return lax.dot_general(
        rows_ref[...], weight_ref[...], (((1,), (1,)), ((), ())), preferred_element_type=f32
    )


def score_block(blocks, proj, hidden, picked):
    count = proj.shape[0]
    score = jnp.sum(proj * hidden.astype(f32), axis=1, keepdims=True)
    row = lax.broadcasted_iota(jnp.int32, (count, LANE), 0)
    lane = lax.broadcasted_iota(jnp.int32, (count, LANE), 1)
    spread = jnp.where(row - SEND * div_send(row) == lane, score, 0.0)
    high = spread.astype(bf16)
    rest = (spread - high.astype(f32)).astype(bf16)
    at = lax.broadcasted_iota(jnp.int32, (blocks, count), 1)
    gather = [jnp.where(div_send(at) == pick, 1.0, 0.0) for pick in picked]
    gather = jnp.concatenate(gather, axis=0).astype(bf16)
    value = jnp.dot(gather, high, preferred_element_type=f32)
    value += jnp.dot(gather, rest, preferred_element_type=f32)
    return [
        value[i * blocks : (i + 1) * blocks].reshape(blocks, 1, LANE)
        for i in range(len(picked))
    ]


def block_index(blocks, count):
    return lax.broadcasted_iota(jnp.int32, (blocks, count), 0)


def begin_kernel(blocks, arrived_ref, weight_ref, hidden_ref, *refs):
    rows_ref, score_ref, proj_hbm, proj_ref, sem = refs
    reorder(arrived_ref[...], rows_ref)
    proj = times_weight(rows_ref, weight_ref)
    proj_ref[...] = proj
    copy = pltpu.make_async_copy(proj_ref, proj_hbm, sem.at[0])
    copy.start()
    score_ref[...] = score_block(
        blocks, proj, hidden_ref[...], [block_index(blocks, proj.shape[0])]
    )[0]
    copy.wait()


def begin(blocks, arrived, weight, hidden):
    count = blocks * SEND
    part, cols = weight.shape
    return pl.pallas_call(
        functools.partial(begin_kernel, blocks),
        in_specs=[VMEM] * 3,
        out_specs=[VMEM] * 2 + [HBM],
        out_shape=[
            plain((count, cols), bf16),
            plain((blocks, 1, LANE), f32),
            out_hbm((count, part), f32),
        ],
        scratch_shapes=[pltpu.VMEM((count, part), f32), pltpu.SemaphoreType.DMA((1,))],
        compiler_params=params(8 * count * cols + 8 * count * part),
        cost_estimate=cost(4 * count * part * cols, 2 * part * cols),
    )(arrived, weight, hidden)


def finish_kernel(shards, blocks, arrived_ref, hidden_ref, weight_ref, *refs):
    before_hbm, score_in = refs[:shards], refs[shards : 2 * shards]
    projs, score_ref = refs[2 * shards : 3 * shards], refs[3 * shards]
    before, sems = refs[3 * shards + 1 :]
    copies = [
        pltpu.make_async_copy(ref, before.at[s], sems.at[s])
        for s, ref in enumerate(before_hbm)
    ]
    for copy in copies:
        copy.start()
    proj = times_weight(arrived_ref, weight_ref)
    rounded = proj.astype(bf16)
    total = proj.shape[0]
    count = total // shards
    picked = [block_index(blocks, total) * shards + s for s in range(shards)]
    scores = score_block(blocks, proj, hidden_ref[...], picked)
    me = lax.axis_index("rep")
    slot = lax.broadcasted_iota(jnp.int32, (count, total), 0)
    row = lax.broadcasted_iota(jnp.int32, (count, total), 1)
    for s in range(shards):
        order = row == slot + SEND * (div_send(slot) * (shards - 1) + s)
        order = jnp.where(order, 1.0, 0.0).astype(bf16)
        copies[s].wait()
        own = before[s] + jnp.dot(order, rounded, preferred_element_type=f32)
        projs[s][...] = own.astype(bf16)
        at = lax.rem(me + shards - s, shards)
        score_ref[pl.ds(at * blocks, blocks)] = score_in[s][...] + scores[s]


def finish(blocks, arrived, hidden, weight, before, scores):
    shards = len(before)
    total, part = hidden.shape
    count = total // shards
    cols = weight.shape[1]
    outs = pl.pallas_call(
        functools.partial(finish_kernel, shards, blocks),
        in_specs=[VMEM] * 3 + [HBM] * shards + [VMEM] * shards,
        out_specs=[VMEM] * (shards + 1),
        out_shape=[plain((count, part), bf16)] * shards
        + [plain((shards * blocks, 1, LANE), f32)],
        scratch_shapes=[
            pltpu.VMEM((shards, count, part), f32),
            pltpu.SemaphoreType.DMA((shards,)),
        ],
        compiler_params=params(20 * total * part),
        cost_estimate=cost(2 * total * part * cols, 2 * part * cols),
    )(arrived, hidden, weight, *in_hbm(*before), *scores)
    return list(outs[:-1]), outs[-1]


def new_state(master, one, two, grad):
    corr_one = 1.0 - beta_one**adam_step
    corr_two = 1.0 - beta_two**adam_step
    rate = learn_rate * corr_two**0.5 / corr_one
    keep = 1.0 - learn_rate * decay_rate
    eps = adam_eps * corr_two**0.5
    m_new = beta_one * one.astype(f32) + (1.0 - beta_one) * grad
    v_new = beta_two * two.astype(f32) + (1.0 - beta_two) * (grad * grad)
    root = lax.rsqrt(v_new)
    below = 1.0 + eps * root
    inverse = pl.reciprocal(below, approx=True)
    inverse = inverse * (2.0 - below * inverse)
    master = keep * master - (rate * m_new) * (root * inverse)
    return master, m_new.astype(bf16), v_new.astype(bf16)


def transpose_rows(hidden, hidden_t):
    base = 0
    for ref in hidden:
        high = base + ref.shape[0]
        hidden_t[:, base:high] = ref[...].astype(f32).T.astype(bf16)
        base = high


def form_grad(hidden_t, rows_refs, grad_ref):
    for i in range(grad_ref.shape[1] // UNIT):
        own = slice(i * UNIT, (i + 1) * UNIT)
        base = 0
        grad = 0.0
        for rows_ref in rows_refs:
            high = base + rows_ref.shape[0]
            grad += jnp.dot(
                hidden_t[:, base:high], rows_ref[:, own], preferred_element_type=f32
            )
            base = high
        grad_ref[:, own] = grad


def state_copies(i, step, low, hbm, vmem, sems, into):
    cols = vmem[0].shape[1]
    rows = pl.ds(pl.multiple_of(i * step, step), step)
    out = []
    for j, (far, near) in enumerate(zip(hbm, vmem)):
        ends = (far.at[0, rows, pl.ds(low, cols)], near.at[rows])
        source, target = ends if into else ends[::-1]
        out.append(pltpu.make_async_copy(source, target, sems.at[j, i]))
    return out


def settle_kernel(fresh, blocks, *refs):
    refs = list(refs)

    def take(number):
        out = refs[:number]
        del refs[:number]
        return out

    size = len(fresh)
    arrived, hidden = take(size), take(1 + size)
    given_ref, weight_ref, *state = take(5)
    scores, (mixed_ref,) = take(size), take(1)
    projs_hbm, outs, news = take(size), take(3), take(3)
    rows_refs, projs = take(size), take(size)
    hidden_t, grad_ref, sems, proj_sems = refs
    part = grad_ref.shape[0]
    count = blocks * SEND
    shards = 1 + size
    proj_copies = []
    for i, s in enumerate(fresh):
        reorder(arrived[i][...], rows_refs[i])
        proj = times_weight(rows_refs[i], weight_ref)
        projs[i][...] = proj
        proj_copies.append(pltpu.make_async_copy(projs[i], projs_hbm[i], proj_sems.at[i]))
        proj_copies[i].start()
        scores[i][...] = score_block(
            blocks, proj, hidden[s][...], [block_index(blocks, count)]
        )[0]
    transpose_rows(hidden, hidden_t)
    form_grad(hidden_t, [given_ref] + rows_refs, grad_ref)

    step = part // sems.shape[1]

    @pl.loop(0, part // step)
    def _(i):
        own = pl.ds(pl.multiple_of(i * step, step), step)
        values = new_state(*[ref[own, :] for ref in state], grad_ref[own, :])
        for ref, value in zip(news, values):
            ref[own, :] = value
        for copy in state_copies(i, step, 0, outs, news, sems, False):
            copy.start()

    row = lax.broadcasted_iota(jnp.int32, (shards * count, count), 0)
    col = lax.broadcasted_iota(jnp.int32, (shards * count, count), 1)
    at, step_of, slot = mixed_place(row, shards)
    total = 0.0
    for s in range(shards):
        order = (step_of == s) & (col == at * SEND + slot)
        order = jnp.where(order, 1.0, 0.0).astype(bf16)
        total += jnp.dot(order, hidden[s][...], preferred_element_type=f32)
    mixed_ref[...] = total.astype(bf16)

    @pl.loop(0, part // step)
    def _(i):
        for copy in state_copies(i, step, 0, outs, news, sems, False):
            copy.wait()

    for copy in proj_copies:
        copy.wait()


def settle(blocks, arrived, given, hidden, weight, held, shapes):
    part, cols = weight.shape
    count = blocks * SEND
    fresh = tuple(range(1, 1 + len(arrived)))
    size = len(fresh)
    total = count * (1 + size)
    step = min(part, 64)
    args = [*arrived, *hidden, given, weight, *held]
    near = [plain((blocks, 1, LANE), f32)] * size + [plain((total, part), bf16)]
    far = [out_hbm((count, part), f32)] * size
    far += [out_hbm(array.shape, array.dtype) for array in shapes]
    scratch = [pltpu.VMEM((part, cols), kind) for kind in (f32, bf16, bf16)]
    scratch += [pltpu.VMEM((count, cols), bf16)] * size
    scratch += [pltpu.VMEM((count, part), f32)] * size
    scratch += [
        pltpu.VMEM((part, total), bf16),
        pltpu.VMEM((part, cols), f32),
        pltpu.SemaphoreType.DMA((3, part // step)),
        pltpu.SemaphoreType.DMA((max(1, size),)),
    ]
    nbytes = 12 * part * cols + 4 * total * cols + 8 * total * part
    outs = pl.pallas_call(
        functools.partial(settle_kernel, fresh, blocks),
        in_specs=[VMEM] * len(args),
        out_specs=[VMEM] * len(near) + [HBM] * len(far),
        out_shape=near + far,
        scratch_shapes=scratch,
        compiler_params=params(nbytes),
        cost_estimate=cost(4 * total * part * cols, 16 * part * cols, part * cols),
    )(*args)
    outs = list(outs)
    return outs[:size], outs[size], outs[size + 1 : -3], outs[-3:]


def update_kernel(low, hidden_ref, rows_ref, *refs):
    state_hbm, outs, state = refs[:3], refs[6:9], refs[9:12]
    hidden_t, grad_ref, in_sems, out_sems = refs[12:]
    part = grad_ref.shape[0]
    steps = in_sems.shape[1]
    step = part // steps
    for i in range(steps):
        for copy in state_copies(i, step, low, state_hbm, state, in_sems, True):
            copy.start()
    transpose_rows([hidden_ref], hidden_t)
    form_grad(hidden_t, [rows_ref], grad_ref)

    @pl.loop(0, steps)
    def _(i):
        for copy in state_copies(i, step, low, state_hbm, state, in_sems, True):
            copy.wait()
        own = pl.ds(pl.multiple_of(i * step, step), step)
        values = new_state(*[ref[own, :] for ref in state], grad_ref[own, :])
        for ref, value in zip(state, values):
            ref[own, :] = value
        for copy in state_copies(i, step, low, outs, state, out_sems, False):
            copy.start()

    @pl.loop(0, steps)
    def _(i):
        for copy in state_copies(i, step, low, outs, state, out_sems, False):
            copy.wait()


def update(low, hidden, rows, state, done):
    total, part = hidden.shape
    cols = rows.shape[1]
    step = min(part, 64)
    scratch = [pltpu.VMEM((part, cols), kind) for kind in (f32, bf16, bf16)]
    scratch += [pltpu.VMEM((part, total), bf16), pltpu.VMEM((part, cols), f32)]
    scratch += [pltpu.SemaphoreType.DMA((3, part // step))] * 2
    return pl.pallas_call(
        functools.partial(update_kernel, low),
        in_specs=[VMEM] * 2 + [HBM] * 6,
        out_specs=[HBM] * 3,
        out_shape=[out_hbm(array.shape, array.dtype) for array in state],
        scratch_shapes=scratch,
        input_output_aliases={5 + i: i for i in range(3)},
        compiler_params=params(12 * part * cols + 2 * total * part),
        cost_estimate=cost(2 * total * part * cols, 16 * part * cols, part * cols),
    )(hidden, rows, *in_hbm(*state, *done))


def close_kernel(shards, gate_up_ref, ids_ref, slots_ref, gates_ref, score_ref, *refs):
    grad_refs, (out_ref, gate_ref) = refs[:-2], refs[-2:]
    part = grad_refs[0].shape[1]
    for s, grad_ref in enumerate(grad_refs):
        low, high, gate, up, sig = swiglu_part(gate_up_ref, shards, s, part)
        grad = grad_ref[...].astype(f32)
        out_ref[:, pl.ds(low, part)] = (
            grad * up * sig * (1.0 + gate * (1.0 - sig))
        ).astype(bf16)
        out_ref[:, pl.ds(high, part)] = (grad * (gate * sig)).astype(bf16)

    ids = ids_ref[...]
    slots = slots_ref[...]
    live = ((ids & (EXP_LOCAL - 1)) == 0) & (slots >= 0)
    place = jnp.where(live, ids // EXP_LOCAL * SEND + slots, -1)
    blocks = score_ref.shape[0] // shards
    value = jnp.zeros(ids.shape, f32)
    for b in range(blocks):
        for slot in range(SEND):
            score = score_ref[b, 0, slot]
            for s in range(1, shards):
                score += score_ref[s * blocks + b, 0, slot]
            value = jnp.where(place == b * SEND + slot, score, value)
    gate_ref[...] = jnp.where(live, value / gates_ref[...].astype(f32), 0.0)


def close(gate_up, ids, slots, gates, score, grads):
    size = gate_up.size
    args = in_hbm(gate_up, ids, slots, gates) + [score] + list(grads)
    shapes = [(gate_up.shape, bf16), (ids.shape, f32)]
    return pl.pallas_call(
        functools.partial(close_kernel, len(grads)),
        grid=(1,),
        in_specs=[block(array.shape) for array in args[:4]]
        + [pl.BlockSpec(memory_space=pltpu.SMEM)]
        + [block(grad.shape) for grad in grads],
        out_specs=[block(shape) for shape, _ in shapes],
        out_shape=[out_hbm(shape, dtype) for shape, dtype in shapes],
        compiler_params=params(8 * size),
        cost_estimate=cost(12 * size, 5 * size, size),
    )(*args)


def per_device(out_grad, expert_ids, slots, gate_weights, saved_gate_up, master, moment1, moment2):
    ep_size = lax.axis_size("ep")
    rep_size = lax.axis_size("rep")
    ids_t, slots_t, gates_t = expert_ids.T, slots.T, gate_weights.T
    gate_up = saved_gate_up[0, 0]
    state = (master, moment1, moment2)
    edges = chunk_edges(out_grad.shape[1])
    steps = range(1, rep_size)

    def shift(value, step):
        perm = [(i, (i + step) % rep_size) for i in range(rep_size)]
        return lax.ppermute(value, "rep", perm)

    def exchange(value):
        return lax.all_to_all(value, "ep", split_axis=0, concat_axis=0, tiled=True)

    send_a, send_b = dispatch(ep_size, edges, ids_t, slots_t, gates_t, out_grad)
    mixed = [send_b] + [shift(send_b, s) for s in steps]
    parts = list(hidden_parts(gate_up, rep_size, send_b))
    hidden = [parts[0]] + [shift(parts[s], s) for s in steps]
    arrived = exchange(send_a.reshape(ep_size, ROWS, -1)).reshape(send_a.shape)
    mixed = mix(mixed, parts[1:])
    arrived_b = exchange(mixed.reshape(ep_size, rep_size * SEND, -1)).reshape(mixed.shape)

    peers = [shift(arrived, s) for s in steps]
    *held, weight_a, weight_b = load_state(edges[1], *state, arrived)
    rows, score_own, proj = begin(ep_size, arrived, weight_a, hidden[0])
    scores, hidden_mixed, before, done = settle(
        ep_size, peers, rows, hidden, weight_a, held, state
    )
    projs, score = finish(
        ep_size, arrived_b, hidden_mixed, weight_b, [proj] + before, [score_own] + scores
    )
    grads = [projs[0]] + [shift(projs[s], rep_size - s) for s in steps]
    score = lax.all_to_all(score, ("rep", "ep"), split_axis=0, concat_axis=0, tiled=True)

    done = update(edges[1], hidden_mixed, arrived_b, state, done)
    grad_gate_up, gate_grad = close(
        gate_up, ids_t, slots_t, gates_t, score, grads
    )
    return (grad_gate_up.reshape(saved_gate_up.shape), gate_grad.T) + tuple(done)


def solution(mesh):
    in_specs = (
        P(("rep", "ep"), None),
        P(("rep", "ep"), None),
        P(("rep", "ep"), None),
        P(("rep", "ep"), None),
        P("rep", "ep", None, None),
        P("ep", "rep", None),
        P("ep", "rep", None),
        P("ep", "rep", None),
    )
    out_specs = (
        P("rep", "ep", None, None),
        P(("rep", "ep"), None),
        P("ep", "rep", None),
        P("ep", "rep", None),
        P("ep", "rep", None),
    )
    return jax.shard_map(
        per_device, mesh=mesh, in_specs=in_specs, out_specs=out_specs, check_vma=False
    )
```

```python
import functools

import jax
import jax.numpy as jnp
from jax import lax
from jax.experimental import pallas as pl
from jax.experimental.pallas import tpu as pltpu
from jax.sharding import PartitionSpec as P

TOPK = 8
EXP_LOCAL = 8
SEND = 12
LANE = 128
UNIT = 512
SETTLE_COST = 525
ROWS = 16

beta_one = 0.9
beta_two = 0.95
learn_rate = 0.002
decay_rate = 0.1
adam_eps = 1e-08
adam_step = 50

f32 = jnp.float32
bf16 = jnp.bfloat16
HBM = pl.BlockSpec(memory_space=pltpu.HBM)
ANY = pl.BlockSpec(memory_space=pl.ANY)
VMEM = pl.BlockSpec(memory_space=pltpu.VMEM)


def in_hbm(*arrays):
    return [pltpu.with_memory_space_constraint(array, pltpu.HBM) for array in arrays]


def plain(dims, dtype):
    return jax.ShapeDtypeStruct(tuple(dims), dtype)


def out_hbm(dims, dtype):
    return pltpu.HBM(tuple(dims), dtype)


def block(dims, at=None):
    at = at or (0,) * len(dims)
    return pl.BlockSpec(tuple(dims), lambda i: at, pipeline_mode=pl.Buffered(1))


def params(nbytes):
    mib = min(60, max(16, 10 + 5 * int(nbytes) // 2**22))
    return pltpu.CompilerParams(vmem_limit_bytes=mib * 2**20)


def cost(flops, nbytes, transcendentals=0):
    return pl.CostEstimate(
        flops=int(flops), bytes_accessed=int(nbytes), transcendentals=int(transcendentals)
    )


def div_send(index):
    return lax.shift_right_logical(index * 10923, 17)


def pack(cols):
    return cols // 4 * 3


def chunk_edges(width):
    units = width // UNIT
    return (0, (units - max(1, units * 3 // 7)) * UNIT, width)


def tail_order(count, total, j, slots_first):
    a = lax.broadcasted_iota(jnp.int32, (count, total), 0)
    b = lax.broadcasted_iota(jnp.int32, (count, total), 1)
    if slots_first:
        block_of = div_send(a)
        inner = a - SEND * block_of
        hit = b == block_of * ROWS + SEND + inner - 4 * j
    else:
        inner = (a & (ROWS - 1)) - SEND + 4 * j
        hit = (b == a - SEND + 4 * j) & ((a & (ROWS - 1)) >= SEND)
    return jnp.where(hit & (inner >= 4 * j) & (inner < 4 * j + 4), 1.0, 0.0).astype(bf16)


def dispatch_kernel(edges, ids_hbm, slots_hbm, gates_hbm, grad_hbm, *refs):
    outs, (ids_ref, slots_ref, gates_ref, grad_ref) = refs[:2], refs[2:6]
    sends, sems, out_sems = refs[6:8], refs[8], refs[9]
    pairs = [
        (ids_hbm, ids_ref),
        (slots_hbm, slots_ref),
        (gates_hbm, gates_ref),
        (grad_hbm, grad_ref),
    ]
    copies = [
        pltpu.make_async_copy(source, target, sems.at[i])
        for i, (source, target) in enumerate(pairs)
    ]
    for copy in copies:
        copy.start()
    rows = outs[0].shape[0]
    tok = ids_ref.shape[1]
    orders = [tail_order(rows, rows, j, False) for j in range(3)]
    for copy in copies[:3]:
        copy.wait()
    ids = ids_ref[...]
    slots = slots_ref[...]
    gates = gates_ref[...].astype(f32)
    live = ((ids & (EXP_LOCAL - 1)) == 0) & (slots >= 0)
    place = jnp.where(live, ids // EXP_LOCAL * ROWS + slots, -1)
    row = lax.broadcasted_iota(jnp.int32, (rows, tok), 0)
    main = jnp.zeros((rows, tok), f32)
    for k in range(TOPK):
        main = jnp.where(row == place[k : k + 1], gates[k : k + 1], main)
    main = main.astype(bf16)
    tails = [
        jnp.dot(order, main, preferred_element_type=f32).astype(bf16) for order in orders
    ]
    copies[3].wait()
    out_copies = []
    for c in (1, 0):
        low, high = edges[c], edges[c + 1]
        part = (high - low) // 4
        for j in range(3):
            total = jnp.dot(
                main,
                grad_ref[:, low + j * part : low + (j + 1) * part],
                preferred_element_type=f32,
            )
            total += jnp.dot(
                tails[j], grad_ref[:, low + 3 * part : high], preferred_element_type=f32
            )
            own = (slice(None), pl.ds(j * part, part))
            sends[c][own] = total.astype(bf16)
            copy = pltpu.make_async_copy(
                sends[c].at[own], outs[c].at[own], out_sems.at[c, j]
            )
            copy.start()
            out_copies.append(copy)
    for copy in out_copies:
        copy.wait()


def dispatch(blocks, edges, ids, slots, gates, out_grad):
    tok, width = out_grad.shape
    rows = blocks * ROWS
    shapes = [(rows, pack(high - low)) for low, high in zip(edges[:-1], edges[1:])]
    return pl.pallas_call(
        functools.partial(dispatch_kernel, edges),
        in_specs=[HBM] * 4,
        out_specs=[HBM] * 2,
        out_shape=[out_hbm(shape, bf16) for shape in shapes],
        scratch_shapes=[
            pltpu.VMEM(ids.shape, jnp.int32),
            pltpu.VMEM(slots.shape, jnp.int32),
            pltpu.VMEM(gates.shape, bf16),
            pltpu.VMEM(out_grad.shape, bf16),
        ]
        + [pltpu.VMEM(shape, bf16) for shape in shapes]
        + [pltpu.SemaphoreType.DMA((4,)), pltpu.SemaphoreType.DMA((2, 3))],
        compiler_params=params(2 * rows * width + 2 * tok * width),
        cost_estimate=cost(2 * rows * tok * width, 4 * tok * width),
    )(*in_hbm(ids, slots, gates, out_grad))


def swiglu_part(gate_up_ref, shards, step, part):
    at = lax.rem(lax.axis_index("rep") + step, shards)
    low = pl.multiple_of(at * part, part)
    high = pl.multiple_of((shards + at) * part, part)
    gate = gate_up_ref[:, pl.ds(low, part)].astype(f32)
    up = gate_up_ref[:, pl.ds(high, part)].astype(f32)
    return low, high, gate, up, jax.nn.sigmoid(gate)


def hidden_kernel(gate_up_ref, after_ref, *out_refs):
    del after_ref
    for s, out_ref in enumerate(out_refs):
        _, _, gate, up, sig = swiglu_part(gate_up_ref, len(out_refs), s, out_ref.shape[1])
        out_ref[...] = (gate * sig * up).astype(bf16)


def hidden_parts(gate_up, shards, after):
    slots, width = gate_up.shape
    shape = (slots, width // 2 // shards)
    return pl.pallas_call(
        hidden_kernel,
        grid=(1,),
        in_specs=[block(gate_up.shape), HBM],
        out_specs=[block(shape)] * shards,
        out_shape=[plain(shape, bf16)] * shards,
        compiler_params=params(3 * slots * width),
        cost_estimate=cost(8 * slots * width, 3 * slots * width, slots * width),
    )(*in_hbm(gate_up, after))


def load_kernel(middle, after_ref, master_hbm, one_hbm, two_hbm, *refs):
    del after_ref
    master_ref, one_ref, two_ref, weight_a, weight_b, rest_ref, sems = refs
    part = master_ref.shape[0]
    rest = rest_ref.shape[1]
    step = part // 4
    copies = []
    for i in range(4):
        own = pl.ds(i * step, step)
        copies.append(
            pltpu.make_async_copy(
                master_hbm.at[0, own, pl.ds(0, middle)], master_ref.at[own], sems.at[i]
            )
        )
    for i in range(4):
        own = pl.ds(i * step, step)
        copies.append(
            pltpu.make_async_copy(
                master_hbm.at[0, own, pl.ds(middle, rest)], rest_ref.at[own], sems.at[4 + i]
            )
        )
    for i, (source, target) in enumerate([(one_hbm, one_ref), (two_hbm, two_ref)]):
        copies.append(
            pltpu.make_async_copy(source.at[0, :, pl.ds(0, middle)], target, sems.at[8 + i])
        )
    for copy in copies:
        copy.start()
    for i in range(4):
        copies[i].wait()
        own = slice(i * step, (i + 1) * step)
        weight_a[own, :] = master_ref[own, :].astype(bf16)
    for i in range(4):
        copies[4 + i].wait()
        own = slice(i * step, (i + 1) * step)
        weight_b[own, :] = rest_ref[own, :].astype(bf16)
    copies[8].wait()
    copies[9].wait()


def load_state(middle, master, one, two, after):
    _, part, width = master.shape
    return pl.pallas_call(
        functools.partial(load_kernel, middle),
        in_specs=[ANY] + [HBM] * 3,
        out_specs=[VMEM] * 5,
        out_shape=[
            pltpu.VMEM((part, middle), f32),
            pltpu.VMEM((part, middle), bf16),
            pltpu.VMEM((part, middle), bf16),
            pltpu.VMEM((part, middle), bf16),
            pltpu.VMEM((part, width - middle), bf16),
        ],
        scratch_shapes=[
            pltpu.VMEM((part, width - middle), f32),
            pltpu.SemaphoreType.DMA((10,)),
        ],
        compiler_params=params(4 * part * (width - middle)),
        cost_estimate=cost(part * width, 14 * part * width),
    )(after, *in_hbm(master, one, two))


def mixed_place(index, shards):
    group = div_send(index)
    bits = shards.bit_length() - 1
    step = group & (shards - 1)
    return lax.shift_right_logical(group, bits), step, index - SEND * group


def mix_kernel(shards, *refs):
    parts, out_ref = refs[:shards], refs[-1]
    part = parts[0].shape[1] // 3
    blocks = parts[0].shape[0] // ROWS
    some = max(1, min(blocks, 32 // shards))
    rows, packed = some * shards * SEND, some * shards * ROWS
    row = lax.broadcasted_iota(jnp.int32, (rows, packed), 0)
    col = lax.broadcasted_iota(jnp.int32, (rows, packed), 1)
    at, step, slot = mixed_place(row, shards)
    base = (step * some + at) * ROWS
    orders = [jnp.where(col == base + slot, 1.0, 0.0).astype(bf16)]
    for j in range(3):
        hit = (col == base + SEND + slot - 4 * j) & (slot >= 4 * j) & (slot < 4 * j + 4)
        orders.append(jnp.where(hit, 1.0, 0.0).astype(bf16))
    for first in range(0, blocks, some):
        stack = jnp.concatenate(
            [ref[first * ROWS : (first + some) * ROWS, :] for ref in parts], axis=0
        )
        own = slice(first * shards * SEND, (first + some) * shards * SEND)
        out_ref[own, : 3 * part] = jnp.dot(
            orders[0], stack, preferred_element_type=f32
        ).astype(bf16)
        tail = jnp.zeros((rows, part), f32)
        for j in range(3):
            tail += jnp.dot(
                orders[1 + j],
                stack[:, j * part : (j + 1) * part],
                preferred_element_type=f32,
            )
        out_ref[own, 3 * part :] = tail.astype(bf16)


def mix(parts, after):
    shards = len(parts)
    rows, packed = parts[0].shape
    shape = (rows // ROWS * SEND * shards, packed // 3 * 4)
    return pl.pallas_call(
        functools.partial(mix_kernel, shards),
        grid=(1,),
        in_specs=[block(part.shape) for part in parts] + [ANY] * len(after),
        out_specs=block(shape),
        out_shape=out_hbm(shape, bf16),
        compiler_params=params(12 * rows * packed * shards),
        cost_estimate=cost(0, 5 * rows * packed * shards),
    )(*in_hbm(parts[0]), *parts[1:], *after)


def reorder(arrived, rows_ref):
    count, width = rows_ref.shape
    part = width // 4
    total = arrived.shape[0]
    slot = lax.broadcasted_iota(jnp.int32, (count, total), 0)
    col = lax.broadcasted_iota(jnp.int32, (count, total), 1)
    order = jnp.where(col == slot + (ROWS - SEND) * div_send(slot), 1.0, 0.0).astype(bf16)
    rows_ref[:, : 3 * part] = jnp.dot(order, arrived, preferred_element_type=f32).astype(bf16)
    tail = jnp.zeros((count, part), f32)
    for j in range(3):
        tail += jnp.dot(
            tail_order(count, total, j, True),
            arrived[:, j * part : (j + 1) * part],
            preferred_element_type=f32,
        )
    rows_ref[:, 3 * part :] = tail.astype(bf16)


def times_weight(rows_ref, weight_ref):
    return lax.dot_general(
        rows_ref[...], weight_ref[...], (((1,), (1,)), ((), ())), preferred_element_type=f32
    )


def score_block(blocks, proj, hidden, picked):
    count = proj.shape[0]
    score = jnp.sum(proj * hidden.astype(f32), axis=1, keepdims=True)
    row = lax.broadcasted_iota(jnp.int32, (count, LANE), 0)
    lane = lax.broadcasted_iota(jnp.int32, (count, LANE), 1)
    spread = jnp.where(row - SEND * div_send(row) == lane, score, 0.0)
    high = spread.astype(bf16)
    rest = (spread - high.astype(f32)).astype(bf16)
    at = lax.broadcasted_iota(jnp.int32, (blocks, count), 1)
    gather = [jnp.where(div_send(at) == pick, 1.0, 0.0) for pick in picked]
    gather = jnp.concatenate(gather, axis=0).astype(bf16)
    value = jnp.dot(gather, high, preferred_element_type=f32)
    value += jnp.dot(gather, rest, preferred_element_type=f32)
    return [
        value[i * blocks : (i + 1) * blocks].reshape(blocks, 1, LANE)
        for i in range(len(picked))
    ]


def block_index(blocks, count):
    return lax.broadcasted_iota(jnp.int32, (blocks, count), 0)


def begin_kernel(blocks, arrived_ref, weight_ref, hidden_ref, *refs):
    rows_ref, score_ref, proj_hbm, proj_ref, sem = refs
    reorder(arrived_ref[...], rows_ref)
    proj = times_weight(rows_ref, weight_ref)
    proj_ref[...] = proj
    copy = pltpu.make_async_copy(proj_ref, proj_hbm, sem.at[0])
    copy.start()
    score_ref[...] = score_block(
        blocks, proj, hidden_ref[...], [block_index(blocks, proj.shape[0])]
    )[0]
    copy.wait()


def begin(blocks, arrived, weight, hidden):
    count = blocks * SEND
    part, cols = weight.shape
    return pl.pallas_call(
        functools.partial(begin_kernel, blocks),
        in_specs=[VMEM] * 3,
        out_specs=[VMEM] * 2 + [HBM],
        out_shape=[
            plain((count, cols), bf16),
            plain((blocks, 1, LANE), f32),
            out_hbm((count, part), f32),
        ],
        scratch_shapes=[pltpu.VMEM((count, part), f32), pltpu.SemaphoreType.DMA((1,))],
        compiler_params=params(8 * count * cols + 8 * count * part),
        cost_estimate=cost(4 * count * part * cols, 2 * part * cols),
    )(arrived, weight, hidden)


def finish_kernel(shards, blocks, arrived_ref, hidden_ref, weight_ref, *refs):
    before_hbm, score_in = refs[:shards], refs[shards : 2 * shards]
    projs, score_ref = refs[2 * shards : 3 * shards], refs[3 * shards]
    before, sems = refs[3 * shards + 1 :]
    copies = [
        pltpu.make_async_copy(ref, before.at[s], sems.at[s])
        for s, ref in enumerate(before_hbm)
    ]
    for copy in copies:
        copy.start()
    proj = times_weight(arrived_ref, weight_ref)
    rounded = proj.astype(bf16)
    total = proj.shape[0]
    count = total // shards
    picked = [block_index(blocks, total) * shards + s for s in range(shards)]
    scores = score_block(blocks, proj, hidden_ref[...], picked)
    me = lax.axis_index("rep")
    slot = lax.broadcasted_iota(jnp.int32, (count, total), 0)
    row = lax.broadcasted_iota(jnp.int32, (count, total), 1)
    for s in range(shards):
        order = row == slot + SEND * (div_send(slot) * (shards - 1) + s)
        order = jnp.where(order, 1.0, 0.0).astype(bf16)
        copies[s].wait()
        own = before[s] + jnp.dot(order, rounded, preferred_element_type=f32)
        projs[s][...] = own.astype(bf16)
        at = lax.rem(me + shards - s, shards)
        score_ref[pl.ds(at * blocks, blocks)] = score_in[s][...] + scores[s]


def finish(blocks, arrived, hidden, weight, before, scores):
    shards = len(before)
    total, part = hidden.shape
    count = total // shards
    cols = weight.shape[1]
    outs = pl.pallas_call(
        functools.partial(finish_kernel, shards, blocks),
        in_specs=[VMEM] * 3 + [HBM] * shards + [VMEM] * shards,
        out_specs=[VMEM] * (shards + 1),
        out_shape=[plain((count, part), bf16)] * shards
        + [plain((shards * blocks, 1, LANE), f32)],
        scratch_shapes=[
            pltpu.VMEM((shards, count, part), f32),
            pltpu.SemaphoreType.DMA((shards,)),
        ],
        compiler_params=params(20 * total * part),
        cost_estimate=cost(2 * total * part * cols, 2 * part * cols),
    )(arrived, hidden, weight, *in_hbm(*before), *scores)
    return list(outs[:-1]), outs[-1]


def new_state(master, one, two, grad):
    corr_one = 1.0 - beta_one**adam_step
    corr_two = 1.0 - beta_two**adam_step
    rate = learn_rate * corr_two**0.5 / corr_one
    keep = 1.0 - learn_rate * decay_rate
    eps = adam_eps * corr_two**0.5
    m_new = beta_one * one.astype(f32) + (1.0 - beta_one) * grad
    v_new = beta_two * two.astype(f32) + (1.0 - beta_two) * (grad * grad)
    root = lax.rsqrt(v_new)
    below = 1.0 + eps * root
    inverse = pl.reciprocal(below, approx=True)
    inverse = inverse * (2.0 - below * inverse)
    master = keep * master - (rate * m_new) * (root * inverse)
    return master, m_new.astype(bf16), v_new.astype(bf16)


def transpose_rows(hidden, hidden_t):
    base = 0
    for ref in hidden:
        high = base + ref.shape[0]
        hidden_t[:, base:high] = ref[...].astype(f32).T.astype(bf16)
        base = high


def form_grad(hidden_t, rows_refs, grad_ref):
    for i in range(grad_ref.shape[1] // UNIT):
        own = slice(i * UNIT, (i + 1) * UNIT)
        base = 0
        grad = 0.0
        for rows_ref in rows_refs:
            high = base + rows_ref.shape[0]
            grad += jnp.dot(
                hidden_t[:, base:high], rows_ref[:, own], preferred_element_type=f32
            )
            base = high
        grad_ref[:, own] = grad


def state_copies(i, step, low, hbm, vmem, sems, into):
    cols = vmem[0].shape[1]
    rows = pl.ds(pl.multiple_of(i * step, step), step)
    out = []
    for j, (far, near) in enumerate(zip(hbm, vmem)):
        ends = (far.at[0, rows, pl.ds(low, cols)], near.at[rows])
        source, target = ends if into else ends[::-1]
        out.append(pltpu.make_async_copy(source, target, sems.at[j, i]))
    return out


def settle_kernel(fresh, blocks, *refs):
    refs = list(refs)

    def take(number):
        out = refs[:number]
        del refs[:number]
        return out

    size = len(fresh)
    arrived, hidden = take(size), take(1 + size)
    given_ref, weight_ref, *state = take(5)
    scores, (mixed_ref,) = take(size), take(1)
    projs_hbm, outs, news = take(size), take(3), take(3)
    rows_refs, projs = take(size), take(size)
    hidden_t, grad_ref, sems, proj_sems = refs
    part = grad_ref.shape[0]
    count = blocks * SEND
    shards = 1 + size
    proj_copies = []
    for i, s in enumerate(fresh):
        reorder(arrived[i][...], rows_refs[i])
        proj = times_weight(rows_refs[i], weight_ref)
        projs[i][...] = proj
        proj_copies.append(pltpu.make_async_copy(projs[i], projs_hbm[i], proj_sems.at[i]))
        proj_copies[i].start()
        scores[i][...] = score_block(
            blocks, proj, hidden[s][...], [block_index(blocks, count)]
        )[0]
    transpose_rows(hidden, hidden_t)
    form_grad(hidden_t, [given_ref] + rows_refs, grad_ref)

    step = part // sems.shape[1]

    @pl.loop(0, part // step)
    def _(i):
        own = pl.ds(pl.multiple_of(i * step, step), step)
        values = new_state(*[ref[own, :] for ref in state], grad_ref[own, :])
        for ref, value in zip(news, values):
            ref[own, :] = value
        for copy in state_copies(i, step, 0, outs, news, sems, False):
            copy.start()

    row = lax.broadcasted_iota(jnp.int32, (shards * count, count), 0)
    col = lax.broadcasted_iota(jnp.int32, (shards * count, count), 1)
    at, step_of, slot = mixed_place(row, shards)
    total = 0.0
    for s in range(shards):
        order = (step_of == s) & (col == at * SEND + slot)
        order = jnp.where(order, 1.0, 0.0).astype(bf16)
        total += jnp.dot(order, hidden[s][...], preferred_element_type=f32)
    mixed_ref[...] = total.astype(bf16)

    @pl.loop(0, part // step)
    def _(i):
        for copy in state_copies(i, step, 0, outs, news, sems, False):
            copy.wait()

    for copy in proj_copies:
        copy.wait()


def settle(blocks, arrived, given, hidden, weight, held, shapes):
    part, cols = weight.shape
    count = blocks * SEND
    fresh = tuple(range(1, 1 + len(arrived)))
    size = len(fresh)
    total = count * (1 + size)
    step = min(part, 64)
    args = [*arrived, *hidden, given, weight, *held]
    near = [plain((blocks, 1, LANE), f32)] * size + [plain((total, part), bf16)]
    far = [out_hbm((count, part), f32)] * size
    far += [out_hbm(array.shape, array.dtype) for array in shapes]
    scratch = [pltpu.VMEM((part, cols), kind) for kind in (f32, bf16, bf16)]
    scratch += [pltpu.VMEM((count, cols), bf16)] * size
    scratch += [pltpu.VMEM((count, part), f32)] * size
    scratch += [
        pltpu.VMEM((part, total), bf16),
        pltpu.VMEM((part, cols), f32),
        pltpu.SemaphoreType.DMA((3, part // step)),
        pltpu.SemaphoreType.DMA((max(1, size),)),
    ]
    nbytes = 12 * part * cols + 4 * total * cols + 8 * total * part
    outs = pl.pallas_call(
        functools.partial(settle_kernel, fresh, blocks),
        in_specs=[VMEM] * len(args),
        out_specs=[VMEM] * len(near) + [HBM] * len(far),
        out_shape=near + far,
        scratch_shapes=scratch,
        compiler_params=params(nbytes),
        cost_estimate=cost(4 * total * part * cols, SETTLE_COST * part * cols, part * cols),
    )(*args)
    outs = list(outs)
    return outs[:size], outs[size], outs[size + 1 : -3], outs[-3:]


def update_kernel(low, shards, hidden_ref, rows_ref, *refs):
    grad_refs, refs = refs[:shards], refs[shards:]
    gate_up_hbm, state_hbm, outs, gate_out = refs[0], refs[1:4], refs[7:10], refs[10]
    state, refs = refs[11:14], refs[14:]
    hidden_t, grad_ref, gate_up_ref, gate_new, in_sems, out_sems, sems = refs
    part = grad_ref.shape[0]
    steps = in_sems.shape[1]
    step = part // steps
    gate_load = pltpu.make_async_copy(gate_up_hbm, gate_up_ref, sems.at[0])
    gate_store = pltpu.make_async_copy(gate_new, gate_out, sems.at[1])
    gate_load.start()
    for i in range(steps):
        for copy in state_copies(i, step, low, state_hbm, state, in_sems, True):
            copy.start()
    transpose_rows([hidden_ref], hidden_t)
    form_grad(hidden_t, [rows_ref], grad_ref)
    gate_load.wait()
    for s, ref in enumerate(grad_refs):
        first, second, gate, up, sig = swiglu_part(gate_up_ref, shards, s, ref.shape[1])
        grad = ref[...].astype(f32)
        gate_new[:, pl.ds(first, ref.shape[1])] = (
            grad * up * sig * (1.0 + gate * (1.0 - sig))
        ).astype(bf16)
        gate_new[:, pl.ds(second, ref.shape[1])] = (grad * (gate * sig)).astype(bf16)
    gate_store.start()

    @pl.loop(0, steps)
    def _(i):
        for copy in state_copies(i, step, low, state_hbm, state, in_sems, True):
            copy.wait()
        own = pl.ds(pl.multiple_of(i * step, step), step)
        values = new_state(*[ref[own, :] for ref in state], grad_ref[own, :])
        for ref, value in zip(state, values):
            ref[own, :] = value
        for copy in state_copies(i, step, low, outs, state, out_sems, False):
            copy.start()

    @pl.loop(0, steps)
    def _(i):
        for copy in state_copies(i, step, low, outs, state, out_sems, False):
            copy.wait()

    gate_store.wait()


def update(low, hidden, rows, grads, gate_up, state, done):
    total, part = hidden.shape
    cols = rows.shape[1]
    step = min(part, 64)
    shards = len(grads)
    scratch = [pltpu.VMEM((part, cols), kind) for kind in (f32, bf16, bf16)]
    scratch += [pltpu.VMEM((part, total), bf16), pltpu.VMEM((part, cols), f32)]
    scratch += [pltpu.VMEM(gate_up.shape, bf16)] * 2
    scratch += [pltpu.SemaphoreType.DMA((3, part // step))] * 2
    scratch += [pltpu.SemaphoreType.DMA((2,))]
    return pl.pallas_call(
        functools.partial(update_kernel, low, shards),
        in_specs=[VMEM] * (2 + shards) + [HBM] * 7,
        out_specs=[HBM] * 4,
        out_shape=[out_hbm(array.shape, array.dtype) for array in state]
        + [out_hbm(gate_up.shape, bf16)],
        scratch_shapes=scratch,
        input_output_aliases={2 + shards + 4 + i: i for i in range(3)},
        compiler_params=params(12 * part * cols + 2 * total * part + 4 * gate_up.size),
        cost_estimate=cost(2 * total * part * cols, 16 * part * cols, part * cols),
    )(hidden, rows, *grads, *in_hbm(gate_up, *state, *done))


def close_kernel(shards, ids_ref, slots_ref, gates_ref, score_ref, after_ref, gate_ref):
    del after_ref
    ids = ids_ref[...]
    slots = slots_ref[...]
    live = ((ids & (EXP_LOCAL - 1)) == 0) & (slots >= 0)
    place = jnp.where(live, ids // EXP_LOCAL * SEND + slots, -1)
    blocks = score_ref.shape[0] // shards
    value = jnp.zeros(ids.shape, f32)
    for b in range(blocks):
        for slot in range(SEND):
            score = score_ref[b, 0, slot]
            for s in range(1, shards):
                score += score_ref[s * blocks + b, 0, slot]
            value = jnp.where(place == b * SEND + slot, score, value)
    gate_ref[...] = jnp.where(live, value / gates_ref[...].astype(f32), 0.0)


def close(shards, ids, slots, gates, score, after):
    return pl.pallas_call(
        functools.partial(close_kernel, shards),
        grid=(1,),
        in_specs=[block(ids.shape)] * 3 + [pl.BlockSpec(memory_space=pltpu.SMEM), HBM],
        out_specs=block(ids.shape),
        out_shape=out_hbm(ids.shape, f32),
        compiler_params=params(0),
        cost_estimate=cost(1 << 20, 1 << 16),
    )(*in_hbm(ids, slots, gates), score, *in_hbm(after))


def per_device(out_grad, expert_ids, slots, gate_weights, saved_gate_up, master, moment1, moment2):
    ep_size = lax.axis_size("ep")
    rep_size = lax.axis_size("rep")
    ids_t, slots_t, gates_t = expert_ids.T, slots.T, gate_weights.T
    gate_up = saved_gate_up[0, 0]
    state = (master, moment1, moment2)
    edges = chunk_edges(out_grad.shape[1])
    steps = range(1, rep_size)

    def shift(value, step):
        perm = [(i, (i + step) % rep_size) for i in range(rep_size)]
        return lax.ppermute(value, "rep", perm)

    def exchange(value):
        return lax.all_to_all(value, "ep", split_axis=0, concat_axis=0, tiled=True)

    send_a, send_b = dispatch(ep_size, edges, ids_t, slots_t, gates_t, out_grad)
    mixed = [send_b] + [shift(send_b, s) for s in steps]
    parts = list(hidden_parts(gate_up, rep_size, send_b))
    hidden = [parts[0]] + [shift(parts[s], s) for s in steps]
    arrived = exchange(send_a.reshape(ep_size, ROWS, -1)).reshape(send_a.shape)
    mixed = mix(mixed, parts[1:])
    arrived_b = exchange(mixed.reshape(ep_size, rep_size * SEND, -1)).reshape(mixed.shape)

    peers = [shift(arrived, s) for s in steps]
    *held, weight_a, weight_b = load_state(edges[1], *state, arrived)
    rows, score_own, proj = begin(ep_size, arrived, weight_a, hidden[0])
    scores, hidden_mixed, before, done = settle(
        ep_size, peers, rows, hidden, weight_a, held, state
    )
    projs, score = finish(
        ep_size, arrived_b, hidden_mixed, weight_b, [proj] + before, [score_own] + scores
    )
    grads = [projs[0]] + [shift(projs[s], rep_size - s) for s in steps]
    score = lax.all_to_all(score, ("rep", "ep"), split_axis=0, concat_axis=0, tiled=True)

    *done, grad_gate_up = update(
        edges[1], hidden_mixed, arrived_b, grads, gate_up, state, done
    )
    gate_grad = close(rep_size, ids_t, slots_t, gates_t, score, grad_gate_up).T
    return (grad_gate_up.reshape(saved_gate_up.shape), gate_grad) + tuple(done)


def solution(mesh):
    in_specs = (
        P(("rep", "ep"), None),
        P(("rep", "ep"), None),
        P(("rep", "ep"), None),
        P(("rep", "ep"), None),
        P("rep", "ep", None, None),
        P("ep", "rep", None),
        P("ep", "rep", None),
        P("ep", "rep", None),
    )
    out_specs = (
        P("rep", "ep", None, None),
        P(("rep", "ep"), None),
        P("ep", "rep", None),
        P("ep", "rep", None),
        P("ep", "rep", None),
    )
    return jax.shard_map(
        per_device, mesh=mesh, in_specs=in_specs, out_specs=out_specs, check_vma=False
    )
```

```python
import functools

import jax
import jax.numpy as jnp
from jax import lax
from jax.experimental import pallas as pl
from jax.experimental.pallas import tpu as pltpu
from jax.sharding import PartitionSpec as P

TOPK = 8
EXP_LOCAL = 8
SEND = 12
LANE = 128
UNIT = 512
ROWS = 16

beta_one = 0.9
beta_two = 0.95
learn_rate = 0.002
decay_rate = 0.1
adam_eps = 1e-08
adam_step = 50

f32 = jnp.float32
bf16 = jnp.bfloat16
HBM = pl.BlockSpec(memory_space=pltpu.HBM)
ANY = pl.BlockSpec(memory_space=pl.ANY)
VMEM = pl.BlockSpec(memory_space=pltpu.VMEM)


def in_hbm(*arrays):
    return [pltpu.with_memory_space_constraint(array, pltpu.HBM) for array in arrays]


def plain(dims, dtype):
    return jax.ShapeDtypeStruct(tuple(dims), dtype)


def out_hbm(dims, dtype):
    return pltpu.HBM(tuple(dims), dtype)


def block(dims, at=None):
    at = at or (0,) * len(dims)
    return pl.BlockSpec(tuple(dims), lambda i: at, pipeline_mode=pl.Buffered(1))


def params(nbytes):
    mib = min(60, max(16, 10 + 5 * int(nbytes) // 2**22))
    return pltpu.CompilerParams(vmem_limit_bytes=mib * 2**20)


def cost(flops, nbytes, transcendentals=0):
    return pl.CostEstimate(
        flops=int(flops), bytes_accessed=int(nbytes), transcendentals=int(transcendentals)
    )


def div_send(index):
    return lax.shift_right_logical(index * 10923, 17)


def pack(cols):
    return cols // 4 * 3


def chunk_edges(width):
    units = width // UNIT
    return (0, (units - max(1, units * 3 // 7)) * UNIT, width)


def tail_order(count, total, j, slots_first):
    a = lax.broadcasted_iota(jnp.int32, (count, total), 0)
    b = lax.broadcasted_iota(jnp.int32, (count, total), 1)
    if slots_first:
        block_of = div_send(a)
        inner = a - SEND * block_of
        hit = b == block_of * ROWS + SEND + inner - 4 * j
    else:
        inner = (a & (ROWS - 1)) - SEND + 4 * j
        hit = (b == a - SEND + 4 * j) & ((a & (ROWS - 1)) >= SEND)
    return jnp.where(hit & (inner >= 4 * j) & (inner < 4 * j + 4), 1.0, 0.0).astype(bf16)


def dispatch_kernel(edges, ids_hbm, slots_hbm, gates_hbm, grad_hbm, *refs):
    outs, (ids_ref, slots_ref, gates_ref, grad_ref, sems) = refs[:2], refs[2:]
    pairs = [
        (ids_hbm, ids_ref),
        (slots_hbm, slots_ref),
        (gates_hbm, gates_ref),
        (grad_hbm, grad_ref),
    ]
    copies = [
        pltpu.make_async_copy(source, target, sems.at[i])
        for i, (source, target) in enumerate(pairs)
    ]
    for copy in copies:
        copy.start()
    rows = outs[0].shape[0]
    tok = ids_ref.shape[1]
    orders = [tail_order(rows, rows, j, False) for j in range(3)]
    for copy in copies[:3]:
        copy.wait()
    ids = ids_ref[...]
    slots = slots_ref[...]
    gates = gates_ref[...].astype(f32)
    live = ((ids & (EXP_LOCAL - 1)) == 0) & (slots >= 0)
    place = jnp.where(live, ids // EXP_LOCAL * ROWS + slots, -1)
    row = lax.broadcasted_iota(jnp.int32, (rows, tok), 0)
    main = jnp.zeros((rows, tok), f32)
    for k in range(TOPK):
        main = jnp.where(row == place[k : k + 1], gates[k : k + 1], main)
    main = main.astype(bf16)
    tails = [
        jnp.dot(order, main, preferred_element_type=f32).astype(bf16) for order in orders
    ]
    copies[3].wait()
    for c in (1, 0):
        low, high = edges[c], edges[c + 1]
        part = (high - low) // 4
        for j in range(3):
            total = jnp.dot(
                main,
                grad_ref[:, low + j * part : low + (j + 1) * part],
                preferred_element_type=f32,
            )
            total += jnp.dot(
                tails[j], grad_ref[:, low + 3 * part : high], preferred_element_type=f32
            )
            outs[c][:, j * part : (j + 1) * part] = total.astype(bf16)


def dispatch(blocks, edges, ids, slots, gates, out_grad):
    tok, width = out_grad.shape
    rows = blocks * ROWS
    shapes = [(rows, pack(high - low)) for low, high in zip(edges[:-1], edges[1:])]
    return pl.pallas_call(
        functools.partial(dispatch_kernel, edges),
        in_specs=[HBM] * 4,
        out_specs=[VMEM] * 2,
        out_shape=[plain(shape, bf16) for shape in shapes],
        scratch_shapes=[
            pltpu.VMEM(ids.shape, jnp.int32),
            pltpu.VMEM(slots.shape, jnp.int32),
            pltpu.VMEM(gates.shape, bf16),
            pltpu.VMEM(out_grad.shape, bf16),
            pltpu.SemaphoreType.DMA((4,)),
        ],
        compiler_params=params(2 * rows * width + 2 * tok * width),
        cost_estimate=cost(2 * rows * tok * width, 4 * tok * width),
    )(*in_hbm(ids, slots, gates, out_grad))


def swiglu_part(gate_up_ref, shards, step, part):
    at = lax.rem(lax.axis_index("rep") + step, shards)
    low = pl.multiple_of(at * part, part)
    high = pl.multiple_of((shards + at) * part, part)
    gate = gate_up_ref[:, pl.ds(low, part)].astype(f32)
    up = gate_up_ref[:, pl.ds(high, part)].astype(f32)
    return low, high, gate, up, jax.nn.sigmoid(gate)


def hidden_kernel(gate_up_ref, after_ref, *out_refs):
    del after_ref
    for s, out_ref in enumerate(out_refs):
        _, _, gate, up, sig = swiglu_part(gate_up_ref, len(out_refs), s, out_ref.shape[1])
        out_ref[...] = (gate * sig * up).astype(bf16)


def hidden_parts(gate_up, shards, after):
    slots, width = gate_up.shape
    shape = (slots, width // 2 // shards)
    return pl.pallas_call(
        hidden_kernel,
        grid=(1,),
        in_specs=[block(gate_up.shape), ANY],
        out_specs=[block(shape)] * shards,
        out_shape=[plain(shape, bf16)] * shards,
        compiler_params=params(3 * slots * width),
        cost_estimate=cost(8 * slots * width, 3 * slots * width, slots * width),
    )(*in_hbm(gate_up), after)


def load_kernel(middle, after_ref, master_hbm, one_hbm, two_hbm, *refs):
    del after_ref
    master_ref, one_ref, two_ref, weight_a, weight_b, rest_ref, sems = refs
    part = master_ref.shape[0]
    rest = rest_ref.shape[1]
    step = part // 4
    copies = []
    for i in range(4):
        own = pl.ds(i * step, step)
        copies.append(
            pltpu.make_async_copy(
                master_hbm.at[0, own, pl.ds(0, middle)], master_ref.at[own], sems.at[i]
            )
        )
    for i in range(4):
        own = pl.ds(i * step, step)
        copies.append(
            pltpu.make_async_copy(
                master_hbm.at[0, own, pl.ds(middle, rest)], rest_ref.at[own], sems.at[4 + i]
            )
        )
    for i, (source, target) in enumerate([(one_hbm, one_ref), (two_hbm, two_ref)]):
        copies.append(
            pltpu.make_async_copy(source.at[0, :, pl.ds(0, middle)], target, sems.at[8 + i])
        )
    for copy in copies:
        copy.start()
    for i in range(4):
        copies[i].wait()
        own = slice(i * step, (i + 1) * step)
        weight_a[own, :] = master_ref[own, :].astype(bf16)
    for i in range(4):
        copies[4 + i].wait()
        own = slice(i * step, (i + 1) * step)
        weight_b[own, :] = rest_ref[own, :].astype(bf16)
    copies[8].wait()
    copies[9].wait()


def load_state(middle, master, one, two, after):
    _, part, width = master.shape
    return pl.pallas_call(
        functools.partial(load_kernel, middle),
        in_specs=[ANY] + [HBM] * 3,
        out_specs=[VMEM] * 5,
        out_shape=[
            pltpu.VMEM((part, middle), f32),
            pltpu.VMEM((part, middle), bf16),
            pltpu.VMEM((part, middle), bf16),
            pltpu.VMEM((part, middle), bf16),
            pltpu.VMEM((part, width - middle), bf16),
        ],
        scratch_shapes=[
            pltpu.VMEM((part, width - middle), f32),
            pltpu.SemaphoreType.DMA((10,)),
        ],
        compiler_params=params(4 * part * (width - middle)),
        cost_estimate=cost(part * width, 14 * part * width),
    )(after, *in_hbm(master, one, two))


def mixed_place(index, shards):
    group = div_send(index)
    bits = shards.bit_length() - 1
    step = group & (shards - 1)
    return lax.shift_right_logical(group, bits), step, index - SEND * group


def mix_kernel(shards, *refs):
    parts, out_ref = refs[:shards], refs[-1]
    part = parts[0].shape[1] // 3
    blocks = parts[0].shape[0] // ROWS
    some = max(1, min(blocks, 32 // shards))
    rows, packed = some * shards * SEND, some * shards * ROWS
    row = lax.broadcasted_iota(jnp.int32, (rows, packed), 0)
    col = lax.broadcasted_iota(jnp.int32, (rows, packed), 1)
    at, step, slot = mixed_place(row, shards)
    base = (step * some + at) * ROWS
    orders = [jnp.where(col == base + slot, 1.0, 0.0).astype(bf16)]
    for j in range(3):
        hit = (col == base + SEND + slot - 4 * j) & (slot >= 4 * j) & (slot < 4 * j + 4)
        orders.append(jnp.where(hit, 1.0, 0.0).astype(bf16))
    for first in range(0, blocks, some):
        stack = jnp.concatenate(
            [ref[first * ROWS : (first + some) * ROWS, :] for ref in parts], axis=0
        )
        own = slice(first * shards * SEND, (first + some) * shards * SEND)
        out_ref[own, : 3 * part] = jnp.dot(
            orders[0], stack, preferred_element_type=f32
        ).astype(bf16)
        tail = jnp.zeros((rows, part), f32)
        for j in range(3):
            tail += jnp.dot(
                orders[1 + j],
                stack[:, j * part : (j + 1) * part],
                preferred_element_type=f32,
            )
        out_ref[own, 3 * part :] = tail.astype(bf16)


def mix(parts):
    shards = len(parts)
    rows, packed = parts[0].shape
    shape = (rows // ROWS * SEND * shards, packed // 3 * 4)
    return pl.pallas_call(
        functools.partial(mix_kernel, shards),
        in_specs=[VMEM] * shards,
        out_specs=VMEM,
        out_shape=plain(shape, bf16),
        compiler_params=params(12 * rows * packed * shards),
        cost_estimate=cost(0, 5 * rows * packed * shards),
    )(*parts)


def reorder(arrived, rows_ref):
    count, width = rows_ref.shape
    part = width // 4
    total = arrived.shape[0]
    slot = lax.broadcasted_iota(jnp.int32, (count, total), 0)
    col = lax.broadcasted_iota(jnp.int32, (count, total), 1)
    order = jnp.where(col == slot + (ROWS - SEND) * div_send(slot), 1.0, 0.0).astype(bf16)
    rows_ref[:, : 3 * part] = jnp.dot(order, arrived, preferred_element_type=f32).astype(bf16)
    tail = jnp.zeros((count, part), f32)
    for j in range(3):
        tail += jnp.dot(
            tail_order(count, total, j, True),
            arrived[:, j * part : (j + 1) * part],
            preferred_element_type=f32,
        )
    rows_ref[:, 3 * part :] = tail.astype(bf16)


def times_weight(rows_ref, weight_ref):
    return lax.dot_general(
        rows_ref[...], weight_ref[...], (((1,), (1,)), ((), ())), preferred_element_type=f32
    )


def score_block(blocks, proj, hidden, picked):
    count = proj.shape[0]
    score = jnp.sum(proj * hidden.astype(f32), axis=1, keepdims=True)
    row = lax.broadcasted_iota(jnp.int32, (count, LANE), 0)
    lane = lax.broadcasted_iota(jnp.int32, (count, LANE), 1)
    spread = jnp.where(row - SEND * div_send(row) == lane, score, 0.0)
    high = spread.astype(bf16)
    rest = (spread - high.astype(f32)).astype(bf16)
    at = lax.broadcasted_iota(jnp.int32, (blocks, count), 1)
    gather = [jnp.where(div_send(at) == pick, 1.0, 0.0) for pick in picked]
    gather = jnp.concatenate(gather, axis=0).astype(bf16)
    value = jnp.dot(gather, high, preferred_element_type=f32)
    value += jnp.dot(gather, rest, preferred_element_type=f32)
    return [
        value[i * blocks : (i + 1) * blocks].reshape(blocks, 1, LANE)
        for i in range(len(picked))
    ]


def block_index(blocks, count):
    return lax.broadcasted_iota(jnp.int32, (blocks, count), 0)


def begin_kernel(blocks, arrived_ref, weight_ref, hidden_ref, *refs):
    rows_ref, score_ref, proj_hbm, proj_ref, sem = refs
    reorder(arrived_ref[...], rows_ref)
    proj = times_weight(rows_ref, weight_ref)
    proj_ref[...] = proj
    copy = pltpu.make_async_copy(proj_ref, proj_hbm, sem.at[0])
    copy.start()
    score_ref[...] = score_block(
        blocks, proj, hidden_ref[...], [block_index(blocks, proj.shape[0])]
    )[0]
    copy.wait()


def begin(blocks, arrived, weight, hidden):
    count = blocks * SEND
    part, cols = weight.shape
    return pl.pallas_call(
        functools.partial(begin_kernel, blocks),
        in_specs=[VMEM] * 3,
        out_specs=[VMEM] * 2 + [HBM],
        out_shape=[
            plain((count, cols), bf16),
            plain((blocks, 1, LANE), f32),
            out_hbm((count, part), f32),
        ],
        scratch_shapes=[pltpu.VMEM((count, part), f32), pltpu.SemaphoreType.DMA((1,))],
        compiler_params=params(8 * count * cols + 8 * count * part),
        cost_estimate=cost(4 * count * part * cols, 2 * part * cols),
    )(arrived, weight, hidden)


def finish_kernel(shards, blocks, arrived_ref, hidden_ref, weight_ref, *refs):
    before_hbm, score_in = refs[:shards], refs[shards : 2 * shards]
    projs, score_ref = refs[2 * shards : 3 * shards], refs[3 * shards]
    before, sems = refs[3 * shards + 1 :]
    copies = [
        pltpu.make_async_copy(ref, before.at[s], sems.at[s])
        for s, ref in enumerate(before_hbm)
    ]
    for copy in copies:
        copy.start()
    proj = times_weight(arrived_ref, weight_ref)
    rounded = proj.astype(bf16)
    total = proj.shape[0]
    count = total // shards
    picked = [block_index(blocks, total) * shards + s for s in range(shards)]
    scores = score_block(blocks, proj, hidden_ref[...], picked)
    me = lax.axis_index("rep")
    slot = lax.broadcasted_iota(jnp.int32, (count, total), 0)
    row = lax.broadcasted_iota(jnp.int32, (count, total), 1)
    for s in range(shards):
        order = row == slot + SEND * (div_send(slot) * (shards - 1) + s)
        order = jnp.where(order, 1.0, 0.0).astype(bf16)
        copies[s].wait()
        own = before[s] + jnp.dot(order, rounded, preferred_element_type=f32)
        projs[s][...] = own.astype(bf16)
        at = lax.rem(me + shards - s, shards)
        score_ref[pl.ds(at * blocks, blocks)] = score_in[s][...] + scores[s]


def finish(blocks, arrived, hidden, weight, before, scores):
    shards = len(before)
    total, part = hidden.shape
    count = total // shards
    cols = weight.shape[1]
    outs = pl.pallas_call(
        functools.partial(finish_kernel, shards, blocks),
        in_specs=[VMEM] * 3 + [HBM] * shards + [VMEM] * shards,
        out_specs=[VMEM] * (shards + 1),
        out_shape=[plain((count, part), bf16)] * shards
        + [plain((shards * blocks, 1, LANE), f32)],
        scratch_shapes=[
            pltpu.VMEM((shards, count, part), f32),
            pltpu.SemaphoreType.DMA((shards,)),
        ],
        compiler_params=params(20 * total * part),
        cost_estimate=cost(2 * total * part * cols, 2 * part * cols),
    )(arrived, hidden, weight, *in_hbm(*before), *scores)
    return list(outs[:-1]), outs[-1]


def new_state(master, one, two, grad):
    corr_one = 1.0 - beta_one**adam_step
    corr_two = 1.0 - beta_two**adam_step
    rate = learn_rate * corr_two**0.5 / corr_one
    keep = 1.0 - learn_rate * decay_rate
    eps = adam_eps * corr_two**0.5
    m_new = beta_one * one.astype(f32) + (1.0 - beta_one) * grad
    v_new = beta_two * two.astype(f32) + (1.0 - beta_two) * (grad * grad)
    root = lax.rsqrt(v_new)
    below = v_new * root + eps
    inverse = root * (2.0 - below * root)
    master = keep * master - (rate * m_new) * inverse
    return master, m_new.astype(bf16), v_new.astype(bf16)


def transpose_rows(hidden, hidden_t):
    base = 0
    for ref in hidden:
        high = base + ref.shape[0]
        hidden_t[:, base:high] = ref[...].astype(f32).T.astype(bf16)
        base = high


def form_grad(hidden_t, rows_refs, grad_ref):
    for i in range(grad_ref.shape[1] // UNIT):
        own = slice(i * UNIT, (i + 1) * UNIT)
        base = 0
        grad = 0.0
        for rows_ref in rows_refs:
            high = base + rows_ref.shape[0]
            grad += jnp.dot(
                hidden_t[:, base:high], rows_ref[:, own], preferred_element_type=f32
            )
            base = high
        grad_ref[:, own] = grad


def state_copies(i, step, low, hbm, vmem, sems, into):
    cols = vmem[0].shape[1]
    rows = pl.ds(pl.multiple_of(i * step, step), step)
    out = []
    for j, (far, near) in enumerate(zip(hbm, vmem)):
        ends = (far.at[0, rows, pl.ds(low, cols)], near.at[rows])
        source, target = ends if into else ends[::-1]
        out.append(pltpu.make_async_copy(source, target, sems.at[j, i]))
    return out


def settle_kernel(fresh, blocks, *refs):
    refs = list(refs)

    def take(number):
        out = refs[:number]
        del refs[:number]
        return out

    size = len(fresh)
    arrived, hidden = take(size), take(1 + size)
    given_ref, weight_ref, *state = take(5)
    scores, (mixed_ref,) = take(size), take(1)
    projs_hbm, outs, news = take(size), take(3), take(3)
    rows_refs, projs = take(size), take(size)
    hidden_t, grad_ref, sems, proj_sems = refs
    part = grad_ref.shape[0]
    count = blocks * SEND
    shards = 1 + size
    proj_copies = []
    for i, s in enumerate(fresh):
        reorder(arrived[i][...], rows_refs[i])
        proj = times_weight(rows_refs[i], weight_ref)
        projs[i][...] = proj
        proj_copies.append(pltpu.make_async_copy(projs[i], projs_hbm[i], proj_sems.at[i]))
        proj_copies[i].start()
        scores[i][...] = score_block(
            blocks, proj, hidden[s][...], [block_index(blocks, count)]
        )[0]
    transpose_rows(hidden, hidden_t)
    form_grad(hidden_t, [given_ref] + rows_refs, grad_ref)

    step = part // sems.shape[1]

    @pl.loop(0, part // step)
    def _(i):
        own = pl.ds(pl.multiple_of(i * step, step), step)
        values = new_state(*[ref[own, :] for ref in state], grad_ref[own, :])
        for ref, value in zip(news, values):
            ref[own, :] = value
        for copy in state_copies(i, step, 0, outs, news, sems, False):
            copy.start()

    row = lax.broadcasted_iota(jnp.int32, (shards * count, count), 0)
    col = lax.broadcasted_iota(jnp.int32, (shards * count, count), 1)
    at, step_of, slot = mixed_place(row, shards)
    total = 0.0
    for s in range(shards):
        order = (step_of == s) & (col == at * SEND + slot)
        order = jnp.where(order, 1.0, 0.0).astype(bf16)
        total += jnp.dot(order, hidden[s][...], preferred_element_type=f32)
    mixed_ref[...] = total.astype(bf16)

    @pl.loop(0, part // step)
    def _(i):
        for copy in state_copies(i, step, 0, outs, news, sems, False):
            copy.wait()

    for copy in proj_copies:
        copy.wait()


def settle(blocks, arrived, given, hidden, weight, held, shapes):
    part, cols = weight.shape
    count = blocks * SEND
    fresh = tuple(range(1, 1 + len(arrived)))
    size = len(fresh)
    total = count * (1 + size)
    step = min(part, 64)
    args = [*arrived, *hidden, given, weight, *held]
    near = [plain((blocks, 1, LANE), f32)] * size + [plain((total, part), bf16)]
    far = [out_hbm((count, part), f32)] * size
    far += [out_hbm(array.shape, array.dtype) for array in shapes]
    scratch = [pltpu.VMEM((part, cols), kind) for kind in (f32, bf16, bf16)]
    scratch += [pltpu.VMEM((count, cols), bf16)] * size
    scratch += [pltpu.VMEM((count, part), f32)] * size
    scratch += [
        pltpu.VMEM((part, total), bf16),
        pltpu.VMEM((part, cols), f32),
        pltpu.SemaphoreType.DMA((3, part // step)),
        pltpu.SemaphoreType.DMA((max(1, size),)),
    ]
    nbytes = 12 * part * cols + 4 * total * cols + 8 * total * part
    outs = pl.pallas_call(
        functools.partial(settle_kernel, fresh, blocks),
        in_specs=[VMEM] * len(args),
        out_specs=[VMEM] * len(near) + [HBM] * len(far),
        out_shape=near + far,
        scratch_shapes=scratch,
        compiler_params=params(nbytes),
        cost_estimate=cost(4 * total * part * cols, 16 * part * cols, part * cols),
    )(*args)
    outs = list(outs)
    return outs[:size], outs[size], outs[size + 1 : -3], outs[-3:]


def update_kernel(low, shards, hidden_ref, rows_ref, *refs):
    grad_refs, refs = refs[:shards], refs[shards:]
    gate_up_hbm, state_hbm, outs, gate_out = refs[0], refs[1:4], refs[7:10], refs[10]
    state, refs = refs[11:14], refs[14:]
    hidden_t, grad_ref, gate_up_ref, gate_new, in_sems, out_sems, sems = refs
    part = grad_ref.shape[0]
    steps = in_sems.shape[1]
    step = part // steps
    gate_load = pltpu.make_async_copy(gate_up_hbm, gate_up_ref, sems.at[0])
    gate_store = pltpu.make_async_copy(gate_new, gate_out, sems.at[1])
    gate_load.start()
    for i in range(steps):
        for copy in state_copies(i, step, low, state_hbm, state, in_sems, True):
            copy.start()
    transpose_rows([hidden_ref], hidden_t)
    form_grad(hidden_t, [rows_ref], grad_ref)
    gate_load.wait()
    for s, ref in enumerate(grad_refs):
        first, second, gate, up, sig = swiglu_part(gate_up_ref, shards, s, ref.shape[1])
        grad = ref[...].astype(f32)
        gate_new[:, pl.ds(first, ref.shape[1])] = (
            grad * up * sig * (1.0 + gate * (1.0 - sig))
        ).astype(bf16)
        gate_new[:, pl.ds(second, ref.shape[1])] = (grad * (gate * sig)).astype(bf16)
    gate_store.start()

    @pl.loop(0, steps)
    def _(i):
        for copy in state_copies(i, step, low, state_hbm, state, in_sems, True):
            copy.wait()
        own = pl.ds(pl.multiple_of(i * step, step), step)
        values = new_state(*[ref[own, :] for ref in state], grad_ref[own, :])
        for ref, value in zip(state, values):
            ref[own, :] = value
        for copy in state_copies(i, step, low, outs, state, out_sems, False):
            copy.start()

    @pl.loop(0, steps)
    def _(i):
        for copy in state_copies(i, step, low, outs, state, out_sems, False):
            copy.wait()

    gate_store.wait()


def update(low, hidden, rows, grads, gate_up, state, done):
    total, part = hidden.shape
    cols = rows.shape[1]
    step = min(part, 64)
    shards = len(grads)
    scratch = [pltpu.VMEM((part, cols), kind) for kind in (f32, bf16, bf16)]
    scratch += [pltpu.VMEM((part, total), bf16), pltpu.VMEM((part, cols), f32)]
    scratch += [pltpu.VMEM(gate_up.shape, bf16)] * 2
    scratch += [pltpu.SemaphoreType.DMA((3, part // step))] * 2
    scratch += [pltpu.SemaphoreType.DMA((2,))]
    return pl.pallas_call(
        functools.partial(update_kernel, low, shards),
        in_specs=[VMEM] * (2 + shards) + [HBM] * 7,
        out_specs=[HBM] * 4,
        out_shape=[out_hbm(array.shape, array.dtype) for array in state]
        + [out_hbm(gate_up.shape, bf16)],
        scratch_shapes=scratch,
        input_output_aliases={2 + shards + 4 + i: i for i in range(3)},
        compiler_params=params(12 * part * cols + 2 * total * part + 4 * gate_up.size),
        cost_estimate=cost(2 * total * part * cols, 16 * part * cols, part * cols),
    )(hidden, rows, *grads, *in_hbm(gate_up, *state, *done))


def close_kernel(shards, ids_ref, slots_ref, gates_ref, score_ref, after_ref, gate_ref):
    del after_ref
    ids = ids_ref[...]
    slots = slots_ref[...]
    live = ((ids & (EXP_LOCAL - 1)) == 0) & (slots >= 0)
    place = jnp.where(live, ids // EXP_LOCAL * SEND + slots, -1)
    blocks = score_ref.shape[0] // shards
    value = jnp.zeros(ids.shape, f32)
    for b in range(blocks):
        for slot in range(SEND):
            score = score_ref[b, 0, slot]
            for s in range(1, shards):
                score += score_ref[s * blocks + b, 0, slot]
            value = jnp.where(place == b * SEND + slot, score, value)
    gate_ref[...] = jnp.where(live, value / gates_ref[...].astype(f32), 0.0)


def close(shards, ids, slots, gates, score, after):
    return pl.pallas_call(
        functools.partial(close_kernel, shards),
        grid=(1,),
        in_specs=[block(ids.shape)] * 3 + [pl.BlockSpec(memory_space=pltpu.SMEM), HBM],
        out_specs=block(ids.shape),
        out_shape=out_hbm(ids.shape, f32),
        compiler_params=params(0),
        cost_estimate=cost(1 << 20, 1 << 16),
    )(*in_hbm(ids, slots, gates), score, *in_hbm(after))


def per_device(out_grad, expert_ids, slots, gate_weights, saved_gate_up, master, moment1, moment2):
    ep_size = lax.axis_size("ep")
    rep_size = lax.axis_size("rep")
    ids_t, slots_t, gates_t = expert_ids.T, slots.T, gate_weights.T
    gate_up = saved_gate_up[0, 0]
    state = (master, moment1, moment2)
    edges = chunk_edges(out_grad.shape[1])
    steps = range(1, rep_size)

    def shift(value, step):
        perm = [(i, (i + step) % rep_size) for i in range(rep_size)]
        return lax.ppermute(value, "rep", perm)

    def exchange(value):
        return lax.all_to_all(value, "ep", split_axis=0, concat_axis=0, tiled=True)

    send_a, send_b = dispatch(ep_size, edges, ids_t, slots_t, gates_t, out_grad)
    mixed = [shift(send_b, s) for s in steps]
    parts = list(hidden_parts(gate_up, rep_size, send_b))
    arrived = exchange(send_a.reshape(ep_size, ROWS, -1)).reshape(send_a.shape)
    parts[1:], mixed = lax.optimization_barrier((parts[1:], mixed))
    hidden = [parts[0]] + [shift(parts[s], s) for s in steps]
    mixed = mix([send_b] + mixed)
    hidden[1:], mixed = lax.optimization_barrier((hidden[1:], mixed))
    arrived_b = exchange(mixed.reshape(ep_size, rep_size * SEND, -1)).reshape(mixed.shape)

    peers = [shift(arrived, s) for s in steps]
    *held, weight_a, weight_b = load_state(edges[1], *state, arrived)
    rows, score_own, proj = begin(ep_size, arrived, weight_a, hidden[0])
    scores, hidden_mixed, before, done = settle(
        ep_size, peers, rows, hidden, weight_a, held, state
    )
    projs, score = finish(
        ep_size, arrived_b, hidden_mixed, weight_b, [proj] + before, [score_own] + scores
    )
    grads = [projs[0]] + [shift(projs[s], rep_size - s) for s in steps]
    score = lax.all_to_all(score, ("rep", "ep"), split_axis=0, concat_axis=0, tiled=True)

    *done, grad_gate_up = update(
        edges[1], hidden_mixed, arrived_b, grads, gate_up, state, done
    )
    gate_grad = close(rep_size, ids_t, slots_t, gates_t, score, grad_gate_up).T
    return (grad_gate_up.reshape(saved_gate_up.shape), gate_grad) + tuple(done)


def solution(mesh):
    in_specs = (
        P(("rep", "ep"), None),
        P(("rep", "ep"), None),
        P(("rep", "ep"), None),
        P(("rep", "ep"), None),
        P("rep", "ep", None, None),
        P("ep", "rep", None),
        P("ep", "rep", None),
        P("ep", "rep", None),
    )
    out_specs = (
        P("rep", "ep", None, None),
        P(("rep", "ep"), None),
        P("ep", "rep", None),
        P("ep", "rep", None),
        P("ep", "rep", None),
    )
    return jax.shard_map(
        per_device, mesh=mesh, in_specs=in_specs, out_specs=out_specs, check_vma=False
    )
```

```python
import functools

import jax
import jax.numpy as jnp
from jax import lax
from jax.experimental import pallas as pl
from jax.experimental.pallas import tpu as pltpu
from jax.sharding import PartitionSpec as P

TOPK = 8
EXP_LOCAL = 8
SEND = 12
LANE = 128
UNIT = 512
ROWS = 16

beta_one = 0.9
beta_two = 0.95
learn_rate = 0.002
decay_rate = 0.1
adam_eps = 1e-08
adam_step = 50

f32 = jnp.float32
bf16 = jnp.bfloat16
HBM = pl.BlockSpec(memory_space=pltpu.HBM)
ANY = pl.BlockSpec(memory_space=pl.ANY)
VMEM = pl.BlockSpec(memory_space=pltpu.VMEM)


def in_hbm(*arrays):
    return [pltpu.with_memory_space_constraint(array, pltpu.HBM) for array in arrays]


def plain(dims, dtype):
    return jax.ShapeDtypeStruct(tuple(dims), dtype)


def out_hbm(dims, dtype):
    return pltpu.HBM(tuple(dims), dtype)


def block(dims, at=None):
    at = at or (0,) * len(dims)
    return pl.BlockSpec(tuple(dims), lambda i: at, pipeline_mode=pl.Buffered(1))


def params(nbytes):
    mib = min(60, max(16, 10 + 5 * int(nbytes) // 2**22))
    return pltpu.CompilerParams(vmem_limit_bytes=mib * 2**20)


def cost(flops, nbytes, transcendentals=0):
    return pl.CostEstimate(
        flops=int(flops), bytes_accessed=int(nbytes), transcendentals=int(transcendentals)
    )


def div_send(index):
    return lax.shift_right_logical(index * 10923, 17)


def pack(cols):
    return cols // 4 * 3


def chunk_edges(width):
    units = width // UNIT
    return (0, (units - max(1, units * 3 // 7)) * UNIT, width)


def tail_order(count, total, j, slots_first):
    a = lax.broadcasted_iota(jnp.int32, (count, total), 0)
    b = lax.broadcasted_iota(jnp.int32, (count, total), 1)
    if slots_first:
        block_of = div_send(a)
        inner = a - SEND * block_of
        hit = b == block_of * ROWS + SEND + inner - 4 * j
    else:
        inner = (a & (ROWS - 1)) - SEND + 4 * j
        hit = (b == a - SEND + 4 * j) & ((a & (ROWS - 1)) >= SEND)
    return jnp.where(hit & (inner >= 4 * j) & (inner < 4 * j + 4), 1.0, 0.0).astype(bf16)


def dispatch_kernel(edges, ids_hbm, slots_hbm, gates_hbm, grad_hbm, *refs):
    outs, (ids_ref, slots_ref, gates_ref, grad_ref, sems) = refs[:2], refs[2:]
    pairs = [(ids_hbm, ids_ref), (slots_hbm, slots_ref), (gates_hbm, gates_ref)]
    for c in (1, 0):
        own = (slice(None), pl.ds(edges[c], edges[c + 1] - edges[c]))
        pairs.append((grad_hbm.at[own], grad_ref.at[own]))
    copies = [
        pltpu.make_async_copy(source, target, sems.at[i])
        for i, (source, target) in enumerate(pairs)
    ]
    for copy in copies:
        copy.start()
    rows = outs[0].shape[0]
    tok = ids_ref.shape[1]
    orders = [tail_order(rows, rows, j, False) for j in range(3)]
    for copy in copies[:3]:
        copy.wait()
    ids = ids_ref[...]
    slots = slots_ref[...]
    gates = gates_ref[...].astype(f32)
    live = ((ids & (EXP_LOCAL - 1)) == 0) & (slots >= 0)
    place = jnp.where(live, ids // EXP_LOCAL * ROWS + slots, -1)
    row = lax.broadcasted_iota(jnp.int32, (rows, tok), 0)
    main = jnp.zeros((rows, tok), f32)
    for k in range(TOPK):
        main = jnp.where(row == place[k : k + 1], gates[k : k + 1], main)
    main = main.astype(bf16)
    tails = [
        jnp.dot(order, main, preferred_element_type=f32).astype(bf16) for order in orders
    ]
    for c in (1, 0):
        copies[4 - c].wait()
        low, high = edges[c], edges[c + 1]
        part = (high - low) // 4
        for j in range(3):
            total = jnp.dot(
                main,
                grad_ref[:, low + j * part : low + (j + 1) * part],
                preferred_element_type=f32,
            )
            total += jnp.dot(
                tails[j], grad_ref[:, low + 3 * part : high], preferred_element_type=f32
            )
            outs[c][:, j * part : (j + 1) * part] = total.astype(bf16)


def dispatch(blocks, edges, ids, slots, gates, out_grad):
    tok, width = out_grad.shape
    rows = blocks * ROWS
    shapes = [(rows, pack(high - low)) for low, high in zip(edges[:-1], edges[1:])]
    return pl.pallas_call(
        functools.partial(dispatch_kernel, edges),
        in_specs=[HBM] * 4,
        out_specs=[VMEM] * 2,
        out_shape=[plain(shape, bf16) for shape in shapes],
        scratch_shapes=[
            pltpu.VMEM(ids.shape, jnp.int32),
            pltpu.VMEM(slots.shape, jnp.int32),
            pltpu.VMEM(gates.shape, bf16),
            pltpu.VMEM(out_grad.shape, bf16),
            pltpu.SemaphoreType.DMA((5,)),
        ],
        compiler_params=params(2 * rows * width + 2 * tok * width),
        cost_estimate=cost(2 * rows * tok * width, 4 * tok * width),
    )(*in_hbm(ids, slots, gates, out_grad))


def swiglu_part(gate_up_ref, shards, step, part):
    at = lax.rem(lax.axis_index("rep") + step, shards)
    low = pl.multiple_of(at * part, part)
    high = pl.multiple_of((shards + at) * part, part)
    gate = gate_up_ref[:, pl.ds(low, part)].astype(f32)
    up = gate_up_ref[:, pl.ds(high, part)].astype(f32)
    return low, high, gate, up, jax.nn.sigmoid(gate)


def hidden_kernel(gate_up_ref, after_ref, *out_refs):
    del after_ref
    for s, out_ref in enumerate(out_refs):
        _, _, gate, up, sig = swiglu_part(gate_up_ref, len(out_refs), s, out_ref.shape[1])
        out_ref[...] = (gate * sig * up).astype(bf16)


def hidden_parts(gate_up, shards, after):
    slots, width = gate_up.shape
    shape = (slots, width // 2 // shards)
    return pl.pallas_call(
        hidden_kernel,
        grid=(1,),
        in_specs=[block(gate_up.shape), ANY],
        out_specs=[block(shape)] * shards,
        out_shape=[plain(shape, bf16)] * shards,
        compiler_params=params(3 * slots * width),
        cost_estimate=cost(8 * slots * width, 3 * slots * width, slots * width),
    )(*in_hbm(gate_up), after)


def load_kernel(middle, after_ref, master_hbm, one_hbm, two_hbm, *refs):
    del after_ref
    master_ref, one_ref, two_ref, weight_a, weight_b, rest_ref, sems = refs
    part = master_ref.shape[0]
    rest = rest_ref.shape[1]
    step = part // 4
    copies = []
    for i in range(4):
        own = pl.ds(i * step, step)
        copies.append(
            pltpu.make_async_copy(
                master_hbm.at[0, own, pl.ds(0, middle)], master_ref.at[own], sems.at[i]
            )
        )
    for i in range(4):
        own = pl.ds(i * step, step)
        copies.append(
            pltpu.make_async_copy(
                master_hbm.at[0, own, pl.ds(middle, rest)], rest_ref.at[own], sems.at[4 + i]
            )
        )
    for i, (source, target) in enumerate([(one_hbm, one_ref), (two_hbm, two_ref)]):
        copies.append(
            pltpu.make_async_copy(source.at[0, :, pl.ds(0, middle)], target, sems.at[8 + i])
        )
    for copy in copies:
        copy.start()
    for i in range(4):
        copies[i].wait()
        own = slice(i * step, (i + 1) * step)
        weight_a[own, :] = master_ref[own, :].astype(bf16)
    for i in range(4):
        copies[4 + i].wait()
        own = slice(i * step, (i + 1) * step)
        weight_b[own, :] = rest_ref[own, :].astype(bf16)
    copies[8].wait()
    copies[9].wait()


def load_state(middle, master, one, two, after):
    _, part, width = master.shape
    return pl.pallas_call(
        functools.partial(load_kernel, middle),
        in_specs=[ANY] + [HBM] * 3,
        out_specs=[VMEM] * 5,
        out_shape=[
            pltpu.VMEM((part, middle), f32),
            pltpu.VMEM((part, middle), bf16),
            pltpu.VMEM((part, middle), bf16),
            pltpu.VMEM((part, middle), bf16),
            pltpu.VMEM((part, width - middle), bf16),
        ],
        scratch_shapes=[
            pltpu.VMEM((part, width - middle), f32),
            pltpu.SemaphoreType.DMA((10,)),
        ],
        compiler_params=params(4 * part * (width - middle)),
        cost_estimate=cost(part * width, 14 * part * width),
    )(after, *in_hbm(master, one, two))


def mixed_place(index, shards):
    group = div_send(index)
    bits = shards.bit_length() - 1
    step = group & (shards - 1)
    return lax.shift_right_logical(group, bits), step, index - SEND * group


def mix_kernel(shards, *refs):
    parts, out_ref = refs[:shards], refs[-1]
    part = parts[0].shape[1] // 3
    blocks = parts[0].shape[0] // ROWS
    some = max(1, min(blocks, 32 // shards))
    rows, packed = some * shards * SEND, some * shards * ROWS
    row = lax.broadcasted_iota(jnp.int32, (rows, packed), 0)
    col = lax.broadcasted_iota(jnp.int32, (rows, packed), 1)
    at, step, slot = mixed_place(row, shards)
    base = (step * some + at) * ROWS
    orders = [jnp.where(col == base + slot, 1.0, 0.0).astype(bf16)]
    for j in range(3):
        hit = (col == base + SEND + slot - 4 * j) & (slot >= 4 * j) & (slot < 4 * j + 4)
        orders.append(jnp.where(hit, 1.0, 0.0).astype(bf16))
    for first in range(0, blocks, some):
        stack = jnp.concatenate(
            [ref[first * ROWS : (first + some) * ROWS, :] for ref in parts], axis=0
        )
        own = slice(first * shards * SEND, (first + some) * shards * SEND)
        out_ref[own, : 3 * part] = jnp.dot(
            orders[0], stack, preferred_element_type=f32
        ).astype(bf16)
        tail = jnp.zeros((rows, part), f32)
        for j in range(3):
            tail += jnp.dot(
                orders[1 + j],
                stack[:, j * part : (j + 1) * part],
                preferred_element_type=f32,
            )
        out_ref[own, 3 * part :] = tail.astype(bf16)


def mix(parts):
    shards = len(parts)
    rows, packed = parts[0].shape
    shape = (rows // ROWS * SEND * shards, packed // 3 * 4)
    return pl.pallas_call(
        functools.partial(mix_kernel, shards),
        in_specs=[VMEM] * shards,
        out_specs=VMEM,
        out_shape=plain(shape, bf16),
        compiler_params=params(12 * rows * packed * shards),
        cost_estimate=cost(0, 5 * rows * packed * shards),
    )(*parts)


def reorder(arrived, rows_ref):
    count, width = rows_ref.shape
    part = width // 4
    total = arrived.shape[0]
    slot = lax.broadcasted_iota(jnp.int32, (count, total), 0)
    col = lax.broadcasted_iota(jnp.int32, (count, total), 1)
    order = jnp.where(col == slot + (ROWS - SEND) * div_send(slot), 1.0, 0.0).astype(bf16)
    rows_ref[:, : 3 * part] = jnp.dot(order, arrived, preferred_element_type=f32).astype(bf16)
    tail = jnp.zeros((count, part), f32)
    for j in range(3):
        tail += jnp.dot(
            tail_order(count, total, j, True),
            arrived[:, j * part : (j + 1) * part],
            preferred_element_type=f32,
        )
    rows_ref[:, 3 * part :] = tail.astype(bf16)


def times_weight(rows_ref, weight_ref):
    return lax.dot_general(
        rows_ref[...], weight_ref[...], (((1,), (1,)), ((), ())), preferred_element_type=f32
    )


def score_block(blocks, proj, hidden, picked):
    count = proj.shape[0]
    score = jnp.sum(proj * hidden.astype(f32), axis=1, keepdims=True)
    row = lax.broadcasted_iota(jnp.int32, (count, LANE), 0)
    lane = lax.broadcasted_iota(jnp.int32, (count, LANE), 1)
    spread = jnp.where(row - SEND * div_send(row) == lane, score, 0.0)
    high = spread.astype(bf16)
    rest = (spread - high.astype(f32)).astype(bf16)
    at = lax.broadcasted_iota(jnp.int32, (blocks, count), 1)
    gather = [jnp.where(div_send(at) == pick, 1.0, 0.0) for pick in picked]
    gather = jnp.concatenate(gather, axis=0).astype(bf16)
    value = jnp.dot(gather, high, preferred_element_type=f32)
    value += jnp.dot(gather, rest, preferred_element_type=f32)
    return [
        value[i * blocks : (i + 1) * blocks].reshape(blocks, 1, LANE)
        for i in range(len(picked))
    ]


def block_index(blocks, count):
    return lax.broadcasted_iota(jnp.int32, (blocks, count), 0)


def begin_kernel(blocks, arrived_ref, weight_ref, hidden_ref, rows_ref, proj_ref, score_ref):
    reorder(arrived_ref[...], rows_ref)
    proj = times_weight(rows_ref, weight_ref)
    proj_ref[...] = proj.astype(bf16)
    score_ref[...] = score_block(
        blocks, proj, hidden_ref[...], [block_index(blocks, proj.shape[0])]
    )[0]


def begin(blocks, arrived, weight, hidden):
    count = blocks * SEND
    part, cols = weight.shape
    return pl.pallas_call(
        functools.partial(begin_kernel, blocks),
        in_specs=[VMEM] * 3,
        out_specs=[VMEM] * 3,
        out_shape=[
            plain((count, cols), bf16),
            plain((count, part), bf16),
            plain((blocks, 1, LANE), f32),
        ],
        compiler_params=params(8 * count * cols + 8 * count * part),
        cost_estimate=cost(4 * count * part * cols, 2 * part * cols),
    )(arrived, weight, hidden)


def finish_kernel(shards, blocks, arrived_ref, hidden_ref, weight_ref, *refs):
    before, score_in = refs[:shards], refs[shards : 2 * shards]
    projs, score_ref = refs[2 * shards : 3 * shards], refs[-1]
    proj = times_weight(arrived_ref, weight_ref)
    rounded = proj.astype(bf16)
    total = proj.shape[0]
    count = total // shards
    picked = [block_index(blocks, total) * shards + s for s in range(shards)]
    scores = score_block(blocks, proj, hidden_ref[...], picked)
    me = lax.axis_index("rep")
    slot = lax.broadcasted_iota(jnp.int32, (count, total), 0)
    row = lax.broadcasted_iota(jnp.int32, (count, total), 1)
    for s in range(shards):
        order = row == slot + SEND * (div_send(slot) * (shards - 1) + s)
        order = jnp.where(order, 1.0, 0.0).astype(bf16)
        own = jnp.dot(order, rounded, preferred_element_type=f32)
        own += before[s][...].astype(f32)
        projs[s][...] = own.astype(bf16)
        at = lax.rem(me + shards - s, shards)
        score_ref[pl.ds(at * blocks, blocks)] = score_in[s][...] + scores[s]


def finish(blocks, arrived, hidden, weight, before, scores):
    shards = len(before)
    total, part = hidden.shape
    count = total // shards
    cols = weight.shape[1]
    outs = pl.pallas_call(
        functools.partial(finish_kernel, shards, blocks),
        in_specs=[VMEM] * (3 + 2 * shards),
        out_specs=[VMEM] * (shards + 1),
        out_shape=[plain((count, part), bf16)] * shards
        + [plain((shards * blocks, 1, LANE), f32)],
        compiler_params=params(20 * total * part),
        cost_estimate=cost(2 * total * part * cols, 2 * part * cols),
    )(arrived, hidden, weight, *before, *scores)
    return list(outs[:-1]), outs[-1]


def new_state(master, one, two, grad):
    corr_one = 1.0 - beta_one**adam_step
    corr_two = 1.0 - beta_two**adam_step
    rate = learn_rate * corr_two**0.5 / corr_one
    keep = 1.0 - learn_rate * decay_rate
    eps = adam_eps * corr_two**0.5
    m_new = beta_one * one.astype(f32) + (1.0 - beta_one) * grad
    v_new = beta_two * two.astype(f32) + (1.0 - beta_two) * (grad * grad)
    root = lax.rsqrt(v_new)
    below = v_new * root + eps
    inverse = root * (2.0 - below * root)
    master = keep * master - (rate * m_new) * inverse
    return master, m_new.astype(bf16), v_new.astype(bf16)


def update_rows(first, count, state, news, grad_ref):
    cols = grad_ref.shape[1]

    @pl.loop(0, count // ROWS)
    def _(i):
        own = pl.ds(pl.multiple_of(first + i * ROWS, ROWS), ROWS)
        for low in range(0, cols, UNIT):
            at = (own, slice(low, low + UNIT))
            values = new_state(*[ref[at] for ref in state], grad_ref[at])
            for ref, value in zip(news, values):
                ref[at] = value


def transpose_rows(hidden, hidden_t):
    base = 0
    for ref in hidden:
        high = base + ref.shape[0]
        hidden_t[:, base:high] = ref[...].astype(f32).T.astype(bf16)
        base = high


def form_grad(hidden_t, rows_refs, grad_ref):
    for i in range(grad_ref.shape[1] // UNIT):
        own = slice(i * UNIT, (i + 1) * UNIT)
        base = 0
        grad = 0.0
        for rows_ref in rows_refs:
            high = base + rows_ref.shape[0]
            grad += jnp.dot(
                hidden_t[:, base:high], rows_ref[:, own], preferred_element_type=f32
            )
            base = high
        grad_ref[:, own] = grad


def state_copies(i, step, low, hbm, vmem, sems, into):
    cols = vmem[0].shape[1]
    rows = pl.ds(pl.multiple_of(i * step, step), step)
    out = []
    for j, (far, near) in enumerate(zip(hbm, vmem)):
        ends = (far.at[0, rows, pl.ds(low, cols)], near.at[rows])
        source, target = ends if into else ends[::-1]
        out.append(pltpu.make_async_copy(source, target, sems.at[j, i]))
    return out


def settle_kernel(fresh, blocks, *refs):
    refs = list(refs)

    def take(number):
        out = refs[:number]
        del refs[:number]
        return out

    size = len(fresh)
    arrived, hidden = take(size), take(1 + size)
    given_ref, weight_ref, *state = take(5)
    scores, projs, (mixed_ref,) = take(size), take(size), take(1)
    outs, news, rows_refs = take(3), take(3), take(size)
    hidden_t, grad_ref, sems = refs
    part = grad_ref.shape[0]
    count = blocks * SEND
    shards = 1 + size
    for i, s in enumerate(fresh):
        reorder(arrived[i][...], rows_refs[i])
        proj = times_weight(rows_refs[i], weight_ref)
        projs[i][...] = proj.astype(bf16)
        scores[i][...] = score_block(
            blocks, proj, hidden[s][...], [block_index(blocks, count)]
        )[0]
    transpose_rows(hidden, hidden_t)
    form_grad(hidden_t, [given_ref] + rows_refs, grad_ref)

    step = part // sems.shape[1]

    @pl.loop(0, part // step)
    def _(i):
        update_rows(i * step, step, state, news, grad_ref)
        for copy in state_copies(i, step, 0, outs, news, sems, False):
            copy.start()

    row = lax.broadcasted_iota(jnp.int32, (shards * count, count), 0)
    col = lax.broadcasted_iota(jnp.int32, (shards * count, count), 1)
    at, step_of, slot = mixed_place(row, shards)
    total = 0.0
    for s in range(shards):
        order = (step_of == s) & (col == at * SEND + slot)
        order = jnp.where(order, 1.0, 0.0).astype(bf16)
        total += jnp.dot(order, hidden[s][...], preferred_element_type=f32)
    mixed_ref[...] = total.astype(bf16)

    @pl.loop(0, part // step)
    def _(i):
        for copy in state_copies(i, step, 0, outs, news, sems, False):
            copy.wait()


def settle(blocks, arrived, given, hidden, weight, held, shapes):
    part, cols = weight.shape
    count = blocks * SEND
    fresh = tuple(range(1, 1 + len(arrived)))
    size = len(fresh)
    total = count * (1 + size)
    step = min(part, 64)
    args = [*arrived, *hidden, given, weight, *held]
    near = [plain((blocks, 1, LANE), f32)] * size + [plain((count, part), bf16)] * size
    near.append(plain((total, part), bf16))
    far = [out_hbm(array.shape, array.dtype) for array in shapes]
    scratch = [pltpu.VMEM((part, cols), kind) for kind in (f32, bf16, bf16)]
    scratch += [pltpu.VMEM((count, cols), bf16)] * size
    scratch += [
        pltpu.VMEM((part, total), bf16),
        pltpu.VMEM((part, cols), f32),
        pltpu.SemaphoreType.DMA((3, part // step)),
    ]
    nbytes = 12 * part * cols + 4 * total * cols + 8 * total * part
    outs = pl.pallas_call(
        functools.partial(settle_kernel, fresh, blocks),
        in_specs=[VMEM] * len(args),
        out_specs=[VMEM] * len(near) + [HBM] * len(far),
        out_shape=near + far,
        scratch_shapes=scratch,
        compiler_params=params(nbytes),
        cost_estimate=cost(4 * total * part * cols, 16 * part * cols, part * cols),
    )(*args)
    outs = list(outs)
    return outs[:size], outs[2 * size], outs[size : 2 * size], outs[-3:]


def update_kernel(low, shards, hidden_ref, rows_ref, *refs):
    grad_refs, refs = refs[:shards], refs[shards:]
    gate_up_hbm, state_hbm, token_hbm, refs = refs[0], refs[1:4], refs[4:7], refs[10:]
    outs, gate_out, place_ref, inverse_ref, refs = refs[:3], *refs[3:6], refs[6:]
    state, tokens, refs = refs[:3], refs[3:6], refs[6:]
    hidden_t, grad_ref, gate_up_ref, gate_new, in_sems, out_sems, sems = refs
    part = grad_ref.shape[0]
    steps = in_sems.shape[1]
    step = part // steps
    gate_load = pltpu.make_async_copy(gate_up_hbm, gate_up_ref, sems.at[0])
    gate_store = pltpu.make_async_copy(gate_new, gate_out, sems.at[1])
    gate_load.start()
    token_loads = [
        pltpu.make_async_copy(source, target, sems.at[2 + i])
        for i, (source, target) in enumerate(zip(token_hbm, tokens))
    ]
    for copy in token_loads:
        copy.start()
    for i in range(steps):
        for copy in state_copies(i, step, low, state_hbm, state, in_sems, True):
            copy.start()
    transpose_rows([hidden_ref], hidden_t)
    form_grad(hidden_t, [rows_ref], grad_ref)
    for copy in token_loads:
        copy.wait()
    ids, slots = tokens[0][...], tokens[1][...]
    live = ((ids & (EXP_LOCAL - 1)) == 0) & (slots >= 0)
    place_ref[...] = jnp.where(live, ids // EXP_LOCAL * SEND + slots, -1)
    inverse_ref[...] = 1.0 / tokens[2][...].astype(f32)
    gate_load.wait()
    for s, ref in enumerate(grad_refs):
        first, second, gate, up, sig = swiglu_part(gate_up_ref, shards, s, ref.shape[1])
        grad = ref[...].astype(f32)
        gate_new[:, pl.ds(first, ref.shape[1])] = (
            grad * up * sig * (1.0 + gate * (1.0 - sig))
        ).astype(bf16)
        gate_new[:, pl.ds(second, ref.shape[1])] = (grad * (gate * sig)).astype(bf16)
    gate_store.start()

    @pl.loop(0, steps)
    def _(i):
        for copy in state_copies(i, step, low, state_hbm, state, in_sems, True):
            copy.wait()
        update_rows(i * step, step, state, state, grad_ref)
        for copy in state_copies(i, step, low, outs, state, out_sems, False):
            copy.start()

    @pl.loop(0, steps)
    def _(i):
        for copy in state_copies(i, step, low, outs, state, out_sems, False):
            copy.wait()

    gate_store.wait()


def update(low, hidden, rows, grads, gate_up, state, tokens, done):
    total, part = hidden.shape
    cols = rows.shape[1]
    step = min(part, 64)
    shards = len(grads)
    scratch = [pltpu.VMEM((part, cols), kind) for kind in (f32, bf16, bf16)]
    scratch += [pltpu.VMEM(token.shape, token.dtype) for token in tokens]
    scratch += [pltpu.VMEM((part, total), bf16), pltpu.VMEM((part, cols), f32)]
    scratch += [pltpu.VMEM(gate_up.shape, bf16)] * 2
    scratch += [pltpu.SemaphoreType.DMA((3, part // step))] * 2
    scratch += [pltpu.SemaphoreType.DMA((5,))]
    return pl.pallas_call(
        functools.partial(update_kernel, low, shards),
        in_specs=[VMEM] * (2 + shards) + [HBM] * 10,
        out_specs=[HBM] * 4 + [VMEM] * 2,
        out_shape=[out_hbm(array.shape, array.dtype) for array in state]
        + [out_hbm(gate_up.shape, bf16)]
        + [plain(tokens[0].shape, kind) for kind in (jnp.int32, f32)],
        scratch_shapes=scratch,
        input_output_aliases={2 + shards + 7 + i: i for i in range(3)},
        compiler_params=params(12 * part * cols + 2 * total * part + 4 * gate_up.size),
        cost_estimate=cost(2 * total * part * cols, 16 * part * cols, part * cols),
    )(hidden, rows, *grads, *in_hbm(gate_up, *state, *tokens, *done))


def close_kernel(shards, place_ref, inverse_ref, score_ref, gate_ref):
    place = place_ref[...]
    blocks = score_ref.shape[0] // shards
    value = jnp.zeros(place.shape, f32)
    for b in range(blocks):
        for slot in range(SEND):
            score = score_ref[b, 0, slot]
            for s in range(1, shards):
                score += score_ref[s * blocks + b, 0, slot]
            value = jnp.where(place == b * SEND + slot, score, value)
    gate_ref[...] = value * inverse_ref[...]


def close(shards, place, inverse, score):
    return pl.pallas_call(
        functools.partial(close_kernel, shards),
        in_specs=[VMEM] * 2 + [pl.BlockSpec(memory_space=pltpu.SMEM)],
        out_specs=VMEM,
        out_shape=plain(place.shape, f32),
        compiler_params=params(0),
        cost_estimate=cost(1 << 20, 1 << 16),
    )(place, inverse, score)


def per_device(out_grad, expert_ids, slots, gate_weights, saved_gate_up, master, moment1, moment2):
    ep_size = lax.axis_size("ep")
    rep_size = lax.axis_size("rep")
    ids_t, slots_t, gates_t = expert_ids.T, slots.T, gate_weights.T
    gate_up = saved_gate_up[0, 0]
    state = (master, moment1, moment2)
    edges = chunk_edges(out_grad.shape[1])
    steps = range(1, rep_size)

    def shift(value, step):
        perm = [(i, (i + step) % rep_size) for i in range(rep_size)]
        return lax.ppermute(value, "rep", perm)

    def exchange(value):
        return lax.all_to_all(value, "ep", split_axis=0, concat_axis=0, tiled=True)

    send_a, send_b = dispatch(ep_size, edges, ids_t, slots_t, gates_t, out_grad)
    mixed = [shift(send_b, s) for s in steps]
    parts = list(hidden_parts(gate_up, rep_size, send_b))
    arrived = exchange(send_a.reshape(ep_size, ROWS, -1)).reshape(send_a.shape)
    parts[1:], mixed = lax.optimization_barrier((parts[1:], mixed))
    hidden = [parts[0]] + [shift(parts[s], s) for s in steps]
    mixed = mix([send_b] + mixed)
    hidden[1:], mixed = lax.optimization_barrier((hidden[1:], mixed))
    arrived_b = exchange(mixed.reshape(ep_size, rep_size * SEND, -1)).reshape(mixed.shape)

    peers = [shift(arrived, s) for s in steps]
    *held, weight_a, weight_b = load_state(edges[1], *state, arrived)
    rows, proj, score_own = begin(ep_size, arrived, weight_a, hidden[0])
    scores, hidden_mixed, before, done = settle(
        ep_size, peers, rows, hidden, weight_a, held, state
    )
    projs, score = finish(
        ep_size, arrived_b, hidden_mixed, weight_b, [proj] + before, [score_own] + scores
    )
    grads = [projs[0]] + [shift(projs[s], rep_size - s) for s in steps]
    score = lax.all_to_all(score, ("rep", "ep"), split_axis=0, concat_axis=0, tiled=True)

    tokens = (ids_t, slots_t, gates_t)
    *done, grad_gate_up, place, inverse = update(
        edges[1], hidden_mixed, arrived_b, grads, gate_up, state, tokens, done
    )
    gate_grad = close(rep_size, place, inverse, score).T
    return (grad_gate_up.reshape(saved_gate_up.shape), gate_grad) + tuple(done)


def solution(mesh):
    in_specs = (
        P(("rep", "ep"), None),
        P(("rep", "ep"), None),
        P(("rep", "ep"), None),
        P(("rep", "ep"), None),
        P("rep", "ep", None, None),
        P("ep", "rep", None),
        P("ep", "rep", None),
        P("ep", "rep", None),
    )
    out_specs = (
        P("rep", "ep", None, None),
        P(("rep", "ep"), None),
        P("ep", "rep", None),
        P("ep", "rep", None),
        P("ep", "rep", None),
    )
    return jax.shard_map(
        per_device, mesh=mesh, in_specs=in_specs, out_specs=out_specs, check_vma=False
    )
```

```python
import functools

import jax
import jax.numpy as jnp
from jax import lax
from jax.experimental import pallas as pl
from jax.experimental.pallas import tpu as pltpu
from jax.sharding import PartitionSpec as P

TOPK = 8
EXP_LOCAL = 8
SEND = 12
LANE = 128
UNIT = 512
ROWS = 16

beta_one = 0.9
beta_two = 0.95
learn_rate = 0.002
decay_rate = 0.1
adam_eps = 1e-08
adam_step = 50

f32 = jnp.float32
bf16 = jnp.bfloat16
HBM = pl.BlockSpec(memory_space=pltpu.HBM)
ANY = pl.BlockSpec(memory_space=pl.ANY)
VMEM = pl.BlockSpec(memory_space=pltpu.VMEM)


def in_hbm(*arrays):
    return [pltpu.with_memory_space_constraint(array, pltpu.HBM) for array in arrays]


def plain(dims, dtype):
    return jax.ShapeDtypeStruct(tuple(dims), dtype)


def out_hbm(dims, dtype):
    return pltpu.HBM(tuple(dims), dtype)


def block(dims, at=None):
    at = at or (0,) * len(dims)
    return pl.BlockSpec(tuple(dims), lambda i: at, pipeline_mode=pl.Buffered(1))


def params(nbytes):
    mib = min(60, max(16, 10 + 5 * int(nbytes) // 2**22))
    return pltpu.CompilerParams(vmem_limit_bytes=mib * 2**20)


def cost(flops, nbytes, transcendentals=0):
    return pl.CostEstimate(
        flops=int(flops), bytes_accessed=int(nbytes), transcendentals=int(transcendentals)
    )


def div_send(index):
    return lax.shift_right_logical(index * 10923, 17)


def pack(cols):
    return cols // 4 * 3


def chunk_edges(width):
    units = width // UNIT
    return (0, (units - max(1, units * 3 // 7)) * UNIT, width)


def tail_order(count, total, j, slots_first):
    a = lax.broadcasted_iota(jnp.int32, (count, total), 0)
    b = lax.broadcasted_iota(jnp.int32, (count, total), 1)
    if slots_first:
        block_of = div_send(a)
        inner = a - SEND * block_of
        hit = b == block_of * ROWS + SEND + inner - 4 * j
    else:
        inner = (a & (ROWS - 1)) - SEND + 4 * j
        hit = (b == a - SEND + 4 * j) & ((a & (ROWS - 1)) >= SEND)
    return jnp.where(hit & (inner >= 4 * j) & (inner < 4 * j + 4), 1.0, 0.0).astype(bf16)


def dispatch_kernel(edges, ids_hbm, slots_hbm, gates_hbm, grad_hbm, *refs):
    outs, (ids_ref, slots_ref, gates_ref, grad_ref, sems) = refs[:2], refs[2:]
    pairs = [(ids_hbm, ids_ref), (slots_hbm, slots_ref), (gates_hbm, gates_ref)]
    for c in (1, 0):
        own = (slice(None), pl.ds(edges[c], edges[c + 1] - edges[c]))
        pairs.append((grad_hbm.at[own], grad_ref.at[own]))
    copies = [
        pltpu.make_async_copy(source, target, sems.at[i])
        for i, (source, target) in enumerate(pairs)
    ]
    for copy in copies:
        copy.start()
    rows = outs[0].shape[0]
    tok = ids_ref.shape[1]
    orders = [tail_order(rows, rows, j, False) for j in range(3)]
    for copy in copies[:3]:
        copy.wait()
    ids = ids_ref[...]
    slots = slots_ref[...]
    gates = gates_ref[...].astype(f32)
    live = ((ids & (EXP_LOCAL - 1)) == 0) & (slots >= 0)
    place = jnp.where(live, ids // EXP_LOCAL * ROWS + slots, -1)
    row = lax.broadcasted_iota(jnp.int32, (rows, tok), 0)
    main = jnp.zeros((rows, tok), f32)
    for k in range(TOPK):
        main = jnp.where(row == place[k : k + 1], gates[k : k + 1], main)
    main = main.astype(bf16)
    tails = [
        jnp.dot(order, main, preferred_element_type=f32).astype(bf16) for order in orders
    ]
    for c in (1, 0):
        copies[4 - c].wait()
        low, high = edges[c], edges[c + 1]
        part = (high - low) // 4
        for j in range(3):
            total = jnp.dot(
                main,
                grad_ref[:, low + j * part : low + (j + 1) * part],
                preferred_element_type=f32,
            )
            total += jnp.dot(
                tails[j], grad_ref[:, low + 3 * part : high], preferred_element_type=f32
            )
            outs[c][:, j * part : (j + 1) * part] = total.astype(bf16)


def dispatch(blocks, edges, ids, slots, gates, out_grad):
    tok, width = out_grad.shape
    rows = blocks * ROWS
    shapes = [(rows, pack(high - low)) for low, high in zip(edges[:-1], edges[1:])]
    return pl.pallas_call(
        functools.partial(dispatch_kernel, edges),
        in_specs=[HBM] * 4,
        out_specs=[VMEM] * 2,
        out_shape=[plain(shape, bf16) for shape in shapes],
        scratch_shapes=[
            pltpu.VMEM(ids.shape, jnp.int32),
            pltpu.VMEM(slots.shape, jnp.int32),
            pltpu.VMEM(gates.shape, bf16),
            pltpu.VMEM(out_grad.shape, bf16),
            pltpu.SemaphoreType.DMA((5,)),
        ],
        compiler_params=params(2 * rows * width + 2 * tok * width),
        cost_estimate=cost(2 * rows * tok * width, 4 * tok * width),
    )(*in_hbm(ids, slots, gates, out_grad))


def swiglu_part(gate_up_ref, shards, step, part):
    at = lax.rem(lax.axis_index("rep") + step, shards)
    low = pl.multiple_of(at * part, part)
    high = pl.multiple_of((shards + at) * part, part)
    gate = gate_up_ref[:, pl.ds(low, part)].astype(f32)
    up = gate_up_ref[:, pl.ds(high, part)].astype(f32)
    return low, high, gate, up, jax.nn.sigmoid(gate)


def hidden_kernel(gate_up_ref, after_ref, *out_refs):
    del after_ref
    for s, out_ref in enumerate(out_refs):
        _, _, gate, up, sig = swiglu_part(gate_up_ref, len(out_refs), s, out_ref.shape[1])
        out_ref[...] = (gate * sig * up).astype(bf16)


def hidden_parts(gate_up, shards, after):
    slots, width = gate_up.shape
    shape = (slots, width // 2 // shards)
    return pl.pallas_call(
        hidden_kernel,
        grid=(1,),
        in_specs=[block(gate_up.shape), ANY],
        out_specs=[block(shape)] * shards,
        out_shape=[plain(shape, bf16)] * shards,
        compiler_params=params(3 * slots * width),
        cost_estimate=cost(8 * slots * width, 3 * slots * width, slots * width),
    )(*in_hbm(gate_up), after)


def load_kernel(middle, after_ref, master_hbm, one_hbm, two_hbm, *refs):
    del after_ref
    master_ref, one_ref, two_ref, weight_a, weight_b, rest_ref, sems = refs
    part = master_ref.shape[0]
    rest = rest_ref.shape[1]
    step = part // 4
    copies = []
    for i in range(4):
        own = pl.ds(i * step, step)
        copies.append(
            pltpu.make_async_copy(
                master_hbm.at[0, own, pl.ds(0, middle)], master_ref.at[own], sems.at[i]
            )
        )
    for i in range(4):
        own = pl.ds(i * step, step)
        copies.append(
            pltpu.make_async_copy(
                master_hbm.at[0, own, pl.ds(middle, rest)], rest_ref.at[own], sems.at[4 + i]
            )
        )
    for i, (source, target) in enumerate([(one_hbm, one_ref), (two_hbm, two_ref)]):
        copies.append(
            pltpu.make_async_copy(source.at[0, :, pl.ds(0, middle)], target, sems.at[8 + i])
        )
    for copy in copies:
        copy.start()
    for i in range(4):
        copies[i].wait()
        own = slice(i * step, (i + 1) * step)
        weight_a[own, :] = master_ref[own, :].astype(bf16)
    for i in range(4):
        copies[4 + i].wait()
        own = slice(i * step, (i + 1) * step)
        weight_b[own, :] = rest_ref[own, :].astype(bf16)
    copies[8].wait()
    copies[9].wait()


def load_state(middle, master, one, two, after):
    _, part, width = master.shape
    return pl.pallas_call(
        functools.partial(load_kernel, middle),
        in_specs=[ANY] + [HBM] * 3,
        out_specs=[VMEM] * 5,
        out_shape=[
            pltpu.VMEM((part, middle), f32),
            pltpu.VMEM((part, middle), bf16),
            pltpu.VMEM((part, middle), bf16),
            pltpu.VMEM((part, middle), bf16),
            pltpu.VMEM((part, width - middle), bf16),
        ],
        scratch_shapes=[
            pltpu.VMEM((part, width - middle), f32),
            pltpu.SemaphoreType.DMA((10,)),
        ],
        compiler_params=params(4 * part * (width - middle)),
        cost_estimate=cost(part * width, 14 * part * width),
    )(after, *in_hbm(master, one, two))


def mixed_place(index, shards):
    group = div_send(index)
    bits = shards.bit_length() - 1
    step = group & (shards - 1)
    return lax.shift_right_logical(group, bits), step, index - SEND * group


def mix_kernel(shards, *refs):
    parts, (out_hbm_ref, out_ref, sems) = refs[:shards], refs[shards:]
    part = parts[0].shape[1] // 3
    copies = []
    blocks = parts[0].shape[0] // ROWS
    some = min(blocks, 32 // shards)
    rows, packed = some * shards * SEND, some * shards * ROWS
    row = lax.broadcasted_iota(jnp.int32, (rows, packed), 0)
    col = lax.broadcasted_iota(jnp.int32, (rows, packed), 1)
    at, step, slot = mixed_place(row, shards)
    base = (step * some + at) * ROWS
    orders = [jnp.where(col == base + slot, 1.0, 0.0).astype(bf16)]
    for j in range(3):
        hit = (col == base + SEND + slot - 4 * j) & (slot >= 4 * j) & (slot < 4 * j + 4)
        orders.append(jnp.where(hit, 1.0, 0.0).astype(bf16))
    for first in range(0, blocks, some):
        stack = jnp.concatenate(
            [ref[first * ROWS : (first + some) * ROWS, :] for ref in parts], axis=0
        )
        own = slice(first * shards * SEND, (first + some) * shards * SEND)
        place = pl.ds(first * shards * SEND, some * shards * SEND)
        index = first // some

        def send(j):
            at = (place, pl.ds(j * part, part))
            copy = pltpu.make_async_copy(out_ref.at[at], out_hbm_ref.at[at], sems.at[j, index])
            copy.start()
            copies.append(copy)

        for j in range(3):
            out_ref[own, j * part : (j + 1) * part] = jnp.dot(
                orders[0], stack[:, j * part : (j + 1) * part], preferred_element_type=f32
            ).astype(bf16)
            send(j)
        tail = jnp.zeros((rows, part), f32)
        for j in range(3):
            tail += jnp.dot(
                orders[1 + j],
                stack[:, j * part : (j + 1) * part],
                preferred_element_type=f32,
            )
        out_ref[own, 3 * part :] = tail.astype(bf16)
        send(3)
    for copy in copies:
        copy.wait()


def mix(parts):
    shards = len(parts)
    rows, packed = parts[0].shape
    shape = (rows // ROWS * SEND * shards, packed // 3 * 4)
    return pl.pallas_call(
        functools.partial(mix_kernel, shards),
        in_specs=[VMEM] * shards,
        out_specs=HBM,
        out_shape=out_hbm(shape, bf16),
        scratch_shapes=[
            pltpu.VMEM(shape, bf16),
            pltpu.SemaphoreType.DMA((4, rows // ROWS // min(rows // ROWS, 32 // shards))),
        ],
        compiler_params=params(12 * rows * packed * shards),
        cost_estimate=cost(0, 5 * rows * packed * shards),
    )(*parts)


def reorder(arrived, rows_ref):
    count, width = rows_ref.shape
    part = width // 4
    total = arrived.shape[0]
    slot = lax.broadcasted_iota(jnp.int32, (count, total), 0)
    col = lax.broadcasted_iota(jnp.int32, (count, total), 1)
    order = jnp.where(col == slot + (ROWS - SEND) * div_send(slot), 1.0, 0.0).astype(bf16)
    rows_ref[:, : 3 * part] = jnp.dot(order, arrived, preferred_element_type=f32).astype(bf16)
    tail = jnp.zeros((count, part), f32)
    for j in range(3):
        tail += jnp.dot(
            tail_order(count, total, j, True),
            arrived[:, j * part : (j + 1) * part],
            preferred_element_type=f32,
        )
    rows_ref[:, 3 * part :] = tail.astype(bf16)


def times_weight(rows_ref, weight_ref):
    return lax.dot_general(
        rows_ref[...], weight_ref[...], (((1,), (1,)), ((), ())), preferred_element_type=f32
    )


def score_block(blocks, proj, hidden, picked):
    count = proj.shape[0]
    score = jnp.sum(proj * hidden.astype(f32), axis=1, keepdims=True)
    row = lax.broadcasted_iota(jnp.int32, (count, LANE), 0)
    lane = lax.broadcasted_iota(jnp.int32, (count, LANE), 1)
    spread = jnp.where(row - SEND * div_send(row) == lane, score, 0.0)
    high = spread.astype(bf16)
    rest = (spread - high.astype(f32)).astype(bf16)
    at = lax.broadcasted_iota(jnp.int32, (blocks, count), 1)
    gather = [jnp.where(div_send(at) == pick, 1.0, 0.0) for pick in picked]
    gather = jnp.concatenate(gather, axis=0).astype(bf16)
    value = jnp.dot(gather, high, preferred_element_type=f32)
    value += jnp.dot(gather, rest, preferred_element_type=f32)
    return [
        value[i * blocks : (i + 1) * blocks].reshape(blocks, 1, LANE)
        for i in range(len(picked))
    ]


def block_index(blocks, count):
    return lax.broadcasted_iota(jnp.int32, (blocks, count), 0)


def begin_kernel(blocks, arrived_ref, weight_ref, *refs):
    hidden, (rows_ref, hidden_t, mixed_ref, score_ref) = refs[:-7], refs[-7:-3]
    proj_hbm, proj_ref, sem = refs[-3:]
    reorder(arrived_ref[...], rows_ref)
    proj = times_weight(rows_ref, weight_ref)
    proj_ref[...] = proj
    copy = pltpu.make_async_copy(proj_ref, proj_hbm, sem.at[0])
    copy.start()
    count = proj.shape[0]
    score_ref[...] = score_block(
        blocks, proj, hidden[0][...], [block_index(blocks, count)]
    )[0]
    transpose_rows(hidden, hidden_t)
    shards = len(hidden)
    row = lax.broadcasted_iota(jnp.int32, (shards * count, count), 0)
    col = lax.broadcasted_iota(jnp.int32, (shards * count, count), 1)
    at, step_of, slot = mixed_place(row, shards)
    total = 0.0
    for s in range(shards):
        order = (step_of == s) & (col == at * SEND + slot)
        order = jnp.where(order, 1.0, 0.0).astype(bf16)
        total += jnp.dot(order, hidden[s][...], preferred_element_type=f32)
    mixed_ref[...] = total.astype(bf16)
    copy.wait()


def begin(blocks, arrived, weight, hidden):
    count = blocks * SEND
    part, cols = weight.shape
    total = count * len(hidden)
    return pl.pallas_call(
        functools.partial(begin_kernel, blocks),
        in_specs=[VMEM] * (2 + len(hidden)),
        out_specs=[VMEM] * 4 + [HBM],
        out_shape=[
            plain((count, cols), bf16),
            plain((part, total), bf16),
            plain((total, part), bf16),
            plain((blocks, 1, LANE), f32),
            out_hbm((count, part), f32),
        ],
        scratch_shapes=[pltpu.VMEM((count, part), f32), pltpu.SemaphoreType.DMA((1,))],
        compiler_params=params(8 * count * cols + 16 * total * part),
        cost_estimate=cost(4 * count * part * cols, 2 * part * cols),
    )(arrived, weight, *hidden)


def finish_kernel(shards, blocks, arrived_ref, hidden_ref, weight_ref, *refs):
    before_hbm, score_in = refs[:shards], refs[shards : 2 * shards]
    projs, (score_ref, before, sems) = refs[2 * shards : 3 * shards], refs[3 * shards :]
    copies = [
        pltpu.make_async_copy(ref, before.at[s], sems.at[s])
        for s, ref in enumerate(before_hbm)
    ]
    for copy in copies:
        copy.start()
    proj = times_weight(arrived_ref, weight_ref)
    rounded = proj.astype(bf16)
    total = proj.shape[0]
    count = total // shards
    picked = [block_index(blocks, total) * shards + s for s in range(shards)]
    scores = score_block(blocks, proj, hidden_ref[...], picked)
    me = lax.axis_index("rep")
    slot = lax.broadcasted_iota(jnp.int32, (count, total), 0)
    row = lax.broadcasted_iota(jnp.int32, (count, total), 1)
    for s in range(shards):
        order = row == slot + SEND * (div_send(slot) * (shards - 1) + s)
        order = jnp.where(order, 1.0, 0.0).astype(bf16)
        own = jnp.dot(order, rounded, preferred_element_type=f32)
        copies[s].wait()
        own += before[s]
        projs[s][...] = own.astype(bf16)
        at = lax.rem(me + shards - s, shards)
        score_ref[pl.ds(at * blocks, blocks)] = score_in[s][...] + scores[s]


def finish(blocks, arrived, hidden, weight, before, scores):
    shards = len(before)
    total, part = hidden.shape
    count = total // shards
    cols = weight.shape[1]
    outs = pl.pallas_call(
        functools.partial(finish_kernel, shards, blocks),
        in_specs=[VMEM] * 3 + [HBM] * shards + [VMEM] * shards,
        out_specs=[VMEM] * (shards + 1),
        out_shape=[plain((count, part), bf16)] * shards
        + [plain((shards * blocks, 1, LANE), f32)],
        scratch_shapes=[
            pltpu.VMEM((shards, count, part), f32),
            pltpu.SemaphoreType.DMA((shards,)),
        ],
        compiler_params=params(20 * total * part),
        cost_estimate=cost(2 * total * part * cols, 2 * part * cols),
    )(arrived, hidden, weight, *in_hbm(*before), *scores)
    return list(outs[:-1]), outs[-1]


def new_state(master, one, two, grad):
    corr_one = 1.0 - beta_one**adam_step
    corr_two = 1.0 - beta_two**adam_step
    rate = learn_rate * corr_two**0.5 / corr_one
    keep = 1.0 - learn_rate * decay_rate
    eps = adam_eps * corr_two**0.5
    m_new = beta_one * one.astype(f32) + (1.0 - beta_one) * grad
    v_new = beta_two * two.astype(f32) + (1.0 - beta_two) * (grad * grad)
    root = lax.rsqrt(v_new)
    below = v_new * root + eps
    inverse = root * (2.0 - below * root)
    master = keep * master - (rate * m_new) * inverse
    return master, m_new.astype(bf16), v_new.astype(bf16)


def update_rows(first, count, state, news, grad_ref):
    cols = grad_ref.shape[1]

    @pl.loop(0, count // ROWS)
    def _(i):
        own = pl.ds(pl.multiple_of(first + i * ROWS, ROWS), ROWS)
        for low in range(0, cols, UNIT):
            at = (own, slice(low, low + UNIT))
            values = new_state(*[ref[at] for ref in state], grad_ref[at])
            for ref, value in zip(news, values):
                ref[at] = value


def transpose_rows(hidden, hidden_t):
    base = 0
    for ref in hidden:
        high = base + ref.shape[0]
        hidden_t[:, base:high] = ref[...].astype(f32).T.astype(bf16)
        base = high


def form_grad(first, count, hidden_t, rows_refs, grad_ref):
    own = slice(first, first + count)
    for low in range(0, grad_ref.shape[1], UNIT):
        base = 0
        grad = 0.0
        for rows_ref in rows_refs:
            high = base + rows_ref.shape[0]
            grad += jnp.dot(
                hidden_t[own, base:high],
                rows_ref[:, low : low + UNIT],
                preferred_element_type=f32,
            )
            base = high
        grad_ref[own, low : low + UNIT] = grad


def state_copies(i, step, low, hbm, vmem, sems, into):
    cols = vmem[0].shape[1]
    rows = pl.ds(pl.multiple_of(i * step, step), step)
    out = []
    for j, (far, near) in enumerate(zip(hbm, vmem)):
        ends = (far.at[0, rows, pl.ds(low, cols)], near.at[rows])
        source, target = ends if into else ends[::-1]
        out.append(pltpu.make_async_copy(source, target, sems.at[j, i]))
    return out


def settle_kernel(fresh, blocks, *refs):
    refs = list(refs)

    def take(number):
        out = refs[:number]
        del refs[:number]
        return out

    size = len(fresh)
    arrived, hidden = take(size), take(size)
    hidden_t, given_ref, weight_ref, *state = take(6)
    scores, projs_hbm, outs = take(size), take(size), take(3)
    news, rows_refs, projs = take(3), take(size), take(size)
    grad_ref, sems, proj_sems = refs
    part = grad_ref.shape[0]
    count = blocks * SEND
    for i in range(size):
        reorder(arrived[i][...], rows_refs[i])
    steps = sems.shape[1]
    step = part // steps
    copies = []
    for i in range(steps):
        form_grad(i * step, step, hidden_t, [given_ref] + rows_refs, grad_ref)
        update_rows(i * step, step, state, news, grad_ref)
        for copy in state_copies(i, step, 0, outs, news, sems, False):
            copy.start()
            copies.append(copy)
    for i in range(size):
        proj = times_weight(rows_refs[i], weight_ref)
        projs[i][...] = proj
        copies.append(pltpu.make_async_copy(projs[i], projs_hbm[i], proj_sems.at[i]))
        copies[-1].start()
        scores[i][...] = score_block(
            blocks, proj, hidden[i][...], [block_index(blocks, count)]
        )[0]
    for copy in copies:
        copy.wait()


def settle(blocks, arrived, given, hidden, hidden_t, weight, held, shapes):
    part, cols = weight.shape
    count = blocks * SEND
    fresh = tuple(range(1, 1 + len(arrived)))
    size = len(fresh)
    total = count * (1 + size)
    step = min(part, 128)
    args = [*arrived, *hidden, hidden_t, given, weight, *held]
    near = [plain((blocks, 1, LANE), f32)] * size
    far = [out_hbm((count, part), f32)] * size
    far += [out_hbm(array.shape, array.dtype) for array in shapes]
    scratch = [pltpu.VMEM((part, cols), kind) for kind in (f32, bf16, bf16)]
    scratch += [pltpu.VMEM((count, cols), bf16)] * size
    scratch += [pltpu.VMEM((count, part), f32)] * size
    scratch += [
        pltpu.VMEM((part, cols), f32),
        pltpu.SemaphoreType.DMA((3, part // step)),
        pltpu.SemaphoreType.DMA((max(1, size),)),
    ]
    nbytes = 12 * part * cols + 4 * total * cols + 8 * total * part
    outs = pl.pallas_call(
        functools.partial(settle_kernel, fresh, blocks),
        in_specs=[VMEM] * len(args),
        out_specs=[VMEM] * len(near) + [HBM] * len(far),
        out_shape=near + far,
        scratch_shapes=scratch,
        compiler_params=params(nbytes),
        cost_estimate=cost(4 * total * part * cols, 16 * part * cols, part * cols),
    )(*args)
    outs = list(outs)
    return outs[:size], outs[size : 2 * size], outs[-3:]


def update_kernel(low, shards, hidden_ref, rows_ref, *refs):
    grad_refs, refs = refs[:shards], refs[shards:]
    gate_up_hbm, state_hbm, token_hbm, refs = refs[0], refs[1:4], refs[4:7], refs[10:]
    outs, gate_out, place_ref, inverse_ref, refs = refs[:3], *refs[3:6], refs[6:]
    state, tokens, refs = refs[:3], refs[3:6], refs[6:]
    hidden_t, grad_ref, gate_up_ref, gate_new, in_sems, out_sems, sems = refs
    part = grad_ref.shape[0]
    steps = in_sems.shape[1]
    step = part // steps
    gate_load = pltpu.make_async_copy(gate_up_hbm, gate_up_ref, sems.at[0])
    gate_store = pltpu.make_async_copy(gate_new, gate_out, sems.at[1])
    gate_load.start()
    token_loads = [
        pltpu.make_async_copy(source, target, sems.at[2 + i])
        for i, (source, target) in enumerate(zip(token_hbm, tokens))
    ]
    for copy in token_loads:
        copy.start()
    for i in range(steps):
        for copy in state_copies(i, step, low, state_hbm, state, in_sems, True):
            copy.start()
    transpose_rows([hidden_ref], hidden_t)
    stores = []
    for i in range(steps):
        if i == min(1, steps - 1):
            for copy in token_loads:
                copy.wait()
            ids, slots = tokens[0][...], tokens[1][...]
            live = ((ids & (EXP_LOCAL - 1)) == 0) & (slots >= 0)
            place_ref[...] = jnp.where(live, ids // EXP_LOCAL * SEND + slots, -1)
            inverse_ref[...] = 1.0 / tokens[2][...].astype(f32)
            gate_load.wait()
            for s, ref in enumerate(grad_refs):
                width = ref.shape[1]
                first, second, gate, up, sig = swiglu_part(gate_up_ref, shards, s, width)
                grad = ref[...].astype(f32)
                gate_new[:, pl.ds(first, width)] = (
                    grad * up * sig * (1.0 + gate * (1.0 - sig))
                ).astype(bf16)
                gate_new[:, pl.ds(second, width)] = (grad * (gate * sig)).astype(bf16)
            gate_store.start()
            stores.append(gate_store)
        form_grad(i * step, step, hidden_t, [rows_ref], grad_ref)
        for copy in state_copies(i, step, low, state_hbm, state, in_sems, True):
            copy.wait()
        update_rows(i * step, step, state, state, grad_ref)
        for copy in state_copies(i, step, low, outs, state, out_sems, False):
            copy.start()
            stores.append(copy)
    for copy in stores:
        copy.wait()


def update(low, hidden, rows, grads, gate_up, state, tokens, done):
    total, part = hidden.shape
    cols = rows.shape[1]
    step = min(part, 128)
    shards = len(grads)
    scratch = [pltpu.VMEM((part, cols), kind) for kind in (f32, bf16, bf16)]
    scratch += [pltpu.VMEM(token.shape, token.dtype) for token in tokens]
    scratch += [pltpu.VMEM((part, total), bf16), pltpu.VMEM((part, cols), f32)]
    scratch += [pltpu.VMEM(gate_up.shape, bf16)] * 2
    scratch += [pltpu.SemaphoreType.DMA((3, part // step))] * 2
    scratch += [pltpu.SemaphoreType.DMA((5,))]
    return pl.pallas_call(
        functools.partial(update_kernel, low, shards),
        in_specs=[VMEM] * (2 + shards) + [HBM] * 10,
        out_specs=[HBM] * 4 + [VMEM] * 2,
        out_shape=[out_hbm(array.shape, array.dtype) for array in state]
        + [out_hbm(gate_up.shape, bf16)]
        + [plain(tokens[0].shape, kind) for kind in (jnp.int32, f32)],
        scratch_shapes=scratch,
        input_output_aliases={2 + shards + 7 + i: i for i in range(3)},
        compiler_params=params(12 * part * cols + 2 * total * part + 4 * gate_up.size),
        cost_estimate=cost(2 * total * part * cols, 16 * part * cols, part * cols),
    )(hidden, rows, *grads, *in_hbm(gate_up, *state, *tokens, *done))


def close_kernel(shards, place_ref, inverse_ref, score_ref, gate_ref):
    place = place_ref[...]
    blocks = score_ref.shape[0] // shards
    value = jnp.zeros(place.shape, f32)
    for b in range(blocks):
        for slot in range(SEND):
            score = score_ref[b, 0, slot]
            for s in range(1, shards):
                score += score_ref[s * blocks + b, 0, slot]
            value = jnp.where(place == b * SEND + slot, score, value)
    gate_ref[...] = value * inverse_ref[...]


def close(shards, place, inverse, score):
    return pl.pallas_call(
        functools.partial(close_kernel, shards),
        in_specs=[VMEM] * 2 + [pl.BlockSpec(memory_space=pltpu.SMEM)],
        out_specs=VMEM,
        out_shape=plain(place.shape, f32),
        compiler_params=params(0),
        cost_estimate=cost(1 << 20, 1 << 16),
    )(place, inverse, score)


def per_device(out_grad, expert_ids, slots, gate_weights, saved_gate_up, master, moment1, moment2):
    ep_size = lax.axis_size("ep")
    rep_size = lax.axis_size("rep")
    ids_t, slots_t, gates_t = expert_ids.T, slots.T, gate_weights.T
    gate_up = saved_gate_up[0, 0]
    state = (master, moment1, moment2)
    edges = chunk_edges(out_grad.shape[1])
    steps = range(1, rep_size)

    def shift(value, step):
        perm = [(i, (i + step) % rep_size) for i in range(rep_size)]
        return lax.ppermute(value, "rep", perm)

    def exchange(value):
        return lax.all_to_all(value, "ep", split_axis=0, concat_axis=0, tiled=True)

    send_a, send_b = dispatch(ep_size, edges, ids_t, slots_t, gates_t, out_grad)
    mixed = [shift(send_b, s) for s in steps]
    parts = list(hidden_parts(gate_up, rep_size, send_b))
    arrived = exchange(send_a.reshape(ep_size, ROWS, -1)).reshape(send_a.shape)
    parts[1:], mixed = lax.optimization_barrier((parts[1:], mixed))
    hidden = [parts[0]] + [shift(parts[s], s) for s in steps]
    mixed = mix([send_b] + mixed)
    hidden[1:], mixed = lax.optimization_barrier((hidden[1:], mixed))
    arrived_b = exchange(mixed.reshape(ep_size, rep_size * SEND, -1)).reshape(mixed.shape)

    peers = [shift(arrived, s) for s in steps]
    *held, weight_a, weight_b = load_state(edges[1], *state, arrived)
    rows, hidden_t, hidden_mixed, score_own, proj = begin(ep_size, arrived, weight_a, hidden)
    scores, before, done = settle(
        ep_size, peers, rows, hidden[1:], hidden_t, weight_a, held, state
    )
    projs, score = finish(
        ep_size, arrived_b, hidden_mixed, weight_b, [proj] + before, [score_own] + scores
    )
    grads = [projs[0]] + [shift(projs[s], rep_size - s) for s in steps]
    score = lax.all_to_all(score, ("rep", "ep"), split_axis=0, concat_axis=0, tiled=True)

    tokens = (ids_t, slots_t, gates_t)
    *done, grad_gate_up, place, inverse = update(
        edges[1], hidden_mixed, arrived_b, grads, gate_up, state, tokens, done
    )
    gate_grad = close(rep_size, place, inverse, score).T
    return (grad_gate_up.reshape(saved_gate_up.shape), gate_grad) + tuple(done)


def solution(mesh):
    in_specs = (
        P(("rep", "ep"), None),
        P(("rep", "ep"), None),
        P(("rep", "ep"), None),
        P(("rep", "ep"), None),
        P("rep", "ep", None, None),
        P("ep", "rep", None),
        P("ep", "rep", None),
        P("ep", "rep", None),
    )
    out_specs = (
        P("rep", "ep", None, None),
        P(("rep", "ep"), None),
        P("ep", "rep", None),
        P("ep", "rep", None),
        P("ep", "rep", None),
    )
    return jax.shard_map(
        per_device, mesh=mesh, in_specs=in_specs, out_specs=out_specs, check_vma=False
    )
```

```python
import functools

import jax
import jax.numpy as jnp
from jax import lax
from jax.experimental import pallas as pl
from jax.experimental.pallas import tpu as pltpu
from jax.sharding import PartitionSpec as P

TOPK = 8
EXP_LOCAL = 8
SEND = 12
LANE = 128
UNIT = 512
ROWS = 16

beta_one = 0.9
beta_two = 0.95
learn_rate = 0.002
decay_rate = 0.1
adam_eps = 1e-08
adam_step = 50

f32 = jnp.float32
bf16 = jnp.bfloat16
HBM = pl.BlockSpec(memory_space=pltpu.HBM)
ANY = pl.BlockSpec(memory_space=pl.ANY)
VMEM = pl.BlockSpec(memory_space=pltpu.VMEM)


def in_hbm(*arrays):
    return [pltpu.with_memory_space_constraint(array, pltpu.HBM) for array in arrays]


def plain(dims, dtype):
    return jax.ShapeDtypeStruct(tuple(dims), dtype)


def out_hbm(dims, dtype):
    return pltpu.HBM(tuple(dims), dtype)


def block(dims, at=None):
    at = at or (0,) * len(dims)
    return pl.BlockSpec(tuple(dims), lambda i: at, pipeline_mode=pl.Buffered(1))


def params(nbytes):
    mib = min(60, max(16, 10 + 5 * int(nbytes) // 2**22))
    return pltpu.CompilerParams(vmem_limit_bytes=mib * 2**20)


def cost(flops, nbytes, transcendentals=0):
    return pl.CostEstimate(
        flops=int(flops), bytes_accessed=int(nbytes), transcendentals=int(transcendentals)
    )


def div_send(index):
    return lax.shift_right_logical(index * 10923, 17)


def pack(cols):
    return cols // 4 * 3


def chunk_edges(width):
    units = width // UNIT
    return (0, (units - max(1, units * 3 // 7)) * UNIT, width)


def tail_order(count, total, j, slots_first):
    a = lax.broadcasted_iota(jnp.int32, (count, total), 0)
    b = lax.broadcasted_iota(jnp.int32, (count, total), 1)
    if slots_first:
        block_of = div_send(a)
        inner = a - SEND * block_of
        hit = b == block_of * ROWS + SEND + inner - 4 * j
    else:
        inner = (a & (ROWS - 1)) - SEND + 4 * j
        hit = (b == a - SEND + 4 * j) & ((a & (ROWS - 1)) >= SEND)
    return jnp.where(hit & (inner >= 4 * j) & (inner < 4 * j + 4), 1.0, 0.0).astype(bf16)


def dispatch_kernel(edges, ids_hbm, slots_hbm, gates_hbm, grad_hbm, *refs):
    outs, (ids_ref, slots_ref, gates_ref, grad_ref, sems) = refs[:2], refs[2:]
    pairs = [(ids_hbm, ids_ref), (slots_hbm, slots_ref), (gates_hbm, gates_ref)]
    for c in (1, 0):
        own = (slice(None), pl.ds(edges[c], edges[c + 1] - edges[c]))
        pairs.append((grad_hbm.at[own], grad_ref.at[own]))
    copies = [
        pltpu.make_async_copy(source, target, sems.at[i])
        for i, (source, target) in enumerate(pairs)
    ]
    for copy in copies:
        copy.start()
    rows = outs[0].shape[0]
    tok = ids_ref.shape[1]
    orders = [tail_order(rows, rows, j, False) for j in range(3)]
    for copy in copies[:3]:
        copy.wait()
    ids = ids_ref[...]
    slots = slots_ref[...]
    gates = gates_ref[...].astype(f32)
    live = ((ids & (EXP_LOCAL - 1)) == 0) & (slots >= 0)
    place = jnp.where(live, ids // EXP_LOCAL * ROWS + slots, -1)
    row = lax.broadcasted_iota(jnp.int32, (rows, tok), 0)
    main = jnp.zeros((rows, tok), f32)
    for k in range(TOPK):
        main = jnp.where(row == place[k : k + 1], gates[k : k + 1], main)
    main = main.astype(bf16)
    tails = [
        jnp.dot(order, main, preferred_element_type=f32).astype(bf16) for order in orders
    ]
    for c in (1, 0):
        copies[4 - c].wait()
        low, high = edges[c], edges[c + 1]
        part = (high - low) // 4
        for j in range(3):
            total = jnp.dot(
                main,
                grad_ref[:, low + j * part : low + (j + 1) * part],
                preferred_element_type=f32,
            )
            total += jnp.dot(
                tails[j], grad_ref[:, low + 3 * part : high], preferred_element_type=f32
            )
            outs[c][:, j * part : (j + 1) * part] = total.astype(bf16)


def dispatch(blocks, edges, ids, slots, gates, out_grad):
    tok, width = out_grad.shape
    rows = blocks * ROWS
    shapes = [(rows, pack(high - low)) for low, high in zip(edges[:-1], edges[1:])]
    return pl.pallas_call(
        functools.partial(dispatch_kernel, edges),
        in_specs=[HBM] * 4,
        out_specs=[VMEM] * 2,
        out_shape=[plain(shape, bf16) for shape in shapes],
        scratch_shapes=[
            pltpu.VMEM(ids.shape, jnp.int32),
            pltpu.VMEM(slots.shape, jnp.int32),
            pltpu.VMEM(gates.shape, bf16),
            pltpu.VMEM(out_grad.shape, bf16),
            pltpu.SemaphoreType.DMA((5,)),
        ],
        compiler_params=params(2 * rows * width + 2 * tok * width),
        cost_estimate=cost(2 * rows * tok * width, 4 * tok * width),
    )(*in_hbm(ids, slots, gates, out_grad))


def swiglu_part(gate_up_ref, shards, step, part):
    at = lax.rem(lax.axis_index("rep") + step, shards)
    low = pl.multiple_of(at * part, part)
    high = pl.multiple_of((shards + at) * part, part)
    gate = gate_up_ref[:, pl.ds(low, part)].astype(f32)
    up = gate_up_ref[:, pl.ds(high, part)].astype(f32)
    return low, high, gate, up, jax.nn.sigmoid(gate)


def hidden_kernel(gate_up_ref, after_ref, *out_refs):
    del after_ref
    for s, out_ref in enumerate(out_refs):
        _, _, gate, up, sig = swiglu_part(gate_up_ref, len(out_refs), s, out_ref.shape[1])
        out_ref[...] = (gate * sig * up).astype(bf16)


def hidden_parts(gate_up, shards, after):
    slots, width = gate_up.shape
    shape = (slots, width // 2 // shards)
    return pl.pallas_call(
        hidden_kernel,
        grid=(1,),
        in_specs=[block(gate_up.shape), ANY],
        out_specs=[block(shape)] * shards,
        out_shape=[plain(shape, bf16)] * shards,
        compiler_params=params(3 * slots * width),
        cost_estimate=cost(8 * slots * width, 3 * slots * width, slots * width),
    )(*in_hbm(gate_up), after)


def load_kernel(middle, after_ref, master_hbm, one_hbm, two_hbm, *refs):
    del after_ref
    master_ref, one_ref, two_ref, weight_a, weight_b, rest_ref, sems = refs
    part = master_ref.shape[0]
    rest = rest_ref.shape[1]
    step = part // 4
    copies = []
    for i in range(4):
        own = pl.ds(i * step, step)
        copies.append(
            pltpu.make_async_copy(
                master_hbm.at[0, own, pl.ds(0, middle)], master_ref.at[own], sems.at[i]
            )
        )
    for i in range(4):
        own = pl.ds(i * step, step)
        copies.append(
            pltpu.make_async_copy(
                master_hbm.at[0, own, pl.ds(middle, rest)], rest_ref.at[own], sems.at[4 + i]
            )
        )
    for i, (source, target) in enumerate([(one_hbm, one_ref), (two_hbm, two_ref)]):
        copies.append(
            pltpu.make_async_copy(source.at[0, :, pl.ds(0, middle)], target, sems.at[8 + i])
        )
    for copy in copies:
        copy.start()
    for i in range(4):
        copies[i].wait()
        own = slice(i * step, (i + 1) * step)
        weight_a[own, :] = master_ref[own, :].astype(bf16)
    for i in range(4):
        copies[4 + i].wait()
        own = slice(i * step, (i + 1) * step)
        weight_b[own, :] = rest_ref[own, :].astype(bf16)
    copies[8].wait()
    copies[9].wait()


def load_state(middle, master, one, two, after):
    _, part, width = master.shape
    return pl.pallas_call(
        functools.partial(load_kernel, middle),
        in_specs=[ANY] + [HBM] * 3,
        out_specs=[VMEM] * 5,
        out_shape=[
            pltpu.VMEM((part, middle), f32),
            pltpu.VMEM((part, middle), bf16),
            pltpu.VMEM((part, middle), bf16),
            pltpu.VMEM((part, middle), bf16),
            pltpu.VMEM((part, width - middle), bf16),
        ],
        scratch_shapes=[
            pltpu.VMEM((part, width - middle), f32),
            pltpu.SemaphoreType.DMA((10,)),
        ],
        compiler_params=params(4 * part * (width - middle)),
        cost_estimate=cost(part * width, 14 * part * width),
    )(after, *in_hbm(master, one, two))


def mixed_place(index, shards):
    group = div_send(index)
    bits = shards.bit_length() - 1
    step = group & (shards - 1)
    return lax.shift_right_logical(group, bits), step, index - SEND * group


def mix_kernel(shards, *refs):
    parts, (out_hbm_ref, out_ref, sems) = refs[:shards], refs[shards:]
    part = parts[0].shape[1] // 3
    copies = []
    blocks = parts[0].shape[0] // ROWS
    some = min(blocks, 32 // shards)
    rows, packed = some * shards * SEND, some * shards * ROWS
    row = lax.broadcasted_iota(jnp.int32, (rows, packed), 0)
    col = lax.broadcasted_iota(jnp.int32, (rows, packed), 1)
    at, step, slot = mixed_place(row, shards)
    base = (step * some + at) * ROWS
    orders = [jnp.where(col == base + slot, 1.0, 0.0).astype(bf16)]
    for j in range(3):
        hit = (col == base + SEND + slot - 4 * j) & (slot >= 4 * j) & (slot < 4 * j + 4)
        orders.append(jnp.where(hit, 1.0, 0.0).astype(bf16))
    for first in range(0, blocks, some):
        stack = jnp.concatenate(
            [ref[first * ROWS : (first + some) * ROWS, :] for ref in parts], axis=0
        )
        own = slice(first * shards * SEND, (first + some) * shards * SEND)
        place = pl.ds(first * shards * SEND, some * shards * SEND)
        index = first // some

        def send(j):
            at = (place, pl.ds(j * part, part))
            copy = pltpu.make_async_copy(out_ref.at[at], out_hbm_ref.at[at], sems.at[j, index])
            copy.start()
            copies.append(copy)

        for j in range(3):
            out_ref[own, j * part : (j + 1) * part] = jnp.dot(
                orders[0], stack[:, j * part : (j + 1) * part], preferred_element_type=f32
            ).astype(bf16)
            send(j)
        tail = jnp.zeros((rows, part), f32)
        for j in range(3):
            tail += jnp.dot(
                orders[1 + j],
                stack[:, j * part : (j + 1) * part],
                preferred_element_type=f32,
            )
        out_ref[own, 3 * part :] = tail.astype(bf16)
        send(3)
    for copy in copies:
        copy.wait()


def mix(parts):
    shards = len(parts)
    rows, packed = parts[0].shape
    shape = (rows // ROWS * SEND * shards, packed // 3 * 4)
    return pl.pallas_call(
        functools.partial(mix_kernel, shards),
        in_specs=[VMEM] * shards,
        out_specs=HBM,
        out_shape=out_hbm(shape, bf16),
        scratch_shapes=[
            pltpu.VMEM(shape, bf16),
            pltpu.SemaphoreType.DMA((4, rows // ROWS // min(rows // ROWS, 32 // shards))),
        ],
        compiler_params=params(12 * rows * packed * shards),
        cost_estimate=cost(0, 5 * rows * packed * shards),
    )(*parts)


def reorder(arrived, rows_ref):
    count, width = rows_ref.shape
    part = width // 4
    total = arrived.shape[0]
    slot = lax.broadcasted_iota(jnp.int32, (count, total), 0)
    col = lax.broadcasted_iota(jnp.int32, (count, total), 1)
    order = jnp.where(col == slot + (ROWS - SEND) * div_send(slot), 1.0, 0.0).astype(bf16)
    rows_ref[:, : 3 * part] = jnp.dot(order, arrived, preferred_element_type=f32).astype(bf16)
    tail = jnp.zeros((count, part), f32)
    for j in range(3):
        tail += jnp.dot(
            tail_order(count, total, j, True),
            arrived[:, j * part : (j + 1) * part],
            preferred_element_type=f32,
        )
    rows_ref[:, 3 * part :] = tail.astype(bf16)


def times_weight(rows_ref, weight_ref):
    return lax.dot_general(
        rows_ref[...], weight_ref[...], (((1,), (1,)), ((), ())), preferred_element_type=f32
    )


def score_block(blocks, proj, hidden, picked):
    count = proj.shape[0]
    score = jnp.sum(proj * hidden.astype(f32), axis=1, keepdims=True)
    row = lax.broadcasted_iota(jnp.int32, (count, LANE), 0)
    lane = lax.broadcasted_iota(jnp.int32, (count, LANE), 1)
    spread = jnp.where(row - SEND * div_send(row) == lane, score, 0.0)
    high = spread.astype(bf16)
    rest = (spread - high.astype(f32)).astype(bf16)
    at = lax.broadcasted_iota(jnp.int32, (blocks, count), 1)
    gather = [jnp.where(div_send(at) == pick, 1.0, 0.0) for pick in picked]
    gather = jnp.concatenate(gather, axis=0).astype(bf16)
    value = jnp.dot(gather, high, preferred_element_type=f32)
    value += jnp.dot(gather, rest, preferred_element_type=f32)
    return [
        value[i * blocks : (i + 1) * blocks].reshape(blocks, 1, LANE)
        for i in range(len(picked))
    ]


def block_index(blocks, count):
    return lax.broadcasted_iota(jnp.int32, (blocks, count), 0)


def begin_kernel(blocks, arrived_ref, weight_ref, *refs):
    hidden, (rows_ref, hidden_t, score_ref) = refs[:-6], refs[-6:-3]
    proj_hbm, proj_ref, sem = refs[-3:]
    reorder(arrived_ref[...], rows_ref)
    proj = times_weight(rows_ref, weight_ref)
    proj_ref[...] = proj
    copy = pltpu.make_async_copy(proj_ref, proj_hbm, sem.at[0])
    copy.start()
    count = proj.shape[0]
    score_ref[...] = score_block(
        blocks, proj, hidden[0][...], [block_index(blocks, count)]
    )[0]
    transpose_rows(hidden, hidden_t)
    copy.wait()


def begin(blocks, arrived, weight, hidden):
    count = blocks * SEND
    part, cols = weight.shape
    total = count * len(hidden)
    return pl.pallas_call(
        functools.partial(begin_kernel, blocks),
        in_specs=[VMEM] * (2 + len(hidden)),
        out_specs=[VMEM] * 3 + [HBM],
        out_shape=[
            plain((count, cols), bf16),
            plain((part, total), bf16),
            plain((blocks, 1, LANE), f32),
            out_hbm((count, part), f32),
        ],
        scratch_shapes=[pltpu.VMEM((count, part), f32), pltpu.SemaphoreType.DMA((1,))],
        compiler_params=params(8 * count * cols + 16 * total * part),
        cost_estimate=cost(4 * count * part * cols, 2 * part * cols),
    )(arrived, weight, *hidden)


def finish_kernel(shards, blocks, arrived_ref, hidden_ref, weight_ref, *refs):
    before_hbm, score_in = refs[:shards], refs[shards : 2 * shards]
    projs, (score_ref, before, sems) = refs[2 * shards : 3 * shards], refs[3 * shards :]
    copies = [
        pltpu.make_async_copy(ref, before.at[s], sems.at[s])
        for s, ref in enumerate(before_hbm)
    ]
    for copy in copies:
        copy.start()
    proj = times_weight(arrived_ref, weight_ref)
    rounded = proj.astype(bf16)
    total = proj.shape[0]
    count = total // shards
    picked = [block_index(blocks, total) * shards + s for s in range(shards)]
    scores = score_block(blocks, proj, hidden_ref[...], picked)
    me = lax.axis_index("rep")
    slot = lax.broadcasted_iota(jnp.int32, (count, total), 0)
    row = lax.broadcasted_iota(jnp.int32, (count, total), 1)
    for s in range(shards):
        order = row == slot + SEND * (div_send(slot) * (shards - 1) + s)
        order = jnp.where(order, 1.0, 0.0).astype(bf16)
        own = jnp.dot(order, rounded, preferred_element_type=f32)
        copies[s].wait()
        own += before[s]
        projs[s][...] = own.astype(bf16)
        at = lax.rem(me + shards - s, shards)
        score_ref[pl.ds(at * blocks, blocks)] = score_in[s][...] + scores[s]


def finish(blocks, arrived, hidden, weight, before, scores):
    shards = len(before)
    total, part = hidden.shape
    count = total // shards
    cols = weight.shape[1]
    outs = pl.pallas_call(
        functools.partial(finish_kernel, shards, blocks),
        in_specs=[VMEM] * 3 + [HBM] * shards + [VMEM] * shards,
        out_specs=[VMEM] * (shards + 1),
        out_shape=[plain((count, part), bf16)] * shards
        + [plain((shards * blocks, 1, LANE), f32)],
        scratch_shapes=[
            pltpu.VMEM((shards, count, part), f32),
            pltpu.SemaphoreType.DMA((shards,)),
        ],
        compiler_params=params(20 * total * part),
        cost_estimate=cost(2 * total * part * cols, 2 * part * cols),
    )(arrived, hidden, weight, *in_hbm(*before), *scores)
    return list(outs[:-1]), outs[-1]


def new_state(master, one, two, grad):
    corr_one = 1.0 - beta_one**adam_step
    corr_two = 1.0 - beta_two**adam_step
    rate = learn_rate * corr_two**0.5 / corr_one
    keep = 1.0 - learn_rate * decay_rate
    eps = adam_eps * corr_two**0.5
    m_new = beta_one * one.astype(f32) + (1.0 - beta_one) * grad
    v_new = beta_two * two.astype(f32) + (1.0 - beta_two) * (grad * grad)
    root = lax.rsqrt(v_new)
    below = v_new * root + eps
    inverse = root * (2.0 - below * root)
    master = keep * master - (rate * m_new) * inverse
    return master, m_new.astype(bf16), v_new.astype(bf16)


def update_rows(first, count, state, news, grad_ref):
    cols = grad_ref.shape[1]

    @pl.loop(0, count // ROWS)
    def _(i):
        own = pl.ds(pl.multiple_of(first + i * ROWS, ROWS), ROWS)
        for low in range(0, cols, UNIT):
            at = (own, slice(low, low + UNIT))
            values = new_state(*[ref[at] for ref in state], grad_ref[at])
            for ref, value in zip(news, values):
                ref[at] = value


def transpose_rows(hidden, hidden_t):
    base = 0
    for ref in hidden:
        high = base + ref.shape[0]
        hidden_t[:, base:high] = ref[...].astype(f32).T.astype(bf16)
        base = high


def form_grad(hidden_t, rows_refs, grad_ref):
    for low in range(0, grad_ref.shape[1], UNIT):
        own = slice(low, low + UNIT)
        base = 0
        grad = 0.0
        for rows_ref in rows_refs:
            high = base + rows_ref.shape[0]
            grad += jnp.dot(
                hidden_t[:, base:high], rows_ref[:, own], preferred_element_type=f32
            )
            base = high
        grad_ref[:, own] = grad


def state_copies(i, step, low, hbm, vmem, sems, into):
    cols = vmem[0].shape[1]
    rows = pl.ds(pl.multiple_of(i * step, step), step)
    out = []
    for j, (far, near) in enumerate(zip(hbm, vmem)):
        ends = (far.at[0, rows, pl.ds(low, cols)], near.at[rows])
        source, target = ends if into else ends[::-1]
        out.append(pltpu.make_async_copy(source, target, sems.at[j, i]))
    return out


def settle_kernel(fresh, blocks, *refs):
    refs = list(refs)

    def take(number):
        out = refs[:number]
        del refs[:number]
        return out

    size = len(fresh)
    arrived, hidden = take(size), take(1 + size)
    hidden_t, given_ref, weight_ref, *state = take(6)
    scores, (mixed_ref,), projs_hbm, outs = take(size), take(1), take(size), take(3)
    news, rows_refs, projs = take(3), take(size), take(size)
    grad_ref, sems, proj_sems = refs
    part = grad_ref.shape[0]
    count = blocks * SEND
    shards = 1 + size
    for i in range(size):
        reorder(arrived[i][...], rows_refs[i])
    form_grad(hidden_t, [given_ref] + rows_refs, grad_ref)
    steps = sems.shape[1]
    step = part // steps

    @pl.loop(0, steps)
    def _(i):
        update_rows(i * step, step, state, news, grad_ref)
        for copy in state_copies(i, step, 0, outs, news, sems, False):
            copy.start()

    copies = []
    for i, s in enumerate(fresh):
        proj = times_weight(rows_refs[i], weight_ref)
        projs[i][...] = proj
        copies.append(pltpu.make_async_copy(projs[i], projs_hbm[i], proj_sems.at[i]))
        copies[i].start()
        scores[i][...] = score_block(
            blocks, proj, hidden[s][...], [block_index(blocks, count)]
        )[0]
    row = lax.broadcasted_iota(jnp.int32, (shards * count, count), 0)
    col = lax.broadcasted_iota(jnp.int32, (shards * count, count), 1)
    at, step_of, slot = mixed_place(row, shards)
    total = 0.0
    for s in range(shards):
        order = (step_of == s) & (col == at * SEND + slot)
        order = jnp.where(order, 1.0, 0.0).astype(bf16)
        total += jnp.dot(order, hidden[s][...], preferred_element_type=f32)
    mixed_ref[...] = total.astype(bf16)

    @pl.loop(0, steps)
    def _(i):
        for copy in state_copies(i, step, 0, outs, news, sems, False):
            copy.wait()

    for copy in copies:
        copy.wait()


def settle(blocks, arrived, given, hidden, hidden_t, weight, held, shapes):
    part, cols = weight.shape
    count = blocks * SEND
    fresh = tuple(range(1, 1 + len(arrived)))
    size = len(fresh)
    total = count * (1 + size)
    step = min(part, 64)
    args = [*arrived, *hidden, hidden_t, given, weight, *held]
    near = [plain((blocks, 1, LANE), f32)] * size + [plain((total, part), bf16)]
    far = [out_hbm((count, part), f32)] * size
    far += [out_hbm(array.shape, array.dtype) for array in shapes]
    scratch = [pltpu.VMEM((part, cols), kind) for kind in (f32, bf16, bf16)]
    scratch += [pltpu.VMEM((count, cols), bf16)] * size
    scratch += [pltpu.VMEM((count, part), f32)] * size
    scratch += [
        pltpu.VMEM((part, cols), f32),
        pltpu.SemaphoreType.DMA((3, part // step)),
        pltpu.SemaphoreType.DMA((max(1, size),)),
    ]
    nbytes = 12 * part * cols + 4 * total * cols + 8 * total * part
    outs = pl.pallas_call(
        functools.partial(settle_kernel, fresh, blocks),
        in_specs=[VMEM] * len(args),
        out_specs=[VMEM] * len(near) + [HBM] * len(far),
        out_shape=near + far,
        scratch_shapes=scratch,
        compiler_params=params(nbytes),
        cost_estimate=cost(4 * total * part * cols, 16 * part * cols, part * cols),
    )(*args)
    outs = list(outs)
    return outs[:size], outs[size], outs[size + 1 : -3], outs[-3:]


def update_kernel(low, shards, hidden_ref, rows_ref, *refs):
    grad_refs, refs = refs[:shards], refs[shards:]
    gate_up_hbm, state_hbm, token_hbm, refs = refs[0], refs[1:4], refs[4:7], refs[10:]
    outs, gate_out, place_ref, inverse_ref, refs = refs[:3], *refs[3:6], refs[6:]
    state, tokens, refs = refs[:3], refs[3:6], refs[6:]
    hidden_t, grad_ref, gate_up_ref, gate_new, in_sems, out_sems, sems = refs
    part = grad_ref.shape[0]
    steps = in_sems.shape[1]
    step = part // steps
    gate_load = pltpu.make_async_copy(gate_up_hbm, gate_up_ref, sems.at[0])
    gate_store = pltpu.make_async_copy(gate_new, gate_out, sems.at[1])
    gate_load.start()
    token_loads = [
        pltpu.make_async_copy(source, target, sems.at[2 + i])
        for i, (source, target) in enumerate(zip(token_hbm, tokens))
    ]
    for copy in token_loads:
        copy.start()
    for i in range(steps):
        for copy in state_copies(i, step, low, state_hbm, state, in_sems, True):
            copy.start()
    transpose_rows([hidden_ref], hidden_t)
    form_grad(hidden_t, [rows_ref], grad_ref)
    for copy in token_loads:
        copy.wait()
    ids, slots = tokens[0][...], tokens[1][...]
    live = ((ids & (EXP_LOCAL - 1)) == 0) & (slots >= 0)
    place_ref[...] = jnp.where(live, ids // EXP_LOCAL * SEND + slots, -1)
    inverse_ref[...] = 1.0 / tokens[2][...].astype(f32)

    @pl.loop(0, steps)
    def _(i):
        for copy in state_copies(i, step, low, state_hbm, state, in_sems, True):
            copy.wait()
        update_rows(i * step, step, state, state, grad_ref)
        for copy in state_copies(i, step, low, outs, state, out_sems, False):
            copy.start()

    gate_load.wait()
    for s, ref in enumerate(grad_refs):
        width = ref.shape[1]
        first, second, gate, up, sig = swiglu_part(gate_up_ref, shards, s, width)
        grad = ref[...].astype(f32)
        gate_new[:, pl.ds(first, width)] = (
            grad * up * sig * (1.0 + gate * (1.0 - sig))
        ).astype(bf16)
        gate_new[:, pl.ds(second, width)] = (grad * (gate * sig)).astype(bf16)
    gate_store.start()

    @pl.loop(0, steps)
    def _(i):
        for copy in state_copies(i, step, low, outs, state, out_sems, False):
            copy.wait()

    gate_store.wait()


def update(low, hidden, rows, grads, gate_up, state, tokens, done):
    total, part = hidden.shape
    cols = rows.shape[1]
    step = min(part, 64)
    shards = len(grads)
    scratch = [pltpu.VMEM((part, cols), kind) for kind in (f32, bf16, bf16)]
    scratch += [pltpu.VMEM(token.shape, token.dtype) for token in tokens]
    scratch += [pltpu.VMEM((part, total), bf16), pltpu.VMEM((part, cols), f32)]
    scratch += [pltpu.VMEM(gate_up.shape, bf16)] * 2
    scratch += [pltpu.SemaphoreType.DMA((3, part // step))] * 2
    scratch += [pltpu.SemaphoreType.DMA((5,))]
    return pl.pallas_call(
        functools.partial(update_kernel, low, shards),
        in_specs=[VMEM] * (2 + shards) + [HBM] * 10,
        out_specs=[HBM] * 4 + [VMEM] * 2,
        out_shape=[out_hbm(array.shape, array.dtype) for array in state]
        + [out_hbm(gate_up.shape, bf16)]
        + [plain(tokens[0].shape, kind) for kind in (jnp.int32, f32)],
        scratch_shapes=scratch,
        input_output_aliases={2 + shards + 7 + i: i for i in range(3)},
        compiler_params=params(12 * part * cols + 2 * total * part + 4 * gate_up.size),
        cost_estimate=cost(2 * total * part * cols, 16 * part * cols, part * cols),
    )(hidden, rows, *grads, *in_hbm(gate_up, *state, *tokens, *done))


def close_kernel(shards, place_ref, inverse_ref, score_ref, gate_ref):
    place = place_ref[...]
    blocks = score_ref.shape[0] // shards
    value = jnp.zeros(place.shape, f32)
    for b in range(blocks):
        for slot in range(SEND):
            score = score_ref[b, 0, slot]
            for s in range(1, shards):
                score += score_ref[s * blocks + b, 0, slot]
            value = jnp.where(place == b * SEND + slot, score, value)
    gate_ref[...] = value * inverse_ref[...]


def close(shards, place, inverse, score):
    return pl.pallas_call(
        functools.partial(close_kernel, shards),
        in_specs=[VMEM] * 2 + [pl.BlockSpec(memory_space=pltpu.SMEM)],
        out_specs=VMEM,
        out_shape=plain(place.shape, f32),
        compiler_params=params(0),
        cost_estimate=cost(1 << 20, 1 << 16),
    )(place, inverse, score)


def per_device(out_grad, expert_ids, slots, gate_weights, saved_gate_up, master, moment1, moment2):
    ep_size = lax.axis_size("ep")
    rep_size = lax.axis_size("rep")
    ids_t, slots_t, gates_t = expert_ids.T, slots.T, gate_weights.T
    gate_up = saved_gate_up[0, 0]
    state = (master, moment1, moment2)
    edges = chunk_edges(out_grad.shape[1])
    steps = range(1, rep_size)

    def shift(value, step):
        perm = [(i, (i + step) % rep_size) for i in range(rep_size)]
        return lax.ppermute(value, "rep", perm)

    def exchange(value):
        return lax.all_to_all(value, "ep", split_axis=0, concat_axis=0, tiled=True)

    send_a, send_b = dispatch(ep_size, edges, ids_t, slots_t, gates_t, out_grad)
    mixed = [shift(send_b, s) for s in steps]
    parts = list(hidden_parts(gate_up, rep_size, send_b))
    arrived = exchange(send_a.reshape(ep_size, ROWS, -1)).reshape(send_a.shape)
    hidden = [parts[0]] + [shift(parts[s], s) for s in steps]
    mixed = mix([send_b] + mixed)
    hidden[1:], mixed = lax.optimization_barrier((hidden[1:], mixed))
    arrived_b = exchange(mixed.reshape(ep_size, rep_size * SEND, -1)).reshape(mixed.shape)

    peers = [shift(arrived, s) for s in steps]
    *held, weight_a, weight_b = load_state(edges[1], *state, arrived)
    rows, hidden_t, score_own, proj = begin(ep_size, arrived, weight_a, hidden)
    scores, hidden_mixed, before, done = settle(
        ep_size, peers, rows, hidden, hidden_t, weight_a, held, state
    )
    projs, score = finish(
        ep_size, arrived_b, hidden_mixed, weight_b, [proj] + before, [score_own] + scores
    )
    grads = [projs[0]] + [shift(projs[s], rep_size - s) for s in steps]
    score = lax.all_to_all(score, ("rep", "ep"), split_axis=0, concat_axis=0, tiled=True)

    tokens = (ids_t, slots_t, gates_t)
    *done, grad_gate_up, place, inverse = update(
        edges[1], hidden_mixed, arrived_b, grads, gate_up, state, tokens, done
    )
    gate_grad = close(rep_size, place, inverse, score).T
    return (grad_gate_up.reshape(saved_gate_up.shape), gate_grad) + tuple(done)


def solution(mesh):
    in_specs = (
        P(("rep", "ep"), None),
        P(("rep", "ep"), None),
        P(("rep", "ep"), None),
        P(("rep", "ep"), None),
        P("rep", "ep", None, None),
        P("ep", "rep", None),
        P("ep", "rep", None),
        P("ep", "rep", None),
    )
    out_specs = (
        P("rep", "ep", None, None),
        P(("rep", "ep"), None),
        P("ep", "rep", None),
        P("ep", "rep", None),
        P("ep", "rep", None),
    )
    return jax.shard_map(
        per_device, mesh=mesh, in_specs=in_specs, out_specs=out_specs, check_vma=False
    )
```

```python
import functools

import jax
import jax.numpy as jnp
from jax import lax
from jax.experimental import pallas as pl
from jax.experimental.pallas import tpu as pltpu
from jax.sharding import PartitionSpec as P

TOPK = 8
EXP_LOCAL = 8
SEND = 12
LANE = 128
UNIT = 512
ROWS = 16

beta_one = 0.9
beta_two = 0.95
learn_rate = 0.002
decay_rate = 0.1
adam_eps = 1e-08
adam_step = 50

f32 = jnp.float32
bf16 = jnp.bfloat16
HBM = pl.BlockSpec(memory_space=pltpu.HBM)
ANY = pl.BlockSpec(memory_space=pl.ANY)
VMEM = pl.BlockSpec(memory_space=pltpu.VMEM)


def in_hbm(*arrays):
    return [pltpu.with_memory_space_constraint(array, pltpu.HBM) for array in arrays]


def plain(dims, dtype):
    return jax.ShapeDtypeStruct(tuple(dims), dtype)


def out_hbm(dims, dtype):
    return pltpu.HBM(tuple(dims), dtype)


def block(dims, at=None):
    at = at or (0,) * len(dims)
    return pl.BlockSpec(tuple(dims), lambda i: at, pipeline_mode=pl.Buffered(1))


def params(nbytes):
    mib = min(60, max(16, 10 + 5 * int(nbytes) // 2**22))
    return pltpu.CompilerParams(vmem_limit_bytes=mib * 2**20)


def cost(flops, nbytes, transcendentals=0):
    return pl.CostEstimate(
        flops=int(flops), bytes_accessed=int(nbytes), transcendentals=int(transcendentals)
    )


def div_send(index):
    return lax.shift_right_logical(index * 10923, 17)


def pack(cols):
    return cols // 4 * 3


def chunk_edges(width):
    units = width // UNIT
    return (0, (units - max(1, units * 3 // 7)) * UNIT, width)


def tail_order(count, total, j, slots_first):
    a = lax.broadcasted_iota(jnp.int32, (count, total), 0)
    b = lax.broadcasted_iota(jnp.int32, (count, total), 1)
    if slots_first:
        block_of = div_send(a)
        inner = a - SEND * block_of
        hit = b == block_of * ROWS + SEND + inner - 4 * j
    else:
        inner = (a & (ROWS - 1)) - SEND + 4 * j
        hit = (b == a - SEND + 4 * j) & ((a & (ROWS - 1)) >= SEND)
    return jnp.where(hit & (inner >= 4 * j) & (inner < 4 * j + 4), 1.0, 0.0).astype(bf16)


def dispatch_kernel(edges, ids_hbm, slots_hbm, gates_hbm, grad_hbm, *refs):
    outs, (ids_ref, slots_ref, gates_ref, grad_ref, sems) = refs[:2], refs[2:]
    pairs = [(ids_hbm, ids_ref), (slots_hbm, slots_ref), (gates_hbm, gates_ref)]
    for c in (1, 0):
        own = (slice(None), pl.ds(edges[c], edges[c + 1] - edges[c]))
        pairs.append((grad_hbm.at[own], grad_ref.at[own]))
    copies = [
        pltpu.make_async_copy(source, target, sems.at[i])
        for i, (source, target) in enumerate(pairs)
    ]
    for copy in copies:
        copy.start()
    rows = outs[0].shape[0]
    tok = ids_ref.shape[1]
    orders = [tail_order(rows, rows, j, False) for j in range(3)]
    for copy in copies[:3]:
        copy.wait()
    ids = ids_ref[...]
    slots = slots_ref[...]
    gates = gates_ref[...].astype(f32)
    live = ((ids & (EXP_LOCAL - 1)) == 0) & (slots >= 0)
    place = jnp.where(live, ids // EXP_LOCAL * ROWS + slots, -1)
    row = lax.broadcasted_iota(jnp.int32, (rows, tok), 0)
    main = jnp.zeros((rows, tok), f32)
    for k in range(TOPK):
        main = jnp.where(row == place[k : k + 1], gates[k : k + 1], main)
    main = main.astype(bf16)
    tails = [
        jnp.dot(order, main, preferred_element_type=f32).astype(bf16) for order in orders
    ]
    for c in (1, 0):
        copies[4 - c].wait()
        low, high = edges[c], edges[c + 1]
        part = (high - low) // 4
        for j in range(3):
            total = jnp.dot(
                main,
                grad_ref[:, low + j * part : low + (j + 1) * part],
                preferred_element_type=f32,
            )
            total += jnp.dot(
                tails[j], grad_ref[:, low + 3 * part : high], preferred_element_type=f32
            )
            outs[c][:, j * part : (j + 1) * part] = total.astype(bf16)


def dispatch(blocks, edges, ids, slots, gates, out_grad):
    tok, width = out_grad.shape
    rows = blocks * ROWS
    shapes = [(rows, pack(high - low)) for low, high in zip(edges[:-1], edges[1:])]
    return pl.pallas_call(
        functools.partial(dispatch_kernel, edges),
        in_specs=[HBM] * 4,
        out_specs=[VMEM] * 2,
        out_shape=[plain(shape, bf16) for shape in shapes],
        scratch_shapes=[
            pltpu.VMEM(ids.shape, jnp.int32),
            pltpu.VMEM(slots.shape, jnp.int32),
            pltpu.VMEM(gates.shape, bf16),
            pltpu.VMEM(out_grad.shape, bf16),
            pltpu.SemaphoreType.DMA((5,)),
        ],
        compiler_params=params(2 * rows * width + 2 * tok * width),
        cost_estimate=cost(2 * rows * tok * width, 4 * tok * width),
    )(*in_hbm(ids, slots, gates, out_grad))


def unit_columns(shards, step, part):
    at = lax.rem(lax.axis_index("rep") + step, shards)
    return pl.multiple_of(at * part, part), pl.multiple_of((shards + at) * part, part)


def hidden_kernel(gate_up_ref, after_ref, *refs):
    del after_ref
    out_refs, factor_ref = refs[:-1], refs[-1]
    for s, out_ref in enumerate(out_refs):
        part = out_ref.shape[1]
        low, high = unit_columns(len(out_refs), s, part)
        gate = gate_up_ref[:, pl.ds(low, part)].astype(f32)
        up = gate_up_ref[:, pl.ds(high, part)].astype(f32)
        sig = jax.nn.sigmoid(gate)
        silu = gate * sig
        out_ref[...] = (silu * up).astype(bf16)
        factor_ref[:, pl.ds(low, part)] = up * sig * (1.0 + gate * (1.0 - sig))
        factor_ref[:, pl.ds(high, part)] = silu


def hidden_parts(gate_up, shards, after):
    slots, width = gate_up.shape
    shape = (slots, width // 2 // shards)
    outs = pl.pallas_call(
        hidden_kernel,
        grid=(1,),
        in_specs=[block(gate_up.shape), ANY],
        out_specs=[block(shape)] * shards + [block(gate_up.shape)],
        out_shape=[out_hbm(shape, bf16)] * shards + [out_hbm(gate_up.shape, f32)],
        compiler_params=params(7 * slots * width),
        cost_estimate=cost(8 * slots * width, 7 * slots * width, slots * width),
    )(*in_hbm(gate_up), after)
    return list(outs[:-1]), outs[-1]


def load_kernel(middle, after_ref, master_hbm, one_hbm, two_hbm, *refs):
    del after_ref
    master_ref, one_ref, two_ref, weight_a, weight_b, rest_ref, sems = refs
    part = master_ref.shape[0]
    rest = rest_ref.shape[1]
    step = part // 4
    copies = []
    for i in range(4):
        own = pl.ds(i * step, step)
        copies.append(
            pltpu.make_async_copy(
                master_hbm.at[0, own, pl.ds(0, middle)], master_ref.at[own], sems.at[i]
            )
        )
    for i in range(4):
        own = pl.ds(i * step, step)
        copies.append(
            pltpu.make_async_copy(
                master_hbm.at[0, own, pl.ds(middle, rest)], rest_ref.at[own], sems.at[4 + i]
            )
        )
    for i, (source, target) in enumerate([(one_hbm, one_ref), (two_hbm, two_ref)]):
        copies.append(
            pltpu.make_async_copy(source.at[0, :, pl.ds(0, middle)], target, sems.at[8 + i])
        )
    for copy in copies:
        copy.start()
    for i in range(4):
        copies[i].wait()
        own = slice(i * step, (i + 1) * step)
        weight_a[own, :] = master_ref[own, :].astype(bf16)
    for i in range(4):
        copies[4 + i].wait()
        own = slice(i * step, (i + 1) * step)
        weight_b[own, :] = rest_ref[own, :].astype(bf16)
    copies[8].wait()
    copies[9].wait()


def load_state(middle, master, one, two, after):
    _, part, width = master.shape
    return pl.pallas_call(
        functools.partial(load_kernel, middle),
        in_specs=[ANY] + [HBM] * 3,
        out_specs=[VMEM] * 5,
        out_shape=[
            pltpu.VMEM((part, middle), f32),
            pltpu.VMEM((part, middle), bf16),
            pltpu.VMEM((part, middle), bf16),
            pltpu.VMEM((part, middle), bf16),
            pltpu.VMEM((part, width - middle), bf16),
        ],
        scratch_shapes=[
            pltpu.VMEM((part, width - middle), f32),
            pltpu.SemaphoreType.DMA((10,)),
        ],
        compiler_params=params(4 * part * (width - middle)),
        cost_estimate=cost(part * width, 14 * part * width),
    )(after, *in_hbm(master, one, two))


def mixed_place(index, shards):
    group = div_send(index)
    bits = shards.bit_length() - 1
    step = group & (shards - 1)
    return lax.shift_right_logical(group, bits), step, index - SEND * group


def mix_kernel(shards, *refs):
    parts, (out_hbm_ref, out_ref, sems) = refs[:shards], refs[shards:]
    part = parts[0].shape[1] // 3
    copies = []
    blocks = parts[0].shape[0] // ROWS
    some = min(blocks, 32 // shards)
    rows, packed = some * shards * SEND, some * shards * ROWS
    row = lax.broadcasted_iota(jnp.int32, (rows, packed), 0)
    col = lax.broadcasted_iota(jnp.int32, (rows, packed), 1)
    at, step, slot = mixed_place(row, shards)
    base = (step * some + at) * ROWS
    orders = [jnp.where(col == base + slot, 1.0, 0.0).astype(bf16)]
    for j in range(3):
        hit = (col == base + SEND + slot - 4 * j) & (slot >= 4 * j) & (slot < 4 * j + 4)
        orders.append(jnp.where(hit, 1.0, 0.0).astype(bf16))
    for first in range(0, blocks, some):
        stack = jnp.concatenate(
            [ref[first * ROWS : (first + some) * ROWS, :] for ref in parts], axis=0
        )
        own = slice(first * shards * SEND, (first + some) * shards * SEND)
        place = pl.ds(first * shards * SEND, some * shards * SEND)
        index = first // some

        def send(j):
            at = (place, pl.ds(j * part, part))
            copy = pltpu.make_async_copy(out_ref.at[at], out_hbm_ref.at[at], sems.at[j, index])
            copy.start()
            copies.append(copy)

        for j in range(3):
            out_ref[own, j * part : (j + 1) * part] = jnp.dot(
                orders[0], stack[:, j * part : (j + 1) * part], preferred_element_type=f32
            ).astype(bf16)
            send(j)
        tail = jnp.zeros((rows, part), f32)
        for j in range(3):
            tail += jnp.dot(
                orders[1 + j],
                stack[:, j * part : (j + 1) * part],
                preferred_element_type=f32,
            )
        out_ref[own, 3 * part :] = tail.astype(bf16)
        send(3)
    for copy in copies:
        copy.wait()


def mix(parts):
    shards = len(parts)
    rows, packed = parts[0].shape
    shape = (rows // ROWS * SEND * shards, packed // 3 * 4)
    return pl.pallas_call(
        functools.partial(mix_kernel, shards),
        in_specs=[VMEM] * shards,
        out_specs=HBM,
        out_shape=out_hbm(shape, bf16),
        scratch_shapes=[
            pltpu.VMEM(shape, bf16),
            pltpu.SemaphoreType.DMA((4, rows // ROWS // min(rows // ROWS, 32 // shards))),
        ],
        compiler_params=params(12 * rows * packed * shards),
        cost_estimate=cost(0, 5 * rows * packed * shards),
    )(*parts)


def reorder(arrived, rows_ref):
    count, width = rows_ref.shape
    part = width // 4
    total = arrived.shape[0]
    slot = lax.broadcasted_iota(jnp.int32, (count, total), 0)
    col = lax.broadcasted_iota(jnp.int32, (count, total), 1)
    order = jnp.where(col == slot + (ROWS - SEND) * div_send(slot), 1.0, 0.0).astype(bf16)
    rows_ref[:, : 3 * part] = jnp.dot(order, arrived, preferred_element_type=f32).astype(bf16)
    tail = jnp.zeros((count, part), f32)
    for j in range(3):
        tail += jnp.dot(
            tail_order(count, total, j, True),
            arrived[:, j * part : (j + 1) * part],
            preferred_element_type=f32,
        )
    rows_ref[:, 3 * part :] = tail.astype(bf16)


def times_weight(rows_ref, weight_ref):
    return lax.dot_general(
        rows_ref[...], weight_ref[...], (((1,), (1,)), ((), ())), preferred_element_type=f32
    )


def score_block(blocks, proj, hidden, picked):
    count = proj.shape[0]
    score = jnp.sum(proj * hidden.astype(f32), axis=1, keepdims=True)
    row = lax.broadcasted_iota(jnp.int32, (count, LANE), 0)
    lane = lax.broadcasted_iota(jnp.int32, (count, LANE), 1)
    spread = jnp.where(row - SEND * div_send(row) == lane, score, 0.0)
    high = spread.astype(bf16)
    rest = (spread - high.astype(f32)).astype(bf16)
    at = lax.broadcasted_iota(jnp.int32, (blocks, count), 1)
    gather = [jnp.where(div_send(at) == pick, 1.0, 0.0) for pick in picked]
    gather = jnp.concatenate(gather, axis=0).astype(bf16)
    value = jnp.dot(gather, high, preferred_element_type=f32)
    value += jnp.dot(gather, rest, preferred_element_type=f32)
    return [
        value[i * blocks : (i + 1) * blocks].reshape(blocks, 1, LANE)
        for i in range(len(picked))
    ]


def block_index(blocks, count):
    return lax.broadcasted_iota(jnp.int32, (blocks, count), 0)


def begin_kernel(blocks, arrived_ref, weight_ref, *refs):
    size = len(refs) - 7
    hidden_hbm, (rows_ref, hidden_ref, hidden_t, score_ref) = refs[:size], refs[size:-3]
    proj_hbm, proj_ref, sems = refs[-3:]
    count = rows_ref.shape[0]
    loads = [
        pltpu.make_async_copy(ref, hidden_ref.at[pl.ds(s * count, count)], sems.at[1 + s])
        for s, ref in enumerate(hidden_hbm)
    ]
    for copy in loads:
        copy.start()
    reorder(arrived_ref[...], rows_ref)
    proj = times_weight(rows_ref, weight_ref)
    proj_ref[...] = proj
    copy = pltpu.make_async_copy(proj_ref, proj_hbm, sems.at[0])
    copy.start()
    for load in loads:
        load.wait()
    score_ref[...] = score_block(
        blocks, proj, hidden_ref[:count], [block_index(blocks, count)]
    )[0]
    transpose_rows([hidden_ref], hidden_t)
    copy.wait()


def begin(blocks, arrived, weight, hidden):
    count = blocks * SEND
    part, cols = weight.shape
    total = count * len(hidden)
    return pl.pallas_call(
        functools.partial(begin_kernel, blocks),
        in_specs=[VMEM] * 2 + [HBM] * len(hidden),
        out_specs=[VMEM] * 4 + [HBM],
        out_shape=[
            plain((count, cols), bf16),
            plain((total, part), bf16),
            plain((part, total), bf16),
            plain((blocks, 1, LANE), f32),
            out_hbm((count, part), f32),
        ],
        scratch_shapes=[
            pltpu.VMEM((count, part), f32),
            pltpu.SemaphoreType.DMA((1 + len(hidden),)),
        ],
        compiler_params=params(8 * count * cols + 16 * total * part),
        cost_estimate=cost(4 * count * part * cols, 2 * part * cols),
    )(arrived, weight, *in_hbm(*hidden))


def finish_kernel(shards, blocks, arrived_ref, hidden_ref, weight_ref, *refs):
    before_hbm, score_in = refs[:shards], refs[shards : 2 * shards]
    projs, (score_ref, before, sems) = refs[2 * shards : 3 * shards], refs[3 * shards :]
    copies = [
        pltpu.make_async_copy(ref, before.at[s], sems.at[s])
        for s, ref in enumerate(before_hbm)
    ]
    for copy in copies:
        copy.start()
    proj = times_weight(arrived_ref, weight_ref)
    rounded = proj.astype(bf16)
    total = proj.shape[0]
    count = total // shards
    picked = [block_index(blocks, total) * shards + s for s in range(shards)]
    scores = score_block(blocks, proj, hidden_ref[...], picked)
    me = lax.axis_index("rep")
    slot = lax.broadcasted_iota(jnp.int32, (count, total), 0)
    row = lax.broadcasted_iota(jnp.int32, (count, total), 1)
    for s in range(shards):
        order = row == slot + SEND * (div_send(slot) * (shards - 1) + s)
        order = jnp.where(order, 1.0, 0.0).astype(bf16)
        own = jnp.dot(order, rounded, preferred_element_type=f32)
        copies[s].wait()
        own += before[s]
        projs[s][...] = own.astype(bf16)
        at = lax.rem(me + shards - s, shards)
        score_ref[pl.ds(at * blocks, blocks)] = score_in[s][...] + scores[s]


def finish(blocks, arrived, hidden, weight, before, scores):
    shards = len(before)
    total, part = hidden.shape
    count = total // shards
    cols = weight.shape[1]
    outs = pl.pallas_call(
        functools.partial(finish_kernel, shards, blocks),
        in_specs=[VMEM] * 3 + [HBM] * shards + [VMEM] * shards,
        out_specs=[VMEM] * (shards + 1),
        out_shape=[plain((count, part), bf16)] * shards
        + [plain((shards * blocks, 1, LANE), f32)],
        scratch_shapes=[
            pltpu.VMEM((shards, count, part), f32),
            pltpu.SemaphoreType.DMA((shards,)),
        ],
        compiler_params=params(20 * total * part),
        cost_estimate=cost(2 * total * part * cols, 2 * part * cols),
    )(arrived, hidden, weight, *in_hbm(*before), *scores)
    return list(outs[:-1]), outs[-1]


def new_state(master, one, two, grad):
    corr_one = 1.0 - beta_one**adam_step
    corr_two = 1.0 - beta_two**adam_step
    rate = learn_rate * corr_two**0.5 / corr_one
    keep = 1.0 - learn_rate * decay_rate
    eps = adam_eps * corr_two**0.5
    m_new = beta_one * one.astype(f32) + (1.0 - beta_one) * grad
    v_new = beta_two * two.astype(f32) + (1.0 - beta_two) * (grad * grad)
    root = lax.rsqrt(v_new)
    below = v_new * root + eps
    inverse = root * (2.0 - below * root)
    master = keep * master - (rate * m_new) * inverse
    return master, m_new.astype(bf16), v_new.astype(bf16)


def update_rows(first, count, state, news, grad_ref):
    cols = grad_ref.shape[1]

    @pl.loop(0, count // ROWS)
    def _(i):
        own = pl.ds(pl.multiple_of(first + i * ROWS, ROWS), ROWS)
        for low in range(0, cols, UNIT):
            at = (own, slice(low, low + UNIT))
            values = new_state(*[ref[at] for ref in state], grad_ref[at])
            for ref, value in zip(news, values):
                ref[at] = value


def transpose_rows(hidden, hidden_t):
    base = 0
    for ref in hidden:
        high = base + ref.shape[0]
        hidden_t[:, base:high] = ref[...].astype(f32).T.astype(bf16)
        base = high


def form_grad(hidden_t, rows_refs, grad_ref):
    for low in range(0, grad_ref.shape[1], UNIT):
        own = slice(low, low + UNIT)
        base = 0
        grad = 0.0
        for rows_ref in rows_refs:
            high = base + rows_ref.shape[0]
            grad += jnp.dot(
                hidden_t[:, base:high], rows_ref[:, own], preferred_element_type=f32
            )
            base = high
        grad_ref[:, own] = grad


def state_copies(i, step, low, hbm, vmem, sems, into):
    cols = vmem[0].shape[1]
    rows = pl.ds(pl.multiple_of(i * step, step), step)
    out = []
    for j, (far, near) in enumerate(zip(hbm, vmem)):
        ends = (far.at[0, rows, pl.ds(low, cols)], near.at[rows])
        source, target = ends if into else ends[::-1]
        out.append(pltpu.make_async_copy(source, target, sems.at[j, i]))
    return out


def settle_kernel(fresh, blocks, *refs):
    refs = list(refs)

    def take(number):
        out = refs[:number]
        del refs[:number]
        return out

    size = len(fresh)
    arrived = take(size)
    hidden_ref, hidden_t, given_ref, weight_ref, *state = take(7)
    scores, (mixed_ref,), projs_hbm, outs = take(size), take(1), take(size), take(3)
    news, rows_refs, projs = take(3), take(size), take(size)
    grad_ref, sems, proj_sems = refs
    part = grad_ref.shape[0]
    count = blocks * SEND
    shards = 1 + size
    for i in range(size):
        reorder(arrived[i][...], rows_refs[i])
    form_grad(hidden_t, [given_ref] + rows_refs, grad_ref)
    steps = sems.shape[1]
    step = part // steps

    @pl.loop(0, steps)
    def _(i):
        update_rows(i * step, step, state, news, grad_ref)
        for copy in state_copies(i, step, 0, outs, news, sems, False):
            copy.start()

    copies = []
    for i, s in enumerate(fresh):
        proj = times_weight(rows_refs[i], weight_ref)
        projs[i][...] = proj
        copies.append(pltpu.make_async_copy(projs[i], projs_hbm[i], proj_sems.at[i]))
        copies[i].start()
        scores[i][...] = score_block(
            blocks,
            proj,
            hidden_ref[s * count : (s + 1) * count],
            [block_index(blocks, count)],
        )[0]
    row = lax.broadcasted_iota(jnp.int32, (shards * count, count), 0)
    col = lax.broadcasted_iota(jnp.int32, (shards * count, count), 1)
    at, step_of, slot = mixed_place(row, shards)
    total = 0.0
    for s in range(shards):
        order = (step_of == s) & (col == at * SEND + slot)
        order = jnp.where(order, 1.0, 0.0).astype(bf16)
        own = hidden_ref[s * count : (s + 1) * count]
        total += jnp.dot(order, own, preferred_element_type=f32)
    mixed_ref[...] = total.astype(bf16)

    @pl.loop(0, steps)
    def _(i):
        for copy in state_copies(i, step, 0, outs, news, sems, False):
            copy.wait()

    for copy in copies:
        copy.wait()


def settle(blocks, arrived, given, hidden, hidden_t, weight, held, shapes):
    part, cols = weight.shape
    count = blocks * SEND
    fresh = tuple(range(1, 1 + len(arrived)))
    size = len(fresh)
    total = count * (1 + size)
    step = min(part, 64)
    args = [*arrived, hidden, hidden_t, given, weight, *held]
    near = [plain((blocks, 1, LANE), f32)] * size + [plain((total, part), bf16)]
    far = [out_hbm((count, part), f32)] * size
    far += [out_hbm(array.shape, array.dtype) for array in shapes]
    scratch = [pltpu.VMEM((part, cols), kind) for kind in (f32, bf16, bf16)]
    scratch += [pltpu.VMEM((count, cols), bf16)] * size
    scratch += [pltpu.VMEM((count, part), f32)] * size
    scratch += [
        pltpu.VMEM((part, cols), f32),
        pltpu.SemaphoreType.DMA((3, part // step)),
        pltpu.SemaphoreType.DMA((max(1, size),)),
    ]
    nbytes = 12 * part * cols + 4 * total * cols + 8 * total * part
    outs = pl.pallas_call(
        functools.partial(settle_kernel, fresh, blocks),
        in_specs=[VMEM] * len(args),
        out_specs=[VMEM] * len(near) + [HBM] * len(far),
        out_shape=near + far,
        scratch_shapes=scratch,
        compiler_params=params(nbytes),
        cost_estimate=cost(4 * total * part * cols, 16 * part * cols, part * cols),
    )(*args)
    outs = list(outs)
    return outs[:size], outs[size], outs[size + 1 : -3], outs[-3:]


def update_kernel(low, shards, hidden_ref, rows_ref, *refs):
    grad_refs, refs = refs[:shards], refs[shards:]
    factor_hbm, state_hbm, token_hbm, refs = refs[0], refs[1:4], refs[4:7], refs[10:]
    outs, gate_out, place_ref, inverse_ref, refs = refs[:3], *refs[3:6], refs[6:]
    state, tokens, refs = refs[:3], refs[3:6], refs[6:]
    hidden_t, grad_ref, factor_ref, gate_new, in_sems, out_sems, sems = refs
    part = grad_ref.shape[0]
    steps = in_sems.shape[1]
    step = part // steps
    gate_load = pltpu.make_async_copy(factor_hbm, factor_ref, sems.at[0])
    gate_store = pltpu.make_async_copy(gate_new, gate_out, sems.at[1])
    gate_load.start()
    token_loads = [
        pltpu.make_async_copy(source, target, sems.at[2 + i])
        for i, (source, target) in enumerate(zip(token_hbm, tokens))
    ]
    for copy in token_loads:
        copy.start()
    for i in range(steps):
        for copy in state_copies(i, step, low, state_hbm, state, in_sems, True):
            copy.start()
    transpose_rows([hidden_ref], hidden_t)
    form_grad(hidden_t, [rows_ref], grad_ref)
    for copy in token_loads:
        copy.wait()
    ids, slots = tokens[0][...], tokens[1][...]
    live = ((ids & (EXP_LOCAL - 1)) == 0) & (slots >= 0)
    place_ref[...] = jnp.where(live, ids // EXP_LOCAL * SEND + slots, -1)
    inverse_ref[...] = 1.0 / tokens[2][...].astype(f32)

    @pl.loop(0, steps)
    def _(i):
        for copy in state_copies(i, step, low, state_hbm, state, in_sems, True):
            copy.wait()
        update_rows(i * step, step, state, state, grad_ref)
        for copy in state_copies(i, step, low, outs, state, out_sems, False):
            copy.start()

    gate_load.wait()
    for s, ref in enumerate(grad_refs):
        width = ref.shape[1]
        grad = ref[...].astype(f32)
        for first in unit_columns(shards, s, width):
            own = pl.ds(first, width)
            gate_new[:, own] = (grad * factor_ref[:, own]).astype(bf16)
    gate_store.start()

    @pl.loop(0, steps)
    def _(i):
        for copy in state_copies(i, step, low, outs, state, out_sems, False):
            copy.wait()

    gate_store.wait()


def update(low, hidden, rows, grads, factors, state, tokens, done):
    total, part = hidden.shape
    cols = rows.shape[1]
    step = min(part, 64)
    shards = len(grads)
    scratch = [pltpu.VMEM((part, cols), kind) for kind in (f32, bf16, bf16)]
    scratch += [pltpu.VMEM(token.shape, token.dtype) for token in tokens]
    scratch += [pltpu.VMEM((part, total), bf16), pltpu.VMEM((part, cols), f32)]
    scratch += [pltpu.VMEM(factors.shape, kind) for kind in (f32, bf16)]
    scratch += [pltpu.SemaphoreType.DMA((3, part // step))] * 2
    scratch += [pltpu.SemaphoreType.DMA((5,))]
    return pl.pallas_call(
        functools.partial(update_kernel, low, shards),
        in_specs=[VMEM] * (2 + shards) + [HBM] * 10,
        out_specs=[HBM] * 4 + [VMEM] * 2,
        out_shape=[out_hbm(array.shape, array.dtype) for array in state]
        + [out_hbm(factors.shape, bf16)]
        + [plain(tokens[0].shape, kind) for kind in (jnp.int32, f32)],
        scratch_shapes=scratch,
        input_output_aliases={2 + shards + 7 + i: i for i in range(3)},
        compiler_params=params(12 * part * cols + 2 * total * part + 6 * factors.size),
        cost_estimate=cost(2 * total * part * cols, 16 * part * cols, part * cols),
    )(hidden, rows, *grads, *in_hbm(factors, *state, *tokens, *done))


def close_kernel(shards, place_ref, inverse_ref, score_ref, gate_ref):
    place = place_ref[...]
    blocks = score_ref.shape[0] // shards
    value = jnp.zeros(place.shape, f32)
    for b in range(blocks):
        for slot in range(SEND):
            score = score_ref[b, 0, slot]
            for s in range(1, shards):
                score += score_ref[s * blocks + b, 0, slot]
            value = jnp.where(place == b * SEND + slot, score, value)
    gate_ref[...] = value * inverse_ref[...]


def close(shards, place, inverse, score):
    return pl.pallas_call(
        functools.partial(close_kernel, shards),
        in_specs=[VMEM] * 2 + [pl.BlockSpec(memory_space=pltpu.SMEM)],
        out_specs=VMEM,
        out_shape=plain(place.shape, f32),
        compiler_params=params(0),
        cost_estimate=cost(1 << 20, 1 << 16),
    )(place, inverse, score)


def per_device(out_grad, expert_ids, slots, gate_weights, saved_gate_up, master, moment1, moment2):
    ep_size = lax.axis_size("ep")
    rep_size = lax.axis_size("rep")
    ids_t, slots_t, gates_t = expert_ids.T, slots.T, gate_weights.T
    gate_up = saved_gate_up[0, 0]
    state = (master, moment1, moment2)
    edges = chunk_edges(out_grad.shape[1])
    steps = range(1, rep_size)

    def shift(value, step):
        perm = [(i, (i + step) % rep_size) for i in range(rep_size)]
        return lax.ppermute(value, "rep", perm)

    def exchange(value):
        return lax.all_to_all(value, "ep", split_axis=0, concat_axis=0, tiled=True)

    send_a, send_b = dispatch(ep_size, edges, ids_t, slots_t, gates_t, out_grad)
    mixed = [shift(send_b, s) for s in steps]
    parts, factors = hidden_parts(gate_up, rep_size, send_b)
    arrived = exchange(send_a.reshape(ep_size, ROWS, -1)).reshape(send_a.shape)
    hidden = [parts[0]] + [shift(parts[s], s) for s in steps]
    mixed = mix([send_b] + mixed)
    hidden[1:], mixed = lax.optimization_barrier((hidden[1:], mixed))
    arrived_b = exchange(mixed.reshape(ep_size, rep_size * SEND, -1)).reshape(mixed.shape)

    peers = [shift(arrived, s) for s in steps]
    *held, weight_a, weight_b = load_state(edges[1], *state, arrived)
    rows, hidden, hidden_t, score_own, proj = begin(ep_size, arrived, weight_a, hidden)
    scores, hidden_mixed, before, done = settle(
        ep_size, peers, rows, hidden, hidden_t, weight_a, held, state
    )
    projs, score = finish(
        ep_size, arrived_b, hidden_mixed, weight_b, [proj] + before, [score_own] + scores
    )
    grads = [projs[0]] + [shift(projs[s], rep_size - s) for s in steps]
    score = lax.all_to_all(score, ("rep", "ep"), split_axis=0, concat_axis=0, tiled=True)

    tokens = (ids_t, slots_t, gates_t)
    *done, grad_gate_up, place, inverse = update(
        edges[1], hidden_mixed, arrived_b, grads, factors, state, tokens, done
    )
    gate_grad = close(rep_size, place, inverse, score).T
    return (grad_gate_up.reshape(saved_gate_up.shape), gate_grad) + tuple(done)


def solution(mesh):
    in_specs = (
        P(("rep", "ep"), None),
        P(("rep", "ep"), None),
        P(("rep", "ep"), None),
        P(("rep", "ep"), None),
        P("rep", "ep", None, None),
        P("ep", "rep", None),
        P("ep", "rep", None),
        P("ep", "rep", None),
    )
    out_specs = (
        P("rep", "ep", None, None),
        P(("rep", "ep"), None),
        P("ep", "rep", None),
        P("ep", "rep", None),
        P("ep", "rep", None),
    )
    return jax.shard_map(
        per_device, mesh=mesh, in_specs=in_specs, out_specs=out_specs, check_vma=False
    )
```

```python
import functools

import jax
import jax.numpy as jnp
from jax import lax
from jax.experimental import pallas as pl
from jax.experimental.pallas import tpu as pltpu
from jax.sharding import PartitionSpec as P

TOPK = 8
EXP_LOCAL = 8
SEND = 12
LANE = 128
UNIT = 512
ROWS = 16

beta_one = 0.9
beta_two = 0.95
learn_rate = 0.002
decay_rate = 0.1
adam_eps = 1e-08
adam_step = 50

f32 = jnp.float32
bf16 = jnp.bfloat16
HBM = pl.BlockSpec(memory_space=pltpu.HBM)
ANY = pl.BlockSpec(memory_space=pl.ANY)
VMEM = pl.BlockSpec(memory_space=pltpu.VMEM)


def in_hbm(*arrays):
    return [pltpu.with_memory_space_constraint(array, pltpu.HBM) for array in arrays]


def plain(dims, dtype):
    return jax.ShapeDtypeStruct(tuple(dims), dtype)


def out_hbm(dims, dtype):
    return pltpu.HBM(tuple(dims), dtype)


def block(dims, at=None):
    at = at or (0,) * len(dims)
    return pl.BlockSpec(tuple(dims), lambda i: at, pipeline_mode=pl.Buffered(1))


def params(nbytes):
    mib = min(60, max(16, 10 + 5 * int(nbytes) // 2**22))
    return pltpu.CompilerParams(vmem_limit_bytes=mib * 2**20)


def cost(flops, nbytes, transcendentals=0):
    return pl.CostEstimate(
        flops=int(flops), bytes_accessed=int(nbytes), transcendentals=int(transcendentals)
    )


def div_send(index):
    return lax.shift_right_logical(index * 10923, 17)


def pack(cols):
    return cols // 4 * 3


def chunk_edges(width):
    units = width // UNIT
    return (0, (units - max(1, units * 3 // 7)) * UNIT, width)


def tail_order(count, total, j, slots_first):
    a = lax.broadcasted_iota(jnp.int32, (count, total), 0)
    b = lax.broadcasted_iota(jnp.int32, (count, total), 1)
    if slots_first:
        block_of = div_send(a)
        inner = a - SEND * block_of
        hit = b == block_of * ROWS + SEND + inner - 4 * j
    else:
        inner = (a & (ROWS - 1)) - SEND + 4 * j
        hit = (b == a - SEND + 4 * j) & ((a & (ROWS - 1)) >= SEND)
    return jnp.where(hit & (inner >= 4 * j) & (inner < 4 * j + 4), 1.0, 0.0).astype(bf16)


def dispatch_kernel(edges, ids_hbm, slots_hbm, gates_hbm, grad_hbm, *refs):
    outs, (ids_ref, slots_ref, gates_ref, grad_ref, sems) = refs[:2], refs[2:]
    pairs = [(ids_hbm, ids_ref), (slots_hbm, slots_ref), (gates_hbm, gates_ref)]
    for c in (1, 0):
        own = (slice(None), pl.ds(edges[c], edges[c + 1] - edges[c]))
        pairs.append((grad_hbm.at[own], grad_ref.at[own]))
    copies = [
        pltpu.make_async_copy(source, target, sems.at[i])
        for i, (source, target) in enumerate(pairs)
    ]
    for copy in copies:
        copy.start()
    rows = outs[0].shape[0]
    tok = ids_ref.shape[1]
    orders = [tail_order(rows, rows, j, False) for j in range(3)]
    for copy in copies[:3]:
        copy.wait()
    ids = ids_ref[...]
    slots = slots_ref[...]
    gates = gates_ref[...].astype(f32)
    live = ((ids & (EXP_LOCAL - 1)) == 0) & (slots >= 0)
    place = jnp.where(live, ids // EXP_LOCAL * ROWS + slots, -1)
    row = lax.broadcasted_iota(jnp.int32, (rows, tok), 0)
    main = jnp.zeros((rows, tok), f32)
    for k in range(TOPK):
        main = jnp.where(row == place[k : k + 1], gates[k : k + 1], main)
    main = main.astype(bf16)
    tails = [
        jnp.dot(order, main, preferred_element_type=f32).astype(bf16) for order in orders
    ]
    for c in (1, 0):
        copies[4 - c].wait()
        low, high = edges[c], edges[c + 1]
        part = (high - low) // 4
        for j in range(3):
            total = jnp.dot(
                main,
                grad_ref[:, low + j * part : low + (j + 1) * part],
                preferred_element_type=f32,
            )
            total += jnp.dot(
                tails[j], grad_ref[:, low + 3 * part : high], preferred_element_type=f32
            )
            outs[c][:, j * part : (j + 1) * part] = total.astype(bf16)


def dispatch(blocks, edges, ids, slots, gates, out_grad):
    tok, width = out_grad.shape
    rows = blocks * ROWS
    shapes = [(rows, pack(high - low)) for low, high in zip(edges[:-1], edges[1:])]
    return pl.pallas_call(
        functools.partial(dispatch_kernel, edges),
        in_specs=[HBM] * 4,
        out_specs=[VMEM] * 2,
        out_shape=[plain(shape, bf16) for shape in shapes],
        scratch_shapes=[
            pltpu.VMEM(ids.shape, jnp.int32),
            pltpu.VMEM(slots.shape, jnp.int32),
            pltpu.VMEM(gates.shape, bf16),
            pltpu.VMEM(out_grad.shape, bf16),
            pltpu.SemaphoreType.DMA((5,)),
        ],
        compiler_params=params(2 * rows * width + 2 * tok * width),
        cost_estimate=cost(2 * rows * tok * width, 4 * tok * width),
    )(*in_hbm(ids, slots, gates, out_grad))


def unit_columns(shards, step, part):
    at = lax.rem(lax.axis_index("rep") + step, shards)
    return pl.multiple_of(at * part, part), pl.multiple_of((shards + at) * part, part)


def hidden_kernel(gate_up_ref, after_ref, *refs):
    del after_ref
    out_refs, factor_ref = refs[:-1], refs[-1]
    for s, out_ref in enumerate(out_refs):
        part = out_ref.shape[1]
        low, high = unit_columns(len(out_refs), s, part)
        gate = gate_up_ref[:, pl.ds(low, part)].astype(f32)
        up = gate_up_ref[:, pl.ds(high, part)].astype(f32)
        sig = jax.nn.sigmoid(gate)
        silu = gate * sig
        out_ref[...] = (silu * up).astype(bf16)
        factor_ref[:, pl.ds(low, part)] = up * sig * (1.0 + gate * (1.0 - sig))
        factor_ref[:, pl.ds(high, part)] = silu


def hidden_parts(gate_up, shards, after):
    slots, width = gate_up.shape
    shape = (slots, width // 2 // shards)
    outs = pl.pallas_call(
        hidden_kernel,
        grid=(1,),
        in_specs=[block(gate_up.shape), ANY],
        out_specs=[block(shape)] * shards + [block(gate_up.shape)],
        out_shape=[out_hbm(shape, bf16)] * shards + [out_hbm(gate_up.shape, f32)],
        compiler_params=params(7 * slots * width),
        cost_estimate=cost(8 * slots * width, 7 * slots * width, slots * width),
    )(*in_hbm(gate_up), after)
    return list(outs[:-1]), outs[-1]


def load_kernel(middle, after_ref, master_hbm, one_hbm, two_hbm, *refs):
    del after_ref
    master_ref, one_ref, two_ref, weight_a, weight_b, rest_ref, sems = refs
    part = master_ref.shape[0]
    rest = rest_ref.shape[1]
    step = part // 4
    copies = []
    for i in range(4):
        own = pl.ds(i * step, step)
        copies.append(
            pltpu.make_async_copy(
                master_hbm.at[0, own, pl.ds(0, middle)], master_ref.at[own], sems.at[i]
            )
        )
    for i in range(4):
        own = pl.ds(i * step, step)
        copies.append(
            pltpu.make_async_copy(
                master_hbm.at[0, own, pl.ds(middle, rest)], rest_ref.at[own], sems.at[4 + i]
            )
        )
    for i, (source, target) in enumerate([(one_hbm, one_ref), (two_hbm, two_ref)]):
        copies.append(
            pltpu.make_async_copy(source.at[0, :, pl.ds(0, middle)], target, sems.at[8 + i])
        )
    for copy in copies:
        copy.start()
    for i in range(4):
        copies[i].wait()
        own = slice(i * step, (i + 1) * step)
        weight_a[own, :] = master_ref[own, :].astype(bf16)
    for i in range(4):
        copies[4 + i].wait()
        own = slice(i * step, (i + 1) * step)
        weight_b[own, :] = rest_ref[own, :].astype(bf16)
    copies[8].wait()
    copies[9].wait()


def load_state(middle, master, one, two, after):
    _, part, width = master.shape
    return pl.pallas_call(
        functools.partial(load_kernel, middle),
        in_specs=[ANY] + [HBM] * 3,
        out_specs=[VMEM] * 5,
        out_shape=[
            pltpu.VMEM((part, middle), f32),
            pltpu.VMEM((part, middle), bf16),
            pltpu.VMEM((part, middle), bf16),
            pltpu.VMEM((part, middle), bf16),
            pltpu.VMEM((part, width - middle), bf16),
        ],
        scratch_shapes=[
            pltpu.VMEM((part, width - middle), f32),
            pltpu.SemaphoreType.DMA((10,)),
        ],
        compiler_params=params(4 * part * (width - middle)),
        cost_estimate=cost(part * width, 14 * part * width),
    )(after, *in_hbm(master, one, two))


def mixed_place(index, shards):
    group = div_send(index)
    bits = shards.bit_length() - 1
    step = group & (shards - 1)
    return lax.shift_right_logical(group, bits), step, index - SEND * group


def mix_kernel(shards, *refs):
    parts, (out_hbm_ref, out_ref, sems) = refs[:shards], refs[shards:]
    part = parts[0].shape[1] // 3
    copies = []
    blocks = parts[0].shape[0] // ROWS
    some = min(blocks, 32 // shards)
    rows, packed = some * shards * SEND, some * shards * ROWS
    row = lax.broadcasted_iota(jnp.int32, (rows, packed), 0)
    col = lax.broadcasted_iota(jnp.int32, (rows, packed), 1)
    at, step, slot = mixed_place(row, shards)
    base = (step * some + at) * ROWS
    orders = [jnp.where(col == base + slot, 1.0, 0.0).astype(bf16)]
    for j in range(3):
        hit = (col == base + SEND + slot - 4 * j) & (slot >= 4 * j) & (slot < 4 * j + 4)
        orders.append(jnp.where(hit, 1.0, 0.0).astype(bf16))
    for first in range(0, blocks, some):
        stack = jnp.concatenate(
            [ref[first * ROWS : (first + some) * ROWS, :] for ref in parts], axis=0
        )
        own = slice(first * shards * SEND, (first + some) * shards * SEND)
        place = pl.ds(first * shards * SEND, some * shards * SEND)
        index = first // some

        def send(j):
            at = (place, pl.ds(j * part, part))
            copy = pltpu.make_async_copy(out_ref.at[at], out_hbm_ref.at[at], sems.at[j, index])
            copy.start()
            copies.append(copy)

        for j in range(3):
            out_ref[own, j * part : (j + 1) * part] = jnp.dot(
                orders[0], stack[:, j * part : (j + 1) * part], preferred_element_type=f32
            ).astype(bf16)
            send(j)
        tail = jnp.zeros((rows, part), f32)
        for j in range(3):
            tail += jnp.dot(
                orders[1 + j],
                stack[:, j * part : (j + 1) * part],
                preferred_element_type=f32,
            )
        out_ref[own, 3 * part :] = tail.astype(bf16)
        send(3)
    for copy in copies:
        copy.wait()


def mix(parts):
    shards = len(parts)
    rows, packed = parts[0].shape
    shape = (rows // ROWS * SEND * shards, packed // 3 * 4)
    return pl.pallas_call(
        functools.partial(mix_kernel, shards),
        in_specs=[VMEM] * shards,
        out_specs=HBM,
        out_shape=out_hbm(shape, bf16),
        scratch_shapes=[
            pltpu.VMEM(shape, bf16),
            pltpu.SemaphoreType.DMA((4, rows // ROWS // min(rows // ROWS, 32 // shards))),
        ],
        compiler_params=params(12 * rows * packed * shards),
        cost_estimate=cost(0, 5 * rows * packed * shards),
    )(*parts)


def reorder(arrived, rows_ref):
    count, width = rows_ref.shape
    part = width // 4
    total = arrived.shape[0]
    slot = lax.broadcasted_iota(jnp.int32, (count, total), 0)
    col = lax.broadcasted_iota(jnp.int32, (count, total), 1)
    order = jnp.where(col == slot + (ROWS - SEND) * div_send(slot), 1.0, 0.0).astype(bf16)
    rows_ref[:, : 3 * part] = jnp.dot(order, arrived, preferred_element_type=f32).astype(bf16)
    tail = jnp.zeros((count, part), f32)
    for j in range(3):
        tail += jnp.dot(
            tail_order(count, total, j, True),
            arrived[:, j * part : (j + 1) * part],
            preferred_element_type=f32,
        )
    rows_ref[:, 3 * part :] = tail.astype(bf16)


def times_weight(rows_ref, weight_ref):
    return lax.dot_general(
        rows_ref[...], weight_ref[...], (((1,), (1,)), ((), ())), preferred_element_type=f32
    )


def score_block(blocks, proj, hidden, picked):
    count = proj.shape[0]
    score = jnp.sum(proj * hidden.astype(f32), axis=1, keepdims=True)
    row = lax.broadcasted_iota(jnp.int32, (count, LANE), 0)
    lane = lax.broadcasted_iota(jnp.int32, (count, LANE), 1)
    spread = jnp.where(row - SEND * div_send(row) == lane, score, 0.0)
    high = spread.astype(bf16)
    rest = (spread - high.astype(f32)).astype(bf16)
    at = lax.broadcasted_iota(jnp.int32, (blocks, count), 1)
    gather = [jnp.where(div_send(at) == pick, 1.0, 0.0) for pick in picked]
    gather = jnp.concatenate(gather, axis=0).astype(bf16)
    value = jnp.dot(gather, high, preferred_element_type=f32)
    value += jnp.dot(gather, rest, preferred_element_type=f32)
    return [
        value[i * blocks : (i + 1) * blocks].reshape(blocks, 1, LANE)
        for i in range(len(picked))
    ]


def block_index(blocks, count):
    return lax.broadcasted_iota(jnp.int32, (blocks, count), 0)


def begin_kernel(blocks, arrived_ref, weight_ref, *refs):
    size = len(refs) - 7
    hidden_hbm, (rows_ref, hidden_ref, hidden_t, score_ref) = refs[:size], refs[size:-3]
    proj_hbm, proj_ref, sems = refs[-3:]
    count = rows_ref.shape[0]
    loads = [
        pltpu.make_async_copy(ref, hidden_ref.at[pl.ds(s * count, count)], sems.at[1 + s])
        for s, ref in enumerate(hidden_hbm)
    ]
    for copy in loads:
        copy.start()
    reorder(arrived_ref[...], rows_ref)
    proj = times_weight(rows_ref, weight_ref)
    proj_ref[...] = proj
    copy = pltpu.make_async_copy(proj_ref, proj_hbm, sems.at[0])
    copy.start()
    for load in loads:
        load.wait()
    score_ref[...] = score_block(
        blocks, proj, hidden_ref[:count], [block_index(blocks, count)]
    )[0]
    transpose_rows([hidden_ref], hidden_t)
    copy.wait()


def begin(blocks, arrived, weight, hidden):
    count = blocks * SEND
    part, cols = weight.shape
    total = count * len(hidden)
    return pl.pallas_call(
        functools.partial(begin_kernel, blocks),
        in_specs=[VMEM] * 2 + [HBM] * len(hidden),
        out_specs=[VMEM] * 4 + [HBM],
        out_shape=[
            plain((count, cols), bf16),
            plain((total, part), bf16),
            plain((part, total), bf16),
            plain((blocks, 1, LANE), f32),
            out_hbm((count, part), f32),
        ],
        scratch_shapes=[
            pltpu.VMEM((count, part), f32),
            pltpu.SemaphoreType.DMA((1 + len(hidden),)),
        ],
        compiler_params=params(8 * count * cols + 16 * total * part),
        cost_estimate=cost(4 * count * part * cols, 2 * part * cols),
    )(arrived, weight, *in_hbm(*hidden))


def finish_kernel(shards, blocks, arrived_ref, hidden_ref, weight_ref, *refs):
    before_hbm, score_in = refs[:shards], refs[shards : 2 * shards]
    projs, (score_ref, before, sems) = refs[2 * shards : 3 * shards], refs[3 * shards :]
    copies = [
        pltpu.make_async_copy(ref, before.at[s], sems.at[s])
        for s, ref in enumerate(before_hbm)
    ]
    for copy in copies:
        copy.start()
    proj = times_weight(arrived_ref, weight_ref)
    rounded = proj.astype(bf16)
    total = proj.shape[0]
    count = total // shards
    picked = [block_index(blocks, total) * shards + s for s in range(shards)]
    scores = score_block(blocks, proj, hidden_ref[...], picked)
    me = lax.axis_index("rep")
    slot = lax.broadcasted_iota(jnp.int32, (count, total), 0)
    row = lax.broadcasted_iota(jnp.int32, (count, total), 1)
    for s in range(shards):
        order = row == slot + SEND * (div_send(slot) * (shards - 1) + s)
        order = jnp.where(order, 1.0, 0.0).astype(bf16)
        own = jnp.dot(order, rounded, preferred_element_type=f32)
        copies[s].wait()
        own += before[s]
        projs[s][...] = own.astype(bf16)
        at = lax.rem(me + shards - s, shards)
        score_ref[pl.ds(at * blocks, blocks)] = score_in[s][...] + scores[s]


def finish(blocks, arrived, hidden, weight, before, scores):
    shards = len(before)
    total, part = hidden.shape
    count = total // shards
    cols = weight.shape[1]
    outs = pl.pallas_call(
        functools.partial(finish_kernel, shards, blocks),
        in_specs=[VMEM] * 3 + [HBM] * shards + [VMEM] * shards,
        out_specs=[VMEM] * (shards + 1),
        out_shape=[plain((count, part), bf16)] * shards
        + [plain((shards * blocks, 1, LANE), f32)],
        scratch_shapes=[
            pltpu.VMEM((shards, count, part), f32),
            pltpu.SemaphoreType.DMA((shards,)),
        ],
        compiler_params=params(20 * total * part),
        cost_estimate=cost(2 * total * part * cols, 2 * part * cols),
    )(arrived, hidden, weight, *in_hbm(*before), *scores)
    return list(outs[:-1]), outs[-1]


def new_state(master, one, two, grad):
    corr_one = 1.0 - beta_one**adam_step
    corr_two = 1.0 - beta_two**adam_step
    rate = learn_rate * corr_two**0.5 / corr_one
    keep = 1.0 - learn_rate * decay_rate
    eps = adam_eps * corr_two**0.5
    m_new = beta_one * one.astype(f32) + (1.0 - beta_one) * grad
    v_new = beta_two * two.astype(f32) + (1.0 - beta_two) * (grad * grad)
    root = lax.rsqrt(v_new)
    below = v_new * root + eps
    inverse = root * (2.0 - below * root)
    master = keep * master - (rate * m_new) * inverse
    return master, m_new.astype(bf16), v_new.astype(bf16)


def update_rows(first, count, state, news, grad_ref):
    cols = grad_ref.shape[1]

    @pl.loop(0, count // ROWS)
    def _(i):
        own = pl.ds(pl.multiple_of(first + i * ROWS, ROWS), ROWS)
        for low in range(0, cols, UNIT):
            at = (own, slice(low, low + UNIT))
            values = new_state(*[ref[at] for ref in state], grad_ref[at])
            for ref, value in zip(news, values):
                ref[at] = value


def transpose_rows(hidden, hidden_t):
    base = 0
    for ref in hidden:
        high = base + ref.shape[0]
        hidden_t[:, base:high] = ref[...].astype(f32).T.astype(bf16)
        base = high


def form_grad(hidden_t, rows_refs, grad_ref):
    for low in range(0, grad_ref.shape[1], UNIT):
        own = slice(low, low + UNIT)
        base = 0
        grad = 0.0
        for rows_ref in rows_refs:
            high = base + rows_ref.shape[0]
            grad += jnp.dot(
                hidden_t[:, base:high], rows_ref[:, own], preferred_element_type=f32
            )
            base = high
        grad_ref[:, own] = grad


def state_copies(i, low, hbm, vmem, sems, into):
    part, cols = vmem[0].shape
    step = part // sems.shape[1]
    rows = pl.ds(pl.multiple_of(i * step, step), step)
    out = []
    for j, (far, near) in enumerate(zip(hbm, vmem)):
        ends = (far.at[0, rows, pl.ds(low, cols)], near.at[rows])
        source, target = ends if into else ends[::-1]
        out.append(pltpu.make_async_copy(source, target, sems.at[j, i]))
    return out


def settle_kernel(fresh, blocks, *refs):
    refs = list(refs)

    def take(number):
        out = refs[:number]
        del refs[:number]
        return out

    size = len(fresh)
    arrived = take(size)
    hidden_ref, hidden_t, given_ref, weight_ref, *state = take(7)
    scores, (mixed_ref,), projs_hbm, outs = take(size), take(1), take(size), take(3)
    news, rows_refs, projs = take(3), take(size), take(size)
    grad_ref, sems, proj_sems = refs
    part = grad_ref.shape[0]
    count = blocks * SEND
    shards = 1 + size
    for i in range(size):
        reorder(arrived[i][...], rows_refs[i])
    form_grad(hidden_t, [given_ref] + rows_refs, grad_ref)
    steps = sems.shape[1]
    step = part // steps

    @pl.loop(0, steps)
    def _(i):
        update_rows(i * step, step, state, news, grad_ref)
        for copy in state_copies(i, 0, outs, news, sems, False):
            copy.start()

    copies = []
    for i, s in enumerate(fresh):
        proj = times_weight(rows_refs[i], weight_ref)
        projs[i][...] = proj
        copies.append(pltpu.make_async_copy(projs[i], projs_hbm[i], proj_sems.at[i]))
        copies[i].start()
        scores[i][...] = score_block(
            blocks,
            proj,
            hidden_ref[s * count : (s + 1) * count],
            [block_index(blocks, count)],
        )[0]
    row = lax.broadcasted_iota(jnp.int32, (shards * count, count), 0)
    col = lax.broadcasted_iota(jnp.int32, (shards * count, count), 1)
    at, step_of, slot = mixed_place(row, shards)
    total = 0.0
    for s in range(shards):
        order = (step_of == s) & (col == at * SEND + slot)
        order = jnp.where(order, 1.0, 0.0).astype(bf16)
        own = hidden_ref[s * count : (s + 1) * count]
        total += jnp.dot(order, own, preferred_element_type=f32)
    mixed_ref[...] = total.astype(bf16)

    @pl.loop(0, steps)
    def _(i):
        for copy in state_copies(i, 0, outs, news, sems, False):
            copy.wait()

    for copy in copies:
        copy.wait()


def settle(blocks, arrived, given, hidden, hidden_t, weight, held, shapes):
    part, cols = weight.shape
    count = blocks * SEND
    fresh = tuple(range(1, 1 + len(arrived)))
    size = len(fresh)
    total = count * (1 + size)
    step = min(part, 128)
    args = [*arrived, hidden, hidden_t, given, weight, *held]
    near = [plain((blocks, 1, LANE), f32)] * size + [plain((total, part), bf16)]
    far = [out_hbm((count, part), f32)] * size
    far += [out_hbm(array.shape, array.dtype) for array in shapes]
    scratch = [pltpu.VMEM((part, cols), kind) for kind in (f32, bf16, bf16)]
    scratch += [pltpu.VMEM((count, cols), bf16)] * size
    scratch += [pltpu.VMEM((count, part), f32)] * size
    scratch += [
        pltpu.VMEM((part, cols), f32),
        pltpu.SemaphoreType.DMA((3, part // step)),
        pltpu.SemaphoreType.DMA((max(1, size),)),
    ]
    nbytes = 12 * part * cols + 4 * total * cols + 8 * total * part
    outs = pl.pallas_call(
        functools.partial(settle_kernel, fresh, blocks),
        in_specs=[VMEM] * len(args),
        out_specs=[VMEM] * len(near) + [HBM] * len(far),
        out_shape=near + far,
        scratch_shapes=scratch,
        compiler_params=params(nbytes),
        cost_estimate=cost(4 * total * part * cols, 16 * part * cols, part * cols),
    )(*args)
    outs = list(outs)
    return outs[:size], outs[size], outs[size + 1 : -3], outs[-3:]


def update_kernel(low, shards, hidden_ref, rows_ref, *refs):
    grad_refs, refs = refs[:shards], refs[shards:]
    factor_hbm, state_hbm, token_hbm, refs = refs[0], refs[1:4], refs[4:7], refs[10:]
    outs, gate_out, place_ref, inverse_ref, refs = refs[:3], *refs[3:6], refs[6:]
    state, tokens, refs = refs[:3], refs[3:6], refs[6:]
    hidden_t, grad_ref, factor_ref, gate_new, in_sems, out_sems, sems = refs
    part = grad_ref.shape[0]
    steps = out_sems.shape[1]
    step = part // steps
    loads = in_sems.shape[1]
    gate_load = pltpu.make_async_copy(factor_hbm, factor_ref, sems.at[0])
    gate_store = pltpu.make_async_copy(gate_new, gate_out, sems.at[1])
    gate_load.start()
    token_loads = [
        pltpu.make_async_copy(source, target, sems.at[2 + i])
        for i, (source, target) in enumerate(zip(token_hbm, tokens))
    ]
    for copy in token_loads:
        copy.start()
    for i in range(loads):
        for copy in state_copies(i, low, state_hbm, state, in_sems, True):
            copy.start()
    transpose_rows([hidden_ref], hidden_t)
    form_grad(hidden_t, [rows_ref], grad_ref)
    for copy in token_loads:
        copy.wait()
    ids, slots = tokens[0][...], tokens[1][...]
    live = ((ids & (EXP_LOCAL - 1)) == 0) & (slots >= 0)
    place_ref[...] = jnp.where(live, ids // EXP_LOCAL * SEND + slots, -1)
    inverse_ref[...] = 1.0 / tokens[2][...].astype(f32)

    for i in range(steps):
        if i % (steps // loads) == 0:
            for copy in state_copies(i * loads // steps, low, state_hbm, state, in_sems, True):
                copy.wait()
        update_rows(i * step, step, state, state, grad_ref)
        for copy in state_copies(i, low, outs, state, out_sems, False):
            copy.start()

    gate_load.wait()
    for s, ref in enumerate(grad_refs):
        width = ref.shape[1]
        grad = ref[...].astype(f32)
        for first in unit_columns(shards, s, width):
            own = pl.ds(first, width)
            gate_new[:, own] = (grad * factor_ref[:, own]).astype(bf16)
    gate_store.start()

    @pl.loop(0, steps)
    def _(i):
        for copy in state_copies(i, low, outs, state, out_sems, False):
            copy.wait()

    gate_store.wait()


def update(low, hidden, rows, grads, factors, state, tokens, done):
    total, part = hidden.shape
    cols = rows.shape[1]
    step = min(part, 128)
    shards = len(grads)
    scratch = [pltpu.VMEM((part, cols), kind) for kind in (f32, bf16, bf16)]
    scratch += [pltpu.VMEM(token.shape, token.dtype) for token in tokens]
    scratch += [pltpu.VMEM((part, total), bf16), pltpu.VMEM((part, cols), f32)]
    scratch += [pltpu.VMEM(factors.shape, kind) for kind in (f32, bf16)]
    steps = part // step
    scratch += [pltpu.SemaphoreType.DMA((3, count)) for count in (min(2, steps), steps)]
    scratch += [pltpu.SemaphoreType.DMA((5,))]
    return pl.pallas_call(
        functools.partial(update_kernel, low, shards),
        in_specs=[VMEM] * (2 + shards) + [HBM] * 10,
        out_specs=[HBM] * 4 + [VMEM] * 2,
        out_shape=[out_hbm(array.shape, array.dtype) for array in state]
        + [out_hbm(factors.shape, bf16)]
        + [plain(tokens[0].shape, kind) for kind in (jnp.int32, f32)],
        scratch_shapes=scratch,
        input_output_aliases={2 + shards + 7 + i: i for i in range(3)},
        compiler_params=params(12 * part * cols + 2 * total * part + 6 * factors.size),
        cost_estimate=cost(2 * total * part * cols, 16 * part * cols, part * cols),
    )(hidden, rows, *grads, *in_hbm(factors, *state, *tokens, *done))


def close_kernel(shards, place_ref, inverse_ref, score_ref, gate_ref):
    place = place_ref[...]
    blocks = score_ref.shape[0] // shards
    value = jnp.zeros(place.shape, f32)
    for b in range(blocks):
        for slot in range(SEND):
            score = score_ref[b, 0, slot]
            for s in range(1, shards):
                score += score_ref[s * blocks + b, 0, slot]
            value = jnp.where(place == b * SEND + slot, score, value)
    gate_ref[...] = value * inverse_ref[...]


def close(shards, place, inverse, score):
    return pl.pallas_call(
        functools.partial(close_kernel, shards),
        in_specs=[VMEM] * 2 + [pl.BlockSpec(memory_space=pltpu.SMEM)],
        out_specs=VMEM,
        out_shape=plain(place.shape, f32),
        compiler_params=params(0),
        cost_estimate=cost(1 << 20, 1 << 16),
    )(place, inverse, score)


def per_device(out_grad, expert_ids, slots, gate_weights, saved_gate_up, master, moment1, moment2):
    ep_size = lax.axis_size("ep")
    rep_size = lax.axis_size("rep")
    ids_t, slots_t, gates_t = expert_ids.T, slots.T, gate_weights.T
    gate_up = saved_gate_up[0, 0]
    state = (master, moment1, moment2)
    edges = chunk_edges(out_grad.shape[1])
    steps = range(1, rep_size)

    def shift(value, step):
        perm = [(i, (i + step) % rep_size) for i in range(rep_size)]
        return lax.ppermute(value, "rep", perm)

    def exchange(value):
        return lax.all_to_all(value, "ep", split_axis=0, concat_axis=0, tiled=True)

    send_a, send_b = dispatch(ep_size, edges, ids_t, slots_t, gates_t, out_grad)
    mixed = [shift(send_b, s) for s in steps]
    parts, factors = hidden_parts(gate_up, rep_size, send_b)
    arrived = exchange(send_a.reshape(ep_size, ROWS, -1)).reshape(send_a.shape)
    hidden = [parts[0]] + [shift(parts[s], s) for s in steps]
    mixed = mix([send_b] + mixed)
    hidden[1:], mixed = lax.optimization_barrier((hidden[1:], mixed))
    arrived_b = exchange(mixed.reshape(ep_size, rep_size * SEND, -1)).reshape(mixed.shape)

    peers = [shift(arrived, s) for s in steps]
    *held, weight_a, weight_b = load_state(edges[1], *state, arrived)
    rows, hidden, hidden_t, score_own, proj = begin(ep_size, arrived, weight_a, hidden)
    scores, hidden_mixed, before, done = settle(
        ep_size, peers, rows, hidden, hidden_t, weight_a, held, state
    )
    projs, score = finish(
        ep_size, arrived_b, hidden_mixed, weight_b, [proj] + before, [score_own] + scores
    )
    grads = [projs[0]] + [shift(projs[s], rep_size - s) for s in steps]
    score = lax.all_to_all(score, ("rep", "ep"), split_axis=0, concat_axis=0, tiled=True)

    tokens = (ids_t, slots_t, gates_t)
    *done, grad_gate_up, place, inverse = update(
        edges[1], hidden_mixed, arrived_b, grads, factors, state, tokens, done
    )
    gate_grad = close(rep_size, place, inverse, score).T
    return (grad_gate_up.reshape(saved_gate_up.shape), gate_grad) + tuple(done)


def solution(mesh):
    in_specs = (
        P(("rep", "ep"), None),
        P(("rep", "ep"), None),
        P(("rep", "ep"), None),
        P(("rep", "ep"), None),
        P("rep", "ep", None, None),
        P("ep", "rep", None),
        P("ep", "rep", None),
        P("ep", "rep", None),
    )
    out_specs = (
        P("rep", "ep", None, None),
        P(("rep", "ep"), None),
        P("ep", "rep", None),
        P("ep", "rep", None),
        P("ep", "rep", None),
    )
    return jax.shard_map(
        per_device, mesh=mesh, in_specs=in_specs, out_specs=out_specs, check_vma=False
    )
```

```python
import functools

import jax
import jax.numpy as jnp
from jax import lax
from jax.experimental import pallas as pl
from jax.experimental.pallas import tpu as pltpu
from jax.sharding import PartitionSpec as P

TOPK = 8
EXP_LOCAL = 8
SEND = 12
LANE = 128
UNIT = 512
ROWS = 16

beta_one = 0.9
beta_two = 0.95
learn_rate = 0.002
decay_rate = 0.1
adam_eps = 1e-08
adam_step = 50

f32 = jnp.float32
bf16 = jnp.bfloat16
HBM = pl.BlockSpec(memory_space=pltpu.HBM)
ANY = pl.BlockSpec(memory_space=pl.ANY)
VMEM = pl.BlockSpec(memory_space=pltpu.VMEM)


def in_hbm(*arrays):
    return [pltpu.with_memory_space_constraint(array, pltpu.HBM) for array in arrays]


def plain(dims, dtype):
    return jax.ShapeDtypeStruct(tuple(dims), dtype)


def out_hbm(dims, dtype):
    return pltpu.HBM(tuple(dims), dtype)


def block(dims, at=None):
    at = at or (0,) * len(dims)
    return pl.BlockSpec(tuple(dims), lambda i: at, pipeline_mode=pl.Buffered(1))


def params(nbytes):
    mib = min(60, max(16, 10 + 5 * int(nbytes) // 2**22))
    return pltpu.CompilerParams(vmem_limit_bytes=mib * 2**20)


def cost(flops, nbytes, transcendentals=0):
    return pl.CostEstimate(
        flops=int(flops), bytes_accessed=int(nbytes), transcendentals=int(transcendentals)
    )


def div_send(index):
    return lax.shift_right_logical(index * 10923, 17)


def pack(cols):
    return cols // 4 * 3


def chunk_edges(width):
    units = width // UNIT
    return (0, (units - max(1, units * 3 // 7)) * UNIT, width)


def tail_order(count, total, j, slots_first):
    a = lax.broadcasted_iota(jnp.int32, (count, total), 0)
    b = lax.broadcasted_iota(jnp.int32, (count, total), 1)
    if slots_first:
        block_of = div_send(a)
        inner = a - SEND * block_of
        hit = b == block_of * ROWS + SEND + inner - 4 * j
    else:
        inner = (a & (ROWS - 1)) - SEND + 4 * j
        hit = (b == a - SEND + 4 * j) & ((a & (ROWS - 1)) >= SEND)
    return jnp.where(hit & (inner >= 4 * j) & (inner < 4 * j + 4), 1.0, 0.0).astype(bf16)


def dispatch_kernel(edges, ids_hbm, slots_hbm, gates_hbm, grad_hbm, *refs):
    outs, (ids_ref, slots_ref, gates_ref, grad_ref, sems) = refs[:2], refs[2:]
    pairs = [(ids_hbm, ids_ref), (slots_hbm, slots_ref), (gates_hbm, gates_ref)]
    for c in (1, 0):
        own = (slice(None), pl.ds(edges[c], edges[c + 1] - edges[c]))
        pairs.append((grad_hbm.at[own], grad_ref.at[own]))
    copies = [
        pltpu.make_async_copy(source, target, sems.at[i])
        for i, (source, target) in enumerate(pairs)
    ]
    for copy in copies:
        copy.start()
    rows = outs[0].shape[0]
    tok = ids_ref.shape[1]
    orders = [tail_order(rows, rows, j, False) for j in range(3)]
    for copy in copies[:3]:
        copy.wait()
    ids = ids_ref[...]
    slots = slots_ref[...]
    gates = gates_ref[...].astype(f32)
    live = ((ids & (EXP_LOCAL - 1)) == 0) & (slots >= 0)
    place = jnp.where(live, ids // EXP_LOCAL * ROWS + slots, -1)
    row = lax.broadcasted_iota(jnp.int32, (rows, tok), 0)
    main = jnp.zeros((rows, tok), f32)
    for k in range(TOPK):
        main = jnp.where(row == place[k : k + 1], gates[k : k + 1], main)
    main = main.astype(bf16)
    tails = [
        jnp.dot(order, main, preferred_element_type=f32).astype(bf16) for order in orders
    ]
    for c in (1, 0):
        copies[4 - c].wait()
        low, high = edges[c], edges[c + 1]
        part = (high - low) // 4
        for j in range(3):
            total = jnp.dot(
                main,
                grad_ref[:, low + j * part : low + (j + 1) * part],
                preferred_element_type=f32,
            )
            total += jnp.dot(
                tails[j], grad_ref[:, low + 3 * part : high], preferred_element_type=f32
            )
            outs[c][:, j * part : (j + 1) * part] = total.astype(bf16)


def dispatch(blocks, edges, ids, slots, gates, out_grad):
    tok, width = out_grad.shape
    rows = blocks * ROWS
    shapes = [(rows, pack(high - low)) for low, high in zip(edges[:-1], edges[1:])]
    return pl.pallas_call(
        functools.partial(dispatch_kernel, edges),
        in_specs=[HBM] * 4,
        out_specs=[VMEM] * 2,
        out_shape=[plain(shape, bf16) for shape in shapes],
        scratch_shapes=[
            pltpu.VMEM(ids.shape, jnp.int32),
            pltpu.VMEM(slots.shape, jnp.int32),
            pltpu.VMEM(gates.shape, bf16),
            pltpu.VMEM(out_grad.shape, bf16),
            pltpu.SemaphoreType.DMA((5,)),
        ],
        compiler_params=params(2 * rows * width + 2 * tok * width),
        cost_estimate=cost(2 * rows * tok * width, 4 * tok * width),
    )(*in_hbm(ids, slots, gates, out_grad))


def unit_columns(shards, step, part):
    at = lax.rem(lax.axis_index("rep") + step, shards)
    return pl.multiple_of(at * part, part), pl.multiple_of((shards + at) * part, part)


def hidden_kernel(gate_up_ref, after_ref, *refs):
    del after_ref
    out_refs, factor_ref = refs[:-1], refs[-1]
    for s, out_ref in enumerate(out_refs):
        part = out_ref.shape[1]
        low, high = unit_columns(len(out_refs), s, part)
        gate = gate_up_ref[:, pl.ds(low, part)].astype(f32)
        up = gate_up_ref[:, pl.ds(high, part)].astype(f32)
        sig = jax.nn.sigmoid(gate)
        silu = gate * sig
        out_ref[...] = (silu * up).astype(bf16)
        factor_ref[:, pl.ds(low, part)] = up * sig * (1.0 + gate * (1.0 - sig))
        factor_ref[:, pl.ds(high, part)] = silu


def hidden_parts(gate_up, shards, after):
    slots, width = gate_up.shape
    shape = (slots, width // 2 // shards)
    outs = pl.pallas_call(
        hidden_kernel,
        grid=(1,),
        in_specs=[block(gate_up.shape), ANY],
        out_specs=[block(shape)] * shards + [block(gate_up.shape)],
        out_shape=[out_hbm(shape, bf16)] * shards + [out_hbm(gate_up.shape, f32)],
        compiler_params=params(7 * slots * width),
        cost_estimate=cost(8 * slots * width, 7 * slots * width, slots * width),
    )(*in_hbm(gate_up), after)
    return list(outs[:-1]), outs[-1]


def load_kernel(middle, after_ref, master_hbm, one_hbm, two_hbm, *refs):
    del after_ref
    master_ref, one_ref, two_ref, weight_a, weight_b, rest_ref, sems = refs
    part = master_ref.shape[0]
    rest = rest_ref.shape[1]
    step = part // 4
    copies = []
    for i in range(4):
        own = pl.ds(i * step, step)
        copies.append(
            pltpu.make_async_copy(
                master_hbm.at[0, own, pl.ds(0, middle)], master_ref.at[own], sems.at[i]
            )
        )
    for i in range(4):
        own = pl.ds(i * step, step)
        copies.append(
            pltpu.make_async_copy(
                master_hbm.at[0, own, pl.ds(middle, rest)], rest_ref.at[own], sems.at[4 + i]
            )
        )
    for i, (source, target) in enumerate([(one_hbm, one_ref), (two_hbm, two_ref)]):
        copies.append(
            pltpu.make_async_copy(source.at[0, :, pl.ds(0, middle)], target, sems.at[8 + i])
        )
    for copy in copies:
        copy.start()
    for i in range(4):
        copies[i].wait()
        own = slice(i * step, (i + 1) * step)
        weight_a[own, :] = master_ref[own, :].astype(bf16)
    for i in range(4):
        copies[4 + i].wait()
        own = slice(i * step, (i + 1) * step)
        weight_b[own, :] = rest_ref[own, :].astype(bf16)
    copies[8].wait()
    copies[9].wait()


def load_state(middle, master, one, two, after):
    _, part, width = master.shape
    return pl.pallas_call(
        functools.partial(load_kernel, middle),
        in_specs=[ANY] + [HBM] * 3,
        out_specs=[VMEM] * 5,
        out_shape=[
            pltpu.VMEM((part, middle), f32),
            pltpu.VMEM((part, middle), bf16),
            pltpu.VMEM((part, middle), bf16),
            pltpu.VMEM((part, middle), bf16),
            pltpu.VMEM((part, width - middle), bf16),
        ],
        scratch_shapes=[
            pltpu.VMEM((part, width - middle), f32),
            pltpu.SemaphoreType.DMA((10,)),
        ],
        compiler_params=params(4 * part * (width - middle)),
        cost_estimate=cost(part * width, 14 * part * width),
    )(after, *in_hbm(master, one, two))


def mixed_place(index, shards):
    group = div_send(index)
    bits = shards.bit_length() - 1
    step = group & (shards - 1)
    return lax.shift_right_logical(group, bits), step, index - SEND * group


def mix_kernel(shards, *refs):
    parts, (out_hbm_ref, out_ref, sems) = refs[:shards], refs[shards:]
    part = parts[0].shape[1] // 3
    copies = []
    blocks = parts[0].shape[0] // ROWS
    some = min(blocks, 32 // shards)
    rows, packed = some * shards * SEND, some * shards * ROWS
    row = lax.broadcasted_iota(jnp.int32, (rows, packed), 0)
    col = lax.broadcasted_iota(jnp.int32, (rows, packed), 1)
    at, step, slot = mixed_place(row, shards)
    base = (step * some + at) * ROWS
    orders = [jnp.where(col == base + slot, 1.0, 0.0).astype(bf16)]
    for j in range(3):
        hit = (col == base + SEND + slot - 4 * j) & (slot >= 4 * j) & (slot < 4 * j + 4)
        orders.append(jnp.where(hit, 1.0, 0.0).astype(bf16))
    for first in range(0, blocks, some):
        stack = jnp.concatenate(
            [ref[first * ROWS : (first + some) * ROWS, :] for ref in parts], axis=0
        )
        own = slice(first * shards * SEND, (first + some) * shards * SEND)
        place = pl.ds(first * shards * SEND, some * shards * SEND)
        index = first // some

        def send(j):
            at = (place, pl.ds(j * part, part))
            copy = pltpu.make_async_copy(out_ref.at[at], out_hbm_ref.at[at], sems.at[j, index])
            copy.start()
            copies.append(copy)

        for j in range(3):
            out_ref[own, j * part : (j + 1) * part] = jnp.dot(
                orders[0], stack[:, j * part : (j + 1) * part], preferred_element_type=f32
            ).astype(bf16)
            send(j)
        tail = jnp.zeros((rows, part), f32)
        for j in range(3):
            tail += jnp.dot(
                orders[1 + j],
                stack[:, j * part : (j + 1) * part],
                preferred_element_type=f32,
            )
        out_ref[own, 3 * part :] = tail.astype(bf16)
        send(3)
    for copy in copies:
        copy.wait()


def mix(parts):
    shards = len(parts)
    rows, packed = parts[0].shape
    shape = (rows // ROWS * SEND * shards, packed // 3 * 4)
    return pl.pallas_call(
        functools.partial(mix_kernel, shards),
        in_specs=[VMEM] * shards,
        out_specs=HBM,
        out_shape=out_hbm(shape, bf16),
        scratch_shapes=[
            pltpu.VMEM(shape, bf16),
            pltpu.SemaphoreType.DMA((4, rows // ROWS // min(rows // ROWS, 32 // shards))),
        ],
        compiler_params=params(12 * rows * packed * shards),
        cost_estimate=cost(0, 5 * rows * packed * shards),
    )(*parts)


def reorder(arrived, rows_ref):
    count, width = rows_ref.shape
    part = width // 4
    total = arrived.shape[0]
    slot = lax.broadcasted_iota(jnp.int32, (count, total), 0)
    col = lax.broadcasted_iota(jnp.int32, (count, total), 1)
    order = jnp.where(col == slot + (ROWS - SEND) * div_send(slot), 1.0, 0.0).astype(bf16)
    rows_ref[:, : 3 * part] = jnp.dot(order, arrived, preferred_element_type=f32).astype(bf16)
    tail = jnp.zeros((count, part), f32)
    for j in range(3):
        tail += jnp.dot(
            tail_order(count, total, j, True),
            arrived[:, j * part : (j + 1) * part],
            preferred_element_type=f32,
        )
    rows_ref[:, 3 * part :] = tail.astype(bf16)


def times_weight(rows_ref, weight_ref):
    return lax.dot_general(
        rows_ref[...], weight_ref[...], (((1,), (1,)), ((), ())), preferred_element_type=f32
    )


def score_block(blocks, proj, hidden, picked):
    count = proj.shape[0]
    score = jnp.sum(proj * hidden.astype(f32), axis=1, keepdims=True)
    row = lax.broadcasted_iota(jnp.int32, (count, LANE), 0)
    lane = lax.broadcasted_iota(jnp.int32, (count, LANE), 1)
    spread = jnp.where(row - SEND * div_send(row) == lane, score, 0.0)
    high = spread.astype(bf16)
    rest = (spread - high.astype(f32)).astype(bf16)
    at = lax.broadcasted_iota(jnp.int32, (blocks, count), 1)
    gather = [jnp.where(div_send(at) == pick, 1.0, 0.0) for pick in picked]
    gather = jnp.concatenate(gather, axis=0).astype(bf16)
    value = jnp.dot(gather, high, preferred_element_type=f32)
    value += jnp.dot(gather, rest, preferred_element_type=f32)
    return [
        value[i * blocks : (i + 1) * blocks].reshape(blocks, 1, LANE)
        for i in range(len(picked))
    ]


def block_index(blocks, count):
    return lax.broadcasted_iota(jnp.int32, (blocks, count), 0)


def begin_kernel(blocks, arrived_ref, weight_ref, *refs):
    size = len(refs) - 7
    hidden, (rows_ref, hidden_ref, hidden_t, score_ref) = refs[:size], refs[size:-3]
    proj_hbm, proj_ref, sems = refs[-3:]
    count = rows_ref.shape[0]
    load = pltpu.make_async_copy(hidden[0], hidden_ref.at[pl.ds(0, count)], sems.at[1])
    load.start()
    for s in range(1, size):
        hidden_ref[s * count : (s + 1) * count] = hidden[s][...]
    reorder(arrived_ref[...], rows_ref)
    proj = times_weight(rows_ref, weight_ref)
    proj_ref[...] = proj
    copy = pltpu.make_async_copy(proj_ref, proj_hbm, sems.at[0])
    copy.start()
    load.wait()
    score_ref[...] = score_block(
        blocks, proj, hidden_ref[:count], [block_index(blocks, count)]
    )[0]
    transpose_rows([hidden_ref], hidden_t)
    copy.wait()


def begin(blocks, arrived, weight, hidden):
    count = blocks * SEND
    part, cols = weight.shape
    total = count * len(hidden)
    return pl.pallas_call(
        functools.partial(begin_kernel, blocks),
        in_specs=[VMEM] * 2 + [HBM] + [VMEM] * (len(hidden) - 1),
        out_specs=[VMEM] * 4 + [HBM],
        out_shape=[
            plain((count, cols), bf16),
            plain((total, part), bf16),
            plain((part, total), bf16),
            plain((blocks, 1, LANE), f32),
            out_hbm((count, part), f32),
        ],
        scratch_shapes=[
            pltpu.VMEM((count, part), f32),
            pltpu.SemaphoreType.DMA((2,)),
        ],
        compiler_params=params(8 * count * cols + 16 * total * part),
        cost_estimate=cost(4 * count * part * cols, 2 * part * cols),
    )(arrived, weight, *in_hbm(hidden[0]), *hidden[1:])


def finish_kernel(shards, blocks, arrived_ref, hidden_ref, weight_ref, *refs):
    before_hbm, refs = refs[: shards - 1], refs[shards - 1 :]
    score_in, projs = refs[:shards], refs[shards : 2 * shards]
    score_ref, before, sems = refs[2 * shards :]
    copies = [
        pltpu.make_async_copy(ref, before.at[s], sems.at[s])
        for s, ref in enumerate(before_hbm)
    ]
    for copy in copies:
        copy.start()
    proj = times_weight(arrived_ref, weight_ref)
    rounded = proj.astype(bf16)
    total = proj.shape[0]
    count = total // shards
    picked = [block_index(blocks, total) * shards + s for s in range(shards)]
    scores = score_block(blocks, proj, hidden_ref[...], picked)
    me = lax.axis_index("rep")
    slot = lax.broadcasted_iota(jnp.int32, (count, total), 0)
    row = lax.broadcasted_iota(jnp.int32, (count, total), 1)
    for s in range(shards):
        order = row == slot + SEND * (div_send(slot) * (shards - 1) + s)
        order = jnp.where(order, 1.0, 0.0).astype(bf16)
        own = jnp.dot(order, rounded, preferred_element_type=f32)
        if s > 0:
            copies[s - 1].wait()
            own += before[s - 1]
        projs[s][...] = own.astype(bf16)
        at = lax.rem(me + shards - s, shards)
        score_ref[pl.ds(at * blocks, blocks)] = score_in[s][...] + scores[s]


def finish(blocks, arrived, hidden, weight, before, scores):
    shards = len(scores)
    total, part = hidden.shape
    count = total // shards
    cols = weight.shape[1]
    outs = pl.pallas_call(
        functools.partial(finish_kernel, shards, blocks),
        in_specs=[VMEM] * 3 + [HBM] * len(before) + [VMEM] * shards,
        out_specs=[VMEM] * (shards + 1),
        out_shape=[plain((count, part), bf16)] * shards
        + [plain((shards * blocks, 1, LANE), f32)],
        scratch_shapes=[
            pltpu.VMEM((max(1, len(before)), count, part), f32),
            pltpu.SemaphoreType.DMA((max(1, len(before)),)),
        ],
        compiler_params=params(20 * total * part),
        cost_estimate=cost(2 * total * part * cols, 2 * part * cols),
    )(arrived, hidden, weight, *in_hbm(*before), *scores)
    return list(outs[:-1]), outs[-1]


def new_state(master, one, two, grad):
    corr_one = 1.0 - beta_one**adam_step
    corr_two = 1.0 - beta_two**adam_step
    rate = learn_rate * corr_two**0.5 / corr_one
    keep = 1.0 - learn_rate * decay_rate
    eps = adam_eps * corr_two**0.5
    m_new = beta_one * one.astype(f32) + (1.0 - beta_one) * grad
    v_new = beta_two * two.astype(f32) + (1.0 - beta_two) * (grad * grad)
    root = lax.rsqrt(v_new)
    below = v_new * root + eps
    inverse = root * (2.0 - below * root)
    master = keep * master - (rate * m_new) * inverse
    return master, m_new.astype(bf16), v_new.astype(bf16)


def update_rows(first, count, state, news, grad_ref):
    cols = grad_ref.shape[1]

    @pl.loop(0, count // ROWS)
    def _(i):
        own = pl.ds(pl.multiple_of(first + i * ROWS, ROWS), ROWS)
        for low in range(0, cols, UNIT):
            at = (own, slice(low, low + UNIT))
            values = new_state(*[ref[at] for ref in state], grad_ref[at])
            for ref, value in zip(news, values):
                ref[at] = value


def transpose_rows(hidden, hidden_t):
    base = 0
    for ref in hidden:
        high = base + ref.shape[0]
        hidden_t[:, base:high] = ref[...].astype(f32).T.astype(bf16)
        base = high


def form_grad(hidden_t, rows_refs, grad_ref):
    for low in range(0, grad_ref.shape[1], UNIT):
        own = slice(low, low + UNIT)
        base = 0
        grad = 0.0
        for rows_ref in rows_refs:
            high = base + rows_ref.shape[0]
            grad += jnp.dot(
                hidden_t[:, base:high], rows_ref[:, own], preferred_element_type=f32
            )
            base = high
        grad_ref[:, own] = grad


def state_copies(i, low, hbm, vmem, sems, into):
    part, cols = vmem[0].shape
    step = part // sems.shape[1]
    rows = pl.ds(pl.multiple_of(i * step, step), step)
    out = []
    for j, (far, near) in enumerate(zip(hbm, vmem)):
        ends = (far.at[0, rows, pl.ds(low, cols)], near.at[rows])
        source, target = ends if into else ends[::-1]
        out.append(pltpu.make_async_copy(source, target, sems.at[j, i]))
    return out


def settle_kernel(fresh, blocks, *refs):
    refs = list(refs)

    def take(number):
        out = refs[:number]
        del refs[:number]
        return out

    size = len(fresh)
    arrived = take(size)
    hidden_ref, hidden_t, given_ref, weight_ref, *state = take(7)
    scores, (mixed_ref,), projs_hbm, outs = take(size), take(1), take(size), take(3)
    news, rows_refs, projs = take(3), take(size), take(size)
    grad_ref, sems, proj_sems = refs
    part = grad_ref.shape[0]
    count = blocks * SEND
    shards = 1 + size
    for i in range(size):
        reorder(arrived[i][...], rows_refs[i])
    form_grad(hidden_t, [given_ref] + rows_refs, grad_ref)
    steps = sems.shape[1]
    step = part // steps

    @pl.loop(0, steps)
    def _(i):
        update_rows(i * step, step, state, news, grad_ref)
        for copy in state_copies(i, 0, outs, news, sems, False):
            copy.start()

    copies = []
    for i, s in enumerate(fresh):
        proj = times_weight(rows_refs[i], weight_ref)
        projs[i][...] = proj
        copies.append(pltpu.make_async_copy(projs[i], projs_hbm[i], proj_sems.at[i]))
        copies[i].start()
        scores[i][...] = score_block(
            blocks,
            proj,
            hidden_ref[s * count : (s + 1) * count],
            [block_index(blocks, count)],
        )[0]
    row = lax.broadcasted_iota(jnp.int32, (shards * count, count), 0)
    col = lax.broadcasted_iota(jnp.int32, (shards * count, count), 1)
    at, step_of, slot = mixed_place(row, shards)
    total = 0.0
    for s in range(shards):
        order = (step_of == s) & (col == at * SEND + slot)
        order = jnp.where(order, 1.0, 0.0).astype(bf16)
        own = hidden_ref[s * count : (s + 1) * count]
        total += jnp.dot(order, own, preferred_element_type=f32)
    mixed_ref[...] = total.astype(bf16)

    @pl.loop(0, steps)
    def _(i):
        for copy in state_copies(i, 0, outs, news, sems, False):
            copy.wait()

    for copy in copies:
        copy.wait()


def settle(blocks, arrived, given, hidden, hidden_t, weight, held, shapes):
    part, cols = weight.shape
    count = blocks * SEND
    fresh = tuple(range(1, 1 + len(arrived)))
    size = len(fresh)
    total = count * (1 + size)
    step = min(part, 128)
    args = [*arrived, hidden, hidden_t, given, weight, *held]
    near = [plain((blocks, 1, LANE), f32)] * size + [plain((total, part), bf16)]
    far = [out_hbm((count, part), f32)] * size
    far += [out_hbm(array.shape, array.dtype) for array in shapes]
    scratch = [pltpu.VMEM((part, cols), kind) for kind in (f32, bf16, bf16)]
    scratch += [pltpu.VMEM((count, cols), bf16)] * size
    scratch += [pltpu.VMEM((count, part), f32)] * size
    scratch += [
        pltpu.VMEM((part, cols), f32),
        pltpu.SemaphoreType.DMA((3, part // step)),
        pltpu.SemaphoreType.DMA((max(1, size),)),
    ]
    nbytes = 12 * part * cols + 4 * total * cols + 8 * total * part
    outs = pl.pallas_call(
        functools.partial(settle_kernel, fresh, blocks),
        in_specs=[VMEM] * len(args),
        out_specs=[VMEM] * len(near) + [HBM] * len(far),
        out_shape=near + far,
        scratch_shapes=scratch,
        compiler_params=params(nbytes),
        cost_estimate=cost(4 * total * part * cols, 16 * part * cols, part * cols),
    )(*args)
    outs = list(outs)
    return outs[:size], outs[size], outs[size + 1 : -3], outs[-3:]


def update_kernel(low, shards, hidden_ref, rows_ref, *refs):
    grad_refs, refs = refs[:shards], refs[shards:]
    factor_hbm, before_hbm, state_hbm, token_hbm = refs[0], refs[1], refs[2:5], refs[5:8]
    refs = refs[11:]
    outs, gate_out, place_ref, inverse_ref, refs = refs[:3], *refs[3:6], refs[6:]
    state, tokens, refs = refs[:3], refs[3:6], refs[6:]
    hidden_t, grad_ref, factor_ref, gate_new, before, in_sems, out_sems, sems = refs
    part = grad_ref.shape[0]
    steps = out_sems.shape[1]
    step = part // steps
    loads = in_sems.shape[1]
    gate_load = pltpu.make_async_copy(factor_hbm, factor_ref, sems.at[0])
    gate_store = pltpu.make_async_copy(gate_new, gate_out, sems.at[1])
    before_load = pltpu.make_async_copy(before_hbm, before, sems.at[5])
    token_loads = [
        pltpu.make_async_copy(source, target, sems.at[2 + i])
        for i, (source, target) in enumerate(zip(token_hbm, tokens))
    ]
    for copy in token_loads:
        copy.start()
    for i in range(loads):
        for copy in state_copies(i, low, state_hbm, state, in_sems, True):
            copy.start()
    gate_load.start()
    before_load.start()
    transpose_rows([hidden_ref], hidden_t)
    form_grad(hidden_t, [rows_ref], grad_ref)
    for copy in token_loads:
        copy.wait()
    ids, slots = tokens[0][...], tokens[1][...]
    live = ((ids & (EXP_LOCAL - 1)) == 0) & (slots >= 0)
    place_ref[...] = jnp.where(live, ids // EXP_LOCAL * SEND + slots, -1)
    inverse_ref[...] = 1.0 / tokens[2][...].astype(f32)

    for i in range(steps):
        if i % (steps // loads) == 0:
            for copy in state_copies(i * loads // steps, low, state_hbm, state, in_sems, True):
                copy.wait()
        update_rows(i * step, step, state, state, grad_ref)
        for copy in state_copies(i, low, outs, state, out_sems, False):
            copy.start()

    gate_load.wait()
    before_load.wait()
    for s, ref in enumerate(grad_refs):
        width = ref.shape[1]
        grad = ref[...].astype(f32)
        if s == 0:
            grad += before[...]
        for first in unit_columns(shards, s, width):
            own = pl.ds(first, width)
            gate_new[:, own] = (grad * factor_ref[:, own]).astype(bf16)
    gate_store.start()

    @pl.loop(0, steps)
    def _(i):
        for copy in state_copies(i, low, outs, state, out_sems, False):
            copy.wait()

    gate_store.wait()


def update(low, hidden, rows, grads, before, factors, state, tokens, done):
    total, part = hidden.shape
    cols = rows.shape[1]
    step = min(part, 128)
    shards = len(grads)
    scratch = [pltpu.VMEM((part, cols), kind) for kind in (f32, bf16, bf16)]
    scratch += [pltpu.VMEM(token.shape, token.dtype) for token in tokens]
    scratch += [pltpu.VMEM((part, total), bf16), pltpu.VMEM((part, cols), f32)]
    scratch += [pltpu.VMEM(factors.shape, kind) for kind in (f32, bf16)]
    scratch += [pltpu.VMEM(before.shape, f32)]
    steps = part // step
    scratch += [pltpu.SemaphoreType.DMA((3, count)) for count in (min(2, steps), steps)]
    scratch += [pltpu.SemaphoreType.DMA((6,))]
    return pl.pallas_call(
        functools.partial(update_kernel, low, shards),
        in_specs=[VMEM] * (2 + shards) + [HBM] * 11,
        out_specs=[HBM] * 4 + [VMEM] * 2,
        out_shape=[out_hbm(array.shape, array.dtype) for array in state]
        + [out_hbm(factors.shape, bf16)]
        + [plain(tokens[0].shape, kind) for kind in (jnp.int32, f32)],
        scratch_shapes=scratch,
        input_output_aliases={2 + shards + 8 + i: i for i in range(3)},
        compiler_params=params(12 * part * cols + 2 * total * part + 6 * factors.size),
        cost_estimate=cost(2 * total * part * cols, 16 * part * cols, part * cols),
    )(hidden, rows, *grads, *in_hbm(factors, before, *state, *tokens, *done))


def close_kernel(shards, place_ref, inverse_ref, score_ref, gate_ref):
    blocks = score_ref.shape[0] // shards
    score = score_ref[:blocks].reshape(blocks, LANE)
    for s in range(1, shards):
        score += score_ref[s * blocks : (s + 1) * blocks].reshape(blocks, LANE)
    high = score.astype(bf16)
    rest = (score - high.astype(f32)).astype(bf16)
    tok = place_ref.shape[1]
    lane = lax.broadcasted_iota(jnp.int32, (LANE, tok), 0)
    row = lax.broadcasted_iota(jnp.int32, (blocks, tok), 0)
    for k in range(place_ref.shape[0]):
        place = place_ref[k : k + 1]
        owner = div_send(place)
        pick = jnp.where(lane == place - SEND * owner, 1.0, 0.0).astype(bf16)
        value = jnp.dot(high, pick, preferred_element_type=f32)
        value += jnp.dot(rest, pick, preferred_element_type=f32)
        value = jnp.sum(jnp.where(row == owner, value, 0.0), axis=0, keepdims=True)
        gate_ref[k : k + 1] = value * inverse_ref[k : k + 1]


def close(shards, place, inverse, score):
    return pl.pallas_call(
        functools.partial(close_kernel, shards),
        in_specs=[VMEM] * 3,
        out_specs=VMEM,
        out_shape=plain(place.shape, f32),
        compiler_params=params(0),
        cost_estimate=cost(1 << 24, 1 << 16),
    )(place, inverse, score)


def per_device(out_grad, expert_ids, slots, gate_weights, saved_gate_up, master, moment1, moment2):
    ep_size = lax.axis_size("ep")
    rep_size = lax.axis_size("rep")
    ids_t, slots_t, gates_t = expert_ids.T, slots.T, gate_weights.T
    gate_up = saved_gate_up[0, 0]
    state = (master, moment1, moment2)
    edges = chunk_edges(out_grad.shape[1])
    steps = range(1, rep_size)

    def shift(value, step):
        perm = [(i, (i + step) % rep_size) for i in range(rep_size)]
        return lax.ppermute(value, "rep", perm)

    def exchange(value):
        return lax.all_to_all(value, "ep", split_axis=0, concat_axis=0, tiled=True)

    send_a, send_b = dispatch(ep_size, edges, ids_t, slots_t, gates_t, out_grad)
    mixed = [shift(send_b, s) for s in steps]
    parts, factors = hidden_parts(gate_up, rep_size, send_b)
    arrived = exchange(send_a.reshape(ep_size, ROWS, -1)).reshape(send_a.shape)
    hidden = [parts[0]] + [shift(parts[s], s) for s in steps]
    mixed = mix([send_b] + mixed)
    hidden[1:], mixed = lax.optimization_barrier((hidden[1:], mixed))
    arrived_b = exchange(mixed.reshape(ep_size, rep_size * SEND, -1)).reshape(mixed.shape)

    peers = [shift(arrived, s) for s in steps]
    *held, weight_a, weight_b = load_state(edges[1], *state, arrived)
    rows, hidden, hidden_t, score_own, proj = begin(ep_size, arrived, weight_a, hidden)
    scores, hidden_mixed, before, done = settle(
        ep_size, peers, rows, hidden, hidden_t, weight_a, held, state
    )
    projs, score = finish(
        ep_size, arrived_b, hidden_mixed, weight_b, before, [score_own] + scores
    )
    grads = [projs[0]] + [shift(projs[s], rep_size - s) for s in steps]
    score = lax.all_to_all(score, ("rep", "ep"), split_axis=0, concat_axis=0, tiled=True)

    tokens = (ids_t, slots_t, gates_t)
    *done, grad_gate_up, place, inverse = update(
        edges[1], hidden_mixed, arrived_b, grads, proj, factors, state, tokens, done
    )
    gate_grad = close(rep_size, place, inverse, score).T
    return (grad_gate_up.reshape(saved_gate_up.shape), gate_grad) + tuple(done)


def solution(mesh):
    in_specs = (
        P(("rep", "ep"), None),
        P(("rep", "ep"), None),
        P(("rep", "ep"), None),
        P(("rep", "ep"), None),
        P("rep", "ep", None, None),
        P("ep", "rep", None),
        P("ep", "rep", None),
        P("ep", "rep", None),
    )
    out_specs = (
        P("rep", "ep", None, None),
        P(("rep", "ep"), None),
        P("ep", "rep", None),
        P("ep", "rep", None),
        P("ep", "rep", None),
    )
    return jax.shard_map(
        per_device, mesh=mesh, in_specs=in_specs, out_specs=out_specs, check_vma=False
    )
```

```python
import functools

import jax
import jax.numpy as jnp
from jax import lax
from jax.experimental import pallas as pl
from jax.experimental.pallas import tpu as pltpu
from jax.sharding import PartitionSpec as P

TOPK = 8
EXP_LOCAL = 8
SEND = 12
LANE = 128
UNIT = 512
ROWS = 16

beta_one = 0.9
beta_two = 0.95
learn_rate = 0.002
decay_rate = 0.1
adam_eps = 1e-08
adam_step = 50

f32 = jnp.float32
bf16 = jnp.bfloat16
HBM = pl.BlockSpec(memory_space=pltpu.HBM)
ANY = pl.BlockSpec(memory_space=pl.ANY)
VMEM = pl.BlockSpec(memory_space=pltpu.VMEM)


def in_hbm(*arrays):
    return [pltpu.with_memory_space_constraint(array, pltpu.HBM) for array in arrays]


def plain(dims, dtype):
    return jax.ShapeDtypeStruct(tuple(dims), dtype)


def out_hbm(dims, dtype):
    return pltpu.HBM(tuple(dims), dtype)


def block(dims, at=None):
    at = at or (0,) * len(dims)
    return pl.BlockSpec(tuple(dims), lambda i: at, pipeline_mode=pl.Buffered(1))


def params(nbytes):
    mib = min(60, max(16, 10 + 5 * int(nbytes) // 2**22))
    return pltpu.CompilerParams(vmem_limit_bytes=mib * 2**20)


def cost(flops, nbytes, transcendentals=0):
    return pl.CostEstimate(
        flops=int(flops), bytes_accessed=int(nbytes), transcendentals=int(transcendentals)
    )


def div_send(index):
    return lax.shift_right_logical(index * 10923, 17)


def pack(cols):
    return cols // 4 * 3


def chunk_edges(width):
    units = width // UNIT
    return (0, (units - max(1, units * 3 // 7)) * UNIT, width)


def tail_order(count, total, j, slots_first):
    a = lax.broadcasted_iota(jnp.int32, (count, total), 0)
    b = lax.broadcasted_iota(jnp.int32, (count, total), 1)
    if slots_first:
        block_of = div_send(a)
        inner = a - SEND * block_of
        hit = b == block_of * ROWS + SEND + inner - 4 * j
    else:
        inner = (a & (ROWS - 1)) - SEND + 4 * j
        hit = (b == a - SEND + 4 * j) & ((a & (ROWS - 1)) >= SEND)
    return jnp.where(hit & (inner >= 4 * j) & (inner < 4 * j + 4), 1.0, 0.0).astype(bf16)


def dispatch_kernel(edges, ids_hbm, slots_hbm, gates_hbm, grad_hbm, *refs):
    outs, (ids_ref, slots_ref, gates_ref, grad_ref, sems) = refs[:2], refs[2:]
    pairs = [(ids_hbm, ids_ref), (slots_hbm, slots_ref), (gates_hbm, gates_ref)]
    for c in (1, 0):
        own = (slice(None), pl.ds(edges[c], edges[c + 1] - edges[c]))
        pairs.append((grad_hbm.at[own], grad_ref.at[own]))
    copies = [
        pltpu.make_async_copy(source, target, sems.at[i])
        for i, (source, target) in enumerate(pairs)
    ]
    for copy in copies:
        copy.start()
    rows = outs[0].shape[0]
    tok = ids_ref.shape[1]
    orders = [tail_order(rows, rows, j, False) for j in range(3)]
    for copy in copies[:3]:
        copy.wait()
    ids = ids_ref[...]
    slots = slots_ref[...]
    gates = gates_ref[...].astype(f32)
    live = ((ids & (EXP_LOCAL - 1)) == 0) & (slots >= 0)
    place = jnp.where(live, ids // EXP_LOCAL * ROWS + slots, -1)
    row = lax.broadcasted_iota(jnp.int32, (rows, tok), 0)
    main = jnp.zeros((rows, tok), f32)
    for k in range(TOPK):
        main = jnp.where(row == place[k : k + 1], gates[k : k + 1], main)
    main = main.astype(bf16)
    tails = [
        jnp.dot(order, main, preferred_element_type=f32).astype(bf16) for order in orders
    ]
    for c in (1, 0):
        copies[4 - c].wait()
        low, high = edges[c], edges[c + 1]
        part = (high - low) // 4
        for j in range(3):
            total = jnp.dot(
                main,
                grad_ref[:, low + j * part : low + (j + 1) * part],
                preferred_element_type=f32,
            )
            total += jnp.dot(
                tails[j], grad_ref[:, low + 3 * part : high], preferred_element_type=f32
            )
            outs[c][:, j * part : (j + 1) * part] = total.astype(bf16)


def dispatch(blocks, edges, ids, slots, gates, out_grad):
    tok, width = out_grad.shape
    rows = blocks * ROWS
    shapes = [(rows, pack(high - low)) for low, high in zip(edges[:-1], edges[1:])]
    return pl.pallas_call(
        functools.partial(dispatch_kernel, edges),
        in_specs=[HBM] * 4,
        out_specs=[VMEM] * 2,
        out_shape=[plain(shape, bf16) for shape in shapes],
        scratch_shapes=[
            pltpu.VMEM(ids.shape, jnp.int32),
            pltpu.VMEM(slots.shape, jnp.int32),
            pltpu.VMEM(gates.shape, bf16),
            pltpu.VMEM(out_grad.shape, bf16),
            pltpu.SemaphoreType.DMA((5,)),
        ],
        compiler_params=params(2 * rows * width + 2 * tok * width),
        cost_estimate=cost(2 * rows * tok * width, 4 * tok * width),
    )(*in_hbm(ids, slots, gates, out_grad))


def unit_columns(shards, step, part):
    at = lax.rem(lax.axis_index("rep") + step, shards)
    return pl.multiple_of(at * part, part), pl.multiple_of((shards + at) * part, part)


def hidden_kernel(gate_up_ref, after_ref, *refs):
    del after_ref
    out_refs, factor_ref = refs[:-1], refs[-1]
    for s, out_ref in enumerate(out_refs):
        part = out_ref.shape[1]
        low, high = unit_columns(len(out_refs), s, part)
        gate = gate_up_ref[:, pl.ds(low, part)].astype(f32)
        up = gate_up_ref[:, pl.ds(high, part)].astype(f32)
        sig = jax.nn.sigmoid(gate)
        silu = gate * sig
        out_ref[...] = (silu * up).astype(bf16)
        factor_ref[:, pl.ds(low, part)] = up * sig * (1.0 + gate * (1.0 - sig))
        factor_ref[:, pl.ds(high, part)] = silu


def hidden_parts(gate_up, shards, after):
    slots, width = gate_up.shape
    shape = (slots, width // 2 // shards)
    outs = pl.pallas_call(
        hidden_kernel,
        grid=(1,),
        in_specs=[block(gate_up.shape), ANY],
        out_specs=[block(shape)] * shards + [block(gate_up.shape)],
        out_shape=[out_hbm(shape, bf16)] * shards + [out_hbm(gate_up.shape, f32)],
        compiler_params=params(7 * slots * width),
        cost_estimate=cost(8 * slots * width, 7 * slots * width, slots * width),
    )(*in_hbm(gate_up), after)
    return list(outs[:-1]), outs[-1]


def load_kernel(middle, after_ref, master_hbm, one_hbm, two_hbm, *refs):
    del after_ref
    master_ref, one_ref, two_ref, weight_a, weight_b, rest_ref, sems = refs
    part = master_ref.shape[0]
    rest = rest_ref.shape[1]
    step = part // 4
    copies = []
    for i in range(4):
        own = pl.ds(i * step, step)
        copies.append(
            pltpu.make_async_copy(
                master_hbm.at[0, own, pl.ds(0, middle)], master_ref.at[own], sems.at[i]
            )
        )
    for i in range(4):
        own = pl.ds(i * step, step)
        copies.append(
            pltpu.make_async_copy(
                master_hbm.at[0, own, pl.ds(middle, rest)], rest_ref.at[own], sems.at[4 + i]
            )
        )
    for i, (source, target) in enumerate([(one_hbm, one_ref), (two_hbm, two_ref)]):
        copies.append(
            pltpu.make_async_copy(source.at[0, :, pl.ds(0, middle)], target, sems.at[8 + i])
        )
    for copy in copies:
        copy.start()
    for i in range(4):
        copies[i].wait()
        own = slice(i * step, (i + 1) * step)
        weight_a[own, :] = master_ref[own, :].astype(bf16)
    for i in range(4):
        copies[4 + i].wait()
        own = slice(i * step, (i + 1) * step)
        weight_b[own, :] = rest_ref[own, :].astype(bf16)
    copies[8].wait()
    copies[9].wait()


def load_state(middle, master, one, two, after):
    _, part, width = master.shape
    return pl.pallas_call(
        functools.partial(load_kernel, middle),
        in_specs=[ANY] + [HBM] * 3,
        out_specs=[VMEM] * 5,
        out_shape=[
            pltpu.VMEM((part, middle), f32),
            pltpu.VMEM((part, middle), bf16),
            pltpu.VMEM((part, middle), bf16),
            pltpu.VMEM((part, middle), bf16),
            pltpu.VMEM((part, width - middle), bf16),
        ],
        scratch_shapes=[
            pltpu.VMEM((part, width - middle), f32),
            pltpu.SemaphoreType.DMA((10,)),
        ],
        compiler_params=params(4 * part * (width - middle)),
        cost_estimate=cost(part * width, 14 * part * width),
    )(after, *in_hbm(master, one, two))


def mixed_place(index, shards):
    group = div_send(index)
    bits = shards.bit_length() - 1
    step = group & (shards - 1)
    return lax.shift_right_logical(group, bits), step, index - SEND * group


def mix_kernel(shards, *refs):
    parts, (out_hbm_ref, out_ref, sems) = refs[:shards], refs[shards:]
    part = parts[0].shape[1] // 3
    copies = []
    blocks = parts[0].shape[0] // ROWS
    some = min(blocks, 32 // shards)
    rows, packed = some * shards * SEND, some * shards * ROWS
    row = lax.broadcasted_iota(jnp.int32, (rows, packed), 0)
    col = lax.broadcasted_iota(jnp.int32, (rows, packed), 1)
    at, step, slot = mixed_place(row, shards)
    base = (step * some + at) * ROWS
    orders = [jnp.where(col == base + slot, 1.0, 0.0).astype(bf16)]
    for j in range(3):
        hit = (col == base + SEND + slot - 4 * j) & (slot >= 4 * j) & (slot < 4 * j + 4)
        orders.append(jnp.where(hit, 1.0, 0.0).astype(bf16))
    for first in range(0, blocks, some):
        stack = jnp.concatenate(
            [ref[first * ROWS : (first + some) * ROWS, :] for ref in parts], axis=0
        )
        own = slice(first * shards * SEND, (first + some) * shards * SEND)
        place = pl.ds(first * shards * SEND, some * shards * SEND)
        index = first // some

        def send(j):
            at = (place, pl.ds(j * part, part))
            copy = pltpu.make_async_copy(out_ref.at[at], out_hbm_ref.at[at], sems.at[j, index])
            copy.start()
            copies.append(copy)

        for j in range(3):
            out_ref[own, j * part : (j + 1) * part] = jnp.dot(
                orders[0], stack[:, j * part : (j + 1) * part], preferred_element_type=f32
            ).astype(bf16)
            send(j)
        tail = jnp.zeros((rows, part), f32)
        for j in range(3):
            tail += jnp.dot(
                orders[1 + j],
                stack[:, j * part : (j + 1) * part],
                preferred_element_type=f32,
            )
        out_ref[own, 3 * part :] = tail.astype(bf16)
        send(3)
    for copy in copies:
        copy.wait()


def mix(parts):
    shards = len(parts)
    rows, packed = parts[0].shape
    shape = (rows // ROWS * SEND * shards, packed // 3 * 4)
    return pl.pallas_call(
        functools.partial(mix_kernel, shards),
        in_specs=[VMEM] * shards,
        out_specs=HBM,
        out_shape=out_hbm(shape, bf16),
        scratch_shapes=[
            pltpu.VMEM(shape, bf16),
            pltpu.SemaphoreType.DMA((4, rows // ROWS // min(rows // ROWS, 32 // shards))),
        ],
        compiler_params=params(12 * rows * packed * shards),
        cost_estimate=cost(0, 5 * rows * packed * shards),
    )(*parts)


def reorder(arrived, rows_ref):
    count, width = rows_ref.shape
    part = width // 4
    total = arrived.shape[0]
    slot = lax.broadcasted_iota(jnp.int32, (count, total), 0)
    col = lax.broadcasted_iota(jnp.int32, (count, total), 1)
    order = jnp.where(col == slot + (ROWS - SEND) * div_send(slot), 1.0, 0.0).astype(bf16)
    rows_ref[:, : 3 * part] = jnp.dot(order, arrived, preferred_element_type=f32).astype(bf16)
    tail = jnp.zeros((count, part), f32)
    for j in range(3):
        tail += jnp.dot(
            tail_order(count, total, j, True),
            arrived[:, j * part : (j + 1) * part],
            preferred_element_type=f32,
        )
    rows_ref[:, 3 * part :] = tail.astype(bf16)


def times_weight(rows_ref, weight_ref):
    return lax.dot_general(
        rows_ref[...], weight_ref[...], (((1,), (1,)), ((), ())), preferred_element_type=f32
    )


def score_block(blocks, proj, hidden, picked):
    count = proj.shape[0]
    score = jnp.sum(proj * hidden.astype(f32), axis=1, keepdims=True)
    row = lax.broadcasted_iota(jnp.int32, (count, LANE), 0)
    lane = lax.broadcasted_iota(jnp.int32, (count, LANE), 1)
    spread = jnp.where(row - SEND * div_send(row) == lane, score, 0.0)
    high = spread.astype(bf16)
    rest = (spread - high.astype(f32)).astype(bf16)
    at = lax.broadcasted_iota(jnp.int32, (blocks, count), 1)
    gather = [jnp.where(div_send(at) == pick, 1.0, 0.0) for pick in picked]
    gather = jnp.concatenate(gather, axis=0).astype(bf16)
    value = jnp.dot(gather, high, preferred_element_type=f32)
    value += jnp.dot(gather, rest, preferred_element_type=f32)
    return [
        value[i * blocks : (i + 1) * blocks].reshape(blocks, 1, LANE)
        for i in range(len(picked))
    ]


def block_index(blocks, count):
    return lax.broadcasted_iota(jnp.int32, (blocks, count), 0)


def begin_kernel(blocks, arrived_ref, weight_ref, *refs):
    size = len(refs) - 7
    hidden, (rows_ref, hidden_ref, hidden_t, score_ref) = refs[:size], refs[size:-3]
    proj_hbm, proj_ref, sems = refs[-3:]
    count = rows_ref.shape[0]
    load = pltpu.make_async_copy(hidden[0], hidden_ref.at[pl.ds(0, count)], sems.at[1])
    load.start()
    for s in range(1, size):
        hidden_ref[s * count : (s + 1) * count] = hidden[s][...]
    reorder(arrived_ref[...], rows_ref)
    proj = times_weight(rows_ref, weight_ref)
    proj_ref[...] = proj
    copy = pltpu.make_async_copy(proj_ref, proj_hbm, sems.at[0])
    copy.start()
    load.wait()
    score_ref[...] = score_block(
        blocks, proj, hidden_ref[:count], [block_index(blocks, count)]
    )[0]
    transpose_rows([hidden_ref], hidden_t)
    copy.wait()


def begin(blocks, arrived, weight, hidden):
    count = blocks * SEND
    part, cols = weight.shape
    total = count * len(hidden)
    return pl.pallas_call(
        functools.partial(begin_kernel, blocks),
        in_specs=[VMEM] * 2 + [HBM] + [VMEM] * (len(hidden) - 1),
        out_specs=[VMEM] * 4 + [HBM],
        out_shape=[
            plain((count, cols), bf16),
            plain((total, part), bf16),
            plain((part, total), bf16),
            plain((blocks, 1, LANE), f32),
            out_hbm((count, part), f32),
        ],
        scratch_shapes=[
            pltpu.VMEM((count, part), f32),
            pltpu.SemaphoreType.DMA((2,)),
        ],
        compiler_params=params(8 * count * cols + 16 * total * part),
        cost_estimate=cost(4 * count * part * cols, 2 * part * cols),
    )(arrived, weight, *in_hbm(hidden[0]), *hidden[1:])


def finish_kernel(shards, blocks, arrived_ref, hidden_ref, weight_ref, *refs):
    before_hbm, score_in = refs[:shards], refs[shards : 2 * shards]
    projs, (score_ref, before, sems) = refs[2 * shards : 3 * shards], refs[3 * shards :]
    copies = [
        pltpu.make_async_copy(ref, before.at[s], sems.at[s])
        for s, ref in enumerate(before_hbm)
    ]
    for copy in copies:
        copy.start()
    proj = times_weight(arrived_ref, weight_ref)
    rounded = proj.astype(bf16)
    total = proj.shape[0]
    count = total // shards
    picked = [block_index(blocks, total) * shards + s for s in range(shards)]
    scores = score_block(blocks, proj, hidden_ref[...], picked)
    me = lax.axis_index("rep")
    slot = lax.broadcasted_iota(jnp.int32, (count, total), 0)
    row = lax.broadcasted_iota(jnp.int32, (count, total), 1)
    for s in range(shards):
        order = row == slot + SEND * (div_send(slot) * (shards - 1) + s)
        order = jnp.where(order, 1.0, 0.0).astype(bf16)
        own = jnp.dot(order, rounded, preferred_element_type=f32)
        copies[s].wait()
        own += before[s]
        projs[s][...] = own.astype(bf16)
        at = lax.rem(me + shards - s, shards)
        score_ref[pl.ds(at * blocks, blocks)] = score_in[s][...] + scores[s]


def finish(blocks, arrived, hidden, weight, before, scores):
    shards = len(before)
    total, part = hidden.shape
    count = total // shards
    cols = weight.shape[1]
    outs = pl.pallas_call(
        functools.partial(finish_kernel, shards, blocks),
        in_specs=[VMEM] * 3 + [HBM] * shards + [VMEM] * shards,
        out_specs=[VMEM] * (shards + 1),
        out_shape=[plain((count, part), bf16)] * shards
        + [plain((shards * blocks, 1, LANE), f32)],
        scratch_shapes=[
            pltpu.VMEM((shards, count, part), f32),
            pltpu.SemaphoreType.DMA((shards,)),
        ],
        compiler_params=params(20 * total * part),
        cost_estimate=cost(2 * total * part * cols, 2 * part * cols),
    )(arrived, hidden, weight, *in_hbm(*before), *scores)
    return list(outs[:-1]), outs[-1]


def new_state(master, one, two, grad):
    corr_one = 1.0 - beta_one**adam_step
    corr_two = 1.0 - beta_two**adam_step
    rate = learn_rate * corr_two**0.5 / corr_one
    keep = 1.0 - learn_rate * decay_rate
    eps = adam_eps * corr_two**0.5
    m_new = beta_one * one.astype(f32) + (1.0 - beta_one) * grad
    v_new = beta_two * two.astype(f32) + (1.0 - beta_two) * (grad * grad)
    root = lax.rsqrt(v_new)
    below = v_new * root + eps
    inverse = root * (2.0 - below * root)
    master = keep * master - (rate * m_new) * inverse
    return master, m_new.astype(bf16), v_new.astype(bf16)


def update_rows(first, count, state, news, grad_ref):
    cols = grad_ref.shape[1]

    @pl.loop(0, count // ROWS)
    def _(i):
        own = pl.ds(pl.multiple_of(first + i * ROWS, ROWS), ROWS)
        for low in range(0, cols, UNIT):
            at = (own, slice(low, low + UNIT))
            values = new_state(*[ref[at] for ref in state], grad_ref[at])
            for ref, value in zip(news, values):
                ref[at] = value


def transpose_rows(hidden, hidden_t):
    base = 0
    for ref in hidden:
        high = base + ref.shape[0]
        hidden_t[:, base:high] = ref[...].astype(f32).T.astype(bf16)
        base = high


def form_grad(hidden_t, rows_refs, grad_ref):
    for low in range(0, grad_ref.shape[1], UNIT):
        own = slice(low, low + UNIT)
        base = 0
        grad = 0.0
        for rows_ref in rows_refs:
            high = base + rows_ref.shape[0]
            grad += jnp.dot(
                hidden_t[:, base:high], rows_ref[:, own], preferred_element_type=f32
            )
            base = high
        grad_ref[:, own] = grad


def state_copies(i, low, hbm, vmem, sems, into):
    part, cols = vmem[0].shape
    step = part // sems.shape[1]
    rows = pl.ds(pl.multiple_of(i * step, step), step)
    out = []
    for j, (far, near) in enumerate(zip(hbm, vmem)):
        ends = (far.at[0, rows, pl.ds(low, cols)], near.at[rows])
        source, target = ends if into else ends[::-1]
        out.append(pltpu.make_async_copy(source, target, sems.at[j, i]))
    return out


def settle_kernel(fresh, blocks, *refs):
    refs = list(refs)

    def take(number):
        out = refs[:number]
        del refs[:number]
        return out

    size = len(fresh)
    arrived = take(size)
    hidden_ref, hidden_t, given_ref, weight_ref, *state = take(7)
    scores, (mixed_ref,), projs_hbm, outs = take(size), take(1), take(size), take(3)
    news, rows_refs, projs = take(3), take(size), take(size)
    grad_ref, sems, proj_sems = refs
    part = grad_ref.shape[0]
    count = blocks * SEND
    shards = 1 + size
    for i in range(size):
        reorder(arrived[i][...], rows_refs[i])
    form_grad(hidden_t, [given_ref] + rows_refs, grad_ref)
    steps = sems.shape[1]
    step = part // steps

    @pl.loop(0, steps)
    def _(i):
        update_rows(i * step, step, state, news, grad_ref)
        for copy in state_copies(i, 0, outs, news, sems, False):
            copy.start()

    copies = []
    for i, s in enumerate(fresh):
        proj = times_weight(rows_refs[i], weight_ref)
        projs[i][...] = proj
        copies.append(pltpu.make_async_copy(projs[i], projs_hbm[i], proj_sems.at[i]))
        copies[i].start()
        scores[i][...] = score_block(
            blocks,
            proj,
            hidden_ref[s * count : (s + 1) * count],
            [block_index(blocks, count)],
        )[0]
    row = lax.broadcasted_iota(jnp.int32, (shards * count, count), 0)
    col = lax.broadcasted_iota(jnp.int32, (shards * count, count), 1)
    at, step_of, slot = mixed_place(row, shards)
    total = 0.0
    for s in range(shards):
        order = (step_of == s) & (col == at * SEND + slot)
        order = jnp.where(order, 1.0, 0.0).astype(bf16)
        own = hidden_ref[s * count : (s + 1) * count]
        total += jnp.dot(order, own, preferred_element_type=f32)
    mixed_ref[...] = total.astype(bf16)

    @pl.loop(0, steps)
    def _(i):
        for copy in state_copies(i, 0, outs, news, sems, False):
            copy.wait()

    for copy in copies:
        copy.wait()


def settle(blocks, arrived, given, hidden, hidden_t, weight, held, shapes):
    part, cols = weight.shape
    count = blocks * SEND
    fresh = tuple(range(1, 1 + len(arrived)))
    size = len(fresh)
    total = count * (1 + size)
    step = min(part, 128)
    args = [*arrived, hidden, hidden_t, given, weight, *held]
    near = [plain((blocks, 1, LANE), f32)] * size + [plain((total, part), bf16)]
    far = [out_hbm((count, part), f32)] * size
    far += [out_hbm(array.shape, array.dtype) for array in shapes]
    scratch = [pltpu.VMEM((part, cols), kind) for kind in (f32, bf16, bf16)]
    scratch += [pltpu.VMEM((count, cols), bf16)] * size
    scratch += [pltpu.VMEM((count, part), f32)] * size
    scratch += [
        pltpu.VMEM((part, cols), f32),
        pltpu.SemaphoreType.DMA((3, part // step)),
        pltpu.SemaphoreType.DMA((max(1, size),)),
    ]
    nbytes = 12 * part * cols + 4 * total * cols + 8 * total * part
    outs = pl.pallas_call(
        functools.partial(settle_kernel, fresh, blocks),
        in_specs=[VMEM] * len(args),
        out_specs=[VMEM] * len(near) + [HBM] * len(far),
        out_shape=near + far,
        scratch_shapes=scratch,
        compiler_params=params(nbytes),
        cost_estimate=cost(4 * total * part * cols, 16 * part * cols, part * cols),
    )(*args)
    outs = list(outs)
    return outs[:size], outs[size], outs[size + 1 : -3], outs[-3:]


def update_kernel(low, shards, hidden_ref, rows_ref, *refs):
    grad_refs, refs = refs[:shards], refs[shards:]
    factor_hbm, state_hbm, token_hbm, refs = refs[0], refs[1:4], refs[4:7], refs[10:]
    outs, gate_out, place_ref, inverse_ref, refs = refs[:3], *refs[3:6], refs[6:]
    state, tokens, refs = refs[:3], refs[3:6], refs[6:]
    hidden_t, grad_ref, factor_ref, gate_new, in_sems, out_sems, sems = refs
    part = grad_ref.shape[0]
    steps = out_sems.shape[1]
    step = part // steps
    loads = in_sems.shape[1]
    gate_load = pltpu.make_async_copy(factor_hbm, factor_ref, sems.at[0])
    gate_store = pltpu.make_async_copy(gate_new, gate_out, sems.at[1])
    gate_load.start()
    token_loads = [
        pltpu.make_async_copy(source, target, sems.at[2 + i])
        for i, (source, target) in enumerate(zip(token_hbm, tokens))
    ]
    for copy in token_loads:
        copy.start()
    for i in range(loads):
        for copy in state_copies(i, low, state_hbm, state, in_sems, True):
            copy.start()
    transpose_rows([hidden_ref], hidden_t)
    form_grad(hidden_t, [rows_ref], grad_ref)
    for copy in token_loads:
        copy.wait()
    ids, slots = tokens[0][...], tokens[1][...]
    live = ((ids & (EXP_LOCAL - 1)) == 0) & (slots >= 0)
    place_ref[...] = jnp.where(live, ids // EXP_LOCAL * SEND + slots, -1)
    inverse_ref[...] = 1.0 / tokens[2][...].astype(f32)

    for i in range(steps):
        if i % (steps // loads) == 0:
            for copy in state_copies(i * loads // steps, low, state_hbm, state, in_sems, True):
                copy.wait()
        update_rows(i * step, step, state, state, grad_ref)
        for copy in state_copies(i, low, outs, state, out_sems, False):
            copy.start()

    gate_load.wait()
    for s, ref in enumerate(grad_refs):
        width = ref.shape[1]
        grad = ref[...].astype(f32)
        for first in unit_columns(shards, s, width):
            own = pl.ds(first, width)
            gate_new[:, own] = (grad * factor_ref[:, own]).astype(bf16)
    gate_store.start()

    @pl.loop(0, steps)
    def _(i):
        for copy in state_copies(i, low, outs, state, out_sems, False):
            copy.wait()

    gate_store.wait()


def update(low, hidden, rows, grads, factors, state, tokens, done):
    total, part = hidden.shape
    cols = rows.shape[1]
    step = min(part, 128)
    shards = len(grads)
    scratch = [pltpu.VMEM((part, cols), kind) for kind in (f32, bf16, bf16)]
    scratch += [pltpu.VMEM(token.shape, token.dtype) for token in tokens]
    scratch += [pltpu.VMEM((part, total), bf16), pltpu.VMEM((part, cols), f32)]
    scratch += [pltpu.VMEM(factors.shape, kind) for kind in (f32, bf16)]
    steps = part // step
    scratch += [pltpu.SemaphoreType.DMA((3, count)) for count in (min(2, steps), steps)]
    scratch += [pltpu.SemaphoreType.DMA((5,))]
    return pl.pallas_call(
        functools.partial(update_kernel, low, shards),
        in_specs=[VMEM] * (2 + shards) + [HBM] * 10,
        out_specs=[HBM] * 4 + [VMEM] * 2,
        out_shape=[out_hbm(array.shape, array.dtype) for array in state]
        + [out_hbm(factors.shape, bf16)]
        + [plain(tokens[0].shape, kind) for kind in (jnp.int32, f32)],
        scratch_shapes=scratch,
        input_output_aliases={2 + shards + 7 + i: i for i in range(3)},
        compiler_params=params(12 * part * cols + 2 * total * part + 6 * factors.size),
        cost_estimate=cost(2 * total * part * cols, 16 * part * cols, part * cols),
    )(hidden, rows, *grads, *in_hbm(factors, *state, *tokens, *done))


def close_kernel(shards, place_ref, inverse_ref, score_ref, gate_ref):
    blocks = score_ref.shape[0] // shards
    score = score_ref[:blocks].reshape(blocks, LANE)
    for s in range(1, shards):
        score += score_ref[s * blocks : (s + 1) * blocks].reshape(blocks, LANE)
    high = score.astype(bf16)
    rest = (score - high.astype(f32)).astype(bf16)
    tok = place_ref.shape[1]
    lane = lax.broadcasted_iota(jnp.int32, (LANE, tok), 0)
    row = lax.broadcasted_iota(jnp.int32, (blocks, tok), 0)
    for k in range(place_ref.shape[0]):
        place = place_ref[k : k + 1]
        owner = div_send(place)
        pick = jnp.where(lane == place - SEND * owner, 1.0, 0.0).astype(bf16)
        value = jnp.dot(high, pick, preferred_element_type=f32)
        value += jnp.dot(rest, pick, preferred_element_type=f32)
        value = jnp.sum(jnp.where(row == owner, value, 0.0), axis=0, keepdims=True)
        gate_ref[k : k + 1] = value * inverse_ref[k : k + 1]


def close(shards, place, inverse, score):
    return pl.pallas_call(
        functools.partial(close_kernel, shards),
        in_specs=[VMEM] * 3,
        out_specs=VMEM,
        out_shape=plain(place.shape, f32),
        compiler_params=params(0),
        cost_estimate=cost(1 << 24, 1 << 16),
    )(place, inverse, score)


def per_device(out_grad, expert_ids, slots, gate_weights, saved_gate_up, master, moment1, moment2):
    ep_size = lax.axis_size("ep")
    rep_size = lax.axis_size("rep")
    ids_t, slots_t, gates_t = expert_ids.T, slots.T, gate_weights.T
    gate_up = saved_gate_up[0, 0]
    state = (master, moment1, moment2)
    edges = chunk_edges(out_grad.shape[1])
    steps = range(1, rep_size)

    def shift(value, step):
        perm = [(i, (i + step) % rep_size) for i in range(rep_size)]
        return lax.ppermute(value, "rep", perm)

    def exchange(value):
        return lax.all_to_all(value, "ep", split_axis=0, concat_axis=0, tiled=True)

    send_a, send_b = dispatch(ep_size, edges, ids_t, slots_t, gates_t, out_grad)
    mixed = [shift(send_b, s) for s in steps]
    parts, factors = hidden_parts(gate_up, rep_size, send_b)
    arrived = exchange(send_a.reshape(ep_size, ROWS, -1)).reshape(send_a.shape)
    hidden = [parts[0]] + [shift(parts[s], s) for s in steps]
    mixed = mix([send_b] + mixed)
    hidden[1:], mixed = lax.optimization_barrier((hidden[1:], mixed))
    arrived_b = exchange(mixed.reshape(ep_size, rep_size * SEND, -1)).reshape(mixed.shape)

    peers = [shift(arrived, s) for s in steps]
    *held, weight_a, weight_b = load_state(edges[1], *state, arrived)
    rows, hidden, hidden_t, score_own, proj = begin(ep_size, arrived, weight_a, hidden)
    scores, hidden_mixed, before, done = settle(
        ep_size, peers, rows, hidden, hidden_t, weight_a, held, state
    )
    projs, score = finish(
        ep_size, arrived_b, hidden_mixed, weight_b, [proj] + before, [score_own] + scores
    )
    grads = [projs[0]] + [shift(projs[s], rep_size - s) for s in steps]
    score = lax.all_to_all(score, ("rep", "ep"), split_axis=0, concat_axis=0, tiled=True)

    tokens = (ids_t, slots_t, gates_t)
    *done, grad_gate_up, place, inverse = update(
        edges[1], hidden_mixed, arrived_b, grads, factors, state, tokens, done
    )
    gate_grad = close(rep_size, place, inverse, score).T
    return (grad_gate_up.reshape(saved_gate_up.shape), gate_grad) + tuple(done)


def solution(mesh):
    in_specs = (
        P(("rep", "ep"), None),
        P(("rep", "ep"), None),
        P(("rep", "ep"), None),
        P(("rep", "ep"), None),
        P("rep", "ep", None, None),
        P("ep", "rep", None),
        P("ep", "rep", None),
        P("ep", "rep", None),
    )
    out_specs = (
        P("rep", "ep", None, None),
        P(("rep", "ep"), None),
        P("ep", "rep", None),
        P("ep", "rep", None),
        P("ep", "rep", None),
    )
    return jax.shard_map(
        per_device, mesh=mesh, in_specs=in_specs, out_specs=out_specs, check_vma=False
    )
```
